32 devices in a mesh: ctx: 8 (over z, y), head: 4 (over x, core).
Axes of the slice: x: 2, y: 2, z: 4, core: 2. Of those that a mesh axis runs over, the one named last changes fastest.
Arguments:
- queries: bfloat16 [16384, 4, 128], P('ctx', 'head'), may hold values from -4 to 4
- keys: bfloat16 [16384, 128], P('ctx'), may hold values from -5 to 5
- values: bfloat16 [16384, 128], P('ctx'), may hold values from -6 to 6
- dout: bfloat16 [16384, 4, 128], P('ctx', 'head'), may hold values from -6 to 6
- selected: int32 [32, 3], P('ctx'), may hold values from 0 to 30, as said below
Outputs:
- grad_queries: bfloat16 [16384, 4, 128], P('ctx', 'head')
- grad_keys: bfloat16 [16384, 128], P('ctx')
- grad_values: bfloat16 [16384, 128], P('ctx')
The draws below stay inside these ranges and needn't reach their ends.
Inputs may be any that keep to these rules, and one draw needn't show every extreme that they name: `selected`: each entry of row g is either g itself, meaning no block, or an earlier block (below g); the entries of a row that are not g differ; g itself appears only in rows that have fewer than 3 earlier blocks to choose from. Over the 4 rows of one index of ctx, all entries that lie on one other index of ctx (block // 4) name the same block, so one index of ctx reads at most one block from each other index. Every row from 4 on names exactly one block among the first 4. The last row names block 30.
All inputs are finite; a program needn't handle non-finite values.
Results may differ from the reference program's by a relative error of at most 0.015.
Values may be sent and summed in bfloat16 or wider, within the bound.
No kernel may reach another device: no remote copies, remote signals or barrier semaphores. Data moves between devices by JAX's collectives and lax.ppermute only.
A program may use at most 192 MiB of HBM per device.

```python
import math
import jax
import jax.numpy as jnp
from jax import lax

D_HEAD = 128
TOP = 3
BLK_DEV = 4
HEADS = 4
SEQ = 16384
NBLK = 32


def draw_queries(key, part):
    base_key = jax.random.fold_in(key, 21)
    result = jnp.clip(jax.random.normal(base_key, (SEQ, HEADS, D_HEAD), jnp.float32), -4.0, 4.0)
    return result.astype(jnp.bfloat16)


def draw_keys(key, part):
    base_key = jax.random.fold_in(key, 33)
    result = jnp.clip(jax.random.normal(base_key, (SEQ, D_HEAD), jnp.float32), -4.0, 4.0)
    return result.astype(jnp.bfloat16)


def draw_selected(key, part):
    blocks_all = NBLK
    devices = NBLK // BLK_DEV
    pick_key = jax.random.fold_in(key, 45)
    rank_key = jax.random.fold_in(key, 46)
    picks = jax.random.randint(pick_key, (devices, devices), 0, BLK_DEV)
    rows = jnp.arange(blocks_all, dtype=jnp.int32)
    cols = jnp.arange(blocks_all, dtype=jnp.int32)
    row_dev = rows // BLK_DEV
    col_owner = cols // BLK_DEV
    cand_hit = (cols % BLK_DEV)[None, :] == picks[row_dev[:, None], col_owner[None, :]]
    eligible = (cols[None, :] < rows[:, None]) & ((col_owner[None, :] == row_dev[:, None]) | cand_hit)
    forced = (col_owner[None, :] == 0) & cand_hit & (row_dev[:, None] >= 1)
    last_pick = (rows[:, None] == blocks_all - 1) & (cols[None, :] == blocks_all - 2)
    forced = forced | last_pick
    ranks = jax.random.randint(rank_key, (blocks_all, blocks_all), 0, 1 << 18)
    scores = ranks * blocks_all + cols[None, :] + jnp.where(forced, (1 << 18) * blocks_all, 0)
    scores = jnp.where(eligible, scores, -1)
    top_scores, top_index = lax.top_k(scores, TOP)
    chosen = jnp.where(top_scores >= 0, top_index, rows[:, None])
    return chosen.astype(jnp.int32)


def steps_of(stream_key, extent, shards, smallest, largest):
    level, own = 1.0, jax.random.fold_in(stream_key, 6)
    for position, shards_of in shards:
        draws = jnp.exp(jax.random.uniform(jax.random.fold_in(own, position), (shards_of,), jnp.float32, smallest / len(shards), largest / len(shards)))
        level = level * jnp.repeat(draws, extent[position] // shards_of).reshape([-1 if axis == position else 1 for axis in range(len(extent))])
    return level


def noise(stream_key, extent, scale, reach, split=(), kind=jnp.bfloat16):
    values = jax.random.normal(stream_key, extent, jnp.float32) * scale
    if len(split) > 0:
        values = steps_of(stream_key, extent, split, -0.22, 0.18) * values
    return jnp.clip(values, min=-reach, max=reach).astype(kind)


def setup_inputs(seed: int = 0) -> dict:
    seeds = jax.random.split(jax.random.key(seed), 6)
    queries = draw_queries(jax.random.fold_in(seeds[5], 71), 0)
    keys = draw_keys(jax.random.fold_in(seeds[5], 71), 0)
    values = noise(seeds[2], (SEQ, D_HEAD), 1.0, 6.0, ((0, 8),))
    dout = noise(seeds[3], (SEQ, HEADS, D_HEAD), 1.0, 6.0, ((0, 8), (1, 4)))
    selected = draw_selected(jax.random.fold_in(seeds[5], 71), 0)
    return dict(queries=queries, keys=keys, values=values, dout=dout, selected=selected)


def block_grads(q_rows, do_rows, key_rows, value_rows, allowed, scaling):
    scores = jnp.dot(q_rows, key_rows.T, preferred_element_type=jnp.float32) * scaling
    masked = jnp.where(allowed, scores, -jnp.inf)
    row_max = lax.optimization_barrier(jnp.max(masked, axis=1, keepdims=True))
    exp_terms = jnp.where(allowed, jnp.exp(masked - row_max), jnp.float32(0.0))
    weights = exp_terms / lax.optimization_barrier(jnp.sum(exp_terms, axis=1, keepdims=True))
    probs_b = weights.astype(jnp.bfloat16)
    attended = jnp.dot(probs_b, value_rows, preferred_element_type=jnp.float32)
    row_delta = lax.optimization_barrier(jnp.sum(do_rows.astype(jnp.float32) * attended, axis=1, keepdims=True))
    dprobs = jnp.dot(do_rows, value_rows.T, preferred_element_type=jnp.float32)
    dscores = (weights * (dprobs - row_delta)).astype(jnp.bfloat16)
    grad_q = (jnp.dot(dscores, key_rows, preferred_element_type=jnp.float32) * scaling).astype(jnp.bfloat16)
    grad_k = jnp.dot(dscores.T, q_rows, preferred_element_type=jnp.float32) * scaling
    grad_v = jnp.dot(probs_b.T, do_rows, preferred_element_type=jnp.float32)
    return (grad_q, grad_k, grad_v)

def reference(queries, keys, values, dout, selected):
    blocks_all = selected.shape[0]
    seq_rows, head_count, feature = queries.shape
    block_len = seq_rows // blocks_all
    scaling = 1.0 / math.sqrt(feature)
    key_blocks = keys.reshape(blocks_all, block_len, feature)
    value_blocks = values.reshape(blocks_all, block_len, feature)
    query_blocks = queries.reshape(blocks_all, block_len * head_count, feature)
    dout_blocks = dout.reshape(blocks_all, block_len * head_count, feature)
    row_pos = jnp.arange(block_len * head_count) // head_count
    col_pos = jnp.arange(4 * block_len)
    col_block = col_pos // block_len
    col_row = col_pos % block_len

    def per_block(running, number):
        acc_keys, acc_values = running
        entries = selected[number].astype(jnp.int32)
        alive_flags = jnp.concatenate([entries != number, jnp.ones((1,), jnp.bool_)])
        listed = jnp.concatenate([entries, number[None].astype(jnp.int32)]).astype(jnp.int32)
        allowed = jnp.where(col_block[None, :] == 3, col_row[None, :] <= row_pos[:, None], alive_flags[col_block][None, :])
        key_rows = key_blocks[listed].reshape(4 * block_len, feature)
        value_rows = value_blocks[listed].reshape(4 * block_len, feature)
        grad_q, grad_k, grad_v = block_grads(query_blocks[number], dout_blocks[number], key_rows, value_rows, allowed, scaling)
        acc_keys = acc_keys.at[listed].add(grad_k.reshape(4, block_len, feature))
        acc_values = acc_values.at[listed].add(grad_v.reshape(4, block_len, feature))
        return ((acc_keys, acc_values), grad_q)
    start = jnp.zeros((blocks_all, block_len, feature), jnp.float32)
    (acc_keys, acc_values), grads_q = lax.scan(per_block, (start, start), jnp.arange(blocks_all, dtype=jnp.int32))
    grad_queries = grads_q.reshape(seq_rows, head_count, feature)
    grad_keys = acc_keys.reshape(seq_rows, feature).astype(jnp.bfloat16)
    grad_values = acc_values.reshape(seq_rows, feature).astype(jnp.bfloat16)
    return (grad_queries, grad_keys, grad_values)
```

```python
import functools
import math

import jax
import jax.numpy as jnp
from jax import lax
from jax.experimental import pallas as pl
from jax.experimental.pallas import tpu as pltpu
from jax.sharding import PartitionSpec as P

F32 = jnp.float32
BF16 = jnp.bfloat16
VMEM_LIMIT = 56 * 1024 * 1024


def dot_nt(a, b):
    return lax.dot_general(a, b, (((1,), (1,)), ((), ())), preferred_element_type=F32)


def dot_nn(a, b):
    return lax.dot_general(a, b, (((1,), (0,)), ((), ())), preferred_element_type=F32)


def pick_kernel(count, slots, keys, values, out, sems):
    which = slots[count]

    def start(source):
        for peer in range(count):
            pltpu.make_async_copy(source.at[slots[peer]], out.at[peer], sems.at[peer]).start()

    @pl.when(which == 0)
    def _():
        start(keys)

    @pl.when(which != 0)
    def _():
        start(values)

    for peer in range(count):
        pltpu.make_async_copy(keys.at[0], out.at[peer], sems.at[peer]).wait()


def local_stats_kernel(factor, blocks_here, table, q, do, keys, values, stats):
    row = pl.program_id(0)
    q_rows = q[...]
    do_rows = do[...]
    block_len = q_rows.shape[0]
    scores = dot_nt(keys[row], q_rows)
    dprobs = dot_nt(values[row], do_rows)
    col = lax.broadcasted_iota(jnp.int32, scores.shape, 0)
    pos = lax.broadcasted_iota(jnp.int32, scores.shape, 1)
    scores = jnp.where(col <= pos, scores, -jnp.inf)
    top = jnp.max(scores, axis=0, keepdims=True)
    terms = jnp.exp2((scores - top) * factor)
    stats[0, 0:1, :] = top
    stats[0, 1:2, :] = jnp.sum(terms, axis=0, keepdims=True)
    stats[0, 2:3, :] = jnp.sum(terms * dprobs, axis=0, keepdims=True)
    stats[0, 3:8, :] = jnp.zeros((5, block_len), F32)
    for t in range(3):
        slot = table[row * 3 + t]

        @pl.when((slot >= 0) & (slot < blocks_here))
        def _():
            scores = dot_nt(keys[slot], q_rows)
            dprobs = dot_nt(values[slot], do_rows)
            old = stats[0, 0:1, :]
            top = jnp.maximum(old, jnp.max(scores, axis=0, keepdims=True))
            shrink = jnp.exp2((old - top) * factor)
            terms = jnp.exp2((scores - top) * factor)
            stats[0, 0:1, :] = top
            stats[0, 1:2, :] = stats[0, 1:2, :] * shrink + jnp.sum(terms, axis=0, keepdims=True)
            stats[0, 2:3, :] = stats[0, 2:3, :] * shrink + jnp.sum(
                terms * dprobs, axis=0, keepdims=True
            )


def remote_kernel(
    factor, scaling, blocks_here, table, q, do, fetched, other, stats,
    keep, send, final, grad_qt,
    rows, acc, s_buf, dp_buf, top_buf, sums, sems,
):
    row = pl.program_id(0)
    core = table[3 * blocks_here]

    @pl.when(row == 0)
    def _():
        first = pltpu.make_async_copy(fetched, rows.at[core], sems.at[0])
        second = pltpu.make_async_copy(other, rows.at[1 - core], sems.at[1])
        first.start()
        second.start()
        acc[...] = jnp.zeros_like(acc)
        first.wait()
        second.wait()

    q_rows = q[...]
    do_rows = do[...]
    top_buf[...] = stats[0, 0:1, :]
    grad_qt[0] = jnp.zeros_like(grad_qt[0])
    for t in range(3):
        slot = table[row * 3 + t] - blocks_here

        @pl.when(slot >= 0)
        def _():
            scores = dot_nt(rows[0, slot], q_rows)
            dp_buf[t] = dot_nt(rows[1, slot], do_rows)
            s_buf[t] = scores
            top_buf[...] = jnp.maximum(top_buf[...], jnp.max(scores, axis=0, keepdims=True))

    top = top_buf[...]
    shrink = jnp.exp2((stats[0, 0:1, :] - top) * factor)
    sums[0:1, :] = stats[0, 1:2, :] * shrink
    sums[1:2, :] = stats[0, 2:3, :] * shrink
    for t in range(3):
        slot = table[row * 3 + t] - blocks_here

        @pl.when(slot >= 0)
        def _():
            terms = jnp.exp2((s_buf[t] - top_buf[...]) * factor)
            s_buf[t] = terms
            sums[0:1, :] += jnp.sum(terms, axis=0, keepdims=True)
            sums[1:2, :] += jnp.sum(terms * dp_buf[t], axis=0, keepdims=True)

    inverse = 1.0 / sums[0:1, :]
    delta = sums[1:2, :] * inverse
    final[0, 0:1, :] = top
    final[0, 1:2, :] = inverse
    final[0, 2:3, :] = delta
    final[0, 3:8, :] = jnp.zeros((5, top.shape[1]), F32)
    for t in range(3):
        slot = table[row * 3 + t] - blocks_here

        @pl.when(slot >= 0)
        def _():
            weights = s_buf[t] * final[0, 1:2, :]
            dscores = (weights * (dp_buf[t] - final[0, 2:3, :])).astype(BF16)
            acc[1, slot] += dot_nn(weights.astype(BF16), do_rows)
            acc[0, slot] += dot_nn(dscores, q_rows)
            grad_qt[0] += dot_nn(rows[0, slot].T, dscores)

    @pl.when(row == pl.num_programs(0) - 1)
    def _():
        keep_scale = jnp.where(core == 0, scaling, 1.0)
        send_scale = jnp.where(core == 0, 1.0, scaling)
        keep[...] = (acc[core] * keep_scale).astype(BF16)
        send[...] = (acc[1 - core] * send_scale).astype(BF16)


def local_kernel(
    factor, scaling, blocks_here, table, q, do, keys, values, final, grad_qt,
    keep, send, grad_q,
    acc, total_qt,
):
    row = pl.program_id(0)
    core = table[3 * blocks_here]

    @pl.when(row == 0)
    def _():
        acc[...] = jnp.zeros_like(acc)

    q_rows = q[...]
    do_rows = do[...]
    top = final[0, 0:1, :]
    inverse = final[0, 1:2, :]
    delta = final[0, 2:3, :]

    def pair(slot, masked):
        key_rows = keys[slot]
        scores = dot_nt(key_rows, q_rows)
        dprobs = dot_nt(values[slot], do_rows)
        weights = jnp.exp2((scores - top) * factor) * inverse
        if masked:
            col = lax.broadcasted_iota(jnp.int32, scores.shape, 0)
            pos = lax.broadcasted_iota(jnp.int32, scores.shape, 1)
            weights = jnp.where(col <= pos, weights, 0.0)
        dscores = (weights * (dprobs - delta)).astype(BF16)
        acc[1, slot] += dot_nn(weights.astype(BF16), do_rows)
        acc[0, slot] += dot_nn(dscores, q_rows)
        total_qt[...] += dot_nn(key_rows.T, dscores)

    total_qt[...] = grad_qt[0]
    pair(row, True)
    for t in range(3):
        slot = table[row * 3 + t]

        @pl.when((slot >= 0) & (slot < blocks_here))
        def _():
            pair(slot, False)

    grad_q[...] = (total_qt[...].T * scaling).astype(BF16)

    @pl.when(row == pl.num_programs(0) - 1)
    def _():
        keep_scale = jnp.where(core == 0, scaling, 1.0)
        send_scale = jnp.where(core == 0, 1.0, scaling)
        keep[...] = (acc[core] * keep_scale).astype(BF16)
        send[...] = (acc[1 - core] * send_scale).astype(BF16)


def owner_kernel(count, asked, mine, theirs, back, out):
    block = pl.program_id(0)
    total = mine[0].astype(F32) + theirs[0].astype(F32)
    for peer in range(count):
        wanted = asked[peer] == block
        total = total + jnp.where(wanted, back[peer].astype(F32), 0.0)
    out[0] = total.astype(BF16)


def params(**more):
    return pltpu.CompilerParams(vmem_limit_bytes=VMEM_LIMIT, **more)


def body(queries, keys, values, dout, selected):
    tok_rows, head_count, feature = queries.shape
    blocks_here = selected.shape[0]
    block_len = tok_rows // blocks_here
    ctx_count = lax.axis_size("ctx")
    ctx_self = lax.axis_index("ctx")
    heads = lax.axis_size("head")
    chips = heads // 2
    core = lax.axis_index("head") % 2
    scaling = 1.0 / math.sqrt(feature)
    factor = scaling * math.log2(math.e)
    local_ids = jnp.arange(blocks_here, dtype=jnp.int32)
    block_ids = ctx_self * blocks_here + local_ids
    owners = selected // blocks_here
    inside = selected % blocks_here
    vacant = selected == block_ids[:, None]
    distant = (owners != ctx_self) & jnp.logical_not(vacant)
    peer_ids = jnp.arange(ctx_count, dtype=jnp.int32)
    matches = distant[:, :, None] & (owners[:, :, None] == peer_ids[None, None, :])
    wanted = jnp.max(jnp.where(matches, inside[:, :, None], -1), axis=(0, 1))
    asked_for = lax.all_to_all(
        wanted.reshape(ctx_count, 1), "ctx", split_axis=0, concat_axis=0, tiled=True
    ).reshape(ctx_count)
    table = jnp.where(vacant, -1, jnp.where(distant, blocks_here + owners, inside))
    info = jnp.concatenate([table.reshape(-1), core.reshape(1)]).astype(jnp.int32)
    picks = jnp.concatenate([jnp.maximum(asked_for, 0), core.reshape(1)]).astype(jnp.int32)

    q2 = queries.reshape(tok_rows, feature)
    do2 = dout.reshape(tok_rows, feature)
    key_blocks = keys.reshape(blocks_here, block_len, feature)
    value_blocks = values.reshape(blocks_here, block_len, feature)
    remote_shape = (ctx_count, block_len, feature)
    local_shape = (blocks_here, block_len, feature)

    any_spec = pl.BlockSpec(memory_space=pl.ANY)
    row_spec = pl.BlockSpec((block_len, feature), lambda i, *_: (i, 0))
    own_spec = pl.BlockSpec(local_shape, lambda i, *_: (0, 0, 0))
    far_spec = pl.BlockSpec(remote_shape, lambda i, *_: (0, 0, 0))
    stat_spec = pl.BlockSpec((1, 8, block_len), lambda i, *_: (i, 0, 0))
    qt_spec = pl.BlockSpec((1, feature, block_len), lambda i, *_: (i, 0, 0))
    stat_type = jax.ShapeDtypeStruct((blocks_here, 8, block_len), F32)
    far_type = jax.ShapeDtypeStruct(remote_shape, BF16)
    own_type = jax.ShapeDtypeStruct(local_shape, BF16)
    qt_type = jax.ShapeDtypeStruct((blocks_here, feature, block_len), F32)
    pair_flops = 2 * block_len * block_len * feature

    def cost(matmuls, size):
        return pl.CostEstimate(
            flops=matmuls * pair_flops, bytes_accessed=size, transcendentals=matmuls * block_len**2
        )

    swap = [(h, h ^ 1) for h in range(heads)]

    send_rows = pl.pallas_call(
        functools.partial(pick_kernel, ctx_count),
        grid_spec=pltpu.PrefetchScalarGridSpec(
            num_scalar_prefetch=1,
            grid=(),
            in_specs=[any_spec, any_spec],
            out_specs=any_spec,
            scratch_shapes=[pltpu.SemaphoreType.DMA((ctx_count,))],
        ),
        out_shape=far_type,
        name="pick_rows",
    )(picks, key_blocks, value_blocks)
    fetched = lax.all_to_all(send_rows, "ctx", split_axis=0, concat_axis=0, tiled=True)
    other = lax.ppermute(fetched, "head", swap)

    stats = pl.pallas_call(
        functools.partial(local_stats_kernel, factor, blocks_here),
        grid_spec=pltpu.PrefetchScalarGridSpec(
            num_scalar_prefetch=1,
            grid=(blocks_here,),
            in_specs=[row_spec, row_spec, own_spec, own_spec],
            out_specs=stat_spec,
        ),
        out_shape=stat_type,
        compiler_params=params(),
        cost_estimate=cost(30, 4 * tok_rows * feature * 2),
        name="local_stats",
    )(info, q2, do2, key_blocks, value_blocks)

    keep_far, send_far, final, grad_qt = pl.pallas_call(
        functools.partial(remote_kernel, factor, scaling, blocks_here),
        grid_spec=pltpu.PrefetchScalarGridSpec(
            num_scalar_prefetch=1,
            grid=(blocks_here,),
            in_specs=[row_spec, row_spec, any_spec, any_spec, stat_spec],
            out_specs=[far_spec, far_spec, stat_spec, qt_spec],
            scratch_shapes=[
                pltpu.VMEM((2,) + remote_shape, BF16),
                pltpu.VMEM((2,) + remote_shape, F32),
                pltpu.VMEM((3, block_len, block_len), F32),
                pltpu.VMEM((3, block_len, block_len), F32),
                pltpu.VMEM((1, block_len), F32),
                pltpu.VMEM((2, block_len), F32),
                pltpu.SemaphoreType.DMA((2,)),
            ],
        ),
        out_shape=[far_type, far_type, stat_type, qt_type],
        compiler_params=params(),
        cost_estimate=cost(60, 8 * tok_rows * feature * 2),
        name="remote_pairs",
    )(info, q2, do2, fetched, other, stats)

    keep_own, send_own, grad_q = pl.pallas_call(
        functools.partial(local_kernel, factor, scaling, blocks_here),
        grid_spec=pltpu.PrefetchScalarGridSpec(
            num_scalar_prefetch=1,
            grid=(blocks_here,),
            in_specs=[row_spec, row_spec, own_spec, own_spec, stat_spec, qt_spec],
            out_specs=[own_spec, own_spec, row_spec],
            scratch_shapes=[
                pltpu.VMEM((2,) + local_shape, F32),
                pltpu.VMEM((feature, block_len), F32),
            ],
        ),
        out_shape=[own_type, own_type, jax.ShapeDtypeStruct((tok_rows, feature), BF16)],
        compiler_params=params(),
        cost_estimate=cost(60, 8 * tok_rows * feature * 2),
        name="local_pairs",
    )(info, q2, do2, key_blocks, value_blocks, final, grad_qt)

    from_far = lax.ppermute(send_far, "head", swap)
    chip_far = (keep_far.astype(F32) + from_far.astype(F32)).astype(BF16)
    back = lax.all_to_all(chip_far, "ctx", split_axis=0, concat_axis=0, tiled=True)
    from_own = lax.ppermute(send_own, "head", swap)

    block_spec = pl.BlockSpec((1, block_len, feature), lambda i, *_: (i, 0, 0))
    mine = pl.pallas_call(
        functools.partial(owner_kernel, ctx_count),
        grid_spec=pltpu.PrefetchScalarGridSpec(
            num_scalar_prefetch=1,
            grid=(blocks_here,),
            in_specs=[block_spec, block_spec, far_spec],
            out_specs=block_spec,
        ),
        out_shape=own_type,
        compiler_params=params(),
        name="owner_sum",
    )(asked_for, keep_own, from_own, back)
    parts = [mine] + [
        lax.ppermute(mine, "head", [(h, (h + 2 * s) % heads) for h in range(heads)])
        for s in range(1, chips)
    ]
    if chips == 2:
        total = parts[0].astype(F32) + parts[1].astype(F32)
    else:
        chip = lax.axis_index("head") // 2
        stack = jnp.stack(parts)[(chip - jnp.arange(chips)) % chips]
        total = jnp.sum(stack.astype(F32), axis=0)
    total = total.astype(BF16).reshape(tok_rows, feature)
    twin = lax.ppermute(total, "head", swap)
    grad_keys = jnp.where(core == 0, total, twin)
    grad_values = jnp.where(core == 0, twin, total)
    return (grad_q.reshape(tok_rows, head_count, feature), grad_keys, grad_values)


def solution(mesh):
    return jax.shard_map(
        body,
        mesh=mesh,
        in_specs=(
            P("ctx", "head", None),
            P("ctx", None),
            P("ctx", None),
            P("ctx", "head", None),
            P("ctx", None),
        ),
        out_specs=(P("ctx", "head", None), P("ctx", None), P("ctx", None)),
        check_vma=False,
    )
```

```python
import functools
import math

import jax
import jax.numpy as jnp
from jax import lax
from jax.experimental import pallas as pl
from jax.experimental.pallas import tpu as pltpu
from jax.sharding import PartitionSpec as P

F32 = jnp.float32
BF16 = jnp.bfloat16
VMEM_LIMIT = 56 * 1024 * 1024


def dot_nt(a, b):
    return lax.dot_general(a, b, (((1,), (1,)), ((), ())), preferred_element_type=F32)


def dot_nn(a, b):
    return lax.dot_general(a, b, (((1,), (0,)), ((), ())), preferred_element_type=F32)


def plan_kernel(blocks_here, shifts, place, chosen, table, *wants):
    ctx_self = place[0]
    best = [jnp.int32(0)] * shifts
    for row in range(blocks_here):
        for t in range(3):
            entry = chosen[row, t]
            owner = lax.div(entry, jnp.int32(blocks_here))
            inside = entry - owner * blocks_here
            apart = ctx_self - owner
            live = entry != ctx_self * blocks_here + row
            slot = jnp.where(apart == 0, inside, blocks_here + apart - 1)
            table[row * 3 + t] = jnp.where(live, slot, -1)
            for s in range(shifts):
                best[s] = jnp.where(live & (apart == s + 1), inside + 1, best[s])
    table[3 * blocks_here] = place[1]
    for s in range(shifts):
        wants[s][0] = best[s]


def pick_kernel(shifts, core, keys, values, *refs):
    asked, outs, (rows, in_sem, out_sems) = refs[:shifts], refs[shifts : 2 * shifts], refs[2 * shifts :]

    @pl.when(core[0] == 0)
    def _():
        pltpu.make_async_copy(keys, rows, in_sem).start()

    @pl.when(core[0] != 0)
    def _():
        pltpu.make_async_copy(values, rows, in_sem).start()

    pltpu.make_async_copy(keys, rows, in_sem).wait()
    copies = [
        pltpu.make_async_copy(
            rows.at[jnp.maximum(asked[s][0] - 1, 0)], outs[s], out_sems.at[s]
        )
        for s in range(shifts)
    ]
    for copy in copies:
        copy.start()
    for copy in copies:
        copy.wait()


def chip_sum_kernel(shifts, mine, theirs, *outs):
    for s in range(shifts):
        outs[s][...] = (mine[s].astype(F32) + theirs[s].astype(F32)).astype(BF16)


def local_stats_kernel(factor, blocks_here, table, q, do, keys, values, stats):
    row = pl.program_id(0)
    q_rows = q[...]
    do_rows = do[...]
    block_len = q_rows.shape[0]
    scores = dot_nt(keys[row], q_rows)
    dprobs = dot_nt(values[row], do_rows)
    col = lax.broadcasted_iota(jnp.int32, scores.shape, 0)
    pos = lax.broadcasted_iota(jnp.int32, scores.shape, 1)
    scores = jnp.where(col <= pos, scores, -jnp.inf)
    top = jnp.max(scores, axis=0, keepdims=True)
    terms = jnp.exp2((scores - top) * factor)
    stats[0, 0:1, :] = top
    stats[0, 1:2, :] = jnp.sum(terms, axis=0, keepdims=True)
    stats[0, 2:3, :] = jnp.sum(terms * dprobs, axis=0, keepdims=True)
    stats[0, 3:8, :] = jnp.zeros((5, block_len), F32)
    for t in range(3):
        slot = table[row * 3 + t]

        @pl.when((slot >= 0) & (slot < blocks_here))
        def _():
            scores = dot_nt(keys[slot], q_rows)
            dprobs = dot_nt(values[slot], do_rows)
            old = stats[0, 0:1, :]
            top = jnp.maximum(old, jnp.max(scores, axis=0, keepdims=True))
            shrink = jnp.exp2((old - top) * factor)
            terms = jnp.exp2((scores - top) * factor)
            stats[0, 0:1, :] = top
            stats[0, 1:2, :] = stats[0, 1:2, :] * shrink + jnp.sum(terms, axis=0, keepdims=True)
            stats[0, 2:3, :] = stats[0, 2:3, :] * shrink + jnp.sum(
                terms * dprobs, axis=0, keepdims=True
            )


def remote_kernel(
    factor, scaling, blocks_here, shifts, table, q, do, stats, *refs
):
    fetched, other, refs = refs[:shifts], refs[shifts : 2 * shifts], refs[2 * shifts :]
    keep, send, final, grad_qt, rows, acc, s_buf, dp_buf, top_buf, sums, sems = refs
    row = pl.program_id(0)
    core = table[3 * blocks_here]

    @pl.when(row == 0)
    def _():
        copies = []
        for s in range(shifts):
            copies.append(pltpu.make_async_copy(fetched[s], rows.at[core, s], sems.at[0, s]))
            copies.append(pltpu.make_async_copy(other[s], rows.at[1 - core, s], sems.at[1, s]))
        for copy in copies:
            copy.start()
        acc[...] = jnp.zeros_like(acc)
        for copy in copies:
            copy.wait()

    q_rows = q[...]
    do_rows = do[...]
    top_buf[...] = stats[0, 0:1, :]
    grad_qt[0] = jnp.zeros_like(grad_qt[0])
    for t in range(3):
        slot = table[row * 3 + t] - blocks_here

        @pl.when(slot >= 0)
        def _():
            scores = dot_nt(rows[0, slot], q_rows)
            dp_buf[t] = dot_nt(rows[1, slot], do_rows)
            s_buf[t] = scores
            top_buf[...] = jnp.maximum(top_buf[...], jnp.max(scores, axis=0, keepdims=True))

    top = top_buf[...]
    shrink = jnp.exp2((stats[0, 0:1, :] - top) * factor)
    sums[0:1, :] = stats[0, 1:2, :] * shrink
    sums[1:2, :] = stats[0, 2:3, :] * shrink
    for t in range(3):
        slot = table[row * 3 + t] - blocks_here

        @pl.when(slot >= 0)
        def _():
            terms = jnp.exp2((s_buf[t] - top_buf[...]) * factor)
            s_buf[t] = terms
            sums[0:1, :] += jnp.sum(terms, axis=0, keepdims=True)
            sums[1:2, :] += jnp.sum(terms * dp_buf[t], axis=0, keepdims=True)

    inverse = 1.0 / sums[0:1, :]
    delta = sums[1:2, :] * inverse
    final[0, 0:1, :] = top
    final[0, 1:2, :] = inverse
    final[0, 2:3, :] = delta
    final[0, 3:8, :] = jnp.zeros((5, top.shape[1]), F32)
    for t in range(3):
        slot = table[row * 3 + t] - blocks_here

        @pl.when(slot >= 0)
        def _():
            weights = s_buf[t] * final[0, 1:2, :]
            dscores = (weights * (dp_buf[t] - final[0, 2:3, :])).astype(BF16)
            acc[1, slot] += dot_nn(weights.astype(BF16), do_rows)
            acc[0, slot] += dot_nn(dscores, q_rows)
            grad_qt[0] += dot_nn(rows[0, slot].T, dscores)

    @pl.when(row == pl.num_programs(0) - 1)
    def _():
        keep_scale = jnp.where(core == 0, scaling, 1.0)
        send_scale = jnp.where(core == 0, 1.0, scaling)
        keep[...] = (acc[core] * keep_scale).astype(BF16)
        send[...] = (acc[1 - core] * send_scale).astype(BF16)


def local_kernel(
    factor, scaling, blocks_here, table, q, do, keys, values, final, grad_qt,
    keep, send, grad_q,
    acc, total_qt,
):
    row = pl.program_id(0)
    core = table[3 * blocks_here]

    @pl.when(row == 0)
    def _():
        acc[...] = jnp.zeros_like(acc)

    q_rows = q[...]
    do_rows = do[...]
    top = final[0, 0:1, :]
    inverse = final[0, 1:2, :]
    delta = final[0, 2:3, :]

    def pair(slot, masked):
        key_rows = keys[slot]
        scores = dot_nt(key_rows, q_rows)
        dprobs = dot_nt(values[slot], do_rows)
        weights = jnp.exp2((scores - top) * factor) * inverse
        if masked:
            col = lax.broadcasted_iota(jnp.int32, scores.shape, 0)
            pos = lax.broadcasted_iota(jnp.int32, scores.shape, 1)
            weights = jnp.where(col <= pos, weights, 0.0)
        dscores = (weights * (dprobs - delta)).astype(BF16)
        acc[1, slot] += dot_nn(weights.astype(BF16), do_rows)
        acc[0, slot] += dot_nn(dscores, q_rows)
        total_qt[...] += dot_nn(key_rows.T, dscores)

    total_qt[...] = grad_qt[0]
    pair(row, True)
    for t in range(3):
        slot = table[row * 3 + t]

        @pl.when((slot >= 0) & (slot < blocks_here))
        def _():
            pair(slot, False)

    grad_q[...] = (total_qt[...].T * scaling).astype(BF16)

    @pl.when(row == pl.num_programs(0) - 1)
    def _():
        keep_scale = jnp.where(core == 0, scaling, 1.0)
        send_scale = jnp.where(core == 0, 1.0, scaling)
        keep[...] = (acc[core] * keep_scale).astype(BF16)
        send[...] = (acc[1 - core] * send_scale).astype(BF16)


def owner_kernel(shifts, mine, theirs, *refs):
    asked, back, (out, acc) = refs[:shifts], refs[shifts : 2 * shifts], refs[2 * shifts :]
    acc[...] = mine[...].astype(F32) + theirs[...].astype(F32)
    for s in range(shifts):
        slot = asked[s][0] - 1

        @pl.when(slot >= 0)
        def _():
            acc[slot] += back[s][...].astype(F32)

    out[...] = acc[...].astype(BF16)


def params(**more):
    return pltpu.CompilerParams(vmem_limit_bytes=VMEM_LIMIT, **more)


def body(queries, keys, values, dout, selected):
    tok_rows, head_count, feature = queries.shape
    blocks_here = selected.shape[0]
    block_len = tok_rows // blocks_here
    ctx_count = lax.axis_size("ctx")
    ctx_self = lax.axis_index("ctx")
    heads = lax.axis_size("head")
    chips = heads // 2
    core = lax.axis_index("head") % 2
    scaling = 1.0 / math.sqrt(feature)
    factor = scaling * math.log2(math.e)
    shifts = ctx_count - 1
    q2 = queries.reshape(tok_rows, feature)
    do2 = dout.reshape(tok_rows, feature)
    key_blocks = keys.reshape(blocks_here, block_len, feature)
    value_blocks = values.reshape(blocks_here, block_len, feature)
    remote_shape = (shifts, block_len, feature)
    local_shape = (blocks_here, block_len, feature)

    any_spec = pl.BlockSpec(memory_space=pl.ANY)
    row_spec = pl.BlockSpec((block_len, feature), lambda i, *_: (i, 0))
    own_spec = pl.BlockSpec(local_shape, lambda i, *_: (0, 0, 0))
    far_spec = pl.BlockSpec(remote_shape, lambda i, *_: (0, 0, 0))
    stat_spec = pl.BlockSpec((1, 8, block_len), lambda i, *_: (i, 0, 0))
    qt_spec = pl.BlockSpec((1, feature, block_len), lambda i, *_: (i, 0, 0))
    stat_type = jax.ShapeDtypeStruct((blocks_here, 8, block_len), F32)
    far_type = jax.ShapeDtypeStruct(remote_shape, BF16)
    own_type = jax.ShapeDtypeStruct(local_shape, BF16)
    qt_type = jax.ShapeDtypeStruct((blocks_here, feature, block_len), F32)
    pair_flops = 2 * block_len * block_len * feature

    def cost(matmuls, size):
        return pl.CostEstimate(
            flops=matmuls * pair_flops, bytes_accessed=size, transcendentals=matmuls * block_len**2
        )

    swap = [(h, h ^ 1) for h in range(heads)]

    smem = pl.BlockSpec(memory_space=pltpu.SMEM)
    whole = pl.BlockSpec(memory_space=pltpu.VMEM)
    block_type = jax.ShapeDtypeStruct((block_len, feature), BF16)
    one_type = jax.ShapeDtypeStruct((1,), jnp.int32)
    info, *wants = pl.pallas_call(
        functools.partial(plan_kernel, blocks_here, shifts),
        in_specs=[smem, smem],
        out_specs=[smem] * (1 + shifts),
        out_shape=[jax.ShapeDtypeStruct((3 * blocks_here + 1,), jnp.int32)] + [one_type] * shifts,
        name="plan",
    )(jnp.stack([ctx_self, core]).astype(jnp.int32), selected)

    def to_owner(array, s):
        return lax.ppermute(array, "ctx", [(c, c - s - 1) for c in range(s + 1, ctx_count)])

    def to_reader(array, s):
        return lax.ppermute(array, "ctx", [(c - s - 1, c) for c in range(s + 1, ctx_count)])

    asked = [to_owner(wants[s], s) for s in range(shifts)]
    sent = pl.pallas_call(
        functools.partial(pick_kernel, shifts),
        in_specs=[smem, any_spec, any_spec] + [smem] * shifts,
        out_specs=[any_spec] * shifts,
        out_shape=[block_type] * shifts,
        scratch_shapes=[
            pltpu.VMEM(local_shape, BF16),
            pltpu.SemaphoreType.DMA,
            pltpu.SemaphoreType.DMA((shifts,)),
        ],
        name="pick_rows",
    )(core.reshape(1).astype(jnp.int32), key_blocks, value_blocks, *asked)
    fetched = [to_reader(sent[s], s) for s in range(shifts)]
    other = [lax.ppermute(rows, "head", swap) for rows in fetched]

    stats = pl.pallas_call(
        functools.partial(local_stats_kernel, factor, blocks_here),
        grid_spec=pltpu.PrefetchScalarGridSpec(
            num_scalar_prefetch=1,
            grid=(blocks_here,),
            in_specs=[row_spec, row_spec, own_spec, own_spec],
            out_specs=stat_spec,
        ),
        out_shape=stat_type,
        compiler_params=params(),
        cost_estimate=cost(30, 4 * tok_rows * feature * 2),
        name="local_stats",
    )(info, q2, do2, key_blocks, value_blocks)

    keep_far, send_far, final, grad_qt = pl.pallas_call(
        functools.partial(remote_kernel, factor, scaling, blocks_here, shifts),
        grid_spec=pltpu.PrefetchScalarGridSpec(
            num_scalar_prefetch=1,
            grid=(blocks_here,),
            in_specs=[row_spec, row_spec, stat_spec] + [any_spec] * (2 * shifts),
            out_specs=[far_spec, far_spec, stat_spec, qt_spec],
            scratch_shapes=[
                pltpu.VMEM((2,) + remote_shape, BF16),
                pltpu.VMEM((2,) + remote_shape, F32),
                pltpu.VMEM((3, block_len, block_len), F32),
                pltpu.VMEM((3, block_len, block_len), F32),
                pltpu.VMEM((1, block_len), F32),
                pltpu.VMEM((2, block_len), F32),
                pltpu.SemaphoreType.DMA((2, shifts)),
            ],
        ),
        out_shape=[far_type, far_type, stat_type, qt_type],
        compiler_params=params(),
        cost_estimate=cost(60, 8 * tok_rows * feature * 2),
        name="remote_pairs",
    )(info, q2, do2, stats, *fetched, *other)

    keep_own, send_own, grad_q = pl.pallas_call(
        functools.partial(local_kernel, factor, scaling, blocks_here),
        grid_spec=pltpu.PrefetchScalarGridSpec(
            num_scalar_prefetch=1,
            grid=(blocks_here,),
            in_specs=[row_spec, row_spec, own_spec, own_spec, stat_spec, qt_spec],
            out_specs=[own_spec, own_spec, row_spec],
            scratch_shapes=[
                pltpu.VMEM((2,) + local_shape, F32),
                pltpu.VMEM((feature, block_len), F32),
            ],
        ),
        out_shape=[own_type, own_type, jax.ShapeDtypeStruct((tok_rows, feature), BF16)],
        compiler_params=params(),
        cost_estimate=cost(60, 8 * tok_rows * feature * 2),
        name="local_pairs",
    )(info, q2, do2, key_blocks, value_blocks, final, grad_qt)

    from_far = lax.ppermute(send_far, "head", swap)
    chip_far = pl.pallas_call(
        functools.partial(chip_sum_kernel, shifts),
        in_specs=[whole, whole],
        out_specs=[whole] * shifts,
        out_shape=[block_type] * shifts,
        compiler_params=params(),
        name="chip_sum",
    )(keep_far, from_far)
    back = [to_owner(chip_far[s], s) for s in range(shifts)]
    from_own = lax.ppermute(send_own, "head", swap)
    mine = pl.pallas_call(
        functools.partial(owner_kernel, shifts),
        in_specs=[whole, whole] + [smem] * shifts + [whole] * shifts,
        out_specs=whole,
        out_shape=own_type,
        scratch_shapes=[pltpu.VMEM(local_shape, F32)],
        compiler_params=params(),
        name="owner_sum",
    )(keep_own, from_own, *asked, *back)
    parts = [mine] + [
        lax.ppermute(mine, "head", [(h, (h + 2 * s) % heads) for h in range(heads)])
        for s in range(1, chips)
    ]
    if chips == 2:
        total = parts[0].astype(F32) + parts[1].astype(F32)
    else:
        chip = lax.axis_index("head") // 2
        stack = jnp.stack(parts)[(chip - jnp.arange(chips)) % chips]
        total = jnp.sum(stack.astype(F32), axis=0)
    total = total.astype(BF16).reshape(tok_rows, feature)
    twin = lax.ppermute(total, "head", swap)
    grad_keys = jnp.where(core == 0, total, twin)
    grad_values = jnp.where(core == 0, twin, total)
    return (grad_q.reshape(tok_rows, head_count, feature), grad_keys, grad_values)


def solution(mesh):
    return jax.shard_map(
        body,
        mesh=mesh,
        in_specs=(
            P("ctx", "head", None),
            P("ctx", None),
            P("ctx", None),
            P("ctx", "head", None),
            P("ctx", None),
        ),
        out_specs=(P("ctx", "head", None), P("ctx", None), P("ctx", None)),
        check_vma=False,
    )
```

```python
import functools
import math

import jax
import jax.numpy as jnp
from jax import lax
from jax.experimental import pallas as pl
from jax.experimental.pallas import tpu as pltpu
from jax.sharding import PartitionSpec as P

F32 = jnp.float32
BF16 = jnp.bfloat16
VMEM_LIMIT = 56 * 1024 * 1024


def dot_nt(a, b):
    return lax.dot_general(a, b, (((1,), (1,)), ((), ())), preferred_element_type=F32)


def dot_nn(a, b):
    return lax.dot_general(a, b, (((1,), (0,)), ((), ())), preferred_element_type=F32)


def plan_kernel(blocks_here, shifts, place, chosen, table, wants):
    ctx_self = place[0]
    best = [jnp.int32(0)] * shifts
    for row in range(blocks_here):
        for t in range(3):
            entry = chosen[row, t]
            owner = lax.div(entry, jnp.int32(blocks_here))
            inside = entry - owner * blocks_here
            apart = ctx_self - owner
            live = entry != ctx_self * blocks_here + row
            slot = jnp.where(apart == 0, inside, blocks_here + apart - 1)
            table[row * 3 + t] = jnp.where(live, slot, -1)
            for s in range(shifts):
                best[s] = jnp.where(live & (apart == s + 1), inside + 1, best[s])
    table[3 * blocks_here] = place[1]
    for peer in range(shifts + 1):
        wants[peer] = jnp.int32(0)
    for s in range(shifts):

        @pl.when(ctx_self > s)
        def _():
            wants[ctx_self - s - 1] = best[s]


def asked_at(asked, shifts, ctx_self, s):
    peer = ctx_self + s + 1
    return jnp.where(peer <= shifts, asked[jnp.minimum(peer, shifts)], 0)


def pick_kernel(shifts, place, asked, keys, values, *refs):
    outs, (rows, in_sem, out_sems) = refs[:shifts], refs[shifts:]
    ctx_self, core = place[0], place[1]

    @pl.when(core == 0)
    def _():
        pltpu.make_async_copy(keys, rows, in_sem).start()

    @pl.when(core != 0)
    def _():
        pltpu.make_async_copy(values, rows, in_sem).start()

    pltpu.make_async_copy(keys, rows, in_sem).wait()
    copies = [
        pltpu.make_async_copy(
            rows.at[jnp.maximum(asked_at(asked, shifts, ctx_self, s) - 1, 0)],
            outs[s],
            out_sems.at[s],
        )
        for s in range(shifts)
    ]
    for copy in copies:
        copy.start()
    for copy in copies:
        copy.wait()


def chip_sum_kernel(shifts, mine, theirs, *outs):
    for s in range(shifts):
        outs[s][...] = (mine[s].astype(F32) + theirs[s].astype(F32)).astype(BF16)


def local_stats_kernel(factor, blocks_here, table, q, do, keys, values, stats):
    row = pl.program_id(0)
    q_rows = q[...]
    do_rows = do[...]
    block_len = q_rows.shape[0]
    scores = dot_nt(keys[row], q_rows)
    dprobs = dot_nt(values[row], do_rows)
    col = lax.broadcasted_iota(jnp.int32, scores.shape, 0)
    pos = lax.broadcasted_iota(jnp.int32, scores.shape, 1)
    scores = jnp.where(col <= pos, scores, -jnp.inf)
    top = jnp.max(scores, axis=0, keepdims=True)
    terms = jnp.exp2((scores - top) * factor)
    stats[0, 0:1, :] = top
    stats[0, 1:2, :] = jnp.sum(terms, axis=0, keepdims=True)
    stats[0, 2:3, :] = jnp.sum(terms * dprobs, axis=0, keepdims=True)
    stats[0, 3:8, :] = jnp.zeros((5, block_len), F32)
    for t in range(3):
        slot = table[row * 3 + t]

        @pl.when((slot >= 0) & (slot < blocks_here))
        def _():
            scores = dot_nt(keys[slot], q_rows)
            dprobs = dot_nt(values[slot], do_rows)
            old = stats[0, 0:1, :]
            top = jnp.maximum(old, jnp.max(scores, axis=0, keepdims=True))
            shrink = jnp.exp2((old - top) * factor)
            terms = jnp.exp2((scores - top) * factor)
            stats[0, 0:1, :] = top
            stats[0, 1:2, :] = stats[0, 1:2, :] * shrink + jnp.sum(terms, axis=0, keepdims=True)
            stats[0, 2:3, :] = stats[0, 2:3, :] * shrink + jnp.sum(
                terms * dprobs, axis=0, keepdims=True
            )


def remote_kernel(
    factor, scaling, blocks_here, shifts, table, q, do, stats, *refs
):
    fetched, other, refs = refs[:shifts], refs[shifts : 2 * shifts], refs[2 * shifts :]
    keep, send, final, grad_qt, rows, acc, s_buf, dp_buf, top_buf, sums, sems = refs
    row = pl.program_id(0)
    core = table[3 * blocks_here]

    @pl.when(row == 0)
    def _():
        copies = []
        for s in range(shifts):
            copies.append(pltpu.make_async_copy(fetched[s], rows.at[core, s], sems.at[0, s]))
            copies.append(pltpu.make_async_copy(other[s], rows.at[1 - core, s], sems.at[1, s]))
        for copy in copies:
            copy.start()
        acc[...] = jnp.zeros_like(acc)
        for copy in copies:
            copy.wait()

    q_rows = q[...]
    do_rows = do[...]
    top_buf[...] = stats[0, 0:1, :]
    grad_qt[0] = jnp.zeros_like(grad_qt[0])
    for t in range(3):
        slot = table[row * 3 + t] - blocks_here

        @pl.when(slot >= 0)
        def _():
            scores = dot_nt(rows[0, slot], q_rows)
            dp_buf[t] = dot_nt(rows[1, slot], do_rows)
            s_buf[t] = scores
            top_buf[...] = jnp.maximum(top_buf[...], jnp.max(scores, axis=0, keepdims=True))

    top = top_buf[...]
    shrink = jnp.exp2((stats[0, 0:1, :] - top) * factor)
    sums[0:1, :] = stats[0, 1:2, :] * shrink
    sums[1:2, :] = stats[0, 2:3, :] * shrink
    for t in range(3):
        slot = table[row * 3 + t] - blocks_here

        @pl.when(slot >= 0)
        def _():
            terms = jnp.exp2((s_buf[t] - top_buf[...]) * factor)
            s_buf[t] = terms
            sums[0:1, :] += jnp.sum(terms, axis=0, keepdims=True)
            sums[1:2, :] += jnp.sum(terms * dp_buf[t], axis=0, keepdims=True)

    inverse = 1.0 / sums[0:1, :]
    delta = sums[1:2, :] * inverse
    final[0, 0:1, :] = top
    final[0, 1:2, :] = inverse
    final[0, 2:3, :] = delta
    final[0, 3:8, :] = jnp.zeros((5, top.shape[1]), F32)
    for t in range(3):
        slot = table[row * 3 + t] - blocks_here

        @pl.when(slot >= 0)
        def _():
            weights = s_buf[t] * final[0, 1:2, :]
            dscores = (weights * (dp_buf[t] - final[0, 2:3, :])).astype(BF16)
            acc[1, slot] += dot_nn(weights.astype(BF16), do_rows)
            acc[0, slot] += dot_nn(dscores, q_rows)
            grad_qt[0] += dot_nn(rows[0, slot].T, dscores)

    @pl.when(row == pl.num_programs(0) - 1)
    def _():
        keep_scale = jnp.where(core == 0, scaling, 1.0)
        send_scale = jnp.where(core == 0, 1.0, scaling)
        keep[...] = (acc[core] * keep_scale).astype(BF16)
        send[...] = (acc[1 - core] * send_scale).astype(BF16)


def local_kernel(
    factor, scaling, blocks_here, table, q, do, keys, values, final, grad_qt,
    keep, send, grad_q,
    acc, total_qt,
):
    row = pl.program_id(0)
    core = table[3 * blocks_here]

    @pl.when(row == 0)
    def _():
        acc[...] = jnp.zeros_like(acc)

    q_rows = q[...]
    do_rows = do[...]
    top = final[0, 0:1, :]
    inverse = final[0, 1:2, :]
    delta = final[0, 2:3, :]

    def pair(slot, masked):
        key_rows = keys[slot]
        scores = dot_nt(key_rows, q_rows)
        dprobs = dot_nt(values[slot], do_rows)
        weights = jnp.exp2((scores - top) * factor) * inverse
        if masked:
            col = lax.broadcasted_iota(jnp.int32, scores.shape, 0)
            pos = lax.broadcasted_iota(jnp.int32, scores.shape, 1)
            weights = jnp.where(col <= pos, weights, 0.0)
        dscores = (weights * (dprobs - delta)).astype(BF16)
        acc[1, slot] += dot_nn(weights.astype(BF16), do_rows)
        acc[0, slot] += dot_nn(dscores, q_rows)
        total_qt[...] += dot_nn(key_rows.T, dscores)

    total_qt[...] = grad_qt[0]
    pair(row, True)
    for t in range(3):
        slot = table[row * 3 + t]

        @pl.when((slot >= 0) & (slot < blocks_here))
        def _():
            pair(slot, False)

    grad_q[...] = (total_qt[...].T * scaling).astype(BF16)

    @pl.when(row == pl.num_programs(0) - 1)
    def _():
        keep_scale = jnp.where(core == 0, scaling, 1.0)
        send_scale = jnp.where(core == 0, 1.0, scaling)
        keep[...] = (acc[core] * keep_scale).astype(BF16)
        send[...] = (acc[1 - core] * send_scale).astype(BF16)


def owner_kernel(shifts, place, asked, mine, theirs, *refs):
    back, (out, acc) = refs[:shifts], refs[shifts:]
    acc[...] = mine[...].astype(F32) + theirs[...].astype(F32)
    for s in range(shifts):
        slot = asked_at(asked, shifts, place[0], s) - 1

        @pl.when(slot >= 0)
        def _():
            acc[slot] += back[s][...].astype(F32)

    out[...] = acc[...].astype(BF16)


def params(**more):
    return pltpu.CompilerParams(vmem_limit_bytes=VMEM_LIMIT, **more)


def body(queries, keys, values, dout, selected):
    tok_rows, head_count, feature = queries.shape
    blocks_here = selected.shape[0]
    block_len = tok_rows // blocks_here
    ctx_count = lax.axis_size("ctx")
    ctx_self = lax.axis_index("ctx")
    heads = lax.axis_size("head")
    chips = heads // 2
    core = lax.axis_index("head") % 2
    scaling = 1.0 / math.sqrt(feature)
    factor = scaling * math.log2(math.e)
    shifts = ctx_count - 1
    q2 = queries.reshape(tok_rows, feature)
    do2 = dout.reshape(tok_rows, feature)
    key_blocks = keys.reshape(blocks_here, block_len, feature)
    value_blocks = values.reshape(blocks_here, block_len, feature)
    remote_shape = (shifts, block_len, feature)
    local_shape = (blocks_here, block_len, feature)

    any_spec = pl.BlockSpec(memory_space=pl.ANY)
    row_spec = pl.BlockSpec((block_len, feature), lambda i, *_: (i, 0))
    own_spec = pl.BlockSpec(local_shape, lambda i, *_: (0, 0, 0))
    far_spec = pl.BlockSpec(remote_shape, lambda i, *_: (0, 0, 0))
    stat_spec = pl.BlockSpec((1, 8, block_len), lambda i, *_: (i, 0, 0))
    qt_spec = pl.BlockSpec((1, feature, block_len), lambda i, *_: (i, 0, 0))
    stat_type = jax.ShapeDtypeStruct((blocks_here, 8, block_len), F32)
    far_type = jax.ShapeDtypeStruct(remote_shape, BF16)
    own_type = jax.ShapeDtypeStruct(local_shape, BF16)
    qt_type = jax.ShapeDtypeStruct((blocks_here, feature, block_len), F32)
    pair_flops = 2 * block_len * block_len * feature

    def cost(matmuls, size):
        return pl.CostEstimate(
            flops=matmuls * pair_flops, bytes_accessed=size, transcendentals=matmuls * block_len**2
        )

    swap = [(h, h ^ 1) for h in range(heads)]

    smem = pl.BlockSpec(memory_space=pltpu.SMEM)
    whole = pl.BlockSpec(memory_space=pltpu.VMEM)
    block_type = jax.ShapeDtypeStruct((block_len, feature), BF16)
    place = jnp.stack([ctx_self, core]).astype(jnp.int32)
    info, wants = pl.pallas_call(
        functools.partial(plan_kernel, blocks_here, shifts),
        in_specs=[smem, smem],
        out_specs=[smem, smem],
        out_shape=[
            jax.ShapeDtypeStruct((3 * blocks_here + 1,), jnp.int32),
            jax.ShapeDtypeStruct((ctx_count,), jnp.int32),
        ],
        name="plan",
    )(place, selected)
    asked = lax.all_to_all(
        wants.reshape(ctx_count, 1), "ctx", split_axis=0, concat_axis=0, tiled=True
    ).reshape(ctx_count)

    def to_owner(array, s):
        return lax.ppermute(array, "ctx", [(c, c - s - 1) for c in range(s + 1, ctx_count)])

    def to_reader(array, s):
        return lax.ppermute(array, "ctx", [(c - s - 1, c) for c in range(s + 1, ctx_count)])

    sent = pl.pallas_call(
        functools.partial(pick_kernel, shifts),
        in_specs=[smem, smem, any_spec, any_spec],
        out_specs=[any_spec] * shifts,
        out_shape=[block_type] * shifts,
        scratch_shapes=[
            pltpu.VMEM(local_shape, BF16),
            pltpu.SemaphoreType.DMA,
            pltpu.SemaphoreType.DMA((shifts,)),
        ],
        name="pick_rows",
    )(place, asked, key_blocks, value_blocks)
    fetched = [to_reader(sent[s], s) for s in range(shifts)]
    stats = pl.pallas_call(
        functools.partial(local_stats_kernel, factor, blocks_here),
        grid_spec=pltpu.PrefetchScalarGridSpec(
            num_scalar_prefetch=1,
            grid=(blocks_here,),
            in_specs=[row_spec, row_spec, own_spec, own_spec],
            out_specs=stat_spec,
        ),
        out_shape=stat_type,
        compiler_params=params(),
        cost_estimate=cost(30, 4 * tok_rows * feature * 2),
        name="local_stats",
    )(info, q2, do2, key_blocks, value_blocks)

    fetched, stats = lax.optimization_barrier((fetched, stats))
    other = [lax.ppermute(rows, "head", swap) for rows in fetched]
    keep_far, send_far, final, grad_qt = pl.pallas_call(
        functools.partial(remote_kernel, factor, scaling, blocks_here, shifts),
        grid_spec=pltpu.PrefetchScalarGridSpec(
            num_scalar_prefetch=1,
            grid=(blocks_here,),
            in_specs=[row_spec, row_spec, stat_spec] + [any_spec] * (2 * shifts),
            out_specs=[far_spec, far_spec, stat_spec, qt_spec],
            scratch_shapes=[
                pltpu.VMEM((2,) + remote_shape, BF16),
                pltpu.VMEM((2,) + remote_shape, F32),
                pltpu.VMEM((3, block_len, block_len), F32),
                pltpu.VMEM((3, block_len, block_len), F32),
                pltpu.VMEM((1, block_len), F32),
                pltpu.VMEM((2, block_len), F32),
                pltpu.SemaphoreType.DMA((2, shifts)),
            ],
        ),
        out_shape=[far_type, far_type, stat_type, qt_type],
        compiler_params=params(),
        cost_estimate=cost(60, 8 * tok_rows * feature * 2),
        name="remote_pairs",
    )(info, q2, do2, stats, *fetched, *other)

    from_far = lax.ppermute(send_far, "head", swap)
    chip_far = pl.pallas_call(
        functools.partial(chip_sum_kernel, shifts),
        in_specs=[whole, whole],
        out_specs=[whole] * shifts,
        out_shape=[block_type] * shifts,
        compiler_params=params(),
        name="chip_sum",
    )(keep_far, from_far)
    chip_far, final = lax.optimization_barrier((chip_far, final))
    back = [to_owner(chip_far[s], s) for s in range(shifts)]
    keep_own, send_own, grad_q = pl.pallas_call(
        functools.partial(local_kernel, factor, scaling, blocks_here),
        grid_spec=pltpu.PrefetchScalarGridSpec(
            num_scalar_prefetch=1,
            grid=(blocks_here,),
            in_specs=[row_spec, row_spec, own_spec, own_spec, stat_spec, qt_spec],
            out_specs=[own_spec, own_spec, row_spec],
            scratch_shapes=[
                pltpu.VMEM((2,) + local_shape, F32),
                pltpu.VMEM((feature, block_len), F32),
            ],
        ),
        out_shape=[own_type, own_type, jax.ShapeDtypeStruct((tok_rows, feature), BF16)],
        compiler_params=params(),
        cost_estimate=cost(60, 8 * tok_rows * feature * 2),
        name="local_pairs",
    )(info, q2, do2, key_blocks, value_blocks, final, grad_qt)

    from_own = lax.ppermute(send_own, "head", swap)
    mine = pl.pallas_call(
        functools.partial(owner_kernel, shifts),
        in_specs=[smem, smem] + [whole] * (2 + shifts),
        out_specs=whole,
        out_shape=own_type,
        scratch_shapes=[pltpu.VMEM(local_shape, F32)],
        compiler_params=params(),
        name="owner_sum",
    )(place, asked, keep_own, from_own, *back)
    parts = [mine] + [
        lax.ppermute(mine, "head", [(h, (h + 2 * s) % heads) for h in range(heads)])
        for s in range(1, chips)
    ]
    if chips == 2:
        total = parts[0].astype(F32) + parts[1].astype(F32)
    else:
        chip = lax.axis_index("head") // 2
        stack = jnp.stack(parts)[(chip - jnp.arange(chips)) % chips]
        total = jnp.sum(stack.astype(F32), axis=0)
    total = total.astype(BF16).reshape(tok_rows, feature)
    twin = lax.ppermute(total, "head", swap)
    grad_keys = jnp.where(core == 0, total, twin)
    grad_values = jnp.where(core == 0, twin, total)
    return (grad_q.reshape(tok_rows, head_count, feature), grad_keys, grad_values)


def solution(mesh):
    return jax.shard_map(
        body,
        mesh=mesh,
        in_specs=(
            P("ctx", "head", None),
            P("ctx", None),
            P("ctx", None),
            P("ctx", "head", None),
            P("ctx", None),
        ),
        out_specs=(P("ctx", "head", None), P("ctx", None), P("ctx", None)),
        check_vma=False,
    )
```

```python
import functools
import math

import jax
import jax.numpy as jnp
from jax import lax
from jax.experimental import pallas as pl
from jax.experimental.pallas import tpu as pltpu
from jax.sharding import PartitionSpec as P

F32 = jnp.float32
BF16 = jnp.bfloat16
VMEM_LIMIT = 56 * 1024 * 1024


def dot_nt(a, b):
    return lax.dot_general(a, b, (((1,), (1,)), ((), ())), preferred_element_type=F32)


def dot_nn(a, b):
    return lax.dot_general(a, b, (((1,), (0,)), ((), ())), preferred_element_type=F32)


def plan_kernel(blocks_here, shifts, place, chosen, table, wants):
    ctx_self = place[0]
    best = [jnp.int32(0)] * shifts
    for row in range(blocks_here):
        for t in range(3):
            entry = chosen[row, t]
            owner = lax.div(entry, jnp.int32(blocks_here))
            inside = entry - owner * blocks_here
            apart = ctx_self - owner
            live = entry != ctx_self * blocks_here + row
            slot = jnp.where(apart == 0, inside, blocks_here + apart - 1)
            table[row * 3 + t] = jnp.where(live, slot, -1)
            for s in range(shifts):
                best[s] = jnp.where(live & (apart == s + 1), inside + 1, best[s])
    table[3 * blocks_here] = place[1]
    for peer in range(shifts + 1):
        wants[peer] = jnp.int32(0)
    for s in range(shifts):

        @pl.when(ctx_self > s)
        def _():
            wants[ctx_self - s - 1] = best[s]


def asked_at(asked, shifts, ctx_self, s):
    peer = ctx_self + s + 1
    return jnp.where(peer <= shifts, asked[jnp.minimum(peer, shifts)], 0)


def pick_kernel(shifts, place, asked, keys, values, *refs):
    outs, (rows, in_sem, out_sems) = refs[:shifts], refs[shifts:]
    ctx_self, core = place[0], place[1]

    @pl.when(core == 0)
    def _():
        pltpu.make_async_copy(keys, rows, in_sem).start()

    @pl.when(core != 0)
    def _():
        pltpu.make_async_copy(values, rows, in_sem).start()

    pltpu.make_async_copy(keys, rows, in_sem).wait()
    copies = [
        pltpu.make_async_copy(
            rows.at[jnp.maximum(asked_at(asked, shifts, ctx_self, s) - 1, 0)],
            outs[s],
            out_sems.at[s],
        )
        for s in range(shifts)
    ]
    for copy in copies:
        copy.start()
    for copy in copies:
        copy.wait()


def chip_sum_kernel(shifts, mine, theirs, *outs):
    for s in range(shifts):
        outs[s][...] = (mine[s].astype(F32) + theirs[s].astype(F32)).astype(BF16)


def chip_sum_kernel(shifts, mine, theirs, *outs):
    for s in range(shifts):
        outs[s][...] = (mine[s].astype(F32) + theirs[s].astype(F32)).astype(BF16)


def pair_terms(key_rows, value_rows, q_rows, do_rows, factor, masked):
    scores = dot_nt(key_rows, q_rows)
    dprobs = dot_nt(value_rows, do_rows)
    if masked:
        col = lax.broadcasted_iota(jnp.int32, scores.shape, 0)
        pos = lax.broadcasted_iota(jnp.int32, scores.shape, 1)
        scores = jnp.where(col <= pos, scores, -jnp.inf)
    top = jnp.max(scores, axis=0, keepdims=True) * factor
    terms = jnp.exp2(scores * factor - top)
    total = jnp.sum(terms, axis=0, keepdims=True)
    weighted = jnp.sum(terms * dprobs, axis=0, keepdims=True)
    return terms, dprobs, top, total, weighted


def local_stats_kernel(factor, blocks_here, table, q, do, keys, values, stats):
    block_len = keys.shape[1]

    def per_row(row, _):
        span = pl.ds(row * block_len, block_len)
        q_rows = q[span, :]
        do_rows = do[span, :]

        def pair(slot, masked):
            return pair_terms(keys[slot], values[slot], q_rows, do_rows, factor, masked)[2:]

        top, total, weighted = pair(row, True)
        stats[row, 0:1, :] = top
        stats[row, 1:2, :] = total
        stats[row, 2:3, :] = weighted
        for t in range(3):
            slot = table[row * 3 + t]

            @pl.when((slot >= 0) & (slot < blocks_here))
            def _():
                more_top, more, more_weighted = pair(slot, False)
                old = stats[row, 0:1, :]
                top = jnp.maximum(old, more_top)
                scale_old = jnp.exp2(old - top)
                scale_new = jnp.exp2(more_top - top)
                stats[row, 0:1, :] = top
                stats[row, 1:2, :] = stats[row, 1:2, :] * scale_old + more * scale_new
                stats[row, 2:3, :] = stats[row, 2:3, :] * scale_old + more_weighted * scale_new

        return 0

    lax.fori_loop(0, blocks_here, per_row, 0)


def remote_kernel(factor, scaling, blocks_here, shifts, table, q, do, stats, *refs):
    fetched, other, refs = refs[:shifts], refs[shifts : 2 * shifts], refs[2 * shifts :]
    keep, send, final, grad_qt, rows, acc, terms_buf, dp_buf, parts = refs
    core = table[3 * blocks_here]
    block_len = rows.shape[2]

    @pl.when(core == 0)
    def _():
        for s in range(shifts):
            rows[0, s] = fetched[s][...]
            rows[1, s] = other[s][...]

    @pl.when(core != 0)
    def _():
        for s in range(shifts):
            rows[0, s] = other[s][...]
            rows[1, s] = fetched[s][...]

    acc[...] = jnp.zeros_like(acc)

    def per_row(row, _):
        span = pl.ds(row * block_len, block_len)
        parts[0, 0:3, :] = stats[row, 0:3, :]
        for t in range(3):
            slot = table[row * 3 + t] - blocks_here

            @pl.when(slot >= 0)
            def _():
                terms, dprobs, top, total, weighted = pair_terms(
                    rows[0, slot], rows[1, slot], q[span, :], do[span, :], factor, False
                )
                terms_buf[t] = terms
                dp_buf[t] = dprobs
                parts[t + 1, 0:1, :] = top
                parts[t + 1, 1:2, :] = total
                parts[t + 1, 2:3, :] = weighted

            @pl.when(slot < 0)
            def _():
                parts[t + 1, 0:1, :] = jnp.full((1, block_len), -jnp.inf, F32)
                parts[t + 1, 1:3, :] = jnp.zeros((2, block_len), F32)

        top = parts[0, 0:1, :]
        for t in range(3):
            top = jnp.maximum(top, parts[t + 1, 0:1, :])
        total = jnp.zeros_like(top)
        weighted = jnp.zeros_like(top)
        for t in range(4):
            scale = jnp.exp2(parts[t, 0:1, :] - top)
            parts[t, 3:4, :] = scale
            total = total + scale * parts[t, 1:2, :]
            weighted = weighted + scale * parts[t, 2:3, :]
        inverse = 1.0 / total
        delta = weighted * inverse
        final[row, 0:1, :] = top + jnp.log2(total)
        final[row, 1:2, :] = delta
        for t in range(3):
            parts[t + 1, 3:4, :] = parts[t + 1, 3:4, :] * inverse
        grad_qt[row] = jnp.zeros_like(grad_qt[row])
        for t in range(3):
            slot = table[row * 3 + t] - blocks_here

            @pl.when(slot >= 0)
            def _():
                weights = terms_buf[t] * parts[t + 1, 3:4, :]
                dscores = (weights * (dp_buf[t] - final[row, 1:2, :])).astype(BF16)
                acc[1, slot] += dot_nn(weights.astype(BF16), do[span, :])
                acc[0, slot] += dot_nn(dscores, q[span, :])
                grad_qt[row] += dot_nn(rows[0, slot].T, dscores)

        return 0

    lax.fori_loop(0, blocks_here, per_row, 0)
    keep_scale = jnp.where(core == 0, scaling, 1.0)
    send_scale = jnp.where(core == 0, 1.0, scaling)
    keep[...] = (acc[core] * keep_scale).astype(BF16)
    send[...] = (acc[1 - core] * send_scale).astype(BF16)


def local_kernel(
    factor, scaling, blocks_here, table, q, do, keys, values, final, grad_qt,
    keep, send, grad_q,
    acc, total_qt,
):
    core = table[3 * blocks_here]
    block_len = keys.shape[1]
    acc[...] = jnp.zeros_like(acc)

    def per_row(row, _):
        span = pl.ds(row * block_len, block_len)

        def pair(slot, masked):
            q_rows = q[span, :]
            do_rows = do[span, :]
            key_rows = keys[slot]
            scores = dot_nt(key_rows, q_rows)
            dprobs = dot_nt(values[slot], do_rows)
            weights = jnp.exp2(scores * factor - final[row, 0:1, :])
            if masked:
                col = lax.broadcasted_iota(jnp.int32, scores.shape, 0)
                pos = lax.broadcasted_iota(jnp.int32, scores.shape, 1)
                weights = jnp.where(col <= pos, weights, 0.0)
            dscores = (weights * (dprobs - final[row, 1:2, :])).astype(BF16)
            acc[1, slot] += dot_nn(weights.astype(BF16), do_rows)
            acc[0, slot] += dot_nn(dscores, q_rows)
            total_qt[...] += dot_nn(key_rows.T, dscores)

        total_qt[...] = grad_qt[row]
        pair(row, True)
        for t in range(3):
            slot = table[row * 3 + t]

            @pl.when((slot >= 0) & (slot < blocks_here))
            def _():
                pair(slot, False)

        grad_q[span, :] = (total_qt[...].T * scaling).astype(BF16)
        return 0

    lax.fori_loop(0, blocks_here, per_row, 0)
    keep_scale = jnp.where(core == 0, scaling, 1.0)
    send_scale = jnp.where(core == 0, 1.0, scaling)
    keep[...] = (acc[core] * keep_scale).astype(BF16)
    send[...] = (acc[1 - core] * send_scale).astype(BF16)


def owner_kernel(shifts, place, asked, mine, theirs, *refs):
    back, (out, acc) = refs[:shifts], refs[shifts:]
    acc[...] = mine[...].astype(F32) + theirs[...].astype(F32)
    for s in range(shifts):
        slot = asked_at(asked, shifts, place[0], s) - 1

        @pl.when(slot >= 0)
        def _():
            acc[slot] += back[s][...].astype(F32)

    out[...] = acc[...].astype(BF16)


def params(size):
    return pltpu.CompilerParams(vmem_limit_bytes=min(size + 12 * 1024 * 1024, VMEM_LIMIT))


def body(queries, keys, values, dout, selected):
    tok_rows, head_count, feature = queries.shape
    blocks_here = selected.shape[0]
    block_len = tok_rows // blocks_here
    ctx_count = lax.axis_size("ctx")
    ctx_self = lax.axis_index("ctx")
    heads = lax.axis_size("head")
    chips = heads // 2
    core = lax.axis_index("head") % 2
    scaling = 1.0 / math.sqrt(feature)
    factor = scaling * math.log2(math.e)
    shifts = ctx_count - 1
    q2 = queries.reshape(tok_rows, feature)
    do2 = dout.reshape(tok_rows, feature)
    key_blocks = keys.reshape(blocks_here, block_len, feature)
    value_blocks = values.reshape(blocks_here, block_len, feature)
    remote_shape = (shifts, block_len, feature)
    local_shape = (blocks_here, block_len, feature)

    any_spec = pl.BlockSpec(memory_space=pl.ANY)
    stat_type = jax.ShapeDtypeStruct((blocks_here, 8, block_len), F32)
    far_type = jax.ShapeDtypeStruct(remote_shape, BF16)
    own_type = jax.ShapeDtypeStruct(local_shape, BF16)
    qt_type = jax.ShapeDtypeStruct((blocks_here, feature, block_len), F32)
    pair_flops = 2 * block_len * block_len * feature

    def cost(matmuls, size):
        return pl.CostEstimate(
            flops=matmuls * pair_flops, bytes_accessed=size, transcendentals=matmuls * block_len**2
        )

    swap = [(h, h ^ 1) for h in range(heads)]

    smem = pl.BlockSpec(memory_space=pltpu.SMEM)
    whole = pl.BlockSpec(memory_space=pltpu.VMEM)
    block_type = jax.ShapeDtypeStruct((block_len, feature), BF16)
    place = jnp.stack([ctx_self, core]).astype(jnp.int32)
    info, wants = pl.pallas_call(
        functools.partial(plan_kernel, blocks_here, shifts),
        in_specs=[smem, smem],
        out_specs=[smem, smem],
        out_shape=[
            jax.ShapeDtypeStruct((3 * blocks_here + 1,), jnp.int32),
            jax.ShapeDtypeStruct((ctx_count,), jnp.int32),
        ],
        name="plan",
    )(place, selected)
    asked = lax.all_to_all(
        wants.reshape(ctx_count, 1), "ctx", split_axis=0, concat_axis=0, tiled=True
    ).reshape(ctx_count)

    def to_owner(array, s):
        return lax.ppermute(array, "ctx", [(c, c - s - 1) for c in range(s + 1, ctx_count)])

    def to_reader(array, s):
        return lax.ppermute(array, "ctx", [(c - s - 1, c) for c in range(s + 1, ctx_count)])

    sent = pl.pallas_call(
        functools.partial(pick_kernel, shifts),
        in_specs=[smem, smem, any_spec, any_spec],
        out_specs=[any_spec] * shifts,
        out_shape=[block_type] * shifts,
        scratch_shapes=[
            pltpu.VMEM(local_shape, BF16),
            pltpu.SemaphoreType.DMA,
            pltpu.SemaphoreType.DMA((shifts,)),
        ],
        name="pick_rows",
    )(place, asked, key_blocks, value_blocks)
    order = sorted(range(shifts), key=lambda s: abs(2 * (s + 1) - ctx_count))

    def by_shift(move, arrays):
        moved = {s: move(arrays[s], s) for s in order}
        return [moved[s] for s in range(shifts)]

    fetched = by_shift(to_reader, sent)
    block_bytes = block_len * feature * 2
    stats = pl.pallas_call(
        functools.partial(local_stats_kernel, factor, blocks_here),
        in_specs=[smem] + [whole] * 4,
        out_specs=whole,
        out_shape=stat_type,
        compiler_params=params(4 * blocks_here * block_bytes),
        cost_estimate=cost(30, 4 * tok_rows * feature * 2),
        name="local_stats",
    )(info, q2, do2, key_blocks, value_blocks)

    arrived, stats = lax.optimization_barrier((fetched, stats))
    other = [lax.ppermute(rows, "head", swap) for rows in arrived]
    pair_bytes = block_len * block_len * 4
    keep_far, send_far, final, grad_qt = pl.pallas_call(
        functools.partial(remote_kernel, factor, scaling, blocks_here, shifts),
        in_specs=[smem] + [whole] * (3 + 2 * shifts),
        out_specs=[whole] * 4,
        out_shape=[far_type, far_type, stat_type, qt_type],
        scratch_shapes=[
            pltpu.VMEM((2,) + remote_shape, BF16),
            pltpu.VMEM((2,) + remote_shape, F32),
            pltpu.VMEM((3, block_len, block_len), F32),
            pltpu.VMEM((3, block_len, block_len), F32),
            pltpu.VMEM((4, 8, block_len), F32),
        ],
        compiler_params=params((10 * shifts + 4 * blocks_here) * block_bytes + 6 * pair_bytes),
        cost_estimate=cost(60, 8 * tok_rows * feature * 2),
        name="remote_pairs",
    )(info, q2, do2, stats, *arrived, *other)

    from_far = lax.ppermute(send_far, "head", swap)
    chip_far = pl.pallas_call(
        functools.partial(chip_sum_kernel, shifts),
        in_specs=[whole, whole],
        out_specs=[whole] * shifts,
        out_shape=[block_type] * shifts,
        compiler_params=params(3 * shifts * block_bytes),
        name="chip_sum",
    )(keep_far, from_far)
    chip_far, final = lax.optimization_barrier((chip_far, final))
    back = by_shift(to_owner, chip_far)
    keep_own, send_own, grad_q = pl.pallas_call(
        functools.partial(local_kernel, factor, scaling, blocks_here),
        in_specs=[smem] + [whole] * 6,
        out_specs=[whole] * 3,
        out_shape=[own_type, own_type, jax.ShapeDtypeStruct((tok_rows, feature), BF16)],
        scratch_shapes=[
            pltpu.VMEM((2,) + local_shape, F32),
            pltpu.VMEM((feature, block_len), F32),
        ],
        compiler_params=params(14 * blocks_here * block_bytes),
        cost_estimate=cost(60, 8 * tok_rows * feature * 2),
        name="local_pairs",
    )(info, q2, do2, key_blocks, value_blocks, final, grad_qt)
    back, keep_own, send_own = lax.optimization_barrier((back, keep_own, send_own))
    from_own = lax.ppermute(send_own, "head", swap)
    mine = pl.pallas_call(
        functools.partial(owner_kernel, shifts),
        in_specs=[smem, smem] + [whole] * (2 + shifts),
        out_specs=whole,
        out_shape=own_type,
        scratch_shapes=[pltpu.VMEM(local_shape, F32)],
        compiler_params=params((5 * blocks_here + shifts) * block_bytes),
        name="owner_sum",
    )(place, asked, keep_own, from_own, *back)
    parts = [mine] + [
        lax.ppermute(mine, "head", [(h, (h + 2 * s) % heads) for h in range(heads)])
        for s in range(1, chips)
    ]
    if chips == 2:
        total = parts[0].astype(F32) + parts[1].astype(F32)
    else:
        chip = lax.axis_index("head") // 2
        stack = jnp.stack(parts)[(chip - jnp.arange(chips)) % chips]
        total = jnp.sum(stack.astype(F32), axis=0)
    total = total.astype(BF16).reshape(tok_rows, feature)
    twin = lax.ppermute(total, "head", swap)
    grad_keys = jnp.where(core == 0, total, twin)
    grad_values = jnp.where(core == 0, twin, total)
    return (grad_q.reshape(tok_rows, head_count, feature), grad_keys, grad_values)


def solution(mesh):
    return jax.shard_map(
        body,
        mesh=mesh,
        in_specs=(
            P("ctx", "head", None),
            P("ctx", None),
            P("ctx", None),
            P("ctx", "head", None),
            P("ctx", None),
        ),
        out_specs=(P("ctx", "head", None), P("ctx", None), P("ctx", None)),
        check_vma=False,
    )
```

```python
import functools
import math

import jax
import jax.numpy as jnp
from jax import lax
from jax.experimental import pallas as pl
from jax.experimental.pallas import tpu as pltpu
from jax.sharding import PartitionSpec as P

F32 = jnp.float32
BF16 = jnp.bfloat16
VMEM_LIMIT = 56 * 1024 * 1024


def dot_nt(a, b):
    return lax.dot_general(a, b, (((1,), (1,)), ((), ())), preferred_element_type=F32)


def dot_nn(a, b):
    return lax.dot_general(a, b, (((1,), (0,)), ((), ())), preferred_element_type=F32)


def plan_kernel(blocks_here, chosen, table):
    ctx_self = lax.axis_index("ctx")
    for row in range(blocks_here):
        for t in range(3):
            entry = chosen[row, t]
            owner = lax.div(entry, jnp.int32(blocks_here))
            inside = entry - owner * blocks_here
            apart = ctx_self - owner
            live = entry != ctx_self * blocks_here + row
            slot = jnp.where(apart == 0, inside, blocks_here + apart - 1)
            table[row * 3 + t] = jnp.where(live, slot, -1)


def pick_kernel(blocks_here, count, chips, far, piece, chosen, keys, values, asked, *outs):
    ctx_self = lax.axis_index("ctx")
    place = lax.axis_index("head")
    core, chip = lax.rem(place, 2), lax.div(place, 2)
    first = ctx_self * blocks_here
    for s in range(count - 1):
        peer = ctx_self + s + 1
        near = jnp.minimum(peer, count - 1)
        found = jnp.int32(0)
        for row in range(blocks_here):
            for t in range(3):
                entry = chosen[near, row * 3 + t]
                hit = (entry >= first) & (entry < first + blocks_here)
                found = jnp.where(hit, entry - first + 1, found)
        asked[s] = jnp.where(peer < count, found, 0)

    def fill(source):
        for s in range(count - 1):
            slot = jnp.maximum(asked[s] - 1, 0)
            if s in far:
                span = pl.ds(pl.multiple_of(chip * piece, piece), piece)
                outs[s][...] = source[slot, span, :]
            else:
                outs[s][...] = source[slot]

    @pl.when(core == 0)
    def _():
        fill(keys)

    @pl.when(core != 0)
    def _():
        fill(values)


def chip_sum_kernel(chips, piece, groups, mine, theirs, *outs):
    chip = lax.div(lax.axis_index("head"), 2)
    outs = list(outs)
    for group in groups:
        for d in range(chips):
            out = outs.pop(0)
            target = lax.rem(chip + d, chips)
            span = pl.ds(pl.multiple_of(target * piece, piece), piece)
            for i, s in enumerate(group):
                total = mine[s, span, :].astype(F32) + theirs[s, span, :].astype(F32)
                out[i] = total.astype(out.dtype)


def head_sum_kernel(count, mine, *refs):
    parts, outs = refs[: len(refs) - count], refs[len(refs) - count :]
    for i in range(count):
        total = mine[i]
        for part in parts:
            total = total + part[i].astype(F32)
        outs[i][...] = total.astype(BF16)


def pair_terms(key_rows, value_rows, q_rows, do_rows, factor, masked):
    scores = dot_nt(key_rows, q_rows)
    dprobs = dot_nt(value_rows, do_rows)
    if masked:
        col = lax.broadcasted_iota(jnp.int32, scores.shape, 0)
        pos = lax.broadcasted_iota(jnp.int32, scores.shape, 1)
        scores = jnp.where(col <= pos, scores, -jnp.inf)
    top = jnp.max(scores, axis=0, keepdims=True) * factor
    terms = jnp.exp2(scores * factor - top)
    total = jnp.sum(terms, axis=0, keepdims=True)
    weighted = jnp.sum(terms * dprobs, axis=0, keepdims=True)
    return terms, dprobs, top, total, weighted


def local_stats_kernel(factor, blocks_here, table, q, do, keys, values, stats):
    block_len = keys.shape[1]

    def per_row(row, _):
        span = pl.ds(row * block_len, block_len)
        q_rows = q[span, :]
        do_rows = do[span, :]

        def pair(slot, masked):
            return pair_terms(keys[slot], values[slot], q_rows, do_rows, factor, masked)[2:]

        top, total, weighted = pair(row, True)
        stats[row, 0:1, :] = top
        stats[row, 1:2, :] = total
        stats[row, 2:3, :] = weighted
        for t in range(3):
            slot = table[row * 3 + t]

            @pl.when((slot >= 0) & (slot < blocks_here))
            def _():
                more_top, more, more_weighted = pair(slot, False)
                old = stats[row, 0:1, :]
                top = jnp.maximum(old, more_top)
                scale_old = jnp.exp2(old - top)
                scale_new = jnp.exp2(more_top - top)
                stats[row, 0:1, :] = top
                stats[row, 1:2, :] = stats[row, 1:2, :] * scale_old + more * scale_new
                stats[row, 2:3, :] = stats[row, 2:3, :] * scale_old + more_weighted * scale_new

        return 0

    lax.fori_loop(0, blocks_here, per_row, 0)


def remote_kernel(
    factor, scaling, blocks_here, chips, far, near, piece, table, q, do, stats, *refs
):
    near_refs, far_refs, refs = refs[:2], refs[2 : 2 + 2 * chips], refs[2 + 2 * chips :]
    keep, send, final, grad_qt, rows, acc, terms_buf, dp_buf, parts = refs
    place = lax.axis_index("head")
    core, chip = lax.rem(place, 2), lax.div(place, 2)
    block_len = rows.shape[2]

    def lay(kind, which):
        for i, s in enumerate(near):
            rows[kind, s] = near_refs[which][i]
        for d in range(chips):
            source = lax.rem(chip + chips - d, chips)
            span = pl.ds(pl.multiple_of(source * piece, piece), piece)
            for i, s in enumerate(far):
                rows[kind, s, span, :] = far_refs[2 * d + which][i]

    @pl.when(core == 0)
    def _():
        lay(0, 0)
        lay(1, 1)

    @pl.when(core != 0)
    def _():
        lay(0, 1)
        lay(1, 0)

    acc[...] = jnp.zeros_like(acc)

    def per_row(row, _):
        span = pl.ds(row * block_len, block_len)
        parts[0, 0:3, :] = stats[row, 0:3, :]
        for t in range(3):
            slot = table[row * 3 + t] - blocks_here

            @pl.when(slot >= 0)
            def _():
                terms, dprobs, top, total, weighted = pair_terms(
                    rows[0, slot], rows[1, slot], q[span, :], do[span, :], factor, False
                )
                terms_buf[t] = terms
                dp_buf[t] = dprobs
                parts[t + 1, 0:1, :] = top
                parts[t + 1, 1:2, :] = total
                parts[t + 1, 2:3, :] = weighted

            @pl.when(slot < 0)
            def _():
                parts[t + 1, 0:1, :] = jnp.full((1, block_len), -jnp.inf, F32)
                parts[t + 1, 1:3, :] = jnp.zeros((2, block_len), F32)

        top = parts[0, 0:1, :]
        for t in range(3):
            top = jnp.maximum(top, parts[t + 1, 0:1, :])
        total = jnp.zeros_like(top)
        weighted = jnp.zeros_like(top)
        for t in range(4):
            scale = jnp.exp2(parts[t, 0:1, :] - top)
            parts[t, 3:4, :] = scale
            total = total + scale * parts[t, 1:2, :]
            weighted = weighted + scale * parts[t, 2:3, :]
        inverse = 1.0 / total
        delta = weighted * inverse
        final[row, 0:1, :] = top + jnp.log2(total)
        final[row, 1:2, :] = delta
        for t in range(3):
            parts[t + 1, 3:4, :] = parts[t + 1, 3:4, :] * inverse
        grad_qt[row] = jnp.zeros_like(grad_qt[row])
        for t in range(3):
            slot = table[row * 3 + t] - blocks_here

            @pl.when(slot >= 0)
            def _():
                weights = terms_buf[t] * parts[t + 1, 3:4, :]
                dscores = (weights * (dp_buf[t] - final[row, 1:2, :])).astype(BF16)
                acc[1, slot] += dot_nn(weights.astype(BF16), do[span, :])
                acc[0, slot] += dot_nn(dscores, q[span, :])
                grad_qt[row] += dot_nn(rows[0, slot].T, dscores)

        return 0

    lax.fori_loop(0, blocks_here, per_row, 0)
    keep_scale = jnp.where(core == 0, scaling, 1.0)
    send_scale = jnp.where(core == 0, 1.0, scaling)
    keep[...] = (acc[core] * keep_scale).astype(BF16)
    send[...] = (acc[1 - core] * send_scale).astype(BF16)


def local_kernel(
    factor, scaling, blocks_here, table, q, do, keys, values, final, grad_qt,
    keep, send, grad_q,
    acc, total_qt,
):
    core = lax.rem(lax.axis_index("head"), 2)
    block_len = keys.shape[1]
    acc[...] = jnp.zeros_like(acc)

    def per_row(row, _):
        span = pl.ds(row * block_len, block_len)

        def pair(slot, masked):
            q_rows = q[span, :]
            do_rows = do[span, :]
            key_rows = keys[slot]
            scores = dot_nt(key_rows, q_rows)
            dprobs = dot_nt(values[slot], do_rows)
            weights = jnp.exp2(scores * factor - final[row, 0:1, :])
            if masked:
                col = lax.broadcasted_iota(jnp.int32, scores.shape, 0)
                pos = lax.broadcasted_iota(jnp.int32, scores.shape, 1)
                weights = jnp.where(col <= pos, weights, 0.0)
            dscores = (weights * (dprobs - final[row, 1:2, :])).astype(BF16)
            acc[1, slot] += dot_nn(weights.astype(BF16), do_rows)
            acc[0, slot] += dot_nn(dscores, q_rows)
            total_qt[...] += dot_nn(key_rows.T, dscores)

        total_qt[...] = grad_qt[row]
        pair(row, True)
        for t in range(3):
            slot = table[row * 3 + t]

            @pl.when((slot >= 0) & (slot < blocks_here))
            def _():
                pair(slot, False)

        grad_q[span, :] = (total_qt[...].T * scaling).astype(BF16)
        return 0

    lax.fori_loop(0, blocks_here, per_row, 0)
    keep_scale = jnp.where(core == 0, scaling, 1.0)
    send_scale = jnp.where(core == 0, 1.0, scaling)
    keep[...] = (acc[core] * keep_scale).astype(BF16)
    send[...] = (acc[1 - core] * send_scale).astype(BF16)


def owner_kernel(chips, shifts, asked, mine, *refs):
    others, back, (out, acc) = refs[: chips - 1], refs[chips - 1 : chips - 1 + shifts], refs[-2:]
    total = mine[...]
    for part in others:
        total = total + part[...].astype(F32)
    acc[...] = total
    for s in range(shifts):
        slot = asked[s] - 1

        @pl.when(slot >= 0)
        def _():
            acc[slot] += back[s][...].astype(F32)

    out[...] = acc[...].astype(BF16)


def spread_kernel(chips, piece, *refs):
    pieces, (grad_k, grad_v) = refs[: 2 * chips], refs[2 * chips :]
    place = lax.axis_index("head")
    core, chip = lax.rem(place, 2), lax.div(place, 2)

    def lay(out, which):
        for d in range(chips):
            source = lax.rem(chip + chips - d, chips)
            span = pl.ds(pl.multiple_of(source * piece, piece), piece)
            out[:, span, :] = pieces[2 * d + which][...]

    @pl.when(core == 0)
    def _():
        lay(grad_k, 0)
        lay(grad_v, 1)

    @pl.when(core != 0)
    def _():
        lay(grad_k, 1)
        lay(grad_v, 0)


def params(size):
    return pltpu.CompilerParams(vmem_limit_bytes=min(size + 12 * 1024 * 1024, VMEM_LIMIT))


def body(queries, keys, values, dout, selected):
    tok_rows, head_count, feature = queries.shape
    blocks_here = selected.shape[0]
    block_len = tok_rows // blocks_here
    ctx_count = lax.axis_size("ctx")
    heads = lax.axis_size("head")
    chips = heads // 2
    piece = block_len // chips
    scaling = 1.0 / math.sqrt(feature)
    factor = scaling * math.log2(math.e)
    shifts = ctx_count - 1
    far = sorted((s for s in range(shifts) if 2 * (s + 1) >= ctx_count), key=lambda s: s)
    near = sorted((s for s in range(shifts) if 2 * (s + 1) < ctx_count), key=lambda s: -s)

    q2 = queries.reshape(tok_rows, feature)
    do2 = dout.reshape(tok_rows, feature)
    key_blocks = keys.reshape(blocks_here, block_len, feature)
    value_blocks = values.reshape(blocks_here, block_len, feature)
    remote_shape = (shifts, block_len, feature)
    local_shape = (blocks_here, block_len, feature)

    smem = pl.BlockSpec(memory_space=pltpu.SMEM)
    whole = pl.BlockSpec(memory_space=pltpu.VMEM)
    stat_type = jax.ShapeDtypeStruct((blocks_here, 8, block_len), F32)
    far_type = jax.ShapeDtypeStruct(remote_shape, BF16)
    own_type = jax.ShapeDtypeStruct(local_shape, BF16)
    block_type = jax.ShapeDtypeStruct((block_len, feature), BF16)
    piece_type = jax.ShapeDtypeStruct((piece, feature), BF16)
    qt_type = jax.ShapeDtypeStruct((blocks_here, feature, block_len), F32)
    pair_flops = 2 * block_len * block_len * feature
    block_bytes = block_len * feature * 2
    pair_bytes = block_len * block_len * 4

    def pieces_type(count, dtype):
        return jax.ShapeDtypeStruct((count, piece, feature), dtype)

    def cost(matmuls, size):
        return pl.CostEstimate(
            flops=matmuls * pair_flops, bytes_accessed=size, transcendentals=matmuls * block_len**2
        )

    def swap(array):
        return lax.ppermute(array, "head", [(h, h ^ 1) for h in range(heads)])

    def to_chip(array, d):
        return lax.ppermute(array, "head", [(h, (h + 2 * d) % heads) for h in range(heads)])

    def to_owner(array, s):
        return lax.ppermute(array, "ctx", [(c, c - s - 1) for c in range(s + 1, ctx_count)])

    def to_reader(array, s):
        return lax.ppermute(array, "ctx", [(c - s - 1, c) for c in range(s + 1, ctx_count)])

    everyone = lax.all_to_all(
        jnp.broadcast_to(selected.reshape(1, 3 * blocks_here), (ctx_count, 3 * blocks_here)),
        "ctx", split_axis=0, concat_axis=0, tiled=True,
    )
    info = pl.pallas_call(
        functools.partial(plan_kernel, blocks_here),
        in_specs=[smem],
        out_specs=smem,
        out_shape=jax.ShapeDtypeStruct((3 * blocks_here,), jnp.int32),
        name="plan",
    )(selected)
    asked, *sent = pl.pallas_call(
        functools.partial(pick_kernel, blocks_here, ctx_count, chips, far, piece),
        in_specs=[smem, whole, whole],
        out_specs=[smem] + [whole] * shifts,
        out_shape=[jax.ShapeDtypeStruct((shifts,), jnp.int32)]
        + [piece_type if s in far else block_type for s in range(shifts)],
        compiler_params=params((2 * blocks_here + shifts) * block_bytes),
        name="pick_rows",
    )(everyone, key_blocks, value_blocks)

    far_mine = jnp.stack([to_reader(sent[s], s) for s in far])
    near_parts = [to_reader(sent[s], s) for s in near]
    far_mine, info = lax.optimization_barrier((far_mine, info))
    far_more = [to_chip(far_mine, d) for d in range(1, chips)]
    stats = pl.pallas_call(
        functools.partial(local_stats_kernel, factor, blocks_here),
        in_specs=[smem] + [whole] * 4,
        out_specs=whole,
        out_shape=stat_type,
        compiler_params=params(4 * blocks_here * block_bytes),
        cost_estimate=cost(30, 4 * tok_rows * feature * 2),
        name="local_stats",
    )(info, q2, do2, key_blocks, value_blocks)
    near_parts, far_held, stats = lax.optimization_barrier((near_parts, far_mine, stats))
    near_mine = jnp.stack(near_parts)
    row_sets = [near_mine, swap(near_mine), far_held, swap(far_held)]
    for part in far_more:
        row_sets += [part, swap(part)]

    keep_far, send_far, final, grad_qt = pl.pallas_call(
        functools.partial(remote_kernel, factor, scaling, blocks_here, chips, far, near, piece),
        in_specs=[smem] + [whole] * (3 + len(row_sets)),
        out_specs=[whole] * 4,
        out_shape=[far_type, far_type, stat_type, qt_type],
        scratch_shapes=[
            pltpu.VMEM((2,) + remote_shape, BF16),
            pltpu.VMEM((2,) + remote_shape, F32),
            pltpu.VMEM((3, block_len, block_len), F32),
            pltpu.VMEM((3, block_len, block_len), F32),
            pltpu.VMEM((4, 8, block_len), F32),
        ],
        compiler_params=params((10 * shifts + 4 * blocks_here) * block_bytes + 6 * pair_bytes),
        cost_estimate=cost(60, 8 * tok_rows * feature * 2),
        name="remote_pairs",
    )(info, q2, do2, stats, *row_sets)

    def chip_sums(mine, theirs, groups):
        types = []
        for group in groups:
            types += [pieces_type(len(group), F32)]
            types += [pieces_type(len(group), BF16)] * (chips - 1)
        sums = pl.pallas_call(
            functools.partial(chip_sum_kernel, chips, piece, groups),
            in_specs=[whole, whole],
            out_specs=[whole] * len(types),
            out_shape=types,
            compiler_params=params(4 * mine.shape[0] * block_bytes),
            name="chip_sum",
        )(mine, theirs)
        return [sums[i * chips : (i + 1) * chips] for i in range(len(groups))]

    def head_sums(mine, parts, count):
        return pl.pallas_call(
            functools.partial(head_sum_kernel, count),
            in_specs=[whole] * (1 + len(parts)),
            out_specs=[whole] * count,
            out_shape=[piece_type] * count,
            compiler_params=params(4 * count * block_bytes),
            name="head_sum",
        )(mine, *parts)

    far_sums, near_sums = chip_sums(keep_far, swap(send_far), [far, near])
    far_sums, near_sums, final = lax.optimization_barrier((far_sums, near_sums, final))
    far_parts = [to_chip(far_sums[d], d) for d in range(1, chips)]
    near_parts = [to_chip(near_sums[d], d) for d in range(1, chips)]
    keep_own, send_own, grad_q = pl.pallas_call(
        functools.partial(local_kernel, factor, scaling, blocks_here),
        in_specs=[smem] + [whole] * 6,
        out_specs=[whole] * 3,
        out_shape=[own_type, own_type, jax.ShapeDtypeStruct((tok_rows, feature), BF16)],
        scratch_shapes=[
            pltpu.VMEM((2,) + local_shape, F32),
            pltpu.VMEM((feature, block_len), F32),
        ],
        compiler_params=params(14 * blocks_here * block_bytes),
        cost_estimate=cost(60, 8 * tok_rows * feature * 2),
        name="local_pairs",
    )(info, q2, do2, key_blocks, value_blocks, final, grad_qt)
    far_parts, keep_own, send_own = lax.optimization_barrier((far_parts, keep_own, send_own))
    far_out = head_sums(far_sums[0], far_parts, len(far))
    back = {s: to_owner(far_out[i], s) for i, s in enumerate(far)}
    near_out = head_sums(near_sums[0], near_parts, len(near))
    near_out, send_own = lax.optimization_barrier((near_out, send_own))
    back.update({s: to_owner(near_out[i], s) for i, s in enumerate(near)})
    (own_sums,) = chip_sums(keep_own, swap(send_own), [list(range(blocks_here))])
    own_parts = [to_chip(own_sums[d], d) for d in range(1, chips)]

    mine = pl.pallas_call(
        functools.partial(owner_kernel, chips, shifts),
        in_specs=[smem] + [whole] * (chips + shifts),
        out_specs=whole,
        out_shape=pieces_type(blocks_here, BF16),
        scratch_shapes=[pltpu.VMEM((blocks_here, piece, feature), F32)],
        compiler_params=params((5 * blocks_here + shifts) * block_bytes),
        name="owner_sum",
    )(asked, own_sums[0], *own_parts, *[back[s] for s in range(shifts)])
    spread = [mine, swap(mine)]
    for d in range(1, chips):
        part = to_chip(mine, d)
        spread += [part, swap(part)]
    grad_keys, grad_values = pl.pallas_call(
        functools.partial(spread_kernel, chips, piece),
        in_specs=[whole] * len(spread),
        out_specs=[whole] * 2,
        out_shape=[own_type] * 2,
        compiler_params=params(4 * blocks_here * block_bytes),
        name="spread",
    )(*spread)
    return (
        grad_q.reshape(tok_rows, head_count, feature),
        grad_keys.reshape(tok_rows, feature),
        grad_values.reshape(tok_rows, feature),
    )


def solution(mesh):
    return jax.shard_map(
        body,
        mesh=mesh,
        in_specs=(
            P("ctx", "head", None),
            P("ctx", None),
            P("ctx", None),
            P("ctx", "head", None),
            P("ctx", None),
        ),
        out_specs=(P("ctx", "head", None), P("ctx", None), P("ctx", None)),
        check_vma=False,
    )
```

```python
import functools
import math

import jax
import jax.numpy as jnp
from jax import lax
from jax.experimental import pallas as pl
from jax.experimental.pallas import tpu as pltpu
from jax.sharding import PartitionSpec as P

F32 = jnp.float32
BF16 = jnp.bfloat16
VMEM_LIMIT = 56 * 1024 * 1024


def dot_nt(a, b):
    return lax.dot_general(a, b, (((1,), (1,)), ((), ())), preferred_element_type=F32)


def dot_nn(a, b):
    return lax.dot_general(a, b, (((1,), (0,)), ((), ())), preferred_element_type=F32)


def slot_of(chosen, blocks_here, row, t):
    ctx_self = lax.axis_index("ctx")
    entry = chosen[row, t]
    owner = lax.div(entry, jnp.int32(blocks_here))
    apart = ctx_self - owner
    slot = jnp.where(apart == 0, entry - owner * blocks_here, blocks_here + apart - 1)
    return jnp.where(entry != ctx_self * blocks_here + row, slot, -1)


def pick_kernel(blocks_here, count, chips, far, piece, chosen, keys, values, asked, *refs):
    outs, sems = refs[:-1], refs[-1]
    ctx_self = lax.axis_index("ctx")
    place = lax.axis_index("head")
    core, chip = lax.rem(place, 2), lax.div(place, 2)
    first = ctx_self * blocks_here
    span = pl.ds(pl.multiple_of(chip * piece, piece), piece)

    def copy(source, s, slot):
        rows = source.at[slot, span, :] if s in far else source.at[slot]
        return pltpu.make_async_copy(rows, outs[s], sems.at[s])

    for s in range(count - 1):
        peer = ctx_self + s + 1
        near = jnp.minimum(peer, count - 1)
        found = jnp.int32(0)
        for row in range(blocks_here):
            for t in range(3):
                entry = chosen[near, row * 3 + t]
                hit = (entry >= first) & (entry < first + blocks_here)
                found = jnp.where(hit, entry - first + 1, found)
        found = jnp.where(peer < count, found, 0)
        asked[s] = found
        slot = jnp.maximum(found - 1, 0)

        @pl.when(core == 0)
        def _():
            copy(keys, s, slot).start()

        @pl.when(core != 0)
        def _():
            copy(values, s, slot).start()

    for s in range(count - 1):
        copy(keys, s, 0).wait()


def chip_sum_kernel(chips, piece, groups, mine, theirs, *outs):
    chip = lax.div(lax.axis_index("head"), 2)
    outs = list(outs)
    for group in groups:
        for d in range(chips):
            out = outs.pop(0)
            target = lax.rem(chip + d, chips)
            span = pl.ds(pl.multiple_of(target * piece, piece), piece)
            for i, s in enumerate(group):
                total = mine[s, span, :].astype(F32) + theirs[s, span, :].astype(F32)
                out[i] = total.astype(out.dtype)


def head_sum_kernel(count, mine, *refs):
    parts, outs = refs[: len(refs) - count], refs[len(refs) - count :]
    for i in range(count):
        total = mine[i]
        for part in parts:
            total = total + part[i].astype(F32)
        outs[i][...] = total.astype(BF16)


def pair_terms(key_rows, value_rows, q_rows, do_rows, factor, masked):
    scores = dot_nt(key_rows, q_rows)
    dprobs = dot_nt(value_rows, do_rows)
    if masked:
        col = lax.broadcasted_iota(jnp.int32, scores.shape, 0)
        pos = lax.broadcasted_iota(jnp.int32, scores.shape, 1)
        scores = jnp.where(col <= pos, scores, -jnp.inf)
    top = jnp.max(scores, axis=0, keepdims=True) * factor
    terms = jnp.exp2(scores * factor - top)
    total = jnp.sum(terms, axis=0, keepdims=True)
    weighted = jnp.sum(terms * dprobs, axis=0, keepdims=True)
    return terms, dprobs, top, total, weighted


def local_stats_kernel(factor, blocks_here, chosen, q, do, keys, values, stats):
    block_len = keys.shape[1]

    def per_row(row, _):
        span = pl.ds(row * block_len, block_len)
        q_rows = q[span, :]
        do_rows = do[span, :]

        def pair(slot, masked):
            return pair_terms(keys[slot], values[slot], q_rows, do_rows, factor, masked)[2:]

        top, total, weighted = pair(row, True)
        stats[row, 0:1, :] = top
        stats[row, 1:2, :] = total
        stats[row, 2:3, :] = weighted
        for t in range(3):
            slot = slot_of(chosen, blocks_here, row, t)

            @pl.when((slot >= 0) & (slot < blocks_here))
            def _():
                more_top, more, more_weighted = pair(slot, False)
                old = stats[row, 0:1, :]
                top = jnp.maximum(old, more_top)
                scale_old = jnp.exp2(old - top)
                scale_new = jnp.exp2(more_top - top)
                stats[row, 0:1, :] = top
                stats[row, 1:2, :] = stats[row, 1:2, :] * scale_old + more * scale_new
                stats[row, 2:3, :] = stats[row, 2:3, :] * scale_old + more_weighted * scale_new

        return 0

    lax.fori_loop(0, blocks_here, per_row, 0)


def remote_kernel(
    factor, scaling, blocks_here, chips, far, near, piece, chosen, q, do, stats, *refs
):
    near_refs, far_refs, refs = refs[:2], refs[2 : 2 + 2 * chips], refs[2 + 2 * chips :]
    keep, send, final, grad_qt, rows, acc, terms_buf, dp_buf, parts = refs
    place = lax.axis_index("head")
    core, chip = lax.rem(place, 2), lax.div(place, 2)
    block_len = rows.shape[2]

    def lay(kind, which):
        for i, s in enumerate(near):
            rows[kind, s] = near_refs[which][i]
        for d in range(chips):
            source = lax.rem(chip + chips - d, chips)
            span = pl.ds(pl.multiple_of(source * piece, piece), piece)
            for i, s in enumerate(far):
                rows[kind, s, span, :] = far_refs[2 * d + which][i]

    @pl.when(core == 0)
    def _():
        lay(0, 0)
        lay(1, 1)

    @pl.when(core != 0)
    def _():
        lay(0, 1)
        lay(1, 0)

    acc[...] = jnp.zeros_like(acc)

    def per_row(row, _):
        span = pl.ds(row * block_len, block_len)
        parts[0, 0:3, :] = stats[row, 0:3, :]
        for t in range(3):
            slot = slot_of(chosen, blocks_here, row, t) - blocks_here

            @pl.when(slot >= 0)
            def _():
                terms, dprobs, top, total, weighted = pair_terms(
                    rows[0, slot], rows[1, slot], q[span, :], do[span, :], factor, False
                )
                terms_buf[t] = terms
                dp_buf[t] = dprobs
                parts[t + 1, 0:1, :] = top
                parts[t + 1, 1:2, :] = total
                parts[t + 1, 2:3, :] = weighted

            @pl.when(slot < 0)
            def _():
                parts[t + 1, 0:1, :] = jnp.full((1, block_len), -jnp.inf, F32)
                parts[t + 1, 1:3, :] = jnp.zeros((2, block_len), F32)

        top = parts[0, 0:1, :]
        for t in range(3):
            top = jnp.maximum(top, parts[t + 1, 0:1, :])
        total = jnp.zeros_like(top)
        weighted = jnp.zeros_like(top)
        for t in range(4):
            scale = jnp.exp2(parts[t, 0:1, :] - top)
            parts[t, 3:4, :] = scale
            total = total + scale * parts[t, 1:2, :]
            weighted = weighted + scale * parts[t, 2:3, :]
        inverse = 1.0 / total
        delta = weighted * inverse
        final[row, 0:1, :] = top + jnp.log2(total)
        final[row, 1:2, :] = delta
        for t in range(3):
            parts[t + 1, 3:4, :] = parts[t + 1, 3:4, :] * inverse
        grad_qt[row] = jnp.zeros_like(grad_qt[row])
        for t in range(3):
            slot = slot_of(chosen, blocks_here, row, t) - blocks_here

            @pl.when(slot >= 0)
            def _():
                weights = terms_buf[t] * parts[t + 1, 3:4, :]
                dscores = (weights * (dp_buf[t] - final[row, 1:2, :])).astype(BF16)
                acc[1, slot] += dot_nn(weights.astype(BF16), do[span, :])
                acc[0, slot] += dot_nn(dscores, q[span, :])
                grad_qt[row] += dot_nn(rows[0, slot].T, dscores)

        return 0

    lax.fori_loop(0, blocks_here, per_row, 0)
    keep_scale = jnp.where(core == 0, scaling, 1.0)
    send_scale = jnp.where(core == 0, 1.0, scaling)
    keep[...] = (acc[core] * keep_scale).astype(BF16)
    send[...] = (acc[1 - core] * send_scale).astype(BF16)


def local_kernel(
    factor, scaling, blocks_here, chosen, q, do, keys, values, final, grad_qt,
    keep, send, grad_q,
    acc, total_qt,
):
    core = lax.rem(lax.axis_index("head"), 2)
    block_len = keys.shape[1]
    acc[...] = jnp.zeros_like(acc)

    def per_row(row, _):
        span = pl.ds(row * block_len, block_len)

        def pair(slot, masked):
            q_rows = q[span, :]
            do_rows = do[span, :]
            key_rows = keys[slot]
            scores = dot_nt(key_rows, q_rows)
            dprobs = dot_nt(values[slot], do_rows)
            weights = jnp.exp2(scores * factor - final[row, 0:1, :])
            if masked:
                col = lax.broadcasted_iota(jnp.int32, scores.shape, 0)
                pos = lax.broadcasted_iota(jnp.int32, scores.shape, 1)
                weights = jnp.where(col <= pos, weights, 0.0)
            dscores = (weights * (dprobs - final[row, 1:2, :])).astype(BF16)
            acc[1, slot] += dot_nn(weights.astype(BF16), do_rows)
            acc[0, slot] += dot_nn(dscores, q_rows)
            total_qt[...] += dot_nn(key_rows.T, dscores)

        total_qt[...] = grad_qt[row]
        pair(row, True)
        for t in range(3):
            slot = slot_of(chosen, blocks_here, row, t)

            @pl.when((slot >= 0) & (slot < blocks_here))
            def _():
                pair(slot, False)

        grad_q[span, :] = (total_qt[...].T * scaling).astype(BF16)
        return 0

    lax.fori_loop(0, blocks_here, per_row, 0)
    keep_scale = jnp.where(core == 0, scaling, 1.0)
    send_scale = jnp.where(core == 0, 1.0, scaling)
    keep[...] = (acc[core] * keep_scale).astype(BF16)
    send[...] = (acc[1 - core] * send_scale).astype(BF16)


def owner_kernel(chips, shifts, asked, mine, *refs):
    others, back, (out, acc) = refs[: chips - 1], refs[chips - 1 : chips - 1 + shifts], refs[-2:]
    total = mine[...]
    for part in others:
        total = total + part[...].astype(F32)
    acc[...] = total
    for s in range(shifts):
        slot = asked[s] - 1

        @pl.when(slot >= 0)
        def _():
            acc[slot] += back[s][...].astype(F32)

    out[...] = acc[...].astype(BF16)


def spread_kernel(chips, piece, *refs):
    pieces, (grad_k, grad_v) = refs[: 2 * chips], refs[2 * chips :]
    place = lax.axis_index("head")
    core, chip = lax.rem(place, 2), lax.div(place, 2)

    def lay(out, which):
        for d in range(chips):
            source = lax.rem(chip + chips - d, chips)
            span = pl.ds(pl.multiple_of(source * piece, piece), piece)
            out[:, span, :] = pieces[2 * d + which][...]

    @pl.when(core == 0)
    def _():
        lay(grad_k, 0)
        lay(grad_v, 1)

    @pl.when(core != 0)
    def _():
        lay(grad_k, 1)
        lay(grad_v, 0)


def params(size):
    return pltpu.CompilerParams(vmem_limit_bytes=min(size + 12 * 1024 * 1024, VMEM_LIMIT))


def body(queries, keys, values, dout, selected):
    tok_rows, head_count, feature = queries.shape
    blocks_here = selected.shape[0]
    block_len = tok_rows // blocks_here
    ctx_count = lax.axis_size("ctx")
    heads = lax.axis_size("head")
    chips = heads // 2
    piece = block_len // chips
    scaling = 1.0 / math.sqrt(feature)
    factor = scaling * math.log2(math.e)
    shifts = ctx_count - 1
    far = [s for s in range(shifts) if 2 * (s + 1) >= ctx_count]
    near = [s for s in range(shifts) if 2 * (s + 1) < ctx_count]

    q2 = queries.reshape(tok_rows, feature)
    do2 = dout.reshape(tok_rows, feature)
    key_blocks = keys.reshape(blocks_here, block_len, feature)
    value_blocks = values.reshape(blocks_here, block_len, feature)
    remote_shape = (shifts, block_len, feature)
    local_shape = (blocks_here, block_len, feature)

    smem = pl.BlockSpec(memory_space=pltpu.SMEM)
    whole = pl.BlockSpec(memory_space=pltpu.VMEM)
    hbm = pl.BlockSpec(memory_space=pltpu.HBM)
    stat_type = jax.ShapeDtypeStruct((blocks_here, 8, block_len), F32)
    far_type = jax.ShapeDtypeStruct(remote_shape, BF16)
    own_type = jax.ShapeDtypeStruct(local_shape, BF16)
    block_type = jax.ShapeDtypeStruct((block_len, feature), BF16)
    piece_type = jax.ShapeDtypeStruct((piece, feature), BF16)
    qt_type = jax.ShapeDtypeStruct((blocks_here, feature, block_len), F32)
    pair_flops = 2 * block_len * block_len * feature
    block_bytes = block_len * feature * 2
    pair_bytes = block_len * block_len * 4

    def pieces_type(count, dtype):
        return jax.ShapeDtypeStruct((count, piece, feature), dtype)

    def cost(matmuls, size):
        return pl.CostEstimate(
            flops=matmuls * pair_flops, bytes_accessed=size, transcendentals=matmuls * block_len**2
        )

    def swap(array):
        return lax.ppermute(array, "head", [(h, h ^ 1) for h in range(heads)])

    def to_chip(array, d):
        return lax.ppermute(array, "head", [(h, (h + 2 * d) % heads) for h in range(heads)])

    def to_owner(array, s):
        return lax.ppermute(array, "ctx", [(c, c - s - 1) for c in range(s + 1, ctx_count)])

    def to_reader(array, s):
        return lax.ppermute(array, "ctx", [(c - s - 1, c) for c in range(s + 1, ctx_count)])

    everyone = lax.all_to_all(
        jnp.broadcast_to(selected.reshape(1, 3 * blocks_here), (ctx_count, 3 * blocks_here)),
        "ctx", split_axis=0, concat_axis=0, tiled=True,
    )
    asked, *sent = pl.pallas_call(
        functools.partial(pick_kernel, blocks_here, ctx_count, chips, far, piece),
        in_specs=[smem, hbm, hbm],
        out_specs=[smem] + [whole] * shifts,
        out_shape=[jax.ShapeDtypeStruct((shifts,), jnp.int32)]
        + [piece_type if s in far else block_type for s in range(shifts)],
        scratch_shapes=[pltpu.SemaphoreType.DMA((shifts,))],
        name="pick_rows",
    )(everyone, key_blocks, value_blocks)

    far_mine = jnp.stack([to_reader(sent[s], s) for s in far])
    near_parts = [to_reader(sent[s], s) for s in near]
    far_mine, chosen = lax.optimization_barrier((far_mine, selected))
    far_more = [to_chip(far_mine, d) for d in range(1, chips)]
    stats = pl.pallas_call(
        functools.partial(local_stats_kernel, factor, blocks_here),
        in_specs=[smem] + [whole] * 4,
        out_specs=whole,
        out_shape=stat_type,
        compiler_params=params(4 * blocks_here * block_bytes),
        cost_estimate=cost(30, 4 * tok_rows * feature * 2),
        name="local_stats",
    )(chosen, q2, do2, key_blocks, value_blocks)
    near_parts, far_held, stats = lax.optimization_barrier((near_parts, far_mine, stats))
    near_mine = jnp.stack(near_parts)
    row_sets = [near_mine, swap(near_mine), far_held, swap(far_held)]
    for part in far_more:
        row_sets += [part, swap(part)]

    keep_far, send_far, final, grad_qt = pl.pallas_call(
        functools.partial(remote_kernel, factor, scaling, blocks_here, chips, far, near, piece),
        in_specs=[smem] + [whole] * (3 + len(row_sets)),
        out_specs=[whole] * 4,
        out_shape=[far_type, far_type, stat_type, qt_type],
        scratch_shapes=[
            pltpu.VMEM((2,) + remote_shape, BF16),
            pltpu.VMEM((2,) + remote_shape, F32),
            pltpu.VMEM((3, block_len, block_len), F32),
            pltpu.VMEM((3, block_len, block_len), F32),
            pltpu.VMEM((4, 8, block_len), F32),
        ],
        compiler_params=params((10 * shifts + 4 * blocks_here) * block_bytes + 6 * pair_bytes),
        cost_estimate=cost(60, 8 * tok_rows * feature * 2),
        name="remote_pairs",
    )(chosen, q2, do2, stats, *row_sets)

    def chip_sums(mine, theirs, groups):
        types = []
        for group in groups:
            types += [pieces_type(len(group), F32)]
            types += [pieces_type(len(group), BF16)] * (chips - 1)
        sums = pl.pallas_call(
            functools.partial(chip_sum_kernel, chips, piece, groups),
            in_specs=[whole, whole],
            out_specs=[whole] * len(types),
            out_shape=types,
            compiler_params=params(4 * mine.shape[0] * block_bytes),
            name="chip_sum",
        )(mine, theirs)
        return [sums[i * chips : (i + 1) * chips] for i in range(len(groups))]

    def head_sums(mine, parts, count):
        return pl.pallas_call(
            functools.partial(head_sum_kernel, count),
            in_specs=[whole] * (1 + len(parts)),
            out_specs=[whole] * count,
            out_shape=[piece_type] * count,
            compiler_params=params(4 * count * block_bytes),
            name="head_sum",
        )(mine, *parts)

    far_sums, near_sums = chip_sums(keep_far, swap(send_far), [far, near])
    far_sums, near_sums, final = lax.optimization_barrier((far_sums, near_sums, final))
    far_parts = [to_chip(far_sums[d], d) for d in range(1, chips)]
    keep_own, send_own, grad_q = pl.pallas_call(
        functools.partial(local_kernel, factor, scaling, blocks_here),
        in_specs=[smem] + [whole] * 6,
        out_specs=[whole] * 3,
        out_shape=[own_type, own_type, jax.ShapeDtypeStruct((tok_rows, feature), BF16)],
        scratch_shapes=[
            pltpu.VMEM((2,) + local_shape, F32),
            pltpu.VMEM((feature, block_len), F32),
        ],
        compiler_params=params(14 * blocks_here * block_bytes),
        cost_estimate=cost(60, 8 * tok_rows * feature * 2),
        name="local_pairs",
    )(chosen, q2, do2, key_blocks, value_blocks, final, grad_qt)
    far_parts, near_sums, keep_own, send_own = lax.optimization_barrier(
        (far_parts, near_sums, keep_own, send_own)
    )
    near_parts = [to_chip(near_sums[d], d) for d in range(1, chips)]
    far_out = head_sums(far_sums[0], far_parts, len(far))
    back = {s: to_owner(far_out[i], s) for i, s in enumerate(far)}
    back[far[0]], keep_own, own_twin = lax.optimization_barrier(
        (back[far[0]], keep_own, swap(send_own))
    )
    (own_sums,) = chip_sums(keep_own, own_twin, [list(range(blocks_here))])
    own_parts = [to_chip(own_sums[d], d) for d in range(1, chips)]
    near_parts, own_mine = lax.optimization_barrier((near_parts, own_sums[0]))
    near_out = head_sums(near_sums[0], near_parts, len(near))
    back.update({s: to_owner(near_out[i], s) for i, s in enumerate(near)})

    mine = pl.pallas_call(
        functools.partial(owner_kernel, chips, shifts),
        in_specs=[smem] + [whole] * (chips + shifts),
        out_specs=whole,
        out_shape=pieces_type(blocks_here, BF16),
        scratch_shapes=[pltpu.VMEM((blocks_here, piece, feature), F32)],
        compiler_params=params((5 * blocks_here + shifts) * block_bytes),
        name="owner_sum",
    )(asked, own_mine, *own_parts, *[back[s] for s in range(shifts)])
    spread = [mine, swap(mine)]
    for d in range(1, chips):
        part = to_chip(mine, d)
        spread += [part, swap(part)]
    grad_keys, grad_values = pl.pallas_call(
        functools.partial(spread_kernel, chips, piece),
        in_specs=[whole] * len(spread),
        out_specs=[whole] * 2,
        out_shape=[own_type] * 2,
        compiler_params=params(4 * blocks_here * block_bytes),
        name="spread",
    )(*spread)
    return (
        grad_q.reshape(tok_rows, head_count, feature),
        grad_keys.reshape(tok_rows, feature),
        grad_values.reshape(tok_rows, feature),
    )


def solution(mesh):
    return jax.shard_map(
        body,
        mesh=mesh,
        in_specs=(
            P("ctx", "head", None),
            P("ctx", None),
            P("ctx", None),
            P("ctx", "head", None),
            P("ctx", None),
        ),
        out_specs=(P("ctx", "head", None), P("ctx", None), P("ctx", None)),
        check_vma=False,
    )
```

```python
import functools
import math

import jax
import jax.numpy as jnp
from jax import lax
from jax.experimental import pallas as pl
from jax.experimental.pallas import tpu as pltpu
from jax.sharding import PartitionSpec as P

F32 = jnp.float32
BF16 = jnp.bfloat16
VMEM_LIMIT = 56 * 1024 * 1024


def dot_nt(a, b):
    return lax.dot_general(a, b, (((1,), (1,)), ((), ())), preferred_element_type=F32)


def dot_nn(a, b):
    return lax.dot_general(a, b, (((1,), (0,)), ((), ())), preferred_element_type=F32)


def slot_of(chosen, blocks_here, row, t):
    ctx_self = lax.axis_index("ctx")
    entry = chosen[row, t]
    owner = lax.div(entry, jnp.int32(blocks_here))
    apart = ctx_self - owner
    slot = jnp.where(apart == 0, entry - owner * blocks_here, blocks_here + apart - 1)
    return jnp.where(entry != ctx_self * blocks_here + row, slot, -1)


def pick_kernel(blocks_here, count, chips, far, piece, chosen, keys, values, asked, *refs):
    outs, sems = refs[:-1], refs[-1]
    ctx_self = lax.axis_index("ctx")
    place = lax.axis_index("head")
    core, chip = lax.rem(place, 2), lax.div(place, 2)
    first = ctx_self * blocks_here
    span = pl.ds(pl.multiple_of(chip * piece, piece), piece)

    def copy(source, s, slot):
        rows = source.at[slot, span, :] if s in far else source.at[slot]
        return pltpu.make_async_copy(rows, outs[s], sems.at[s])

    for s in range(count - 1):
        peer = ctx_self + s + 1
        near = jnp.minimum(peer, count - 1)
        found = jnp.int32(0)
        for row in range(blocks_here):
            for t in range(3):
                entry = chosen[near, row * 3 + t]
                hit = (entry >= first) & (entry < first + blocks_here)
                found = jnp.where(hit, entry - first + 1, found)
        found = jnp.where(peer < count, found, 0)
        asked[s] = found
        slot = jnp.maximum(found - 1, 0)

        @pl.when(core == 0)
        def _():
            copy(keys, s, slot).start()

        @pl.when(core != 0)
        def _():
            copy(values, s, slot).start()

    for s in range(count - 1):
        copy(keys, s, 0).wait()


def chip_sum_kernel(chips, piece, groups, mine, theirs, *outs):
    chip = lax.div(lax.axis_index("head"), 2)
    outs = list(outs)
    for group in groups:
        for d in range(chips):
            out = outs.pop(0)
            target = lax.rem(chip + d, chips)
            span = pl.ds(pl.multiple_of(target * piece, piece), piece)
            for i, s in enumerate(group):
                total = mine[s, span, :].astype(F32) + theirs[s, span, :].astype(F32)
                out[i] = total.astype(out.dtype)


def head_sum_kernel(count, mine, *refs):
    parts, outs = refs[: len(refs) - count], refs[len(refs) - count :]
    for i in range(count):
        total = mine[i]
        for part in parts:
            total = total + part[i].astype(F32)
        outs[i][...] = total.astype(BF16)


def fold(array, reduce):
    rows, lanes = array.shape
    return reduce(array.reshape(rows // 8, 8, lanes), axis=0)


def causal(array, first_col, first_pos, other):
    col = lax.broadcasted_iota(jnp.int32, array.shape, 0) + first_col
    pos = lax.broadcasted_iota(jnp.int32, array.shape, 1) + first_pos
    return jnp.where(col <= pos, array, other)


def row_sums(s_ref, dp_ref, factor):
    block_len = s_ref.shape[0]
    step = min(64, block_len)
    spans = [pl.ds(c, step) for c in range(0, block_len, step)]
    top = fold(s_ref[spans[0], :], jnp.max)
    for span in spans[1:]:
        top = jnp.maximum(top, fold(s_ref[span, :], jnp.max))
    top = jnp.max(top, axis=0, keepdims=True) * factor
    total = weighted = jnp.zeros((8, block_len), F32)
    for span in spans:
        terms = jnp.exp2(s_ref[span, :] * factor - top)
        total = total + fold(terms, jnp.sum)
        weighted = weighted + fold(terms * dp_ref[span, :], jnp.sum)
    total = jnp.sum(total, axis=0, keepdims=True)
    return top, total, jnp.sum(weighted, axis=0, keepdims=True)


def local_stats_kernel(factor, blocks_here, chosen, q, do, keys, values, stats, s_buf, dp_buf):
    block_len = keys.shape[1]
    half = block_len // 2

    def per_row(row, _):
        start = row * block_len
        span = pl.ds(start, block_len)
        late = pl.ds(start + half, half)

        s_buf[:half, :] = causal(dot_nt(keys[row, :half], q[span, :]), 0, 0, -jnp.inf)
        s_buf[half:, :half] = jnp.full((half, half), -jnp.inf, F32)
        s_buf[half:, half:] = causal(dot_nt(keys[row, half:], q[late, :]), 0, 0, -jnp.inf)
        dp_buf[:half, :] = dot_nt(values[row, :half], do[span, :])
        dp_buf[half:, :half] = jnp.zeros((half, half), F32)
        dp_buf[half:, half:] = dot_nt(values[row, half:], do[late, :])
        top, total, weighted = row_sums(s_buf, dp_buf, factor)
        stats[row, 0:1, :] = top
        stats[row, 1:2, :] = total
        stats[row, 2:3, :] = weighted
        for t in range(3):
            slot = slot_of(chosen, blocks_here, row, t)

            @pl.when((slot >= 0) & (slot < blocks_here))
            def _():
                s_buf[...] = dot_nt(keys[slot], q[span, :])
                dp_buf[...] = dot_nt(values[slot], do[span, :])
                more_top, more, more_weighted = row_sums(s_buf, dp_buf, factor)
                old = stats[row, 0:1, :]
                top = jnp.maximum(old, more_top)
                scale_old = jnp.exp2(old - top)
                scale_new = jnp.exp2(more_top - top)
                stats[row, 0:1, :] = top
                stats[row, 1:2, :] = stats[row, 1:2, :] * scale_old + more * scale_new
                stats[row, 2:3, :] = stats[row, 2:3, :] * scale_old + more_weighted * scale_new

        return 0

    lax.fori_loop(0, blocks_here, per_row, 0)


def remote_kernel(
    factor, scaling, blocks_here, chips, far, near, piece, chosen, q, do, stats, *refs
):
    near_refs, far_refs, refs = refs[:2], refs[2 : 2 + 2 * chips], refs[2 + 2 * chips :]
    keep, send, final, grad_qt, rows, acc, s_buf, dp_buf, parts = refs
    place = lax.axis_index("head")
    core, chip = lax.rem(place, 2), lax.div(place, 2)
    block_len = rows.shape[2]
    half = block_len // 2

    def lay(kind, which):
        for i, s in enumerate(near):
            rows[kind, s] = near_refs[which][i]
        for d in range(chips):
            source = lax.rem(chip + chips - d, chips)
            span = pl.ds(pl.multiple_of(source * piece, piece), piece)
            for i, s in enumerate(far):
                rows[kind, s, span, :] = far_refs[2 * d + which][i]

    @pl.when(core == 0)
    def _():
        lay(0, 0)
        lay(1, 1)

    @pl.when(core != 0)
    def _():
        lay(0, 1)
        lay(1, 0)

    acc[...] = jnp.zeros_like(acc)

    def per_row(row, _):
        span = pl.ds(row * block_len, block_len)
        parts[0, 0:3, :] = stats[row, 0:3, :]
        for t in range(3):
            slot = slot_of(chosen, blocks_here, row, t) - blocks_here

            @pl.when(slot >= 0)
            def _():
                s_buf[t] = dot_nt(rows[0, slot], q[span, :])
                dp_buf[t] = dot_nt(rows[1, slot], do[span, :])
                top, total, weighted = row_sums(s_buf.at[t], dp_buf.at[t], factor)
                parts[t + 1, 0:1, :] = top
                parts[t + 1, 1:2, :] = total
                parts[t + 1, 2:3, :] = weighted

            @pl.when(slot < 0)
            def _():
                parts[t + 1, 0:1, :] = jnp.full((1, block_len), -jnp.inf, F32)
                parts[t + 1, 1:3, :] = jnp.zeros((2, block_len), F32)

        top = parts[0, 0:1, :]
        for t in range(3):
            top = jnp.maximum(top, parts[t + 1, 0:1, :])
        total = jnp.zeros_like(top)
        weighted = jnp.zeros_like(top)
        for t in range(4):
            scale = jnp.exp2(parts[t, 0:1, :] - top)
            total = total + scale * parts[t, 1:2, :]
            weighted = weighted + scale * parts[t, 2:3, :]
        final[row, 0:1, :] = top + jnp.log2(total)
        final[row, 1:2, :] = weighted / total
        grad_qt[row] = jnp.zeros_like(grad_qt[row])
        for t in range(3):
            slot = slot_of(chosen, blocks_here, row, t) - blocks_here

            @pl.when(slot >= 0)
            def _():
                level = final[row, 0:1, :]
                delta = final[row, 1:2, :]
                for c in (0, half):
                    cut = pl.ds(c, half)
                    weights = jnp.exp2(s_buf[t, cut, :] * factor - level)
                    dscores = (weights * (dp_buf[t, cut, :] - delta)).astype(BF16)
                    acc[1, slot, cut, :] += dot_nn(weights.astype(BF16), do[span, :])
                    acc[0, slot, cut, :] += dot_nn(dscores, q[span, :])
                    grad_qt[row] += dot_nn(rows[0, slot, cut, :].T, dscores)

        return 0

    lax.fori_loop(0, blocks_here, per_row, 0)
    keep_scale = jnp.where(core == 0, scaling, 1.0)
    send_scale = jnp.where(core == 0, 1.0, scaling)
    keep[...] = (acc[core] * keep_scale).astype(BF16)
    send[...] = (acc[1 - core] * send_scale).astype(BF16)


def local_kernel(
    factor, scaling, blocks_here, chosen, q, do, keys, values, final, grad_qt,
    keep, send, grad_q,
    acc, total_qt,
):
    core = lax.rem(lax.axis_index("head"), 2)
    block_len = keys.shape[1]
    half = block_len // 2
    acc[...] = jnp.zeros_like(acc)

    def per_row(row, _):
        start = row * block_len
        span = pl.ds(start, block_len)

        def part(slot, c, first, masked):
            cut = pl.ds(c, half)
            q_rows = q[pl.ds(start + first, block_len - first), :]
            do_rows = do[pl.ds(start + first, block_len - first), :]
            key_rows = keys[slot, cut, :]
            scores = dot_nt(key_rows, q_rows)
            dprobs = dot_nt(values[slot, cut, :], do_rows)
            weights = jnp.exp2(scores * factor - final[row, 0:1, first:])
            if masked:
                weights = causal(weights, c, first, 0.0)
            dscores = (weights * (dprobs - final[row, 1:2, first:])).astype(BF16)
            acc[1, slot, cut, :] += dot_nn(weights.astype(BF16), do_rows)
            acc[0, slot, cut, :] += dot_nn(dscores, q_rows)
            total_qt[:, first:] += dot_nn(key_rows.T, dscores)

        total_qt[...] = grad_qt[row]
        part(row, 0, 0, True)
        part(row, half, half, True)
        for t in range(3):
            slot = slot_of(chosen, blocks_here, row, t)

            @pl.when((slot >= 0) & (slot < blocks_here))
            def _():
                part(slot, 0, 0, False)
                part(slot, half, 0, False)

        grad_q[span, :] = (total_qt[...].T * scaling).astype(BF16)
        return 0

    lax.fori_loop(0, blocks_here, per_row, 0)
    keep_scale = jnp.where(core == 0, scaling, 1.0)
    send_scale = jnp.where(core == 0, 1.0, scaling)
    keep[...] = (acc[core] * keep_scale).astype(BF16)
    send[...] = (acc[1 - core] * send_scale).astype(BF16)


def owner_kernel(chips, shifts, asked, mine, *refs):
    others, back, (out, acc) = refs[: chips - 1], refs[chips - 1 : chips - 1 + shifts], refs[-2:]
    total = mine[...]
    for part in others:
        total = total + part[...].astype(F32)
    acc[...] = total
    for s in range(shifts):
        slot = asked[s] - 1

        @pl.when(slot >= 0)
        def _():
            acc[slot] += back[s][...].astype(F32)

    out[...] = acc[...].astype(BF16)


def spread_kernel(chips, piece, *refs):
    pieces, (grad_k, grad_v) = refs[: 2 * chips], refs[2 * chips :]
    place = lax.axis_index("head")
    core, chip = lax.rem(place, 2), lax.div(place, 2)

    def lay(out, which):
        for d in range(chips):
            source = lax.rem(chip + chips - d, chips)
            span = pl.ds(pl.multiple_of(source * piece, piece), piece)
            out[:, span, :] = pieces[2 * d + which][...]

    @pl.when(core == 0)
    def _():
        lay(grad_k, 0)
        lay(grad_v, 1)

    @pl.when(core != 0)
    def _():
        lay(grad_k, 1)
        lay(grad_v, 0)


def params(size):
    return pltpu.CompilerParams(vmem_limit_bytes=min(size + 12 * 1024 * 1024, VMEM_LIMIT))


def body(queries, keys, values, dout, selected):
    tok_rows, head_count, feature = queries.shape
    blocks_here = selected.shape[0]
    block_len = tok_rows // blocks_here
    ctx_count = lax.axis_size("ctx")
    heads = lax.axis_size("head")
    chips = heads // 2
    piece = block_len // chips
    scaling = 1.0 / math.sqrt(feature)
    factor = scaling * math.log2(math.e)
    shifts = ctx_count - 1
    far = [s for s in range(shifts) if 2 * (s + 1) >= ctx_count]
    near = [s for s in range(shifts) if 2 * (s + 1) < ctx_count]

    q2 = queries.reshape(tok_rows, feature)
    do2 = dout.reshape(tok_rows, feature)
    key_blocks = keys.reshape(blocks_here, block_len, feature)
    value_blocks = values.reshape(blocks_here, block_len, feature)
    remote_shape = (shifts, block_len, feature)
    local_shape = (blocks_here, block_len, feature)

    smem = pl.BlockSpec(memory_space=pltpu.SMEM)
    whole = pl.BlockSpec(memory_space=pltpu.VMEM)
    hbm = pl.BlockSpec(memory_space=pltpu.HBM)
    stat_type = jax.ShapeDtypeStruct((blocks_here, 8, block_len), F32)
    far_type = jax.ShapeDtypeStruct(remote_shape, BF16)
    own_type = jax.ShapeDtypeStruct(local_shape, BF16)
    block_type = jax.ShapeDtypeStruct((block_len, feature), BF16)
    piece_type = jax.ShapeDtypeStruct((piece, feature), BF16)
    qt_type = jax.ShapeDtypeStruct((blocks_here, feature, block_len), F32)
    pair_flops = 2 * block_len * block_len * feature
    block_bytes = block_len * feature * 2
    pair_bytes = block_len * block_len * 4

    def pieces_type(count, dtype):
        return jax.ShapeDtypeStruct((count, piece, feature), dtype)

    def cost(matmuls, size):
        return pl.CostEstimate(
            flops=matmuls * pair_flops, bytes_accessed=size, transcendentals=matmuls * block_len**2
        )

    def swap(array):
        return lax.ppermute(array, "head", [(h, h ^ 1) for h in range(heads)])

    def to_chip(array, d):
        return lax.ppermute(array, "head", [(h, (h + 2 * d) % heads) for h in range(heads)])

    def to_owner(array, s):
        return lax.ppermute(array, "ctx", [(c, c - s - 1) for c in range(s + 1, ctx_count)])

    def to_reader(array, s):
        return lax.ppermute(array, "ctx", [(c - s - 1, c) for c in range(s + 1, ctx_count)])

    everyone = lax.all_to_all(
        jnp.broadcast_to(selected.reshape(1, 3 * blocks_here), (ctx_count, 3 * blocks_here)),
        "ctx", split_axis=0, concat_axis=0, tiled=True,
    )
    asked, *sent = pl.pallas_call(
        functools.partial(pick_kernel, blocks_here, ctx_count, chips, far, piece),
        in_specs=[smem, hbm, hbm],
        out_specs=[smem] + [whole] * shifts,
        out_shape=[jax.ShapeDtypeStruct((shifts,), jnp.int32)]
        + [piece_type if s in far else block_type for s in range(shifts)],
        scratch_shapes=[pltpu.SemaphoreType.DMA((shifts,))],
        name="pick_rows",
    )(everyone, key_blocks, value_blocks)

    far_mine = jnp.stack([to_reader(sent[s], s) for s in far])
    near_parts = [to_reader(sent[s], s) for s in near]
    far_mine, chosen = lax.optimization_barrier((far_mine, selected))
    far_more = [to_chip(far_mine, d) for d in range(1, chips)]
    stats = pl.pallas_call(
        functools.partial(local_stats_kernel, factor, blocks_here),
        in_specs=[smem] + [whole] * 4,
        out_specs=whole,
        out_shape=stat_type,
        scratch_shapes=[pltpu.VMEM((block_len, block_len), F32)] * 2,
        compiler_params=params(4 * blocks_here * block_bytes + 2 * pair_bytes),
        cost_estimate=cost(30, 4 * tok_rows * feature * 2),
        name="local_stats",
    )(chosen, q2, do2, key_blocks, value_blocks)
    near_parts, far_held, stats = lax.optimization_barrier((near_parts, far_mine, stats))
    near_mine = jnp.stack(near_parts)
    row_sets = [near_mine, swap(near_mine), far_held, swap(far_held)]
    for part in far_more:
        row_sets += [part, swap(part)]

    keep_far, send_far, final, grad_qt = pl.pallas_call(
        functools.partial(remote_kernel, factor, scaling, blocks_here, chips, far, near, piece),
        in_specs=[smem] + [whole] * (3 + len(row_sets)),
        out_specs=[whole] * 4,
        out_shape=[far_type, far_type, stat_type, qt_type],
        scratch_shapes=[
            pltpu.VMEM((2,) + remote_shape, BF16),
            pltpu.VMEM((2,) + remote_shape, F32),
            pltpu.VMEM((3, block_len, block_len), F32),
            pltpu.VMEM((3, block_len, block_len), F32),
            pltpu.VMEM((4, 8, block_len), F32),
        ],
        compiler_params=params((10 * shifts + 4 * blocks_here) * block_bytes + 6 * pair_bytes),
        cost_estimate=cost(60, 8 * tok_rows * feature * 2),
        name="remote_pairs",
    )(chosen, q2, do2, stats, *row_sets)

    def chip_sums(mine, theirs, groups):
        types = []
        for group in groups:
            types += [pieces_type(len(group), F32)]
            types += [pieces_type(len(group), BF16)] * (chips - 1)
        sums = pl.pallas_call(
            functools.partial(chip_sum_kernel, chips, piece, groups),
            in_specs=[whole, whole],
            out_specs=[whole] * len(types),
            out_shape=types,
            compiler_params=params(4 * mine.shape[0] * block_bytes),
            name="chip_sum",
        )(mine, theirs)
        return [sums[i * chips : (i + 1) * chips] for i in range(len(groups))]

    def head_sums(mine, parts, count):
        return pl.pallas_call(
            functools.partial(head_sum_kernel, count),
            in_specs=[whole] * (1 + len(parts)),
            out_specs=[whole] * count,
            out_shape=[piece_type] * count,
            compiler_params=params(4 * count * block_bytes),
            name="head_sum",
        )(mine, *parts)

    far_sums, near_sums = chip_sums(keep_far, swap(send_far), [far, near])
    far_sums, near_sums, final = lax.optimization_barrier((far_sums, near_sums, final))
    far_parts = [to_chip(far_sums[d], d) for d in range(1, chips)]
    keep_own, send_own, grad_q = pl.pallas_call(
        functools.partial(local_kernel, factor, scaling, blocks_here),
        in_specs=[smem] + [whole] * 6,
        out_specs=[whole] * 3,
        out_shape=[own_type, own_type, jax.ShapeDtypeStruct((tok_rows, feature), BF16)],
        scratch_shapes=[
            pltpu.VMEM((2,) + local_shape, F32),
            pltpu.VMEM((feature, block_len), F32),
        ],
        compiler_params=params(14 * blocks_here * block_bytes),
        cost_estimate=cost(60, 8 * tok_rows * feature * 2),
        name="local_pairs",
    )(chosen, q2, do2, key_blocks, value_blocks, final, grad_qt)
    far_parts, near_sums, keep_own, send_own = lax.optimization_barrier(
        (far_parts, near_sums, keep_own, send_own)
    )
    near_parts = [to_chip(near_sums[d], d) for d in range(1, chips)]
    far_out = head_sums(far_sums[0], far_parts, len(far))
    back = {s: to_owner(far_out[i], s) for i, s in enumerate(far)}
    back[far[0]], keep_own, own_twin = lax.optimization_barrier(
        (back[far[0]], keep_own, swap(send_own))
    )
    (own_sums,) = chip_sums(keep_own, own_twin, [list(range(blocks_here))])
    own_parts = [to_chip(own_sums[d], d) for d in range(1, chips)]
    near_parts, own_mine = lax.optimization_barrier((near_parts, own_sums[0]))
    near_out = head_sums(near_sums[0], near_parts, len(near))
    back.update({s: to_owner(near_out[i], s) for i, s in enumerate(near)})

    mine = pl.pallas_call(
        functools.partial(owner_kernel, chips, shifts),
        in_specs=[smem] + [whole] * (chips + shifts),
        out_specs=whole,
        out_shape=pieces_type(blocks_here, BF16),
        scratch_shapes=[pltpu.VMEM((blocks_here, piece, feature), F32)],
        compiler_params=params((5 * blocks_here + shifts) * block_bytes),
        name="owner_sum",
    )(asked, own_mine, *own_parts, *[back[s] for s in range(shifts)])
    spread = [mine, swap(mine)]
    for d in range(1, chips):
        part = to_chip(mine, d)
        spread += [part, swap(part)]
    grad_keys, grad_values = pl.pallas_call(
        functools.partial(spread_kernel, chips, piece),
        in_specs=[whole] * len(spread),
        out_specs=[whole] * 2,
        out_shape=[own_type] * 2,
        compiler_params=params(4 * blocks_here * block_bytes),
        name="spread",
    )(*spread)
    return (
        grad_q.reshape(tok_rows, head_count, feature),
        grad_keys.reshape(tok_rows, feature),
        grad_values.reshape(tok_rows, feature),
    )


def solution(mesh):
    return jax.shard_map(
        body,
        mesh=mesh,
        in_specs=(
            P("ctx", "head", None),
            P("ctx", None),
            P("ctx", None),
            P("ctx", "head", None),
            P("ctx", None),
        ),
        out_specs=(P("ctx", "head", None), P("ctx", None), P("ctx", None)),
        check_vma=False,
    )
```

```python
import functools
import math

import jax
import jax.numpy as jnp
from jax import lax
from jax.experimental import pallas as pl
from jax.experimental.pallas import tpu as pltpu
from jax.sharding import PartitionSpec as P

F32 = jnp.float32
BF16 = jnp.bfloat16
VMEM_LIMIT = 56 * 1024 * 1024


def dot_nt(a, b):
    return lax.dot_general(a, b, (((1,), (1,)), ((), ())), preferred_element_type=F32)


def dot_nn(a, b):
    return lax.dot_general(a, b, (((1,), (0,)), ((), ())), preferred_element_type=F32)


def slot_of(chosen, blocks_here, row, t):
    ctx_self = lax.axis_index("ctx")
    entry = chosen[row, t]
    owner = lax.div(entry, jnp.int32(blocks_here))
    apart = ctx_self - owner
    slot = jnp.where(apart == 0, entry - owner * blocks_here, blocks_here + apart - 1)
    return jnp.where(entry != ctx_self * blocks_here + row, slot, -1)


def pick_kernel(blocks_here, count, chips, far, piece, chosen, keys, values, asked, *refs):
    outs, sems = refs[:-1], refs[-1]
    ctx_self = lax.axis_index("ctx")
    place = lax.axis_index("head")
    core, chip = lax.rem(place, 2), lax.div(place, 2)
    first = ctx_self * blocks_here
    span = pl.ds(pl.multiple_of(chip * piece, piece), piece)

    def copy(source, s, slot):
        rows = source.at[slot, span, :] if s in far else source.at[slot]
        return pltpu.make_async_copy(rows, outs[s], sems.at[s])

    for s in range(count - 1):
        peer = ctx_self + s + 1
        near = jnp.minimum(peer, count - 1)
        found = jnp.int32(0)
        for row in range(blocks_here):
            for t in range(3):
                entry = chosen[near, row * 3 + t]
                hit = (entry >= first) & (entry < first + blocks_here)
                found = jnp.where(hit, entry - first + 1, found)
        found = jnp.where(peer < count, found, 0)
        asked[s] = found
        slot = jnp.maximum(found - 1, 0)

        @pl.when(core == 0)
        def _():
            copy(keys, s, slot).start()

        @pl.when(core != 0)
        def _():
            copy(values, s, slot).start()

    for s in range(count - 1):
        copy(keys, s, 0).wait()


def chip_sum_kernel(chips, piece, groups, mine, theirs, *outs):
    chip = lax.div(lax.axis_index("head"), 2)
    outs = list(outs)
    for group in groups:
        for d in range(chips):
            out = outs.pop(0)
            target = lax.rem(chip + d, chips)
            span = pl.ds(pl.multiple_of(target * piece, piece), piece)
            for i, s in enumerate(group):
                total = mine[s, span, :].astype(F32) + theirs[s, span, :].astype(F32)
                out[i] = total.astype(out.dtype)


def head_sum_kernel(count, mine, *refs):
    parts, outs = refs[: len(refs) - count], refs[len(refs) - count :]
    for i in range(count):
        total = mine[i]
        for part in parts:
            total = total + part[i].astype(F32)
        outs[i][...] = total.astype(BF16)


def fold(array, reduce):
    rows, lanes = array.shape
    return reduce(array.reshape(rows // 8, 8, lanes), axis=0)


def causal(array, first_col, first_pos, other):
    col = lax.broadcasted_iota(jnp.int32, array.shape, 0) + first_col
    pos = lax.broadcasted_iota(jnp.int32, array.shape, 1) + first_pos
    return jnp.where(col <= pos, array, other)


def row_sums(s_ref, dp_ref, factor):
    block_len = s_ref.shape[0]
    step = min(64, block_len)
    spans = [pl.ds(c, step) for c in range(0, block_len, step)]
    top = fold(s_ref[spans[0], :], jnp.max)
    for span in spans[1:]:
        top = jnp.maximum(top, fold(s_ref[span, :], jnp.max))
    top = jnp.max(top, axis=0, keepdims=True) * factor
    total = weighted = jnp.zeros((8, block_len), F32)
    for span in spans:
        terms = jnp.exp2(s_ref[span, :] * factor - top)
        total = total + fold(terms, jnp.sum)
        weighted = weighted + fold(terms * dp_ref[span, :], jnp.sum)
    total = jnp.sum(total, axis=0, keepdims=True)
    return top, total, jnp.sum(weighted, axis=0, keepdims=True)


def local_stats_kernel(factor, blocks_here, chosen, q, do, keys, values, stats, s_buf, dp_buf):
    block_len = keys.shape[1]
    half = block_len // 2

    def per_row(row, _):
        start = row * block_len
        span = pl.ds(start, block_len)
        late = pl.ds(start + half, half)

        s_buf[:half, :] = causal(dot_nt(keys[row, :half], q[span, :]), 0, 0, -jnp.inf)
        s_buf[half:, :half] = jnp.full((half, half), -jnp.inf, F32)
        s_buf[half:, half:] = causal(dot_nt(keys[row, half:], q[late, :]), 0, 0, -jnp.inf)
        dp_buf[:half, :] = dot_nt(values[row, :half], do[span, :])
        dp_buf[half:, :half] = jnp.zeros((half, half), F32)
        dp_buf[half:, half:] = dot_nt(values[row, half:], do[late, :])
        top, total, weighted = row_sums(s_buf, dp_buf, factor)
        stats[row, 0:1, :] = top
        stats[row, 1:2, :] = total
        stats[row, 2:3, :] = weighted
        for t in range(3):
            slot = slot_of(chosen, blocks_here, row, t)

            @pl.when((slot >= 0) & (slot < blocks_here))
            def _():
                s_buf[...] = dot_nt(keys[slot], q[span, :])
                dp_buf[...] = dot_nt(values[slot], do[span, :])
                more_top, more, more_weighted = row_sums(s_buf, dp_buf, factor)
                old = stats[row, 0:1, :]
                top = jnp.maximum(old, more_top)
                scale_old = jnp.exp2(old - top)
                scale_new = jnp.exp2(more_top - top)
                stats[row, 0:1, :] = top
                stats[row, 1:2, :] = stats[row, 1:2, :] * scale_old + more * scale_new
                stats[row, 2:3, :] = stats[row, 2:3, :] * scale_old + more_weighted * scale_new

        return 0

    lax.fori_loop(0, blocks_here, per_row, 0)


def remote_kernel(
    factor, scaling, blocks_here, chips, far, near, piece, chosen, q, do, stats, *refs
):
    near_refs, far_refs, refs = refs[:2], refs[2 : 2 + 2 * chips], refs[2 + 2 * chips :]
    keep, send, final, grad_qt, rows, acc, s_buf, dp_buf, parts = refs
    place = lax.axis_index("head")
    core, chip = lax.rem(place, 2), lax.div(place, 2)
    block_len = rows.shape[2]
    half = block_len // 2

    def lay(kind, which):
        for i, s in enumerate(near):
            rows[kind, s] = near_refs[which][i]
        for d in range(chips):
            source = lax.rem(chip + chips - d, chips)
            span = pl.ds(pl.multiple_of(source * piece, piece), piece)
            for i, s in enumerate(far):
                rows[kind, s, span, :] = far_refs[2 * d + which][i]

    @pl.when(core == 0)
    def _():
        lay(0, 0)
        lay(1, 1)

    @pl.when(core != 0)
    def _():
        lay(0, 1)
        lay(1, 0)

    acc[...] = jnp.zeros_like(acc)

    reads = lax.axis_index("ctx") > 0

    @pl.when(jnp.logical_not(reads))
    def _():
        grad_qt[...] = jnp.zeros_like(grad_qt)
        final[:, 0:1, :] = stats[:, 0:1, :] + jnp.log2(stats[:, 1:2, :])
        final[:, 1:2, :] = stats[:, 2:3, :] / stats[:, 1:2, :]

    def per_row(row, _):
        span = pl.ds(row * block_len, block_len)
        parts[0, 0:3, :] = stats[row, 0:3, :]
        slots = [slot_of(chosen, blocks_here, row, t) - blocks_here for t in range(3)]
        for t in range(3):
            slot = jnp.maximum(slots[t], 0)
            s_buf[t] = dot_nt(rows[0, slot], q[span, :])
            dp_buf[t] = dot_nt(rows[1, slot], do[span, :])
        for t in range(3):
            live = slots[t] >= 0
            top, total, weighted = row_sums(s_buf.at[t], dp_buf.at[t], factor)
            parts[t + 1, 0:1, :] = jnp.where(live, top, -jnp.inf)
            parts[t + 1, 1:2, :] = total
            parts[t + 1, 2:3, :] = weighted

        top = parts[0, 0:1, :]
        for t in range(3):
            top = jnp.maximum(top, parts[t + 1, 0:1, :])
        total = jnp.zeros_like(top)
        weighted = jnp.zeros_like(top)
        for t in range(4):
            scale = jnp.exp2(parts[t, 0:1, :] - top)
            total = total + scale * parts[t, 1:2, :]
            weighted = weighted + scale * parts[t, 2:3, :]
        final[row, 0:1, :] = top + jnp.log2(total)
        final[row, 1:2, :] = weighted / total
        grad_qt[row] = jnp.zeros_like(grad_qt[row])
        for t in range(3):
            slot = jnp.maximum(slots[t], 0)
            level = final[row, 0:1, :] + jnp.where(slots[t] >= 0, 0.0, jnp.inf)
            delta = final[row, 1:2, :]
            for c in (0, half):
                cut = pl.ds(c, half)
                weights = jnp.exp2(s_buf[t, cut, :] * factor - level)
                dscores = (weights * (dp_buf[t, cut, :] - delta)).astype(BF16)
                acc[1, slot, cut, :] += dot_nn(weights.astype(BF16), do[span, :])
                acc[0, slot, cut, :] += dot_nn(dscores, q[span, :])
                grad_qt[row] += dot_nn(rows[0, slot, cut, :].T, dscores)

        return 0

    lax.fori_loop(0, jnp.where(reads, blocks_here, 0), per_row, 0)
    keep_scale = jnp.where(core == 0, scaling, 1.0)
    send_scale = jnp.where(core == 0, 1.0, scaling)
    keep[...] = (acc[core] * keep_scale).astype(BF16)
    send[...] = (acc[1 - core] * send_scale).astype(BF16)


def local_kernel(
    factor, scaling, blocks_here, chosen, q, do, keys, values, final, grad_qt,
    keep, send, grad_q,
    acc, total_qt,
):
    core = lax.rem(lax.axis_index("head"), 2)
    block_len = keys.shape[1]
    half = block_len // 2
    acc[...] = jnp.zeros_like(acc)

    def per_row(row, _):
        start = row * block_len
        span = pl.ds(start, block_len)

        def part(slot, c, first, masked):
            cut = pl.ds(c, half)
            q_rows = q[pl.ds(start + first, block_len - first), :]
            do_rows = do[pl.ds(start + first, block_len - first), :]
            key_rows = keys[slot, cut, :]
            scores = dot_nt(key_rows, q_rows)
            dprobs = dot_nt(values[slot, cut, :], do_rows)
            weights = jnp.exp2(scores * factor - final[row, 0:1, first:])
            if masked:
                weights = causal(weights, c, first, 0.0)
            dscores = (weights * (dprobs - final[row, 1:2, first:])).astype(BF16)
            acc[1, slot, cut, :] += dot_nn(weights.astype(BF16), do_rows)
            acc[0, slot, cut, :] += dot_nn(dscores, q_rows)
            total_qt[:, first:] += dot_nn(key_rows.T, dscores)

        total_qt[...] = grad_qt[row]
        part(row, 0, 0, True)
        part(row, half, half, True)
        for t in range(3):
            slot = slot_of(chosen, blocks_here, row, t)

            @pl.when((slot >= 0) & (slot < blocks_here))
            def _():
                part(slot, 0, 0, False)
                part(slot, half, 0, False)

        grad_q[span, :] = (total_qt[...].T * scaling).astype(BF16)
        return 0

    lax.fori_loop(0, blocks_here, per_row, 0)
    keep_scale = jnp.where(core == 0, scaling, 1.0)
    send_scale = jnp.where(core == 0, 1.0, scaling)
    keep[...] = (acc[core] * keep_scale).astype(BF16)
    send[...] = (acc[1 - core] * send_scale).astype(BF16)


def owner_kernel(chips, shifts, asked, mine, *refs):
    others, back, (out, acc) = refs[: chips - 1], refs[chips - 1 : chips - 1 + shifts], refs[-2:]
    total = mine[...]
    for part in others:
        total = total + part[...].astype(F32)
    acc[...] = total
    for s in range(shifts):
        slot = asked[s] - 1

        @pl.when(slot >= 0)
        def _():
            acc[slot] += back[s][...].astype(F32)

    out[...] = acc[...].astype(BF16)


def spread_kernel(chips, piece, *refs):
    pieces, (grad_k, grad_v) = refs[: 2 * chips], refs[2 * chips :]
    place = lax.axis_index("head")
    core, chip = lax.rem(place, 2), lax.div(place, 2)

    def lay(out, which):
        for d in range(chips):
            source = lax.rem(chip + chips - d, chips)
            span = pl.ds(pl.multiple_of(source * piece, piece), piece)
            out[:, span, :] = pieces[2 * d + which][...]

    @pl.when(core == 0)
    def _():
        lay(grad_k, 0)
        lay(grad_v, 1)

    @pl.when(core != 0)
    def _():
        lay(grad_k, 1)
        lay(grad_v, 0)


def params(size):
    return pltpu.CompilerParams(vmem_limit_bytes=min(size + 12 * 1024 * 1024, VMEM_LIMIT))


def body(queries, keys, values, dout, selected):
    tok_rows, head_count, feature = queries.shape
    blocks_here = selected.shape[0]
    block_len = tok_rows // blocks_here
    ctx_count = lax.axis_size("ctx")
    heads = lax.axis_size("head")
    chips = heads // 2
    piece = block_len // chips
    scaling = 1.0 / math.sqrt(feature)
    factor = scaling * math.log2(math.e)
    shifts = ctx_count - 1
    far = [s for s in range(shifts) if 2 * (s + 1) >= ctx_count]
    near = [s for s in range(shifts) if 2 * (s + 1) < ctx_count]

    q2 = queries.reshape(tok_rows, feature)
    do2 = dout.reshape(tok_rows, feature)
    key_blocks = keys.reshape(blocks_here, block_len, feature)
    value_blocks = values.reshape(blocks_here, block_len, feature)
    remote_shape = (shifts, block_len, feature)
    local_shape = (blocks_here, block_len, feature)

    smem = pl.BlockSpec(memory_space=pltpu.SMEM)
    whole = pl.BlockSpec(memory_space=pltpu.VMEM)
    hbm = pl.BlockSpec(memory_space=pltpu.HBM)
    stat_type = jax.ShapeDtypeStruct((blocks_here, 8, block_len), F32)
    far_type = jax.ShapeDtypeStruct(remote_shape, BF16)
    own_type = jax.ShapeDtypeStruct(local_shape, BF16)
    block_type = jax.ShapeDtypeStruct((block_len, feature), BF16)
    piece_type = jax.ShapeDtypeStruct((piece, feature), BF16)
    qt_type = jax.ShapeDtypeStruct((blocks_here, feature, block_len), F32)
    pair_flops = 2 * block_len * block_len * feature
    block_bytes = block_len * feature * 2
    pair_bytes = block_len * block_len * 4

    def pieces_type(count, dtype):
        return jax.ShapeDtypeStruct((count, piece, feature), dtype)

    def cost(matmuls, size):
        return pl.CostEstimate(
            flops=matmuls * pair_flops, bytes_accessed=size, transcendentals=matmuls * block_len**2
        )

    def swap(array):
        return lax.ppermute(array, "head", [(h, h ^ 1) for h in range(heads)])

    def to_chip(array, d):
        return lax.ppermute(array, "head", [(h, (h + 2 * d) % heads) for h in range(heads)])

    def to_owner(array, s):
        return lax.ppermute(array, "ctx", [(c, c - s - 1) for c in range(s + 1, ctx_count)])

    def to_reader(array, s):
        return lax.ppermute(array, "ctx", [(c - s - 1, c) for c in range(s + 1, ctx_count)])

    everyone = lax.all_to_all(
        jnp.broadcast_to(selected.reshape(1, 3 * blocks_here), (ctx_count, 3 * blocks_here)),
        "ctx", split_axis=0, concat_axis=0, tiled=True,
    )
    asked, *sent = pl.pallas_call(
        functools.partial(pick_kernel, blocks_here, ctx_count, chips, far, piece),
        in_specs=[smem, hbm, hbm],
        out_specs=[smem] + [whole] * shifts,
        out_shape=[jax.ShapeDtypeStruct((shifts,), jnp.int32)]
        + [piece_type if s in far else block_type for s in range(shifts)],
        scratch_shapes=[pltpu.SemaphoreType.DMA((shifts,))],
        name="pick_rows",
    )(everyone, key_blocks, value_blocks)

    far_mine = jnp.stack([to_reader(sent[s], s) for s in far])
    near_parts = [to_reader(sent[s], s) for s in near]
    far_mine, chosen = lax.optimization_barrier((far_mine, selected))
    far_more = [to_chip(far_mine, d) for d in range(1, chips)]
    stats = pl.pallas_call(
        functools.partial(local_stats_kernel, factor, blocks_here),
        in_specs=[smem] + [whole] * 4,
        out_specs=whole,
        out_shape=stat_type,
        scratch_shapes=[pltpu.VMEM((block_len, block_len), F32)] * 2,
        compiler_params=params(4 * blocks_here * block_bytes + 2 * pair_bytes),
        cost_estimate=cost(30, 4 * tok_rows * feature * 2),
        name="local_stats",
    )(chosen, q2, do2, key_blocks, value_blocks)
    near_parts, far_held, stats = lax.optimization_barrier((near_parts, far_mine, stats))
    near_mine = jnp.stack(near_parts)
    row_sets = [near_mine, swap(near_mine), far_held, swap(far_held)]
    for part in far_more:
        row_sets += [part, swap(part)]

    keep_far, send_far, final, grad_qt = pl.pallas_call(
        functools.partial(remote_kernel, factor, scaling, blocks_here, chips, far, near, piece),
        in_specs=[smem] + [whole] * (3 + len(row_sets)),
        out_specs=[whole] * 4,
        out_shape=[far_type, far_type, stat_type, qt_type],
        scratch_shapes=[
            pltpu.VMEM((2,) + remote_shape, BF16),
            pltpu.VMEM((2,) + remote_shape, F32),
            pltpu.VMEM((3, block_len, block_len), F32),
            pltpu.VMEM((3, block_len, block_len), F32),
            pltpu.VMEM((4, 8, block_len), F32),
        ],
        compiler_params=params((10 * shifts + 4 * blocks_here) * block_bytes + 6 * pair_bytes),
        cost_estimate=cost(60, 8 * tok_rows * feature * 2),
        name="remote_pairs",
    )(chosen, q2, do2, stats, *row_sets)

    def chip_sums(mine, theirs, groups):
        types = []
        for group in groups:
            types += [pieces_type(len(group), F32)]
            types += [pieces_type(len(group), BF16)] * (chips - 1)
        sums = pl.pallas_call(
            functools.partial(chip_sum_kernel, chips, piece, groups),
            in_specs=[whole, whole],
            out_specs=[whole] * len(types),
            out_shape=types,
            compiler_params=params(4 * mine.shape[0] * block_bytes),
            name="chip_sum",
        )(mine, theirs)
        return [sums[i * chips : (i + 1) * chips] for i in range(len(groups))]

    def head_sums(mine, parts, count):
        return pl.pallas_call(
            functools.partial(head_sum_kernel, count),
            in_specs=[whole] * (1 + len(parts)),
            out_specs=[whole] * count,
            out_shape=[piece_type] * count,
            compiler_params=params(4 * count * block_bytes),
            name="head_sum",
        )(mine, *parts)

    far_sums, near_sums = chip_sums(keep_far, swap(send_far), [far, near])
    far_sums, near_sums, final = lax.optimization_barrier((far_sums, near_sums, final))
    far_parts = [to_chip(far_sums[d], d) for d in range(1, chips)]
    keep_own, send_own, grad_q = pl.pallas_call(
        functools.partial(local_kernel, factor, scaling, blocks_here),
        in_specs=[smem] + [whole] * 6,
        out_specs=[whole] * 3,
        out_shape=[own_type, own_type, jax.ShapeDtypeStruct((tok_rows, feature), BF16)],
        scratch_shapes=[
            pltpu.VMEM((2,) + local_shape, F32),
            pltpu.VMEM((feature, block_len), F32),
        ],
        compiler_params=params(14 * blocks_here * block_bytes),
        cost_estimate=cost(60, 8 * tok_rows * feature * 2),
        name="local_pairs",
    )(chosen, q2, do2, key_blocks, value_blocks, final, grad_qt)
    far_parts, near_sums, keep_own, send_own = lax.optimization_barrier(
        (far_parts, near_sums, keep_own, send_own)
    )
    near_parts = [to_chip(near_sums[d], d) for d in range(1, chips)]
    far_out = head_sums(far_sums[0], far_parts, len(far))
    back = {s: to_owner(far_out[i], s) for i, s in enumerate(far)}
    back[far[0]], keep_own, own_twin = lax.optimization_barrier(
        (back[far[0]], keep_own, swap(send_own))
    )
    (own_sums,) = chip_sums(keep_own, own_twin, [list(range(blocks_here))])
    own_parts = [to_chip(own_sums[d], d) for d in range(1, chips)]
    near_parts, own_mine = lax.optimization_barrier((near_parts, own_sums[0]))
    near_out = head_sums(near_sums[0], near_parts, len(near))
    back.update({s: to_owner(near_out[i], s) for i, s in enumerate(near)})

    mine = pl.pallas_call(
        functools.partial(owner_kernel, chips, shifts),
        in_specs=[smem] + [whole] * (chips + shifts),
        out_specs=whole,
        out_shape=pieces_type(blocks_here, BF16),
        scratch_shapes=[pltpu.VMEM((blocks_here, piece, feature), F32)],
        compiler_params=params((5 * blocks_here + shifts) * block_bytes),
        name="owner_sum",
    )(asked, own_mine, *own_parts, *[back[s] for s in range(shifts)])
    spread = [mine, swap(mine)]
    for d in range(1, chips):
        part = to_chip(mine, d)
        spread += [part, swap(part)]
    grad_keys, grad_values = pl.pallas_call(
        functools.partial(spread_kernel, chips, piece),
        in_specs=[whole] * len(spread),
        out_specs=[whole] * 2,
        out_shape=[own_type] * 2,
        compiler_params=params(4 * blocks_here * block_bytes),
        name="spread",
    )(*spread)
    return (
        grad_q.reshape(tok_rows, head_count, feature),
        grad_keys.reshape(tok_rows, feature),
        grad_values.reshape(tok_rows, feature),
    )


def solution(mesh):
    return jax.shard_map(
        body,
        mesh=mesh,
        in_specs=(
            P("ctx", "head", None),
            P("ctx", None),
            P("ctx", None),
            P("ctx", "head", None),
            P("ctx", None),
        ),
        out_specs=(P("ctx", "head", None), P("ctx", None), P("ctx", None)),
        check_vma=False,
    )
```

```python
import functools
import math

import jax
import jax.numpy as jnp
from jax import lax
from jax.experimental import pallas as pl
from jax.experimental.pallas import tpu as pltpu
from jax.sharding import PartitionSpec as P

F32 = jnp.float32
BF16 = jnp.bfloat16
VMEM_LIMIT = 56 * 1024 * 1024


def dot_nt(a, b):
    return lax.dot_general(a, b, (((1,), (1,)), ((), ())), preferred_element_type=F32)


def dot_nn(a, b):
    return lax.dot_general(a, b, (((1,), (0,)), ((), ())), preferred_element_type=F32)


def slot_of(chosen, blocks_here, row, t):
    ctx_self = lax.axis_index("ctx")
    entry = chosen[row, t]
    owner = lax.div(entry, jnp.int32(blocks_here))
    apart = ctx_self - owner
    slot = jnp.where(apart == 0, entry - owner * blocks_here, blocks_here + apart - 1)
    return jnp.where(entry != ctx_self * blocks_here + row, slot, -1)


def pick_kernel(blocks_here, count, chips, far, piece, chosen, keys, values, asked, *refs):
    outs, sems = refs[:-1], refs[-1]
    ctx_self = lax.axis_index("ctx")
    place = lax.axis_index("head")
    core, chip = lax.rem(place, 2), lax.div(place, 2)
    first = ctx_self * blocks_here
    span = pl.ds(pl.multiple_of(chip * piece, piece), piece)

    def copy(source, s, slot):
        rows = source.at[slot, span, :] if s in far else source.at[slot]
        return pltpu.make_async_copy(rows, outs[s], sems.at[s])

    for s in range(count - 1):
        peer = ctx_self + s + 1
        near = jnp.minimum(peer, count - 1)
        found = jnp.int32(0)
        for row in range(blocks_here):
            for t in range(3):
                entry = chosen[near, row * 3 + t]
                hit = (entry >= first) & (entry < first + blocks_here)
                found = jnp.where(hit, entry - first + 1, found)
        found = jnp.where(peer < count, found, 0)
        asked[s] = found
        slot = jnp.maximum(found - 1, 0)

        @pl.when(core == 0)
        def _():
            copy(keys, s, slot).start()

        @pl.when(core != 0)
        def _():
            copy(values, s, slot).start()

    for s in range(count - 1):
        copy(keys, s, 0).wait()


def chip_sum_kernel(chips, piece, mine, theirs, *outs):
    chip = lax.div(lax.axis_index("head"), 2)
    for d, out in enumerate(outs):
        target = lax.rem(chip + d, chips)
        span = pl.ds(pl.multiple_of(target * piece, piece), piece)
        for s in range(mine.shape[0]):
            total = mine[s, span, :].astype(F32) + theirs[s, span, :].astype(F32)
            out[s] = total.astype(out.dtype)


def head_sum_kernel(mine, *refs):
    parts, out = refs[:-1], refs[-1]
    ctx_self = lax.axis_index("ctx")
    out[...] = jnp.zeros_like(out)
    for s in range(mine.shape[0]):

        @pl.when(ctx_self > s)
        def _():
            total = mine[s]
            for part in parts:
                total = total + part[s].astype(F32)
            out[ctx_self - s - 1] = total.astype(BF16)


def fold(array, reduce):
    rows, lanes = array.shape
    return reduce(array.reshape(rows // 8, 8, lanes), axis=0)


def causal(array, first_col, first_pos, other):
    col = lax.broadcasted_iota(jnp.int32, array.shape, 0) + first_col
    pos = lax.broadcasted_iota(jnp.int32, array.shape, 1) + first_pos
    return jnp.where(col <= pos, array, other)


def row_sums(s_ref, dp_ref, factor):
    block_len = s_ref.shape[0]
    step = min(64, block_len)
    spans = [pl.ds(c, step) for c in range(0, block_len, step)]
    top = fold(s_ref[spans[0], :], jnp.max)
    for span in spans[1:]:
        top = jnp.maximum(top, fold(s_ref[span, :], jnp.max))
    top = jnp.max(top, axis=0, keepdims=True) * factor
    total = weighted = jnp.zeros((8, block_len), F32)
    for span in spans:
        terms = jnp.exp2(s_ref[span, :] * factor - top)
        total = total + fold(terms, jnp.sum)
        weighted = weighted + fold(terms * dp_ref[span, :], jnp.sum)
    total = jnp.sum(total, axis=0, keepdims=True)
    return top, total, jnp.sum(weighted, axis=0, keepdims=True)


def local_stats_kernel(factor, blocks_here, chosen, q, do, keys, values, stats, s_buf, dp_buf):
    block_len = keys.shape[1]
    half = block_len // 2

    def per_row(row, _):
        start = row * block_len
        span = pl.ds(start, block_len)
        late = pl.ds(start + half, half)

        s_buf[:half, :] = causal(dot_nt(keys[row, :half], q[span, :]), 0, 0, -jnp.inf)
        s_buf[half:, :half] = jnp.full((half, half), -jnp.inf, F32)
        s_buf[half:, half:] = causal(dot_nt(keys[row, half:], q[late, :]), 0, 0, -jnp.inf)
        dp_buf[:half, :] = dot_nt(values[row, :half], do[span, :])
        dp_buf[half:, :half] = jnp.zeros((half, half), F32)
        dp_buf[half:, half:] = dot_nt(values[row, half:], do[late, :])
        top, total, weighted = row_sums(s_buf, dp_buf, factor)
        stats[row, 0:1, :] = top
        stats[row, 1:2, :] = total
        stats[row, 2:3, :] = weighted
        for t in range(3):
            slot = slot_of(chosen, blocks_here, row, t)

            @pl.when((slot >= 0) & (slot < blocks_here))
            def _():
                s_buf[...] = dot_nt(keys[slot], q[span, :])
                dp_buf[...] = dot_nt(values[slot], do[span, :])
                more_top, more, more_weighted = row_sums(s_buf, dp_buf, factor)
                old = stats[row, 0:1, :]
                top = jnp.maximum(old, more_top)
                scale_old = jnp.exp2(old - top)
                scale_new = jnp.exp2(more_top - top)
                stats[row, 0:1, :] = top
                stats[row, 1:2, :] = stats[row, 1:2, :] * scale_old + more * scale_new
                stats[row, 2:3, :] = stats[row, 2:3, :] * scale_old + more_weighted * scale_new

        return 0

    lax.fori_loop(0, blocks_here, per_row, 0)


def remote_kernel(
    factor, scaling, blocks_here, chips, far, near, piece, chosen, q, do, stats, *refs
):
    near_refs, far_refs, refs = refs[:2], refs[2 : 2 + 2 * chips], refs[2 + 2 * chips :]
    keep, send, final, grad_qt, rows, acc, s_buf, dp_buf, parts = refs
    place = lax.axis_index("head")
    core, chip = lax.rem(place, 2), lax.div(place, 2)
    block_len = rows.shape[2]
    half = block_len // 2

    def lay(kind, which):
        for i, s in enumerate(near):
            rows[kind, s] = near_refs[which][i]
        for d in range(chips):
            source = lax.rem(chip + chips - d, chips)
            span = pl.ds(pl.multiple_of(source * piece, piece), piece)
            for i, s in enumerate(far):
                rows[kind, s, span, :] = far_refs[2 * d + which][i]

    @pl.when(core == 0)
    def _():
        lay(0, 0)
        lay(1, 1)

    @pl.when(core != 0)
    def _():
        lay(0, 1)
        lay(1, 0)

    acc[...] = jnp.zeros_like(acc)

    def per_row(row, _):
        span = pl.ds(row * block_len, block_len)
        parts[0, 0:3, :] = stats[row, 0:3, :]
        for t in range(3):
            slot = slot_of(chosen, blocks_here, row, t) - blocks_here

            @pl.when(slot >= 0)
            def _():
                s_buf[t] = dot_nt(rows[0, slot], q[span, :])
                dp_buf[t] = dot_nt(rows[1, slot], do[span, :])
                top, total, weighted = row_sums(s_buf.at[t], dp_buf.at[t], factor)
                parts[t + 1, 0:1, :] = top
                parts[t + 1, 1:2, :] = total
                parts[t + 1, 2:3, :] = weighted

            @pl.when(slot < 0)
            def _():
                parts[t + 1, 0:1, :] = jnp.full((1, block_len), -jnp.inf, F32)
                parts[t + 1, 1:3, :] = jnp.zeros((2, block_len), F32)

        top = parts[0, 0:1, :]
        for t in range(3):
            top = jnp.maximum(top, parts[t + 1, 0:1, :])
        total = jnp.zeros_like(top)
        weighted = jnp.zeros_like(top)
        for t in range(4):
            scale = jnp.exp2(parts[t, 0:1, :] - top)
            total = total + scale * parts[t, 1:2, :]
            weighted = weighted + scale * parts[t, 2:3, :]
        final[row, 0:1, :] = top + jnp.log2(total)
        final[row, 1:2, :] = weighted / total
        grad_qt[row] = jnp.zeros_like(grad_qt[row])
        for t in range(3):
            slot = slot_of(chosen, blocks_here, row, t) - blocks_here

            @pl.when(slot >= 0)
            def _():
                level = final[row, 0:1, :]
                delta = final[row, 1:2, :]
                for c in (0, half):
                    cut = pl.ds(c, half)
                    weights = jnp.exp2(s_buf[t, cut, :] * factor - level)
                    dscores = (weights * (dp_buf[t, cut, :] - delta)).astype(BF16)
                    acc[1, slot, cut, :] += dot_nn(weights.astype(BF16), do[span, :])
                    acc[0, slot, cut, :] += dot_nn(dscores, q[span, :])
                    grad_qt[row] += dot_nn(rows[0, slot, cut, :].T, dscores)

        return 0

    lax.fori_loop(0, blocks_here, per_row, 0)
    keep_scale = jnp.where(core == 0, scaling, 1.0)
    send_scale = jnp.where(core == 0, 1.0, scaling)
    keep[...] = (acc[core] * keep_scale).astype(BF16)
    send[...] = (acc[1 - core] * send_scale).astype(BF16)


def local_kernel(
    factor, scaling, blocks_here, chips, piece, chosen, q, do, keys, values, final, grad_qt, *refs
):
    pieces, (grad_q, acc, total_qt) = refs[: 2 * chips], refs[2 * chips :]
    place = lax.axis_index("head")
    core, chip = lax.rem(place, 2), lax.div(place, 2)
    block_len = keys.shape[1]
    half = block_len // 2
    acc[...] = jnp.zeros_like(acc)

    def per_row(row, _):
        start = row * block_len
        span = pl.ds(start, block_len)

        def part(slot, c, first, masked):
            cut = pl.ds(c, half)
            q_rows = q[pl.ds(start + first, block_len - first), :]
            do_rows = do[pl.ds(start + first, block_len - first), :]
            key_rows = keys[slot, cut, :]
            scores = dot_nt(key_rows, q_rows)
            dprobs = dot_nt(values[slot, cut, :], do_rows)
            weights = jnp.exp2(scores * factor - final[row, 0:1, first:])
            if masked:
                weights = causal(weights, c, first, 0.0)
            dscores = (weights * (dprobs - final[row, 1:2, first:])).astype(BF16)
            acc[1, slot, cut, :] += dot_nn(weights.astype(BF16), do_rows)
            acc[0, slot, cut, :] += dot_nn(dscores, q_rows)
            total_qt[:, first:] += dot_nn(key_rows.T, dscores)

        total_qt[...] = grad_qt[row]
        part(row, 0, 0, True)
        part(row, half, half, True)
        for t in range(3):
            slot = slot_of(chosen, blocks_here, row, t)

            @pl.when((slot >= 0) & (slot < blocks_here))
            def _():
                part(slot, 0, 0, False)
                part(slot, half, 0, False)

        grad_q[span, :] = (total_qt[...].T * scaling).astype(BF16)
        return 0

    lax.fori_loop(0, blocks_here, per_row, 0)
    scales = [jnp.where(core == 0, scaling, 1.0), jnp.where(core == 0, 1.0, scaling)]
    for d in range(chips):
        target = lax.rem(chip + d, chips)
        span = pl.ds(pl.multiple_of(target * piece, piece), piece)
        for which, kind in enumerate((core, 1 - core)):
            out = pieces[2 * d + which]
            out[...] = (acc[kind, :, span, :] * scales[which]).astype(out.dtype)


def owner_kernel(shifts, asked, mine, back, *refs):
    others, (out, acc) = refs[:-2], refs[-2:]
    ctx_self = lax.axis_index("ctx")
    total = mine[...]
    for part in others:
        total = total + part[...].astype(F32)
    acc[...] = total
    for s in range(shifts):
        slot = asked[s] - 1

        @pl.when(slot >= 0)
        def _():
            acc[slot] += back[ctx_self + s + 1].astype(F32)

    out[...] = acc[...].astype(BF16)


def spread_kernel(chips, piece, *refs):
    pieces, (grad_k, grad_v) = refs[: 2 * chips], refs[2 * chips :]
    place = lax.axis_index("head")
    core, chip = lax.rem(place, 2), lax.div(place, 2)

    def lay(out, which):
        for d in range(chips):
            source = lax.rem(chip + chips - d, chips)
            span = pl.ds(pl.multiple_of(source * piece, piece), piece)
            out[:, span, :] = pieces[2 * d + which][...]

    @pl.when(core == 0)
    def _():
        lay(grad_k, 0)
        lay(grad_v, 1)

    @pl.when(core != 0)
    def _():
        lay(grad_k, 1)
        lay(grad_v, 0)


def params(size):
    return pltpu.CompilerParams(vmem_limit_bytes=min(size + 12 * 1024 * 1024, VMEM_LIMIT))


def body(queries, keys, values, dout, selected):
    tok_rows, head_count, feature = queries.shape
    blocks_here = selected.shape[0]
    block_len = tok_rows // blocks_here
    ctx_count = lax.axis_size("ctx")
    heads = lax.axis_size("head")
    chips = heads // 2
    piece = block_len // chips
    scaling = 1.0 / math.sqrt(feature)
    factor = scaling * math.log2(math.e)
    shifts = ctx_count - 1
    far = [s for s in range(shifts) if 2 * (s + 1) >= ctx_count]
    near = [s for s in range(shifts) if 2 * (s + 1) < ctx_count]

    q2 = queries.reshape(tok_rows, feature)
    do2 = dout.reshape(tok_rows, feature)
    key_blocks = keys.reshape(blocks_here, block_len, feature)
    value_blocks = values.reshape(blocks_here, block_len, feature)
    remote_shape = (shifts, block_len, feature)
    local_shape = (blocks_here, block_len, feature)

    smem = pl.BlockSpec(memory_space=pltpu.SMEM)
    whole = pl.BlockSpec(memory_space=pltpu.VMEM)
    hbm = pl.BlockSpec(memory_space=pltpu.HBM)
    stat_type = jax.ShapeDtypeStruct((blocks_here, 8, block_len), F32)
    far_type = jax.ShapeDtypeStruct(remote_shape, BF16)
    own_type = jax.ShapeDtypeStruct(local_shape, BF16)
    block_type = jax.ShapeDtypeStruct((block_len, feature), BF16)
    piece_type = jax.ShapeDtypeStruct((piece, feature), BF16)
    qt_type = jax.ShapeDtypeStruct((blocks_here, feature, block_len), F32)
    pair_flops = 2 * block_len * block_len * feature
    block_bytes = block_len * feature * 2
    pair_bytes = block_len * block_len * 4

    def pieces_type(count, dtype):
        return jax.ShapeDtypeStruct((count, piece, feature), dtype)

    def cost(matmuls, size):
        return pl.CostEstimate(
            flops=matmuls * pair_flops, bytes_accessed=size, transcendentals=matmuls * block_len**2
        )

    def swap(array):
        return lax.ppermute(array, "head", [(h, h ^ 1) for h in range(heads)])

    def to_chip(array, d):
        return lax.ppermute(array, "head", [(h, (h + 2 * d) % heads) for h in range(heads)])

    def to_chip_twin(array, d):
        return lax.ppermute(array, "head", [(h, ((h + 2 * d) % heads) ^ 1) for h in range(heads)])

    def to_reader(array, s):
        return lax.ppermute(array, "ctx", [(c - s - 1, c) for c in range(s + 1, ctx_count)])

    everyone = lax.all_to_all(
        jnp.broadcast_to(selected.reshape(1, 3 * blocks_here), (ctx_count, 3 * blocks_here)),
        "ctx", split_axis=0, concat_axis=0, tiled=True,
    )
    asked, *sent = pl.pallas_call(
        functools.partial(pick_kernel, blocks_here, ctx_count, chips, far, piece),
        in_specs=[smem, hbm, hbm],
        out_specs=[smem] + [whole] * shifts,
        out_shape=[jax.ShapeDtypeStruct((shifts,), jnp.int32)]
        + [piece_type if s in far else block_type for s in range(shifts)],
        scratch_shapes=[pltpu.SemaphoreType.DMA((shifts,))],
        name="pick_rows",
    )(everyone, key_blocks, value_blocks)

    far_mine = jnp.stack([to_reader(sent[s], s) for s in far])
    near_parts = [to_reader(sent[s], s) for s in near]
    far_mine, chosen = lax.optimization_barrier((far_mine, selected))
    far_more = [to_chip(far_mine, d) for d in range(1, chips)]
    stats = pl.pallas_call(
        functools.partial(local_stats_kernel, factor, blocks_here),
        in_specs=[smem] + [whole] * 4,
        out_specs=whole,
        out_shape=stat_type,
        scratch_shapes=[pltpu.VMEM((block_len, block_len), F32)] * 2,
        compiler_params=params(4 * blocks_here * block_bytes + 2 * pair_bytes),
        cost_estimate=cost(30, 4 * tok_rows * feature * 2),
        name="local_stats",
    )(chosen, q2, do2, key_blocks, value_blocks)
    near_parts, far_held, stats = lax.optimization_barrier((near_parts, far_mine, stats))
    near_mine = jnp.stack(near_parts)
    row_sets = [near_mine, swap(near_mine), far_held, swap(far_held)]
    for part in far_more:
        row_sets += [part, swap(part)]

    keep_far, send_far, final, grad_qt = pl.pallas_call(
        functools.partial(remote_kernel, factor, scaling, blocks_here, chips, far, near, piece),
        in_specs=[smem] + [whole] * (3 + len(row_sets)),
        out_specs=[whole] * 4,
        out_shape=[far_type, far_type, stat_type, qt_type],
        scratch_shapes=[
            pltpu.VMEM((2,) + remote_shape, BF16),
            pltpu.VMEM((2,) + remote_shape, F32),
            pltpu.VMEM((3, block_len, block_len), F32),
            pltpu.VMEM((3, block_len, block_len), F32),
            pltpu.VMEM((4, 8, block_len), F32),
        ],
        compiler_params=params((10 * shifts + 4 * blocks_here) * block_bytes + 6 * pair_bytes),
        cost_estimate=cost(60, 8 * tok_rows * feature * 2),
        name="remote_pairs",
    )(chosen, q2, do2, stats, *row_sets)

    far_sums = pl.pallas_call(
        functools.partial(chip_sum_kernel, chips, piece),
        in_specs=[whole, whole],
        out_specs=[whole] * chips,
        out_shape=[pieces_type(shifts, F32)] + [pieces_type(shifts, BF16)] * (chips - 1),
        compiler_params=params(4 * shifts * block_bytes),
        name="chip_sum",
    )(keep_far, swap(send_far))
    far_sums, final = lax.optimization_barrier((far_sums, final))
    far_parts = [to_chip(far_sums[d], d) for d in range(1, chips)]
    *own_pieces, grad_q = pl.pallas_call(
        functools.partial(local_kernel, factor, scaling, blocks_here, chips, piece),
        in_specs=[smem] + [whole] * 6,
        out_specs=[whole] * (2 * chips + 1),
        out_shape=[pieces_type(blocks_here, F32)]
        + [pieces_type(blocks_here, BF16)] * (2 * chips - 1)
        + [jax.ShapeDtypeStruct((tok_rows, feature), BF16)],
        scratch_shapes=[
            pltpu.VMEM((2,) + local_shape, F32),
            pltpu.VMEM((feature, block_len), F32),
        ],
        compiler_params=params(14 * blocks_here * block_bytes),
        cost_estimate=cost(60, 8 * tok_rows * feature * 2),
        name="local_pairs",
    )(chosen, q2, do2, key_blocks, value_blocks, final, grad_qt)
    far_parts, own_mine = lax.optimization_barrier((far_parts, own_pieces[0]))
    own_parts = [swap(own_pieces[1])]
    for d in range(1, chips):
        own_parts += [to_chip(own_pieces[2 * d], d), to_chip_twin(own_pieces[2 * d + 1], d)]
    returned = pl.pallas_call(
        head_sum_kernel,
        in_specs=[whole] * chips,
        out_specs=whole,
        out_shape=pieces_type(ctx_count, BF16),
        compiler_params=params(4 * ctx_count * block_bytes),
        name="head_sum",
    )(far_sums[0], *far_parts)
    back = lax.all_to_all(returned, "ctx", split_axis=0, concat_axis=0, tiled=True)

    mine = pl.pallas_call(
        functools.partial(owner_kernel, shifts),
        in_specs=[smem] + [whole] * (2 + len(own_parts)),
        out_specs=whole,
        out_shape=pieces_type(blocks_here, BF16),
        scratch_shapes=[pltpu.VMEM((blocks_here, piece, feature), F32)],
        compiler_params=params((5 * blocks_here + ctx_count) * block_bytes),
        name="owner_sum",
    )(asked, own_mine, back, *own_parts)
    spread = [mine, swap(mine)]
    for d in range(1, chips):
        part = to_chip(mine, d)
        spread += [part, swap(part)]
    grad_keys, grad_values = pl.pallas_call(
        functools.partial(spread_kernel, chips, piece),
        in_specs=[whole] * len(spread),
        out_specs=[whole] * 2,
        out_shape=[own_type] * 2,
        compiler_params=params(4 * blocks_here * block_bytes),
        name="spread",
    )(*spread)
    return (
        grad_q.reshape(tok_rows, head_count, feature),
        grad_keys.reshape(tok_rows, feature),
        grad_values.reshape(tok_rows, feature),
    )


def solution(mesh):
    return jax.shard_map(
        body,
        mesh=mesh,
        in_specs=(
            P("ctx", "head", None),
            P("ctx", None),
            P("ctx", None),
            P("ctx", "head", None),
            P("ctx", None),
        ),
        out_specs=(P("ctx", "head", None), P("ctx", None), P("ctx", None)),
        check_vma=False,
    )
```

```python
import functools
import math

import jax
import jax.numpy as jnp
from jax import lax
from jax.experimental import pallas as pl
from jax.experimental.pallas import tpu as pltpu
from jax.sharding import PartitionSpec as P

F32 = jnp.float32
BF16 = jnp.bfloat16
VMEM_LIMIT = 56 * 1024 * 1024


def dot_nt(a, b):
    return lax.dot_general(a, b, (((1,), (1,)), ((), ())), preferred_element_type=F32)


def dot_nn(a, b):
    return lax.dot_general(a, b, (((1,), (0,)), ((), ())), preferred_element_type=F32)


def slot_of(chosen, blocks_here, row, t):
    ctx_self = lax.axis_index("ctx")
    entry = chosen[row, t]
    owner = lax.div(entry, jnp.int32(blocks_here))
    apart = ctx_self - owner
    slot = jnp.where(apart == 0, entry - owner * blocks_here, blocks_here + apart - 1)
    return jnp.where(entry != ctx_self * blocks_here + row, slot, -1)


def pick_kernel(blocks_here, count, chips, far, piece, chosen, keys, values, asked, *refs):
    outs, sems = refs[:-1], refs[-1]
    ctx_self = lax.axis_index("ctx")
    place = lax.axis_index("head")
    core, chip = lax.rem(place, 2), lax.div(place, 2)
    first = ctx_self * blocks_here
    span = pl.ds(pl.multiple_of(chip * piece, piece), piece)

    def copy(source, s, slot):
        rows = source.at[slot, span, :] if s in far else source.at[slot]
        return pltpu.make_async_copy(rows, outs[s], sems.at[s])

    for s in range(count - 1):
        peer = ctx_self + s + 1
        near = jnp.minimum(peer, count - 1)
        found = jnp.int32(0)
        for row in range(blocks_here):
            for t in range(3):
                entry = chosen[near, row * 3 + t]
                hit = (entry >= first) & (entry < first + blocks_here)
                found = jnp.where(hit, entry - first + 1, found)
        found = jnp.where(peer < count, found, 0)
        asked[s] = found
        slot = jnp.maximum(found - 1, 0)

        @pl.when(core == 0)
        def _():
            copy(keys, s, slot).start()

        @pl.when(core != 0)
        def _():
            copy(values, s, slot).start()

    for s in range(count - 1):
        copy(keys, s, 0).wait()


def chip_sum_kernel(chips, piece, far, near, mine, theirs, *outs):
    chip = lax.div(lax.axis_index("head"), 2)
    for d in range(chips):
        target = lax.rem(chip + d, chips)
        span = pl.ds(pl.multiple_of(target * piece, piece), piece)
        for i, s in enumerate(far):
            total = mine[s, span, :].astype(F32) + theirs[s, span, :].astype(F32)
            outs[d][i] = total.astype(outs[d].dtype)
    for i, s in enumerate(near):
        outs[chips + i][...] = (mine[s].astype(F32) + theirs[s].astype(F32)).astype(BF16)


def own_sum_kernel(chips, piece, near, asked, mine, theirs, *refs):
    back, outs, acc = refs[: len(near)], refs[len(near) : -1], refs[-1]
    chip = lax.div(lax.axis_index("head"), 2)
    acc[...] = mine[...].astype(F32) + theirs[...].astype(F32)
    for i, s in enumerate(near):
        slot = asked[s] - 1

        @pl.when(slot >= 0)
        def _():
            acc[slot] += back[i][...].astype(F32)

    for d in range(chips):
        target = lax.rem(chip + d, chips)
        span = pl.ds(pl.multiple_of(target * piece, piece), piece)
        outs[d][...] = acc[:, span, :].astype(outs[d].dtype)


def head_sum_kernel(count, mine, *refs):
    parts, outs = refs[: len(refs) - count], refs[len(refs) - count :]
    for i in range(count):
        total = mine[i]
        for part in parts:
            total = total + part[i].astype(F32)
        outs[i][...] = total.astype(BF16)


def fold(array, reduce):
    rows, lanes = array.shape
    return reduce(array.reshape(rows // 8, 8, lanes), axis=0)


def causal(array, first_col, first_pos, other):
    col = lax.broadcasted_iota(jnp.int32, array.shape, 0) + first_col
    pos = lax.broadcasted_iota(jnp.int32, array.shape, 1) + first_pos
    return jnp.where(col <= pos, array, other)


def row_sums(s_ref, dp_ref, factor):
    block_len = s_ref.shape[0]
    step = min(64, block_len)
    spans = [pl.ds(c, step) for c in range(0, block_len, step)]
    top = fold(s_ref[spans[0], :], jnp.max)
    for span in spans[1:]:
        top = jnp.maximum(top, fold(s_ref[span, :], jnp.max))
    top = jnp.max(top, axis=0, keepdims=True) * factor
    total = weighted = jnp.zeros((8, block_len), F32)
    for span in spans:
        terms = jnp.exp2(s_ref[span, :] * factor - top)
        total = total + fold(terms, jnp.sum)
        weighted = weighted + fold(terms * dp_ref[span, :], jnp.sum)
    total = jnp.sum(total, axis=0, keepdims=True)
    return top, total, jnp.sum(weighted, axis=0, keepdims=True)


def local_stats_kernel(factor, blocks_here, chosen, q, do, keys, values, stats, s_buf, dp_buf):
    block_len = keys.shape[1]
    half = block_len // 2

    def per_row(row, _):
        start = row * block_len
        span = pl.ds(start, block_len)
        late = pl.ds(start + half, half)

        s_buf[:half, :] = causal(dot_nt(keys[row, :half], q[span, :]), 0, 0, -jnp.inf)
        s_buf[half:, :half] = jnp.full((half, half), -jnp.inf, F32)
        s_buf[half:, half:] = causal(dot_nt(keys[row, half:], q[late, :]), 0, 0, -jnp.inf)
        dp_buf[:half, :] = dot_nt(values[row, :half], do[span, :])
        dp_buf[half:, :half] = jnp.zeros((half, half), F32)
        dp_buf[half:, half:] = dot_nt(values[row, half:], do[late, :])
        top, total, weighted = row_sums(s_buf, dp_buf, factor)
        stats[row, 0:1, :] = top
        stats[row, 1:2, :] = total
        stats[row, 2:3, :] = weighted
        for t in range(3):
            slot = slot_of(chosen, blocks_here, row, t)

            @pl.when((slot >= 0) & (slot < blocks_here))
            def _():
                s_buf[...] = dot_nt(keys[slot], q[span, :])
                dp_buf[...] = dot_nt(values[slot], do[span, :])
                more_top, more, more_weighted = row_sums(s_buf, dp_buf, factor)
                old = stats[row, 0:1, :]
                top = jnp.maximum(old, more_top)
                scale_old = jnp.exp2(old - top)
                scale_new = jnp.exp2(more_top - top)
                stats[row, 0:1, :] = top
                stats[row, 1:2, :] = stats[row, 1:2, :] * scale_old + more * scale_new
                stats[row, 2:3, :] = stats[row, 2:3, :] * scale_old + more_weighted * scale_new

        return 0

    lax.fori_loop(0, blocks_here, per_row, 0)


def remote_kernel(
    factor, scaling, blocks_here, chips, far, near, piece, chosen, q, do, stats, *refs
):
    near_refs, far_refs, refs = refs[:2], refs[2 : 2 + 2 * chips], refs[2 + 2 * chips :]
    keep, send, final, grad_qt, rows, acc, s_buf, dp_buf, parts = refs
    place = lax.axis_index("head")
    core, chip = lax.rem(place, 2), lax.div(place, 2)
    block_len = rows.shape[2]
    half = block_len // 2

    def lay(kind, which):
        for i, s in enumerate(near):
            rows[kind, s] = near_refs[which][i]
        for d in range(chips):
            source = lax.rem(chip + chips - d, chips)
            span = pl.ds(pl.multiple_of(source * piece, piece), piece)
            for i, s in enumerate(far):
                rows[kind, s, span, :] = far_refs[2 * d + which][i]

    @pl.when(core == 0)
    def _():
        lay(0, 0)
        lay(1, 1)

    @pl.when(core != 0)
    def _():
        lay(0, 1)
        lay(1, 0)

    acc[...] = jnp.zeros_like(acc)

    def per_row(row, _):
        span = pl.ds(row * block_len, block_len)
        parts[0, 0:3, :] = stats[row, 0:3, :]
        for t in range(3):
            slot = slot_of(chosen, blocks_here, row, t) - blocks_here

            @pl.when(slot >= 0)
            def _():
                s_buf[t] = dot_nt(rows[0, slot], q[span, :])
                dp_buf[t] = dot_nt(rows[1, slot], do[span, :])
                top, total, weighted = row_sums(s_buf.at[t], dp_buf.at[t], factor)
                parts[t + 1, 0:1, :] = top
                parts[t + 1, 1:2, :] = total
                parts[t + 1, 2:3, :] = weighted

            @pl.when(slot < 0)
            def _():
                parts[t + 1, 0:1, :] = jnp.full((1, block_len), -jnp.inf, F32)
                parts[t + 1, 1:3, :] = jnp.zeros((2, block_len), F32)

        top = parts[0, 0:1, :]
        for t in range(3):
            top = jnp.maximum(top, parts[t + 1, 0:1, :])
        total = jnp.zeros_like(top)
        weighted = jnp.zeros_like(top)
        for t in range(4):
            scale = jnp.exp2(parts[t, 0:1, :] - top)
            total = total + scale * parts[t, 1:2, :]
            weighted = weighted + scale * parts[t, 2:3, :]
        final[row, 0:1, :] = top + jnp.log2(total)
        final[row, 1:2, :] = weighted / total
        grad_qt[row] = jnp.zeros_like(grad_qt[row])
        for t in range(3):
            slot = slot_of(chosen, blocks_here, row, t) - blocks_here

            @pl.when(slot >= 0)
            def _():
                level = final[row, 0:1, :]
                delta = final[row, 1:2, :]
                for c in (0, half):
                    cut = pl.ds(c, half)
                    weights = jnp.exp2(s_buf[t, cut, :] * factor - level)
                    dscores = (weights * (dp_buf[t, cut, :] - delta)).astype(BF16)
                    acc[1, slot, cut, :] += dot_nn(weights.astype(BF16), do[span, :])
                    acc[0, slot, cut, :] += dot_nn(dscores, q[span, :])
                    grad_qt[row] += dot_nn(rows[0, slot, cut, :].T, dscores)

        return 0

    lax.fori_loop(0, blocks_here, per_row, 0)
    keep_scale = jnp.where(core == 0, scaling, 1.0)
    send_scale = jnp.where(core == 0, 1.0, scaling)
    keep[...] = (acc[core] * keep_scale).astype(BF16)
    send[...] = (acc[1 - core] * send_scale).astype(BF16)


def local_kernel(
    factor, scaling, blocks_here, chosen, q, do, keys, values, final, grad_qt,
    keep, send, grad_q,
    acc, total_qt,
):
    core = lax.rem(lax.axis_index("head"), 2)
    block_len = keys.shape[1]
    half = block_len // 2
    acc[...] = jnp.zeros_like(acc)

    def per_row(row, _):
        start = row * block_len
        span = pl.ds(start, block_len)

        def part(slot, c, first, masked):
            cut = pl.ds(c, half)
            q_rows = q[pl.ds(start + first, block_len - first), :]
            do_rows = do[pl.ds(start + first, block_len - first), :]
            key_rows = keys[slot, cut, :]
            scores = dot_nt(key_rows, q_rows)
            dprobs = dot_nt(values[slot, cut, :], do_rows)
            weights = jnp.exp2(scores * factor - final[row, 0:1, first:])
            if masked:
                weights = causal(weights, c, first, 0.0)
            dscores = (weights * (dprobs - final[row, 1:2, first:])).astype(BF16)
            acc[1, slot, cut, :] += dot_nn(weights.astype(BF16), do_rows)
            acc[0, slot, cut, :] += dot_nn(dscores, q_rows)
            total_qt[:, first:] += dot_nn(key_rows.T, dscores)

        total_qt[...] = grad_qt[row]
        part(row, 0, 0, True)
        part(row, half, half, True)
        for t in range(3):
            slot = slot_of(chosen, blocks_here, row, t)

            @pl.when((slot >= 0) & (slot < blocks_here))
            def _():
                part(slot, 0, 0, False)
                part(slot, half, 0, False)

        grad_q[span, :] = (total_qt[...].T * scaling).astype(BF16)
        return 0

    lax.fori_loop(0, blocks_here, per_row, 0)
    keep_scale = jnp.where(core == 0, scaling, 1.0)
    send_scale = jnp.where(core == 0, 1.0, scaling)
    keep[...] = (acc[core] * keep_scale).astype(BF16)
    send[...] = (acc[1 - core] * send_scale).astype(BF16)


def owner_kernel(chips, far, asked, mine, *refs):
    others, back, (out, acc) = refs[: chips - 1], refs[chips - 1 : -2], refs[-2:]
    total = mine[...]
    for part in others:
        total = total + part[...].astype(F32)
    acc[...] = total
    for i, s in enumerate(far):
        slot = asked[s] - 1

        @pl.when(slot >= 0)
        def _():
            acc[slot] += back[i][...].astype(F32)

    out[...] = acc[...].astype(BF16)


def spread_kernel(chips, piece, *refs):
    pieces, (grad_k, grad_v) = refs[: 2 * chips], refs[2 * chips :]
    place = lax.axis_index("head")
    core, chip = lax.rem(place, 2), lax.div(place, 2)

    def lay(out, which):
        for d in range(chips):
            source = lax.rem(chip + chips - d, chips)
            span = pl.ds(pl.multiple_of(source * piece, piece), piece)
            out[:, span, :] = pieces[2 * d + which][...]

    @pl.when(core == 0)
    def _():
        lay(grad_k, 0)
        lay(grad_v, 1)

    @pl.when(core != 0)
    def _():
        lay(grad_k, 1)
        lay(grad_v, 0)


def params(size):
    return pltpu.CompilerParams(vmem_limit_bytes=min(size + 12 * 1024 * 1024, VMEM_LIMIT))


def body(queries, keys, values, dout, selected):
    tok_rows, head_count, feature = queries.shape
    blocks_here = selected.shape[0]
    block_len = tok_rows // blocks_here
    ctx_count = lax.axis_size("ctx")
    heads = lax.axis_size("head")
    chips = heads // 2
    piece = block_len // chips
    scaling = 1.0 / math.sqrt(feature)
    factor = scaling * math.log2(math.e)
    shifts = ctx_count - 1
    far = [s for s in range(shifts) if 2 * (s + 1) >= ctx_count]
    near = [s for s in range(shifts) if 2 * (s + 1) < ctx_count]

    q2 = queries.reshape(tok_rows, feature)
    do2 = dout.reshape(tok_rows, feature)
    key_blocks = keys.reshape(blocks_here, block_len, feature)
    value_blocks = values.reshape(blocks_here, block_len, feature)
    remote_shape = (shifts, block_len, feature)
    local_shape = (blocks_here, block_len, feature)

    smem = pl.BlockSpec(memory_space=pltpu.SMEM)
    whole = pl.BlockSpec(memory_space=pltpu.VMEM)
    hbm = pl.BlockSpec(memory_space=pltpu.HBM)
    stat_type = jax.ShapeDtypeStruct((blocks_here, 8, block_len), F32)
    far_type = jax.ShapeDtypeStruct(remote_shape, BF16)
    own_type = jax.ShapeDtypeStruct(local_shape, BF16)
    block_type = jax.ShapeDtypeStruct((block_len, feature), BF16)
    piece_type = jax.ShapeDtypeStruct((piece, feature), BF16)
    qt_type = jax.ShapeDtypeStruct((blocks_here, feature, block_len), F32)
    pair_flops = 2 * block_len * block_len * feature
    block_bytes = block_len * feature * 2
    pair_bytes = block_len * block_len * 4

    def pieces_type(count, dtype):
        return jax.ShapeDtypeStruct((count, piece, feature), dtype)

    def cost(matmuls, size):
        return pl.CostEstimate(
            flops=matmuls * pair_flops, bytes_accessed=size, transcendentals=matmuls * block_len**2
        )

    def swap(array):
        return lax.ppermute(array, "head", [(h, h ^ 1) for h in range(heads)])

    def to_chip(array, d):
        return lax.ppermute(array, "head", [(h, (h + 2 * d) % heads) for h in range(heads)])

    def to_owner(array, s):
        return lax.ppermute(array, "ctx", [(c, c - s - 1) for c in range(s + 1, ctx_count)])

    def to_reader(array, s):
        return lax.ppermute(array, "ctx", [(c - s - 1, c) for c in range(s + 1, ctx_count)])

    everyone = lax.all_to_all(
        jnp.broadcast_to(selected.reshape(1, 3 * blocks_here), (ctx_count, 3 * blocks_here)),
        "ctx", split_axis=0, concat_axis=0, tiled=True,
    )
    asked, *sent = pl.pallas_call(
        functools.partial(pick_kernel, blocks_here, ctx_count, chips, far, piece),
        in_specs=[smem, hbm, hbm],
        out_specs=[smem] + [whole] * shifts,
        out_shape=[jax.ShapeDtypeStruct((shifts,), jnp.int32)]
        + [piece_type if s in far else block_type for s in range(shifts)],
        scratch_shapes=[pltpu.SemaphoreType.DMA((shifts,))],
        name="pick_rows",
    )(everyone, key_blocks, value_blocks)

    far_mine = jnp.stack([to_reader(sent[s], s) for s in far])
    near_parts = [to_reader(sent[s], s) for s in near]
    far_mine, chosen = lax.optimization_barrier((far_mine, selected))
    far_more = [to_chip(far_mine, d) for d in range(1, chips)]
    stats = pl.pallas_call(
        functools.partial(local_stats_kernel, factor, blocks_here),
        in_specs=[smem] + [whole] * 4,
        out_specs=whole,
        out_shape=stat_type,
        scratch_shapes=[pltpu.VMEM((block_len, block_len), F32)] * 2,
        compiler_params=params(4 * blocks_here * block_bytes + 2 * pair_bytes),
        cost_estimate=cost(30, 4 * tok_rows * feature * 2),
        name="local_stats",
    )(chosen, q2, do2, key_blocks, value_blocks)
    near_parts, far_held, stats = lax.optimization_barrier((near_parts, far_mine, stats))
    near_mine = jnp.stack(near_parts)
    row_sets = [near_mine, swap(near_mine), far_held, swap(far_held)]
    for part in far_more:
        row_sets += [part, swap(part)]

    keep_far, send_far, final, grad_qt = pl.pallas_call(
        functools.partial(remote_kernel, factor, scaling, blocks_here, chips, far, near, piece),
        in_specs=[smem] + [whole] * (3 + len(row_sets)),
        out_specs=[whole] * 4,
        out_shape=[far_type, far_type, stat_type, qt_type],
        scratch_shapes=[
            pltpu.VMEM((2,) + remote_shape, BF16),
            pltpu.VMEM((2,) + remote_shape, F32),
            pltpu.VMEM((3, block_len, block_len), F32),
            pltpu.VMEM((3, block_len, block_len), F32),
            pltpu.VMEM((4, 8, block_len), F32),
        ],
        compiler_params=params((10 * shifts + 4 * blocks_here) * block_bytes + 6 * pair_bytes),
        cost_estimate=cost(60, 8 * tok_rows * feature * 2),
        name="remote_pairs",
    )(chosen, q2, do2, stats, *row_sets)

    def head_sums(mine, parts, count):
        return pl.pallas_call(
            functools.partial(head_sum_kernel, count),
            in_specs=[whole] * (1 + len(parts)),
            out_specs=[whole] * count,
            out_shape=[piece_type] * count,
            compiler_params=params(4 * count * block_bytes),
            name="head_sum",
        )(mine, *parts)

    chip_far = pl.pallas_call(
        functools.partial(chip_sum_kernel, chips, piece, far, near),
        in_specs=[whole, whole],
        out_specs=[whole] * (chips + len(near)),
        out_shape=[pieces_type(len(far), F32)]
        + [pieces_type(len(far), BF16)] * (chips - 1)
        + [block_type] * len(near),
        compiler_params=params(4 * shifts * block_bytes),
        name="chip_sum",
    )(keep_far, swap(send_far))
    chip_far, final = lax.optimization_barrier((chip_far, final))
    far_sums, near_sums = chip_far[:chips], chip_far[chips:]
    far_parts = [to_chip(far_sums[d], d) for d in range(1, chips)]
    near_back = [to_owner(near_sums[i], s) for i, s in enumerate(near)]
    keep_own, send_own, grad_q = pl.pallas_call(
        functools.partial(local_kernel, factor, scaling, blocks_here),
        in_specs=[smem] + [whole] * 6,
        out_specs=[whole] * 3,
        out_shape=[own_type, own_type, jax.ShapeDtypeStruct((tok_rows, feature), BF16)],
        scratch_shapes=[
            pltpu.VMEM((2,) + local_shape, F32),
            pltpu.VMEM((feature, block_len), F32),
        ],
        compiler_params=params(14 * blocks_here * block_bytes),
        cost_estimate=cost(60, 8 * tok_rows * feature * 2),
        name="local_pairs",
    )(chosen, q2, do2, key_blocks, value_blocks, final, grad_qt)
    far_parts, near_back, keep_own, send_own = lax.optimization_barrier(
        (far_parts, near_back, keep_own, send_own)
    )
    own_sums = pl.pallas_call(
        functools.partial(own_sum_kernel, chips, piece, near),
        in_specs=[smem] + [whole] * (2 + len(near)),
        out_specs=[whole] * chips,
        out_shape=[pieces_type(blocks_here, F32)]
        + [pieces_type(blocks_here, BF16)] * (chips - 1),
        scratch_shapes=[pltpu.VMEM(local_shape, F32)],
        compiler_params=params((8 * blocks_here + len(near)) * block_bytes),
        name="own_sum",
    )(asked, keep_own, swap(send_own), *near_back)
    own_parts = [to_chip(own_sums[d], d) for d in range(1, chips)]
    far_out = head_sums(far_sums[0], far_parts, len(far))
    far_back = [to_owner(far_out[i], s) for i, s in enumerate(far)]
    mine = pl.pallas_call(
        functools.partial(owner_kernel, chips, far),
        in_specs=[smem] + [whole] * (chips + len(far)),
        out_specs=whole,
        out_shape=pieces_type(blocks_here, BF16),
        scratch_shapes=[pltpu.VMEM((blocks_here, piece, feature), F32)],
        compiler_params=params((5 * blocks_here + shifts) * block_bytes),
        name="owner_sum",
    )(asked, own_sums[0], *own_parts, *far_back)
    spread = [mine, swap(mine)]
    for d in range(1, chips):
        part = to_chip(mine, d)
        spread += [part, swap(part)]
    grad_keys, grad_values = pl.pallas_call(
        functools.partial(spread_kernel, chips, piece),
        in_specs=[whole] * len(spread),
        out_specs=[whole] * 2,
        out_shape=[own_type] * 2,
        compiler_params=params(4 * blocks_here * block_bytes),
        name="spread",
    )(*spread)
    return (
        grad_q.reshape(tok_rows, head_count, feature),
        grad_keys.reshape(tok_rows, feature),
        grad_values.reshape(tok_rows, feature),
    )


def solution(mesh):
    return jax.shard_map(
        body,
        mesh=mesh,
        in_specs=(
            P("ctx", "head", None),
            P("ctx", None),
            P("ctx", None),
            P("ctx", "head", None),
            P("ctx", None),
        ),
        out_specs=(P("ctx", "head", None), P("ctx", None), P("ctx", None)),
        check_vma=False,
    )
```

```python
import functools
import math

import jax
import jax.numpy as jnp
from jax import lax
from jax.experimental import pallas as pl
from jax.experimental.pallas import tpu as pltpu
from jax.sharding import PartitionSpec as P

F32 = jnp.float32
BF16 = jnp.bfloat16
VMEM_LIMIT = 56 * 1024 * 1024


def dot_nt(a, b):
    return lax.dot_general(a, b, (((1,), (1,)), ((), ())), preferred_element_type=F32)


def dot_nn(a, b):
    return lax.dot_general(a, b, (((1,), (0,)), ((), ())), preferred_element_type=F32)


def slot_of(chosen, blocks_here, row, t):
    ctx_self = lax.axis_index("ctx")
    entry = chosen[row, t]
    owner = lax.div(entry, jnp.int32(blocks_here))
    apart = ctx_self - owner
    slot = jnp.where(apart == 0, entry - owner * blocks_here, blocks_here + apart - 1)
    return jnp.where(entry != ctx_self * blocks_here + row, slot, -1)


def pick_kernel(blocks_here, count, chips, far, piece, chosen, keys, values, asked, *refs):
    outs, sems = refs[:-1], refs[-1]
    ctx_self = lax.axis_index("ctx")
    place = lax.axis_index("head")
    core, chip = lax.rem(place, 2), lax.div(place, 2)
    first = ctx_self * blocks_here
    span = pl.ds(pl.multiple_of(chip * piece, piece), piece)

    def copy(source, s, slot):
        rows = source.at[slot, span, :] if s in far else source.at[slot]
        return pltpu.make_async_copy(rows, outs[s], sems.at[s])

    for s in range(count - 1):
        peer = ctx_self + s + 1
        near = jnp.minimum(peer, count - 1)
        found = jnp.int32(0)
        for row in range(blocks_here):
            for t in range(3):
                entry = chosen[near, row * 3 + t]
                hit = (entry >= first) & (entry < first + blocks_here)
                found = jnp.where(hit, entry - first + 1, found)
        found = jnp.where(peer < count, found, 0)
        asked[s] = found
        slot = jnp.maximum(found - 1, 0)

        @pl.when(core == 0)
        def _():
            copy(keys, s, slot).start()

        @pl.when(core != 0)
        def _():
            copy(values, s, slot).start()

    for s in range(count - 1):
        copy(keys, s, 0).wait()


def chip_sum_kernel(chips, piece, far, near, mine, theirs, *outs):
    chip = lax.div(lax.axis_index("head"), 2)
    for d in range(chips):
        target = lax.rem(chip + d, chips)
        span = pl.ds(pl.multiple_of(target * piece, piece), piece)
        for i, s in enumerate(far):
            total = mine[s, span, :].astype(F32) + theirs[s, span, :].astype(F32)
            outs[d][i] = total.astype(outs[d].dtype)
    for i, s in enumerate(near):
        outs[chips + i][...] = (mine[s].astype(F32) + theirs[s].astype(F32)).astype(BF16)


def own_sum_kernel(chips, piece, near, asked, mine, theirs, *refs):
    back, outs, acc = refs[: len(near)], refs[len(near) : -1], refs[-1]
    chip = lax.div(lax.axis_index("head"), 2)
    acc[...] = mine[...].astype(F32) + theirs[...].astype(F32)
    for i, s in enumerate(near):
        slot = asked[s] - 1

        @pl.when(slot >= 0)
        def _():
            acc[slot] += back[i][...].astype(F32)

    for d in range(chips):
        target = lax.rem(chip + d, chips)
        span = pl.ds(pl.multiple_of(target * piece, piece), piece)
        outs[d][...] = acc[:, span, :].astype(outs[d].dtype)


def head_sum_kernel(count, mine, *refs):
    parts, outs = refs[: len(refs) - count], refs[len(refs) - count :]
    for i in range(count):
        total = mine[i]
        for part in parts:
            total = total + part[i].astype(F32)
        outs[i][...] = total.astype(BF16)


def fold(array, reduce):
    rows, lanes = array.shape
    return reduce(array.reshape(rows // 8, 8, lanes), axis=0)


def causal(array, first_col, first_pos, other):
    col = lax.broadcasted_iota(jnp.int32, array.shape, 0) + first_col
    pos = lax.broadcasted_iota(jnp.int32, array.shape, 1) + first_pos
    return jnp.where(col <= pos, array, other)


def row_sums(s_ref, dp_ref, factor):
    block_len = s_ref.shape[0]
    step = min(64, block_len)
    spans = [pl.ds(c, step) for c in range(0, block_len, step)]
    top = fold(s_ref[spans[0], :], jnp.max)
    for span in spans[1:]:
        top = jnp.maximum(top, fold(s_ref[span, :], jnp.max))
    top = jnp.max(top, axis=0, keepdims=True) * factor
    total = weighted = jnp.zeros((8, block_len), F32)
    for span in spans:
        terms = jnp.exp2(s_ref[span, :] * factor - top)
        total = total + fold(terms, jnp.sum)
        weighted = weighted + fold(terms * dp_ref[span, :], jnp.sum)
    total = jnp.sum(total, axis=0, keepdims=True)
    return top, total, jnp.sum(weighted, axis=0, keepdims=True)


def local_stats_kernel(factor, blocks_here, chosen, q, do, keys, values, stats, s_buf, dp_buf):
    block_len = keys.shape[1]
    half = block_len // 2

    def per_row(row, _):
        start = row * block_len
        span = pl.ds(start, block_len)
        late = pl.ds(start + half, half)

        s_buf[:half, :] = causal(dot_nt(keys[row, :half], q[span, :]), 0, 0, -jnp.inf)
        s_buf[half:, :half] = jnp.full((half, half), -jnp.inf, F32)
        s_buf[half:, half:] = causal(dot_nt(keys[row, half:], q[late, :]), 0, 0, -jnp.inf)
        dp_buf[:half, :] = dot_nt(values[row, :half], do[span, :])
        dp_buf[half:, :half] = jnp.zeros((half, half), F32)
        dp_buf[half:, half:] = dot_nt(values[row, half:], do[late, :])
        top, total, weighted = row_sums(s_buf, dp_buf, factor)
        stats[row, 0:1, :] = top
        stats[row, 1:2, :] = total
        stats[row, 2:3, :] = weighted
        for t in range(3):
            slot = slot_of(chosen, blocks_here, row, t)

            @pl.when((slot >= 0) & (slot < blocks_here))
            def _():
                s_buf[...] = dot_nt(keys[slot], q[span, :])
                dp_buf[...] = dot_nt(values[slot], do[span, :])
                more_top, more, more_weighted = row_sums(s_buf, dp_buf, factor)
                old = stats[row, 0:1, :]
                top = jnp.maximum(old, more_top)
                scale_old = jnp.exp2(old - top)
                scale_new = jnp.exp2(more_top - top)
                stats[row, 0:1, :] = top
                stats[row, 1:2, :] = stats[row, 1:2, :] * scale_old + more * scale_new
                stats[row, 2:3, :] = stats[row, 2:3, :] * scale_old + more_weighted * scale_new

        return 0

    lax.fori_loop(0, blocks_here, per_row, 0)


def remote_kernel(
    factor, scaling, blocks_here, chips, far, near, piece, chosen, q, do, stats, *refs
):
    near_refs, far_refs, refs = refs[:2], refs[2 : 2 + 2 * chips], refs[2 + 2 * chips :]
    keep, send, final, grad_qt, rows, acc, s_buf, dp_buf, parts = refs
    place = lax.axis_index("head")
    core, chip = lax.rem(place, 2), lax.div(place, 2)
    block_len = rows.shape[2]
    half = block_len // 2

    def lay(kind, which):
        for i, s in enumerate(near):
            rows[kind, s] = near_refs[which][i]
        for d in range(chips):
            source = lax.rem(chip + chips - d, chips)
            span = pl.ds(pl.multiple_of(source * piece, piece), piece)
            for i, s in enumerate(far):
                rows[kind, s, span, :] = far_refs[2 * d + which][i]

    @pl.when(core == 0)
    def _():
        lay(0, 0)
        lay(1, 1)

    @pl.when(core != 0)
    def _():
        lay(0, 1)
        lay(1, 0)

    acc[...] = jnp.zeros_like(acc)

    def per_row(row, _):
        span = pl.ds(row * block_len, block_len)
        parts[0, 0:3, :] = stats[row, 0:3, :]
        for t in range(3):
            slot = slot_of(chosen, blocks_here, row, t) - blocks_here

            @pl.when(slot >= 0)
            def _():
                s_buf[t] = dot_nt(rows[0, slot], q[span, :])
                dp_buf[t] = dot_nt(rows[1, slot], do[span, :])
                top, total, weighted = row_sums(s_buf.at[t], dp_buf.at[t], factor)
                parts[t + 1, 0:1, :] = top
                parts[t + 1, 1:2, :] = total
                parts[t + 1, 2:3, :] = weighted

            @pl.when(slot < 0)
            def _():
                parts[t + 1, 0:1, :] = jnp.full((1, block_len), -jnp.inf, F32)
                parts[t + 1, 1:3, :] = jnp.zeros((2, block_len), F32)

        top = parts[0, 0:1, :]
        for t in range(3):
            top = jnp.maximum(top, parts[t + 1, 0:1, :])
        total = jnp.zeros_like(top)
        weighted = jnp.zeros_like(top)
        for t in range(4):
            scale = jnp.exp2(parts[t, 0:1, :] - top)
            total = total + scale * parts[t, 1:2, :]
            weighted = weighted + scale * parts[t, 2:3, :]
        final[row, 0:1, :] = top + jnp.log2(total)
        final[row, 1:2, :] = weighted / total
        grad_qt[row] = jnp.zeros_like(grad_qt[row])
        for t in range(3):
            slot = slot_of(chosen, blocks_here, row, t) - blocks_here

            @pl.when(slot >= 0)
            def _():
                level = final[row, 0:1, :]
                delta = final[row, 1:2, :]
                for c in (0, half):
                    cut = pl.ds(c, half)
                    weights = jnp.exp2(s_buf[t, cut, :] * factor - level)
                    dscores = (weights * (dp_buf[t, cut, :] - delta)).astype(BF16)
                    acc[1, slot, cut, :] += dot_nn(weights.astype(BF16), do[span, :])
                    acc[0, slot, cut, :] += dot_nn(dscores, q[span, :])
                    grad_qt[row] += dot_nn(rows[0, slot, cut, :].T, dscores)

        return 0

    lax.fori_loop(0, blocks_here, per_row, 0)
    keep_scale = jnp.where(core == 0, scaling, 1.0)
    send_scale = jnp.where(core == 0, 1.0, scaling)
    keep[...] = (acc[core] * keep_scale).astype(BF16)
    send[...] = (acc[1 - core] * send_scale).astype(BF16)


def local_kernel(
    factor, scaling, blocks_here, chosen, q, do, keys, values, final, grad_qt,
    keep, send, grad_q,
    acc, total_qt,
):
    core = lax.rem(lax.axis_index("head"), 2)
    block_len = keys.shape[1]
    half = block_len // 2
    acc[...] = jnp.zeros_like(acc)

    def per_row(row, _):
        start = row * block_len
        span = pl.ds(start, block_len)

        def part(slot, c, first, masked):
            cut = pl.ds(c, half)
            q_rows = q[pl.ds(start + first, block_len - first), :]
            do_rows = do[pl.ds(start + first, block_len - first), :]
            key_rows = keys[slot, cut, :]
            scores = dot_nt(key_rows, q_rows)
            dprobs = dot_nt(values[slot, cut, :], do_rows)
            weights = jnp.exp2(scores * factor - final[row, 0:1, first:])
            if masked:
                weights = causal(weights, c, first, 0.0)
            dscores = (weights * (dprobs - final[row, 1:2, first:])).astype(BF16)
            acc[1, slot, cut, :] += dot_nn(weights.astype(BF16), do_rows)
            acc[0, slot, cut, :] += dot_nn(dscores, q_rows)
            total_qt[:, first:] += dot_nn(key_rows.T, dscores)

        total_qt[...] = grad_qt[row]
        part(row, 0, 0, True)
        part(row, half, half, True)
        for t in range(3):
            slot = slot_of(chosen, blocks_here, row, t)

            @pl.when((slot >= 0) & (slot < blocks_here))
            def _():
                part(slot, 0, 0, False)
                part(slot, half, 0, False)

        grad_q[span, :] = (total_qt[...].T * scaling).astype(BF16)
        return 0

    lax.fori_loop(0, blocks_here, per_row, 0)
    keep_scale = jnp.where(core == 0, scaling, 1.0)
    send_scale = jnp.where(core == 0, 1.0, scaling)
    keep[...] = (acc[core] * keep_scale).astype(BF16)
    send[...] = (acc[1 - core] * send_scale).astype(BF16)


def owner_kernel(chips, far, asked, mine, *refs):
    others, back, (out, acc) = refs[: chips - 1], refs[chips - 1 : -2], refs[-2:]
    total = mine[...]
    for part in others:
        total = total + part[...].astype(F32)
    acc[...] = total
    for i, s in enumerate(far):
        slot = asked[s] - 1

        @pl.when(slot >= 0)
        def _():
            acc[slot] += back[i][...].astype(F32)

    out[...] = acc[...].astype(BF16)


def spread_kernel(chips, piece, *refs):
    pieces, (grad_k, grad_v) = refs[: 2 * chips], refs[2 * chips :]
    place = lax.axis_index("head")
    core, chip = lax.rem(place, 2), lax.div(place, 2)

    def lay(out, which):
        for d in range(chips):
            source = lax.rem(chip + chips - d, chips)
            span = pl.ds(pl.multiple_of(source * piece, piece), piece)
            out[:, span, :] = pieces[2 * d + which][...]

    @pl.when(core == 0)
    def _():
        lay(grad_k, 0)
        lay(grad_v, 1)

    @pl.when(core != 0)
    def _():
        lay(grad_k, 1)
        lay(grad_v, 0)


def params(size):
    return pltpu.CompilerParams(vmem_limit_bytes=min(size + 12 * 1024 * 1024, VMEM_LIMIT))


def body(queries, keys, values, dout, selected):
    tok_rows, head_count, feature = queries.shape
    blocks_here = selected.shape[0]
    block_len = tok_rows // blocks_here
    ctx_count = lax.axis_size("ctx")
    heads = lax.axis_size("head")
    chips = heads // 2
    piece = block_len // chips
    scaling = 1.0 / math.sqrt(feature)
    factor = scaling * math.log2(math.e)
    shifts = ctx_count - 1
    far = [s for s in range(shifts) if 2 * (s + 1) >= ctx_count]
    near = [s for s in range(shifts) if 2 * (s + 1) < ctx_count]

    q2 = queries.reshape(tok_rows, feature)
    do2 = dout.reshape(tok_rows, feature)
    key_blocks = keys.reshape(blocks_here, block_len, feature)
    value_blocks = values.reshape(blocks_here, block_len, feature)
    remote_shape = (shifts, block_len, feature)
    local_shape = (blocks_here, block_len, feature)

    smem = pl.BlockSpec(memory_space=pltpu.SMEM)
    whole = pl.BlockSpec(memory_space=pltpu.VMEM)
    hbm = pl.BlockSpec(memory_space=pltpu.HBM)
    stat_type = jax.ShapeDtypeStruct((blocks_here, 8, block_len), F32)
    far_type = jax.ShapeDtypeStruct(remote_shape, BF16)
    own_type = jax.ShapeDtypeStruct(local_shape, BF16)
    block_type = jax.ShapeDtypeStruct((block_len, feature), BF16)
    piece_type = jax.ShapeDtypeStruct((piece, feature), BF16)
    qt_type = jax.ShapeDtypeStruct((blocks_here, feature, block_len), F32)
    pair_flops = 2 * block_len * block_len * feature
    block_bytes = block_len * feature * 2
    pair_bytes = block_len * block_len * 4

    def pieces_type(count, dtype):
        return jax.ShapeDtypeStruct((count, piece, feature), dtype)

    def cost(matmuls, size):
        return pl.CostEstimate(
            flops=matmuls * pair_flops, bytes_accessed=size, transcendentals=matmuls * block_len**2
        )

    def swap(array):
        return lax.ppermute(array, "head", [(h, h ^ 1) for h in range(heads)])

    def to_chip(array, d):
        return lax.ppermute(array, "head", [(h, (h + 2 * d) % heads) for h in range(heads)])

    def to_owner(array, s):
        return lax.ppermute(array, "ctx", [(c, c - s - 1) for c in range(s + 1, ctx_count)])

    def to_reader(array, s):
        return lax.ppermute(array, "ctx", [(c - s - 1, c) for c in range(s + 1, ctx_count)])

    everyone = lax.all_to_all(
        jnp.broadcast_to(selected.reshape(1, 3 * blocks_here), (ctx_count, 3 * blocks_here)),
        "ctx", split_axis=0, concat_axis=0, tiled=True,
    )
    asked, *sent = pl.pallas_call(
        functools.partial(pick_kernel, blocks_here, ctx_count, chips, far, piece),
        in_specs=[smem, hbm, hbm],
        out_specs=[smem] + [whole] * shifts,
        out_shape=[jax.ShapeDtypeStruct((shifts,), jnp.int32)]
        + [piece_type if s in far else block_type for s in range(shifts)],
        scratch_shapes=[pltpu.SemaphoreType.DMA((shifts,))],
        name="pick_rows",
    )(everyone, key_blocks, value_blocks)

    far_mine = jnp.stack([to_reader(sent[s], s) for s in far])
    near_parts = [to_reader(sent[near[0]], near[0])]
    far_mine, chosen, *later = lax.optimization_barrier(
        (far_mine, selected, *[sent[s] for s in near[1:]])
    )
    far_more = [to_chip(far_mine, d) for d in range(1, chips)]
    near_parts += [to_reader(rows, s) for rows, s in zip(later, near[1:])]
    stats = pl.pallas_call(
        functools.partial(local_stats_kernel, factor, blocks_here),
        in_specs=[smem] + [whole] * 4,
        out_specs=whole,
        out_shape=stat_type,
        scratch_shapes=[pltpu.VMEM((block_len, block_len), F32)] * 2,
        compiler_params=params(4 * blocks_here * block_bytes + 2 * pair_bytes),
        cost_estimate=cost(30, 4 * tok_rows * feature * 2),
        name="local_stats",
    )(chosen, q2, do2, key_blocks, value_blocks)
    near_parts, far_held, stats = lax.optimization_barrier((near_parts, far_mine, stats))
    near_mine = jnp.stack(near_parts)
    row_sets = [near_mine, swap(near_mine), far_held, swap(far_held)]
    for part in far_more:
        row_sets += [part, swap(part)]

    keep_far, send_far, final, grad_qt = pl.pallas_call(
        functools.partial(remote_kernel, factor, scaling, blocks_here, chips, far, near, piece),
        in_specs=[smem] + [whole] * (3 + len(row_sets)),
        out_specs=[whole] * 4,
        out_shape=[far_type, far_type, stat_type, qt_type],
        scratch_shapes=[
            pltpu.VMEM((2,) + remote_shape, BF16),
            pltpu.VMEM((2,) + remote_shape, F32),
            pltpu.VMEM((3, block_len, block_len), F32),
            pltpu.VMEM((3, block_len, block_len), F32),
            pltpu.VMEM((4, 8, block_len), F32),
        ],
        compiler_params=params((10 * shifts + 4 * blocks_here) * block_bytes + 6 * pair_bytes),
        cost_estimate=cost(60, 8 * tok_rows * feature * 2),
        name="remote_pairs",
    )(chosen, q2, do2, stats, *row_sets)

    def head_sums(mine, parts, count):
        return pl.pallas_call(
            functools.partial(head_sum_kernel, count),
            in_specs=[whole] * (1 + len(parts)),
            out_specs=[whole] * count,
            out_shape=[piece_type] * count,
            compiler_params=params(4 * count * block_bytes),
            name="head_sum",
        )(mine, *parts)

    chip_far = pl.pallas_call(
        functools.partial(chip_sum_kernel, chips, piece, far, near),
        in_specs=[whole, whole],
        out_specs=[whole] * (chips + len(near)),
        out_shape=[pieces_type(len(far), F32)]
        + [pieces_type(len(far), BF16)] * (chips - 1)
        + [block_type] * len(near),
        compiler_params=params(4 * shifts * block_bytes),
        name="chip_sum",
    )(keep_far, swap(send_far))
    chip_far, final = lax.optimization_barrier((chip_far, final))
    far_sums, near_sums = chip_far[:chips], chip_far[chips:]
    far_parts = [to_chip(far_sums[d], d) for d in range(1, chips)]
    near_back = [to_owner(near_sums[i], s) for i, s in enumerate(near)]
    keep_own, send_own, grad_q = pl.pallas_call(
        functools.partial(local_kernel, factor, scaling, blocks_here),
        in_specs=[smem] + [whole] * 6,
        out_specs=[whole] * 3,
        out_shape=[own_type, own_type, jax.ShapeDtypeStruct((tok_rows, feature), BF16)],
        scratch_shapes=[
            pltpu.VMEM((2,) + local_shape, F32),
            pltpu.VMEM((feature, block_len), F32),
        ],
        compiler_params=params(14 * blocks_here * block_bytes),
        cost_estimate=cost(60, 8 * tok_rows * feature * 2),
        name="local_pairs",
    )(chosen, q2, do2, key_blocks, value_blocks, final, grad_qt)
    far_parts, near_back, keep_own, send_own = lax.optimization_barrier(
        (far_parts, near_back, keep_own, send_own)
    )
    own_sums = pl.pallas_call(
        functools.partial(own_sum_kernel, chips, piece, near),
        in_specs=[smem] + [whole] * (2 + len(near)),
        out_specs=[whole] * chips,
        out_shape=[pieces_type(blocks_here, F32)]
        + [pieces_type(blocks_here, BF16)] * (chips - 1),
        scratch_shapes=[pltpu.VMEM(local_shape, F32)],
        compiler_params=params((8 * blocks_here + len(near)) * block_bytes),
        name="own_sum",
    )(asked, keep_own, swap(send_own), *near_back)
    own_parts = [to_chip(own_sums[d], d) for d in range(1, chips)]
    far_out = head_sums(far_sums[0], far_parts, len(far))
    far_back = [to_owner(far_out[i], s) for i, s in enumerate(far)]
    mine = pl.pallas_call(
        functools.partial(owner_kernel, chips, far),
        in_specs=[smem] + [whole] * (chips + len(far)),
        out_specs=whole,
        out_shape=pieces_type(blocks_here, BF16),
        scratch_shapes=[pltpu.VMEM((blocks_here, piece, feature), F32)],
        compiler_params=params((5 * blocks_here + shifts) * block_bytes),
        name="owner_sum",
    )(asked, own_sums[0], *own_parts, *far_back)
    spread = [mine, swap(mine)]
    for d in range(1, chips):
        part = to_chip(mine, d)
        spread += [part, swap(part)]
    grad_keys, grad_values = pl.pallas_call(
        functools.partial(spread_kernel, chips, piece),
        in_specs=[whole] * len(spread),
        out_specs=[whole] * 2,
        out_shape=[own_type] * 2,
        compiler_params=params(4 * blocks_here * block_bytes),
        name="spread",
    )(*spread)
    return (
        grad_q.reshape(tok_rows, head_count, feature),
        grad_keys.reshape(tok_rows, feature),
        grad_values.reshape(tok_rows, feature),
    )


def solution(mesh):
    return jax.shard_map(
        body,
        mesh=mesh,
        in_specs=(
            P("ctx", "head", None),
            P("ctx", None),
            P("ctx", None),
            P("ctx", "head", None),
            P("ctx", None),
        ),
        out_specs=(P("ctx", "head", None), P("ctx", None), P("ctx", None)),
        check_vma=False,
    )
```

```python
import functools
import math

import jax
import jax.numpy as jnp
from jax import lax
from jax.experimental import pallas as pl
from jax.experimental.pallas import tpu as pltpu
from jax.sharding import PartitionSpec as P

F32 = jnp.float32
BF16 = jnp.bfloat16
VMEM_LIMIT = 56 * 1024 * 1024


def dot_nt(a, b):
    return lax.dot_general(a, b, (((1,), (1,)), ((), ())), preferred_element_type=F32)


def dot_nn(a, b):
    return lax.dot_general(a, b, (((1,), (0,)), ((), ())), preferred_element_type=F32)


def slot_of(chosen, blocks_here, row, t):
    ctx_self = lax.axis_index("ctx")
    entry = chosen[row, t]
    owner = lax.div(entry, jnp.int32(blocks_here))
    apart = ctx_self - owner
    slot = jnp.where(apart == 0, entry - owner * blocks_here, blocks_here + apart - 1)
    return jnp.where(entry != ctx_self * blocks_here + row, slot, -1)


def pick_kernel(blocks_here, count, chips, far, piece, chosen, keys, values, asked, *refs):
    outs, sems = refs[:-1], refs[-1]
    ctx_self = lax.axis_index("ctx")
    place = lax.axis_index("head")
    core, chip = lax.rem(place, 2), lax.div(place, 2)
    first = ctx_self * blocks_here
    span = pl.ds(pl.multiple_of(chip * piece, piece), piece)

    def copy(source, s, slot):
        rows = source.at[slot, span, :] if s in far else source.at[slot]
        return pltpu.make_async_copy(rows, outs[s], sems.at[s])

    for s in range(count - 1):
        peer = ctx_self + s + 1
        near = jnp.minimum(peer, count - 1)
        found = jnp.int32(0)
        for row in range(blocks_here):
            for t in range(3):
                entry = chosen[near, row * 3 + t]
                hit = (entry >= first) & (entry < first + blocks_here)
                found = jnp.where(hit, entry - first + 1, found)
        found = jnp.where(peer < count, found, 0)
        asked[s] = found
        slot = jnp.maximum(found - 1, 0)

        @pl.when(core == 0)
        def _():
            copy(keys, s, slot).start()

        @pl.when(core != 0)
        def _():
            copy(values, s, slot).start()

    for s in range(count - 1):
        copy(keys, s, 0).wait()


def chip_sum_kernel(chips, piece, far, near, mine, theirs, *outs):
    chip = lax.div(lax.axis_index("head"), 2)
    for d in range(chips):
        target = lax.rem(chip + d, chips)
        span = pl.ds(pl.multiple_of(target * piece, piece), piece)
        for i, s in enumerate(far):
            total = mine[s, span, :].astype(F32) + theirs[s, span, :].astype(F32)
            outs[d][i] = total.astype(outs[d].dtype)
    for i, s in enumerate(near):
        outs[chips + i][...] = (mine[s].astype(F32) + theirs[s].astype(F32)).astype(BF16)


def own_sum_kernel(chips, piece, near, asked, mine, theirs, *refs):
    back, outs, acc = refs[: len(near)], refs[len(near) : -1], refs[-1]
    chip = lax.div(lax.axis_index("head"), 2)
    acc[...] = mine[...].astype(F32) + theirs[...].astype(F32)
    for i, s in enumerate(near):
        slot = asked[s] - 1

        @pl.when(slot >= 0)
        def _():
            acc[slot] += back[i][...].astype(F32)

    for d in range(chips):
        target = lax.rem(chip + d, chips)
        span = pl.ds(pl.multiple_of(target * piece, piece), piece)
        outs[d][...] = acc[:, span, :].astype(outs[d].dtype)


def head_sum_kernel(count, mine, *refs):
    parts, outs = refs[: len(refs) - count], refs[len(refs) - count :]
    for i in range(count):
        total = mine[i]
        for part in parts:
            total = total + part[i].astype(F32)
        outs[i][...] = total.astype(BF16)


def fold(array, reduce):
    rows, lanes = array.shape
    return reduce(array.reshape(rows // 8, 8, lanes), axis=0)


def causal(array, first_col, first_pos, other):
    col = lax.broadcasted_iota(jnp.int32, array.shape, 0) + first_col
    pos = lax.broadcasted_iota(jnp.int32, array.shape, 1) + first_pos
    return jnp.where(col <= pos, array, other)


def row_sums(s_ref, dp_ref, factor):
    block_len = s_ref.shape[0]
    step = min(64, block_len)
    spans = [pl.ds(c, step) for c in range(0, block_len, step)]
    top = fold(s_ref[spans[0], :], jnp.max)
    for span in spans[1:]:
        top = jnp.maximum(top, fold(s_ref[span, :], jnp.max))
    top = jnp.max(top, axis=0, keepdims=True) * factor
    total = weighted = jnp.zeros((8, block_len), F32)
    for span in spans:
        terms = jnp.exp2(s_ref[span, :] * factor - top)
        total = total + fold(terms, jnp.sum)
        weighted = weighted + fold(terms * dp_ref[span, :], jnp.sum)
    total = jnp.sum(total, axis=0, keepdims=True)
    return top, total, jnp.sum(weighted, axis=0, keepdims=True)


def local_stats_kernel(factor, blocks_here, chosen, q, do, keys, values, stats, s_buf, dp_buf):
    block_len = keys.shape[1]
    half = block_len // 2

    def per_row(row, _):
        start = row * block_len
        span = pl.ds(start, block_len)
        late = pl.ds(start + half, half)

        s_buf[:half, :] = causal(dot_nt(keys[row, :half], q[span, :]), 0, 0, -jnp.inf)
        s_buf[half:, :half] = jnp.full((half, half), -jnp.inf, F32)
        s_buf[half:, half:] = causal(dot_nt(keys[row, half:], q[late, :]), 0, 0, -jnp.inf)
        dp_buf[:half, :] = dot_nt(values[row, :half], do[span, :])
        dp_buf[half:, :half] = jnp.zeros((half, half), F32)
        dp_buf[half:, half:] = dot_nt(values[row, half:], do[late, :])
        top, total, weighted = row_sums(s_buf, dp_buf, factor)
        stats[row, 0:1, :] = top
        stats[row, 1:2, :] = total
        stats[row, 2:3, :] = weighted
        for t in range(3):
            slot = slot_of(chosen, blocks_here, row, t)

            @pl.when((slot >= 0) & (slot < blocks_here))
            def _():
                s_buf[...] = dot_nt(keys[slot], q[span, :])
                dp_buf[...] = dot_nt(values[slot], do[span, :])
                more_top, more, more_weighted = row_sums(s_buf, dp_buf, factor)
                old = stats[row, 0:1, :]
                top = jnp.maximum(old, more_top)
                scale_old = jnp.exp2(old - top)
                scale_new = jnp.exp2(more_top - top)
                stats[row, 0:1, :] = top
                stats[row, 1:2, :] = stats[row, 1:2, :] * scale_old + more * scale_new
                stats[row, 2:3, :] = stats[row, 2:3, :] * scale_old + more_weighted * scale_new

        return 0

    lax.fori_loop(0, blocks_here, per_row, 0)


def remote_kernel(
    factor, scaling, blocks_here, chips, far, near, piece, chosen, q, do, stats, *refs
):
    near_refs, far_refs, refs = refs[:2], refs[2 : 2 + 2 * chips], refs[2 + 2 * chips :]
    keep, send, final, grad_qt, rows, acc, s_buf, dp_buf, parts = refs
    place = lax.axis_index("head")
    core, chip = lax.rem(place, 2), lax.div(place, 2)
    block_len = rows.shape[2]

    def lay(kind, which):
        for i, s in enumerate(near):
            rows[kind, s] = near_refs[which][i]
        for d in range(chips):
            source = lax.rem(chip + chips - d, chips)
            span = pl.ds(pl.multiple_of(source * piece, piece), piece)
            for i, s in enumerate(far):
                rows[kind, s, span, :] = far_refs[2 * d + which][i]

    @pl.when(core == 0)
    def _():
        lay(0, 0)
        lay(1, 1)

    @pl.when(core != 0)
    def _():
        lay(0, 1)
        lay(1, 0)

    acc[...] = jnp.zeros_like(acc)

    def per_row(row, _):
        span = pl.ds(row * block_len, block_len)
        parts[0, 0:3, :] = stats[row, 0:3, :]
        for t in range(3):
            slot = slot_of(chosen, blocks_here, row, t) - blocks_here

            @pl.when(slot >= 0)
            def _():
                s_buf[t] = dot_nt(rows[0, slot], q[span, :])
                dp_buf[t] = dot_nt(rows[1, slot], do[span, :])
                top, total, weighted = row_sums(s_buf.at[t], dp_buf.at[t], factor)
                parts[t + 1, 0:1, :] = top
                parts[t + 1, 1:2, :] = total
                parts[t + 1, 2:3, :] = weighted

            @pl.when(slot < 0)
            def _():
                parts[t + 1, 0:1, :] = jnp.full((1, block_len), -jnp.inf, F32)
                parts[t + 1, 1:3, :] = jnp.zeros((2, block_len), F32)

        top = parts[0, 0:1, :]
        for t in range(3):
            top = jnp.maximum(top, parts[t + 1, 0:1, :])
        total = jnp.zeros_like(top)
        weighted = jnp.zeros_like(top)
        for t in range(4):
            scale = jnp.exp2(parts[t, 0:1, :] - top)
            total = total + scale * parts[t, 1:2, :]
            weighted = weighted + scale * parts[t, 2:3, :]
        final[row, 0:1, :] = top + jnp.log2(total)
        final[row, 1:2, :] = weighted / total
        grad_qt[row] = jnp.zeros_like(grad_qt[row])
        for t in range(3):
            slot = slot_of(chosen, blocks_here, row, t) - blocks_here

            @pl.when(slot >= 0)
            def _():
                level = final[row, 0:1, :]
                delta = final[row, 1:2, :]
                weights = jnp.exp2(s_buf[t] * factor - level)
                dscores = (weights * (dp_buf[t] - delta)).astype(BF16)
                acc[1, slot] += dot_nn(weights.astype(BF16), do[span, :])
                acc[0, slot] += dot_nn(dscores, q[span, :])
                grad_qt[row] += dot_nn(rows[0, slot].T, dscores)

        return 0

    lax.fori_loop(0, blocks_here, per_row, 0)
    keep_scale = jnp.where(core == 0, scaling, 1.0)
    send_scale = jnp.where(core == 0, 1.0, scaling)
    keep[...] = (acc[core] * keep_scale).astype(BF16)
    send[...] = (acc[1 - core] * send_scale).astype(BF16)


def local_kernel(
    factor, scaling, blocks_here, chosen, q, do, keys, values, final, grad_qt,
    keep, send, grad_q,
    acc, total_qt,
):
    core = lax.rem(lax.axis_index("head"), 2)
    block_len = keys.shape[1]
    half = block_len // 2
    acc[...] = jnp.zeros_like(acc)

    def per_row(row, _):
        start = row * block_len
        span = pl.ds(start, block_len)

        def rows_from(ref, first):
            return ref[pl.ds(start + first, block_len - first), :]

        def products(slot, c, first):
            cut = pl.ds(c, half)
            scores = dot_nt(keys[slot, cut, :], rows_from(q, first))
            return scores, dot_nt(values[slot, cut, :], rows_from(do, first))

        def pair(slot, seconds, masked):
            parts = ((0, 0), (half, seconds))
            ready = [products(slot, c, first) for c, first in parts]
            sides = []
            for (c, first), (scores, dprobs) in zip(parts, ready):
                weights = jnp.exp2(scores * factor - final[row, 0:1, first:])
                if masked:
                    weights = causal(weights, c, first, 0.0)
                dscores = (weights * (dprobs - final[row, 1:2, first:])).astype(BF16)
                sides.append((weights.astype(BF16), dscores))
            for (c, first), (weights, dscores) in zip(parts, sides):
                cut = pl.ds(c, half)
                acc[1, slot, cut, :] += dot_nn(weights, rows_from(do, first))
                acc[0, slot, cut, :] += dot_nn(dscores, rows_from(q, first))
                total_qt[:, first:] += dot_nn(keys[slot, cut, :].T, dscores)

        total_qt[...] = grad_qt[row]
        pair(row, half, True)
        for t in range(3):
            slot = slot_of(chosen, blocks_here, row, t)

            @pl.when((slot >= 0) & (slot < blocks_here))
            def _():
                pair(slot, 0, False)

        grad_q[span, :] = (total_qt[...].T * scaling).astype(BF16)
        return 0

    lax.fori_loop(0, blocks_here, per_row, 0)
    keep_scale = jnp.where(core == 0, scaling, 1.0)
    send_scale = jnp.where(core == 0, 1.0, scaling)
    keep[...] = (acc[core] * keep_scale).astype(BF16)
    send[...] = (acc[1 - core] * send_scale).astype(BF16)


def owner_kernel(chips, far, asked, mine, *refs):
    others, back, (out, acc) = refs[: chips - 1], refs[chips - 1 : -2], refs[-2:]
    total = mine[...]
    for part in others:
        total = total + part[...].astype(F32)
    acc[...] = total
    for i, s in enumerate(far):
        slot = asked[s] - 1

        @pl.when(slot >= 0)
        def _():
            acc[slot] += back[i][...].astype(F32)

    out[...] = acc[...].astype(BF16)


def spread_kernel(chips, piece, *refs):
    pieces, (grad_k, grad_v) = refs[: 2 * chips], refs[2 * chips :]
    place = lax.axis_index("head")
    core, chip = lax.rem(place, 2), lax.div(place, 2)

    def lay(out, which):
        for d in range(chips):
            source = lax.rem(chip + chips - d, chips)
            span = pl.ds(pl.multiple_of(source * piece, piece), piece)
            out[:, span, :] = pieces[2 * d + which][...]

    @pl.when(core == 0)
    def _():
        lay(grad_k, 0)
        lay(grad_v, 1)

    @pl.when(core != 0)
    def _():
        lay(grad_k, 1)
        lay(grad_v, 0)


def params(size):
    return pltpu.CompilerParams(vmem_limit_bytes=min(size + 12 * 1024 * 1024, VMEM_LIMIT))


def body(queries, keys, values, dout, selected):
    tok_rows, head_count, feature = queries.shape
    blocks_here = selected.shape[0]
    block_len = tok_rows // blocks_here
    ctx_count = lax.axis_size("ctx")
    heads = lax.axis_size("head")
    chips = heads // 2
    piece = block_len // chips
    scaling = 1.0 / math.sqrt(feature)
    factor = scaling * math.log2(math.e)
    shifts = ctx_count - 1
    far = [s for s in range(shifts) if 2 * (s + 1) >= ctx_count]
    near = [s for s in range(shifts) if 2 * (s + 1) < ctx_count]

    q2 = queries.reshape(tok_rows, feature)
    do2 = dout.reshape(tok_rows, feature)
    key_blocks = keys.reshape(blocks_here, block_len, feature)
    value_blocks = values.reshape(blocks_here, block_len, feature)
    remote_shape = (shifts, block_len, feature)
    local_shape = (blocks_here, block_len, feature)

    smem = pl.BlockSpec(memory_space=pltpu.SMEM)
    whole = pl.BlockSpec(memory_space=pltpu.VMEM)
    hbm = pl.BlockSpec(memory_space=pltpu.HBM)
    stat_type = jax.ShapeDtypeStruct((blocks_here, 8, block_len), F32)
    far_type = jax.ShapeDtypeStruct(remote_shape, BF16)
    own_type = jax.ShapeDtypeStruct(local_shape, BF16)
    block_type = jax.ShapeDtypeStruct((block_len, feature), BF16)
    piece_type = jax.ShapeDtypeStruct((piece, feature), BF16)
    qt_type = jax.ShapeDtypeStruct((blocks_here, feature, block_len), F32)
    pair_flops = 2 * block_len * block_len * feature
    block_bytes = block_len * feature * 2
    pair_bytes = block_len * block_len * 4

    def pieces_type(count, dtype):
        return jax.ShapeDtypeStruct((count, piece, feature), dtype)

    def cost(matmuls, size):
        return pl.CostEstimate(
            flops=matmuls * pair_flops, bytes_accessed=size, transcendentals=matmuls * block_len**2
        )

    def swap(array):
        return lax.ppermute(array, "head", [(h, h ^ 1) for h in range(heads)])

    def to_chip(array, d):
        return lax.ppermute(array, "head", [(h, (h + 2 * d) % heads) for h in range(heads)])

    def to_owner(array, s):
        return lax.ppermute(array, "ctx", [(c, c - s - 1) for c in range(s + 1, ctx_count)])

    def to_reader(array, s):
        return lax.ppermute(array, "ctx", [(c - s - 1, c) for c in range(s + 1, ctx_count)])

    everyone = lax.all_to_all(
        jnp.broadcast_to(selected.reshape(1, 3 * blocks_here), (ctx_count, 3 * blocks_here)),
        "ctx", split_axis=0, concat_axis=0, tiled=True,
    )
    asked, *sent = pl.pallas_call(
        functools.partial(pick_kernel, blocks_here, ctx_count, chips, far, piece),
        in_specs=[smem, hbm, hbm],
        out_specs=[smem] + [whole] * shifts,
        out_shape=[jax.ShapeDtypeStruct((shifts,), jnp.int32)]
        + [piece_type if s in far else block_type for s in range(shifts)],
        scratch_shapes=[pltpu.SemaphoreType.DMA((shifts,))],
        name="pick_rows",
    )(everyone, key_blocks, value_blocks)

    far_mine = jnp.stack([to_reader(sent[s], s) for s in far])
    near_parts = [to_reader(sent[s], s) for s in near]
    far_mine, chosen = lax.optimization_barrier((far_mine, selected))
    far_more = [to_chip(far_mine, d) for d in range(1, chips)]
    stats = pl.pallas_call(
        functools.partial(local_stats_kernel, factor, blocks_here),
        in_specs=[smem] + [whole] * 4,
        out_specs=whole,
        out_shape=stat_type,
        scratch_shapes=[pltpu.VMEM((block_len, block_len), F32)] * 2,
        compiler_params=params(4 * blocks_here * block_bytes + 2 * pair_bytes),
        cost_estimate=cost(30, 4 * tok_rows * feature * 2),
        name="local_stats",
    )(chosen, q2, do2, key_blocks, value_blocks)
    near_parts, far_held, stats = lax.optimization_barrier((near_parts, far_mine, stats))
    near_mine = jnp.stack(near_parts)
    row_sets = [near_mine, swap(near_mine), far_held, swap(far_held)]
    for part in far_more:
        row_sets += [part, swap(part)]

    keep_far, send_far, final, grad_qt = pl.pallas_call(
        functools.partial(remote_kernel, factor, scaling, blocks_here, chips, far, near, piece),
        in_specs=[smem] + [whole] * (3 + len(row_sets)),
        out_specs=[whole] * 4,
        out_shape=[far_type, far_type, stat_type, qt_type],
        scratch_shapes=[
            pltpu.VMEM((2,) + remote_shape, BF16),
            pltpu.VMEM((2,) + remote_shape, F32),
            pltpu.VMEM((3, block_len, block_len), F32),
            pltpu.VMEM((3, block_len, block_len), F32),
            pltpu.VMEM((4, 8, block_len), F32),
        ],
        compiler_params=params((10 * shifts + 4 * blocks_here) * block_bytes + 6 * pair_bytes),
        cost_estimate=cost(60, 8 * tok_rows * feature * 2),
        name="remote_pairs",
    )(chosen, q2, do2, stats, *row_sets)

    def head_sums(mine, parts, count):
        return pl.pallas_call(
            functools.partial(head_sum_kernel, count),
            in_specs=[whole] * (1 + len(parts)),
            out_specs=[whole] * count,
            out_shape=[piece_type] * count,
            compiler_params=params(4 * count * block_bytes),
            name="head_sum",
        )(mine, *parts)

    chip_far = pl.pallas_call(
        functools.partial(chip_sum_kernel, chips, piece, far, near),
        in_specs=[whole, whole],
        out_specs=[whole] * (chips + len(near)),
        out_shape=[pieces_type(len(far), F32)]
        + [pieces_type(len(far), BF16)] * (chips - 1)
        + [block_type] * len(near),
        compiler_params=params(4 * shifts * block_bytes),
        name="chip_sum",
    )(keep_far, swap(send_far))
    chip_far, final = lax.optimization_barrier((chip_far, final))
    far_sums, near_sums = chip_far[:chips], chip_far[chips:]
    far_parts = [to_chip(far_sums[d], d) for d in range(1, chips)]
    near_back = [to_owner(near_sums[i], s) for i, s in enumerate(near)]
    keep_own, send_own, grad_q = pl.pallas_call(
        functools.partial(local_kernel, factor, scaling, blocks_here),
        in_specs=[smem] + [whole] * 6,
        out_specs=[whole] * 3,
        out_shape=[own_type, own_type, jax.ShapeDtypeStruct((tok_rows, feature), BF16)],
        scratch_shapes=[
            pltpu.VMEM((2,) + local_shape, F32),
            pltpu.VMEM((feature, block_len), F32),
        ],
        compiler_params=params(14 * blocks_here * block_bytes),
        cost_estimate=cost(60, 8 * tok_rows * feature * 2),
        name="local_pairs",
    )(chosen, q2, do2, key_blocks, value_blocks, final, grad_qt)
    far_parts, near_back, keep_own, send_own = lax.optimization_barrier(
        (far_parts, near_back, keep_own, send_own)
    )
    own_sums = pl.pallas_call(
        functools.partial(own_sum_kernel, chips, piece, near),
        in_specs=[smem] + [whole] * (2 + len(near)),
        out_specs=[whole] * chips,
        out_shape=[pieces_type(blocks_here, F32)]
        + [pieces_type(blocks_here, BF16)] * (chips - 1),
        scratch_shapes=[pltpu.VMEM(local_shape, F32)],
        compiler_params=params((8 * blocks_here + len(near)) * block_bytes),
        name="own_sum",
    )(asked, keep_own, swap(send_own), *near_back)
    own_parts = [to_chip(own_sums[d], d) for d in range(1, chips)]
    far_out = head_sums(far_sums[0], far_parts, len(far))
    far_back = [to_owner(far_out[i], s) for i, s in enumerate(far)]
    mine = pl.pallas_call(
        functools.partial(owner_kernel, chips, far),
        in_specs=[smem] + [whole] * (chips + len(far)),
        out_specs=whole,
        out_shape=pieces_type(blocks_here, BF16),
        scratch_shapes=[pltpu.VMEM((blocks_here, piece, feature), F32)],
        compiler_params=params((5 * blocks_here + shifts) * block_bytes),
        name="owner_sum",
    )(asked, own_sums[0], *own_parts, *far_back)
    spread = [mine, swap(mine)]
    for d in range(1, chips):
        part = to_chip(mine, d)
        spread += [part, swap(part)]
    grad_keys, grad_values = pl.pallas_call(
        functools.partial(spread_kernel, chips, piece),
        in_specs=[whole] * len(spread),
        out_specs=[whole] * 2,
        out_shape=[own_type] * 2,
        compiler_params=params(4 * blocks_here * block_bytes),
        name="spread",
    )(*spread)
    return (
        grad_q.reshape(tok_rows, head_count, feature),
        grad_keys.reshape(tok_rows, feature),
        grad_values.reshape(tok_rows, feature),
    )


def solution(mesh):
    return jax.shard_map(
        body,
        mesh=mesh,
        in_specs=(
            P("ctx", "head", None),
            P("ctx", None),
            P("ctx", None),
            P("ctx", "head", None),
            P("ctx", None),
        ),
        out_specs=(P("ctx", "head", None), P("ctx", None), P("ctx", None)),
        check_vma=False,
    )
```

```python
import functools
import math

import jax
import jax.numpy as jnp
from jax import lax
from jax.experimental import pallas as pl
from jax.experimental.pallas import tpu as pltpu
from jax.sharding import PartitionSpec as P

F32 = jnp.float32
BF16 = jnp.bfloat16
VMEM_LIMIT = 56 * 1024 * 1024


def dot_nt(a, b):
    return lax.dot_general(a, b, (((1,), (1,)), ((), ())), preferred_element_type=F32)


def dot_nn(a, b):
    return lax.dot_general(a, b, (((1,), (0,)), ((), ())), preferred_element_type=F32)


def slot_of(chosen, blocks_here, row, t):
    ctx_self = lax.axis_index("ctx")
    entry = chosen[row, t]
    owner = lax.div(entry, jnp.int32(blocks_here))
    apart = ctx_self - owner
    slot = jnp.where(apart == 0, entry - owner * blocks_here, blocks_here + apart - 1)
    return jnp.where(entry != ctx_self * blocks_here + row, slot, -1)


def pick_kernel(blocks_here, count, chips, far, piece, chosen, keys, values, asked, *refs):
    outs, sems = refs[:-1], refs[-1]
    ctx_self = lax.axis_index("ctx")
    place = lax.axis_index("head")
    core, chip = lax.rem(place, 2), lax.div(place, 2)
    first = ctx_self * blocks_here
    span = pl.ds(pl.multiple_of(chip * piece, piece), piece)

    def copy(source, s, slot):
        rows = source.at[slot, span, :] if s in far else source.at[slot]
        return pltpu.make_async_copy(rows, outs[s], sems.at[s])

    for s in range(count - 1):
        peer = ctx_self + s + 1
        near = jnp.minimum(peer, count - 1)
        found = jnp.int32(0)
        for row in range(blocks_here):
            for t in range(3):
                entry = chosen[near, row * 3 + t]
                hit = (entry >= first) & (entry < first + blocks_here)
                found = jnp.where(hit, entry - first + 1, found)
        found = jnp.where(peer < count, found, 0)
        asked[s] = found
        slot = jnp.maximum(found - 1, 0)

        @pl.when(core == 0)
        def _():
            copy(keys, s, slot).start()

        @pl.when(core != 0)
        def _():
            copy(values, s, slot).start()

    for s in range(count - 1):
        copy(keys, s, 0).wait()


def chip_sum_kernel(chips, piece, far, near, mine, theirs, *outs):
    chip = lax.div(lax.axis_index("head"), 2)
    for d in range(chips):
        target = lax.rem(chip + d, chips)
        span = pl.ds(pl.multiple_of(target * piece, piece), piece)
        for i, s in enumerate(far):
            total = mine[s, span, :].astype(F32) + theirs[s, span, :].astype(F32)
            outs[d][i] = total.astype(outs[d].dtype)
    for i, s in enumerate(near):
        outs[chips + i][...] = (mine[s].astype(F32) + theirs[s].astype(F32)).astype(BF16)


def own_sum_kernel(chips, piece, near, asked, mine, theirs, *refs):
    back, outs, acc = refs[: len(near)], refs[len(near) : -1], refs[-1]
    chip = lax.div(lax.axis_index("head"), 2)
    acc[...] = mine[...].astype(F32) + theirs[...].astype(F32)
    for i, s in enumerate(near):
        slot = asked[s] - 1

        @pl.when(slot >= 0)
        def _():
            acc[slot] += back[i][...].astype(F32)

    for d in range(chips):
        target = lax.rem(chip + d, chips)
        span = pl.ds(pl.multiple_of(target * piece, piece), piece)
        outs[d][...] = acc[:, span, :].astype(outs[d].dtype)


def head_sum_kernel(count, mine, *refs):
    parts, outs = refs[: len(refs) - count], refs[len(refs) - count :]
    for i in range(count):
        total = mine[i]
        for part in parts:
            total = total + part[i].astype(F32)
        outs[i][...] = total.astype(BF16)


def fold(array, reduce):
    rows, lanes = array.shape
    return reduce(array.reshape(rows // 8, 8, lanes), axis=0)


def causal(array, first_col, first_pos, other):
    col = lax.broadcasted_iota(jnp.int32, array.shape, 0) + first_col
    pos = lax.broadcasted_iota(jnp.int32, array.shape, 1) + first_pos
    return jnp.where(col <= pos, array, other)


def row_sums(s_ref, dp_ref, factor):
    block_len = s_ref.shape[0]
    step = min(64, block_len)
    spans = [pl.ds(c, step) for c in range(0, block_len, step)]
    top = fold(s_ref[spans[0], :], jnp.max)
    for span in spans[1:]:
        top = jnp.maximum(top, fold(s_ref[span, :], jnp.max))
    top = jnp.max(top, axis=0, keepdims=True) * factor
    total = weighted = jnp.zeros((8, block_len), F32)
    for span in spans:
        terms = jnp.exp2(s_ref[span, :] * factor - top)
        total = total + fold(terms, jnp.sum)
        weighted = weighted + fold(terms * dp_ref[span, :], jnp.sum)
    total = jnp.sum(total, axis=0, keepdims=True)
    return top, total, jnp.sum(weighted, axis=0, keepdims=True)


def local_stats_kernel(factor, blocks_here, chosen, q, do, keys, values, stats, s_buf, dp_buf):
    block_len = keys.shape[1]
    half = block_len // 2

    def per_row(row, _):
        start = row * block_len
        span = pl.ds(start, block_len)
        late = pl.ds(start + half, half)

        s_buf[:half, :] = causal(dot_nt(keys[row, :half], q[span, :]), 0, 0, -jnp.inf)
        s_buf[half:, :half] = jnp.full((half, half), -jnp.inf, F32)
        s_buf[half:, half:] = causal(dot_nt(keys[row, half:], q[late, :]), 0, 0, -jnp.inf)
        dp_buf[:half, :] = dot_nt(values[row, :half], do[span, :])
        dp_buf[half:, :half] = jnp.zeros((half, half), F32)
        dp_buf[half:, half:] = dot_nt(values[row, half:], do[late, :])
        top, total, weighted = row_sums(s_buf, dp_buf, factor)
        stats[row, 0:1, :] = top
        stats[row, 1:2, :] = total
        stats[row, 2:3, :] = weighted
        for t in range(3):
            slot = slot_of(chosen, blocks_here, row, t)

            @pl.when((slot >= 0) & (slot < blocks_here))
            def _():
                s_buf[...] = dot_nt(keys[slot], q[span, :])
                dp_buf[...] = dot_nt(values[slot], do[span, :])
                more_top, more, more_weighted = row_sums(s_buf, dp_buf, factor)
                old = stats[row, 0:1, :]
                top = jnp.maximum(old, more_top)
                scale_old = jnp.exp2(old - top)
                scale_new = jnp.exp2(more_top - top)
                stats[row, 0:1, :] = top
                stats[row, 1:2, :] = stats[row, 1:2, :] * scale_old + more * scale_new
                stats[row, 2:3, :] = stats[row, 2:3, :] * scale_old + more_weighted * scale_new

        return 0

    lax.fori_loop(0, blocks_here, per_row, 0)


def remote_kernel(
    factor, scaling, blocks_here, chips, far, near, piece, chosen, q, do, stats, *refs
):
    near_refs, far_refs, refs = refs[:2], refs[2 : 2 + 2 * chips], refs[2 + 2 * chips :]
    keep, send, final, grad_qt, rows, acc, s_buf, dp_buf, parts = refs
    place = lax.axis_index("head")
    core, chip = lax.rem(place, 2), lax.div(place, 2)
    block_len = rows.shape[2]

    def lay(kind, which):
        for i, s in enumerate(near):
            rows[kind, s] = near_refs[which][i]
        for d in range(chips):
            source = lax.rem(chip + chips - d, chips)
            span = pl.ds(pl.multiple_of(source * piece, piece), piece)
            for i, s in enumerate(far):
                rows[kind, s, span, :] = far_refs[2 * d + which][i]

    @pl.when(core == 0)
    def _():
        lay(0, 0)
        lay(1, 1)

    @pl.when(core != 0)
    def _():
        lay(0, 1)
        lay(1, 0)

    acc[...] = jnp.zeros_like(acc)

    def per_row(row, _):
        span = pl.ds(row * block_len, block_len)
        parts[0, 0:3, :] = stats[row, 0:3, :]
        for t in range(3):
            slot = slot_of(chosen, blocks_here, row, t) - blocks_here

            @pl.when(slot >= 0)
            def _():
                s_buf[t] = dot_nt(rows[0, slot], q[span, :])
                dp_buf[t] = dot_nt(rows[1, slot], do[span, :])
                top, total, weighted = row_sums(s_buf.at[t], dp_buf.at[t], factor)
                parts[t + 1, 0:1, :] = top
                parts[t + 1, 1:2, :] = total
                parts[t + 1, 2:3, :] = weighted

            @pl.when(slot < 0)
            def _():
                parts[t + 1, 0:1, :] = jnp.full((1, block_len), -jnp.inf, F32)
                parts[t + 1, 1:3, :] = jnp.zeros((2, block_len), F32)

        top = parts[0, 0:1, :]
        for t in range(3):
            top = jnp.maximum(top, parts[t + 1, 0:1, :])
        total = jnp.zeros_like(top)
        weighted = jnp.zeros_like(top)
        for t in range(4):
            scale = jnp.exp2(parts[t, 0:1, :] - top)
            total = total + scale * parts[t, 1:2, :]
            weighted = weighted + scale * parts[t, 2:3, :]
        final[row, 0:1, :] = top + jnp.log2(total)
        final[row, 1:2, :] = weighted / total
        grad_qt[row] = jnp.zeros_like(grad_qt[row])
        for t in range(3):
            slot = slot_of(chosen, blocks_here, row, t) - blocks_here

            @pl.when(slot >= 0)
            def _():
                level = final[row, 0:1, :]
                delta = final[row, 1:2, :]
                weights = jnp.exp2(s_buf[t] * factor - level)
                dscores = (weights * (dp_buf[t] - delta)).astype(BF16)
                acc[1, slot] += dot_nn(weights.astype(BF16), do[span, :])
                acc[0, slot] += dot_nn(dscores, q[span, :])
                grad_qt[row] += dot_nn(rows[0, slot].T, dscores)

        return 0

    lax.fori_loop(0, blocks_here, per_row, 0)
    keep_scale = jnp.where(core == 0, scaling, 1.0)
    send_scale = jnp.where(core == 0, 1.0, scaling)
    keep[...] = (acc[core] * keep_scale).astype(BF16)
    send[...] = (acc[1 - core] * send_scale).astype(BF16)


def local_kernel(
    factor, scaling, blocks_here, chosen, q, do, keys, values, final, grad_qt,
    keep, send, grad_q,
    acc, total_qt,
):
    core = lax.rem(lax.axis_index("head"), 2)
    block_len = keys.shape[1]
    half = block_len // 2
    acc[...] = jnp.zeros_like(acc)

    def per_row(row, _):
        start = row * block_len
        span = pl.ds(start, block_len)

        def rows_from(ref, first):
            return ref[pl.ds(start + first, block_len - first), :]

        def products(slot, c, first):
            cut = pl.ds(c, half)
            scores = dot_nt(keys[slot, cut, :], rows_from(q, first))
            return scores, dot_nt(values[slot, cut, :], rows_from(do, first))

        def pair(slot, seconds, masked):
            parts = ((0, 0), (half, seconds))
            ready = [products(slot, c, first) for c, first in parts]
            sides = []
            for (c, first), (scores, dprobs) in zip(parts, ready):
                weights = jnp.exp2(scores * factor - final[row, 0:1, first:])
                if masked:
                    weights = causal(weights, c, first, 0.0)
                dscores = (weights * (dprobs - final[row, 1:2, first:])).astype(BF16)
                sides.append((weights.astype(BF16), dscores))
            for (c, first), (weights, dscores) in zip(parts, sides):
                cut = pl.ds(c, half)
                acc[1, slot, cut, :] += dot_nn(weights, rows_from(do, first))
                acc[0, slot, cut, :] += dot_nn(dscores, rows_from(q, first))
                total_qt[:, first:] += dot_nn(keys[slot, cut, :].T, dscores)

        total_qt[...] = grad_qt[row]
        pair(row, half, True)
        for t in range(3):
            slot = slot_of(chosen, blocks_here, row, t)

            @pl.when((slot >= 0) & (slot < blocks_here))
            def _():
                pair(slot, 0, False)

        grad_q[span, :] = (total_qt[...].T * scaling).astype(BF16)
        return 0

    lax.fori_loop(0, blocks_here, per_row, 0)
    keep_scale = jnp.where(core == 0, scaling, 1.0)
    send_scale = jnp.where(core == 0, 1.0, scaling)
    keep[...] = (acc[core] * keep_scale).astype(BF16)
    send[...] = (acc[1 - core] * send_scale).astype(BF16)


def far_return_kernel(far, asked, *refs):
    back, acc = refs[:-1], refs[-1]
    acc[...] = jnp.zeros_like(acc)
    for i, s in enumerate(far):
        slot = asked[s] - 1

        @pl.when(slot >= 0)
        def _():
            acc[slot] += back[i][...].astype(F32)


def owner_kernel(returned, mine, *refs):
    others, out = refs[:-1], refs[-1]
    total = mine[...] + returned[...]
    for part in others:
        total = total + part[...].astype(F32)
    out[...] = total.astype(BF16)


def spread_kernel(chips, piece, *refs):
    pieces, (grad_k, grad_v) = refs[: 2 * chips], refs[2 * chips :]
    place = lax.axis_index("head")
    core, chip = lax.rem(place, 2), lax.div(place, 2)

    def lay(out, which):
        for d in range(chips):
            source = lax.rem(chip + chips - d, chips)
            span = pl.ds(pl.multiple_of(source * piece, piece), piece)
            out[:, span, :] = pieces[2 * d + which][...]

    @pl.when(core == 0)
    def _():
        lay(grad_k, 0)
        lay(grad_v, 1)

    @pl.when(core != 0)
    def _():
        lay(grad_k, 1)
        lay(grad_v, 0)


def params(size):
    return pltpu.CompilerParams(vmem_limit_bytes=min(size + 12 * 1024 * 1024, VMEM_LIMIT))


def body(queries, keys, values, dout, selected):
    tok_rows, head_count, feature = queries.shape
    blocks_here = selected.shape[0]
    block_len = tok_rows // blocks_here
    ctx_count = lax.axis_size("ctx")
    heads = lax.axis_size("head")
    chips = heads // 2
    piece = block_len // chips
    scaling = 1.0 / math.sqrt(feature)
    factor = scaling * math.log2(math.e)
    shifts = ctx_count - 1
    far = [s for s in range(shifts) if 2 * (s + 1) >= ctx_count]
    near = [s for s in range(shifts) if 2 * (s + 1) < ctx_count]

    q2 = queries.reshape(tok_rows, feature)
    do2 = dout.reshape(tok_rows, feature)
    key_blocks = keys.reshape(blocks_here, block_len, feature)
    value_blocks = values.reshape(blocks_here, block_len, feature)
    remote_shape = (shifts, block_len, feature)
    local_shape = (blocks_here, block_len, feature)

    smem = pl.BlockSpec(memory_space=pltpu.SMEM)
    whole = pl.BlockSpec(memory_space=pltpu.VMEM)
    hbm = pl.BlockSpec(memory_space=pltpu.HBM)
    stat_type = jax.ShapeDtypeStruct((blocks_here, 8, block_len), F32)
    far_type = jax.ShapeDtypeStruct(remote_shape, BF16)
    own_type = jax.ShapeDtypeStruct(local_shape, BF16)
    block_type = jax.ShapeDtypeStruct((block_len, feature), BF16)
    piece_type = jax.ShapeDtypeStruct((piece, feature), BF16)
    qt_type = jax.ShapeDtypeStruct((blocks_here, feature, block_len), F32)
    pair_flops = 2 * block_len * block_len * feature
    block_bytes = block_len * feature * 2
    pair_bytes = block_len * block_len * 4

    def pieces_type(count, dtype):
        return jax.ShapeDtypeStruct((count, piece, feature), dtype)

    def cost(matmuls, size):
        return pl.CostEstimate(
            flops=matmuls * pair_flops, bytes_accessed=size, transcendentals=matmuls * block_len**2
        )

    def swap(array):
        return lax.ppermute(array, "head", [(h, h ^ 1) for h in range(heads)])

    def to_chip(array, d):
        return lax.ppermute(array, "head", [(h, (h + 2 * d) % heads) for h in range(heads)])

    def to_owner(array, s):
        return lax.ppermute(array, "ctx", [(c, c - s - 1) for c in range(s + 1, ctx_count)])

    def to_reader(array, s):
        return lax.ppermute(array, "ctx", [(c - s - 1, c) for c in range(s + 1, ctx_count)])

    everyone = lax.all_to_all(
        jnp.broadcast_to(selected.reshape(1, 3 * blocks_here), (ctx_count, 3 * blocks_here)),
        "ctx", split_axis=0, concat_axis=0, tiled=True,
    )
    asked, *sent = pl.pallas_call(
        functools.partial(pick_kernel, blocks_here, ctx_count, chips, far, piece),
        in_specs=[smem, hbm, hbm],
        out_specs=[smem] + [whole] * shifts,
        out_shape=[jax.ShapeDtypeStruct((shifts,), jnp.int32)]
        + [piece_type if s in far else block_type for s in range(shifts)],
        scratch_shapes=[pltpu.SemaphoreType.DMA((shifts,))],
        name="pick_rows",
    )(everyone, key_blocks, value_blocks)

    far_mine = jnp.stack([to_reader(sent[s], s) for s in far])
    near_parts = [to_reader(sent[s], s) for s in near]
    far_mine, chosen = lax.optimization_barrier((far_mine, selected))
    far_more = [to_chip(far_mine, d) for d in range(1, chips)]
    stats = pl.pallas_call(
        functools.partial(local_stats_kernel, factor, blocks_here),
        in_specs=[smem] + [whole] * 4,
        out_specs=whole,
        out_shape=stat_type,
        scratch_shapes=[pltpu.VMEM((block_len, block_len), F32)] * 2,
        compiler_params=params(4 * blocks_here * block_bytes + 2 * pair_bytes),
        cost_estimate=cost(30, 4 * tok_rows * feature * 2),
        name="local_stats",
    )(chosen, q2, do2, key_blocks, value_blocks)
    near_parts, far_held, stats = lax.optimization_barrier((near_parts, far_mine, stats))
    near_mine = jnp.stack(near_parts)
    row_sets = [near_mine, swap(near_mine), far_held, swap(far_held)]
    for part in far_more:
        row_sets += [part, swap(part)]

    keep_far, send_far, final, grad_qt = pl.pallas_call(
        functools.partial(remote_kernel, factor, scaling, blocks_here, chips, far, near, piece),
        in_specs=[smem] + [whole] * (3 + len(row_sets)),
        out_specs=[whole] * 4,
        out_shape=[far_type, far_type, stat_type, qt_type],
        scratch_shapes=[
            pltpu.VMEM((2,) + remote_shape, BF16),
            pltpu.VMEM((2,) + remote_shape, F32),
            pltpu.VMEM((3, block_len, block_len), F32),
            pltpu.VMEM((3, block_len, block_len), F32),
            pltpu.VMEM((4, 8, block_len), F32),
        ],
        compiler_params=params((10 * shifts + 4 * blocks_here) * block_bytes + 6 * pair_bytes),
        cost_estimate=cost(60, 8 * tok_rows * feature * 2),
        name="remote_pairs",
    )(chosen, q2, do2, stats, *row_sets)

    def head_sums(mine, parts, count):
        return pl.pallas_call(
            functools.partial(head_sum_kernel, count),
            in_specs=[whole] * (1 + len(parts)),
            out_specs=[whole] * count,
            out_shape=[piece_type] * count,
            compiler_params=params(4 * count * block_bytes),
            name="head_sum",
        )(mine, *parts)

    chip_far = pl.pallas_call(
        functools.partial(chip_sum_kernel, chips, piece, far, near),
        in_specs=[whole, whole],
        out_specs=[whole] * (chips + len(near)),
        out_shape=[pieces_type(len(far), F32)]
        + [pieces_type(len(far), BF16)] * (chips - 1)
        + [block_type] * len(near),
        compiler_params=params(4 * shifts * block_bytes),
        name="chip_sum",
    )(keep_far, swap(send_far))
    chip_far, final = lax.optimization_barrier((chip_far, final))
    far_sums, near_sums = chip_far[:chips], chip_far[chips:]
    far_parts = [to_chip(far_sums[d], d) for d in range(1, chips)]
    near_back = [to_owner(near_sums[i], s) for i, s in enumerate(near)]
    keep_own, send_own, grad_q = pl.pallas_call(
        functools.partial(local_kernel, factor, scaling, blocks_here),
        in_specs=[smem] + [whole] * 6,
        out_specs=[whole] * 3,
        out_shape=[own_type, own_type, jax.ShapeDtypeStruct((tok_rows, feature), BF16)],
        scratch_shapes=[
            pltpu.VMEM((2,) + local_shape, F32),
            pltpu.VMEM((feature, block_len), F32),
        ],
        compiler_params=params(14 * blocks_here * block_bytes),
        cost_estimate=cost(60, 8 * tok_rows * feature * 2),
        name="local_pairs",
    )(chosen, q2, do2, key_blocks, value_blocks, final, grad_qt)
    far_parts, near_back, keep_own, send_own = lax.optimization_barrier(
        (far_parts, near_back, keep_own, send_own)
    )
    own_sums = pl.pallas_call(
        functools.partial(own_sum_kernel, chips, piece, near),
        in_specs=[smem] + [whole] * (2 + len(near)),
        out_specs=[whole] * chips,
        out_shape=[pieces_type(blocks_here, F32)]
        + [pieces_type(blocks_here, BF16)] * (chips - 1),
        scratch_shapes=[pltpu.VMEM(local_shape, F32)],
        compiler_params=params((8 * blocks_here + len(near)) * block_bytes),
        name="own_sum",
    )(asked, keep_own, swap(send_own), *near_back)
    own_parts = [to_chip(own_sums[d], d) for d in range(1, chips)]
    far_out = head_sums(far_sums[0], far_parts, len(far))
    far_back = [to_owner(far_out[i], s) for i, s in enumerate(far)]
    returned = pl.pallas_call(
        functools.partial(far_return_kernel, far),
        in_specs=[smem] + [whole] * len(far),
        out_specs=whole,
        out_shape=pieces_type(blocks_here, F32),
        compiler_params=params((2 * blocks_here + len(far)) * block_bytes),
        cost_estimate=cost(600, 8 * tok_rows * feature * 2),
        name="far_returns",
    )(asked, *far_back)
    mine = pl.pallas_call(
        owner_kernel,
        in_specs=[whole] * (1 + chips),
        out_specs=whole,
        out_shape=pieces_type(blocks_here, BF16),
        compiler_params=params(6 * blocks_here * block_bytes),
        name="owner_sum",
    )(returned, own_sums[0], *own_parts)
    spread = [mine, swap(mine)]
    for d in range(1, chips):
        part = to_chip(mine, d)
        spread += [part, swap(part)]
    grad_keys, grad_values = pl.pallas_call(
        functools.partial(spread_kernel, chips, piece),
        in_specs=[whole] * len(spread),
        out_specs=[whole] * 2,
        out_shape=[own_type] * 2,
        compiler_params=params(4 * blocks_here * block_bytes),
        name="spread",
    )(*spread)
    return (
        grad_q.reshape(tok_rows, head_count, feature),
        grad_keys.reshape(tok_rows, feature),
        grad_values.reshape(tok_rows, feature),
    )


def solution(mesh):
    return jax.shard_map(
        body,
        mesh=mesh,
        in_specs=(
            P("ctx", "head", None),
            P("ctx", None),
            P("ctx", None),
            P("ctx", "head", None),
            P("ctx", None),
        ),
        out_specs=(P("ctx", "head", None), P("ctx", None), P("ctx", None)),
        check_vma=False,
    )
```

```python
import functools
import math

import jax
import jax.numpy as jnp
from jax import lax
from jax.experimental import pallas as pl
from jax.experimental.pallas import tpu as pltpu
from jax.sharding import PartitionSpec as P

F32 = jnp.float32
BF16 = jnp.bfloat16
VMEM_LIMIT = 56 * 1024 * 1024


def dot_nt(a, b):
    return lax.dot_general(a, b, (((1,), (1,)), ((), ())), preferred_element_type=F32)


def dot_nn(a, b):
    return lax.dot_general(a, b, (((1,), (0,)), ((), ())), preferred_element_type=F32)


def slot_of(chosen, blocks_here, row, t):
    ctx_self = lax.axis_index("ctx")
    entry = chosen[row, t]
    owner = lax.div(entry, jnp.int32(blocks_here))
    apart = ctx_self - owner
    slot = jnp.where(apart == 0, entry - owner * blocks_here, blocks_here + apart - 1)
    return jnp.where(entry != ctx_self * blocks_here + row, slot, -1)


def pick_kernel(blocks_here, count, chips, far, piece, chosen, keys, values, asked, *refs):
    outs, sems = refs[:-1], refs[-1]
    ctx_self = lax.axis_index("ctx")
    place = lax.axis_index("head")
    core, chip = lax.rem(place, 2), lax.div(place, 2)
    first = ctx_self * blocks_here
    span = pl.ds(pl.multiple_of(chip * piece, piece), piece)

    def copy(source, s, slot):
        rows = source.at[slot, span, :] if s in far else source.at[slot]
        return pltpu.make_async_copy(rows, outs[s], sems.at[s])

    for s in range(count - 1):
        peer = ctx_self + s + 1
        near = jnp.minimum(peer, count - 1)
        found = jnp.int32(0)
        for row in range(blocks_here):
            for t in range(3):
                entry = chosen[near, row * 3 + t]
                hit = (entry >= first) & (entry < first + blocks_here)
                found = jnp.where(hit, entry - first + 1, found)
        found = jnp.where(peer < count, found, 0)
        asked[s] = found
        slot = jnp.maximum(found - 1, 0)

        @pl.when(core == 0)
        def _():
            copy(keys, s, slot).start()

        @pl.when(core != 0)
        def _():
            copy(values, s, slot).start()

    for s in range(count - 1):
        copy(keys, s, 0).wait()


def chip_sum_kernel(chips, piece, far, near, mine, theirs, *outs):
    chip = lax.div(lax.axis_index("head"), 2)
    for d in range(chips):
        target = lax.rem(chip + d, chips)
        span = pl.ds(pl.multiple_of(target * piece, piece), piece)
        for i, s in enumerate(far):
            total = mine[s, span, :].astype(F32) + theirs[s, span, :].astype(F32)
            outs[d][i] = total.astype(outs[d].dtype)
    for i, s in enumerate(near):
        outs[chips + i][...] = (mine[s].astype(F32) + theirs[s].astype(F32)).astype(BF16)


def own_sum_kernel(chips, piece, near, asked, mine, theirs, *refs):
    back, outs, acc = refs[: len(near)], refs[len(near) : -1], refs[-1]
    chip = lax.div(lax.axis_index("head"), 2)
    acc[...] = mine[...].astype(F32) + theirs[...].astype(F32)
    for i, s in enumerate(near):
        slot = asked[s] - 1

        @pl.when(slot >= 0)
        def _():
            acc[slot] += back[i][...].astype(F32)

    for d in range(chips):
        target = lax.rem(chip + d, chips)
        span = pl.ds(pl.multiple_of(target * piece, piece), piece)
        outs[d][...] = acc[:, span, :].astype(outs[d].dtype)


def head_sum_kernel(count, mine, *refs):
    parts, outs = refs[: len(refs) - count], refs[len(refs) - count :]
    for i in range(count):
        total = mine[i]
        for part in parts:
            total = total + part[i].astype(F32)
        outs[i][...] = total.astype(BF16)


def fold(array, reduce):
    rows, lanes = array.shape
    return reduce(array.reshape(rows // 8, 8, lanes), axis=0)


def causal(array, first_col, first_pos, other):
    col = lax.broadcasted_iota(jnp.int32, array.shape, 0) + first_col
    pos = lax.broadcasted_iota(jnp.int32, array.shape, 1) + first_pos
    return jnp.where(col <= pos, array, other)


def row_sums(s_ref, dp_ref, factor):
    block_len = s_ref.shape[0]
    step = min(64, block_len)
    spans = [pl.ds(c, step) for c in range(0, block_len, step)]
    top = fold(s_ref[spans[0], :], jnp.max)
    for span in spans[1:]:
        top = jnp.maximum(top, fold(s_ref[span, :], jnp.max))
    top = jnp.max(top, axis=0, keepdims=True) * factor
    total = weighted = jnp.zeros((8, block_len), F32)
    for span in spans:
        terms = jnp.exp2(s_ref[span, :] * factor - top)
        total = total + fold(terms, jnp.sum)
        weighted = weighted + fold(terms * dp_ref[span, :], jnp.sum)
    total = jnp.sum(total, axis=0, keepdims=True)
    return top, total, jnp.sum(weighted, axis=0, keepdims=True)


def local_stats_kernel(factor, blocks_here, chosen, q, do, keys, values, stats, s_buf, dp_buf):
    block_len = keys.shape[1]
    half = block_len // 2

    def per_row(row, _):
        start = row * block_len
        span = pl.ds(start, block_len)
        late = pl.ds(start + half, half)

        s_buf[:half, :] = causal(dot_nt(keys[row, :half], q[span, :]), 0, 0, -jnp.inf)
        s_buf[half:, :half] = jnp.full((half, half), -jnp.inf, F32)
        s_buf[half:, half:] = causal(dot_nt(keys[row, half:], q[late, :]), 0, 0, -jnp.inf)
        dp_buf[:half, :] = dot_nt(values[row, :half], do[span, :])
        dp_buf[half:, :half] = jnp.zeros((half, half), F32)
        dp_buf[half:, half:] = dot_nt(values[row, half:], do[late, :])
        top, total, weighted = row_sums(s_buf, dp_buf, factor)
        stats[row, 0:1, :] = top
        stats[row, 1:2, :] = total
        stats[row, 2:3, :] = weighted
        for t in range(3):
            slot = slot_of(chosen, blocks_here, row, t)

            @pl.when((slot >= 0) & (slot < blocks_here))
            def _():
                s_buf[...] = dot_nt(keys[slot], q[span, :])
                dp_buf[...] = dot_nt(values[slot], do[span, :])
                more_top, more, more_weighted = row_sums(s_buf, dp_buf, factor)
                old = stats[row, 0:1, :]
                top = jnp.maximum(old, more_top)
                scale_old = jnp.exp2(old - top)
                scale_new = jnp.exp2(more_top - top)
                stats[row, 0:1, :] = top
                stats[row, 1:2, :] = stats[row, 1:2, :] * scale_old + more * scale_new
                stats[row, 2:3, :] = stats[row, 2:3, :] * scale_old + more_weighted * scale_new

        return 0

    lax.fori_loop(0, blocks_here, per_row, 0)


def remote_kernel(
    factor, scaling, blocks_here, chips, far, near, piece, chosen, q, do, stats, *refs
):
    near_refs, far_refs, refs = refs[:2], refs[2 : 2 + 2 * chips], refs[2 + 2 * chips :]
    keep, send, final, grad_qt, rows, acc, s_buf, dp_buf, parts = refs
    place = lax.axis_index("head")
    core, chip = lax.rem(place, 2), lax.div(place, 2)
    block_len = rows.shape[2]

    def lay(kind, which):
        for i, s in enumerate(near):
            rows[kind, s] = near_refs[which][i]
        for d in range(chips):
            source = lax.rem(chip + chips - d, chips)
            span = pl.ds(pl.multiple_of(source * piece, piece), piece)
            for i, s in enumerate(far):
                rows[kind, s, span, :] = far_refs[2 * d + which][i]

    @pl.when(core == 0)
    def _():
        lay(0, 0)
        lay(1, 1)

    @pl.when(core != 0)
    def _():
        lay(0, 1)
        lay(1, 0)

    acc[...] = jnp.zeros_like(acc)

    def per_row(row, _):
        span = pl.ds(row * block_len, block_len)
        parts[0, 0:3, :] = stats[row, 0:3, :]
        for t in range(3):
            slot = slot_of(chosen, blocks_here, row, t) - blocks_here

            @pl.when(slot >= 0)
            def _():
                s_buf[t] = dot_nt(rows[0, slot], q[span, :])
                dp_buf[t] = dot_nt(rows[1, slot], do[span, :])
                top, total, weighted = row_sums(s_buf.at[t], dp_buf.at[t], factor)
                parts[t + 1, 0:1, :] = top
                parts[t + 1, 1:2, :] = total
                parts[t + 1, 2:3, :] = weighted

            @pl.when(slot < 0)
            def _():
                parts[t + 1, 0:1, :] = jnp.full((1, block_len), -jnp.inf, F32)
                parts[t + 1, 1:3, :] = jnp.zeros((2, block_len), F32)

        top = parts[0, 0:1, :]
        for t in range(3):
            top = jnp.maximum(top, parts[t + 1, 0:1, :])
        total = jnp.zeros_like(top)
        weighted = jnp.zeros_like(top)
        for t in range(4):
            scale = jnp.exp2(parts[t, 0:1, :] - top)
            total = total + scale * parts[t, 1:2, :]
            weighted = weighted + scale * parts[t, 2:3, :]
        final[row, 0:1, :] = top + jnp.log2(total)
        final[row, 1:2, :] = weighted / total
        grad_qt[row] = jnp.zeros_like(grad_qt[row])
        for t in range(3):
            slot = slot_of(chosen, blocks_here, row, t) - blocks_here

            @pl.when(slot >= 0)
            def _():
                level = final[row, 0:1, :]
                delta = final[row, 1:2, :]
                weights = jnp.exp2(s_buf[t] * factor - level)
                dscores = (weights * (dp_buf[t] - delta)).astype(BF16)
                acc[1, slot] += dot_nn(weights.astype(BF16), do[span, :])
                acc[0, slot] += dot_nn(dscores, q[span, :])
                grad_qt[row] += dot_nn(rows[0, slot].T, dscores)

        return 0

    lax.fori_loop(0, blocks_here, per_row, 0)
    keep_scale = jnp.where(core == 0, scaling, 1.0)
    send_scale = jnp.where(core == 0, 1.0, scaling)
    keep[...] = (acc[core] * keep_scale).astype(BF16)
    send[...] = (acc[1 - core] * send_scale).astype(BF16)


def local_kernel(
    factor, scaling, blocks_here, chosen, q, do, keys, values, final, grad_qt,
    keep, send, grad_q,
    acc, total_qt,
):
    core = lax.rem(lax.axis_index("head"), 2)
    block_len = keys.shape[1]
    half = block_len // 2
    acc[...] = jnp.zeros_like(acc)

    def per_row(row, _):
        start = row * block_len
        span = pl.ds(start, block_len)

        def rows_from(ref, first):
            return ref[pl.ds(start + first, block_len - first), :]

        def products(slot, c, first):
            cut = pl.ds(c, half)
            scores = dot_nt(keys[slot, cut, :], rows_from(q, first))
            return scores, dot_nt(values[slot, cut, :], rows_from(do, first))

        def pair(slot, seconds, masked):
            parts = ((0, 0), (half, seconds))
            ready = [products(slot, c, first) for c, first in parts]
            sides = []
            for (c, first), (scores, dprobs) in zip(parts, ready):
                weights = jnp.exp2(scores * factor - final[row, 0:1, first:])
                if masked:
                    weights = causal(weights, c, first, 0.0)
                dscores = (weights * (dprobs - final[row, 1:2, first:])).astype(BF16)
                sides.append((weights.astype(BF16), dscores))
            for (c, first), (weights, dscores) in zip(parts, sides):
                cut = pl.ds(c, half)
                acc[1, slot, cut, :] += dot_nn(weights, rows_from(do, first))
                acc[0, slot, cut, :] += dot_nn(dscores, rows_from(q, first))
                total_qt[:, first:] += dot_nn(keys[slot, cut, :].T, dscores)

        total_qt[...] = grad_qt[row]
        pair(row, half, True)
        for t in range(3):
            slot = slot_of(chosen, blocks_here, row, t)

            @pl.when((slot >= 0) & (slot < blocks_here))
            def _():
                pair(slot, 0, False)

        grad_q[span, :] = (total_qt[...].T * scaling).astype(BF16)
        return 0

    lax.fori_loop(0, blocks_here, per_row, 0)
    keep_scale = jnp.where(core == 0, scaling, 1.0)
    send_scale = jnp.where(core == 0, 1.0, scaling)
    keep[...] = (acc[core] * keep_scale).astype(BF16)
    send[...] = (acc[1 - core] * send_scale).astype(BF16)


def far_return_kernel(far, asked, *refs):
    back, acc = refs[:-1], refs[-1]
    acc[...] = jnp.zeros_like(acc)
    for i, s in enumerate(far):
        slot = asked[s] - 1

        @pl.when(slot >= 0)
        def _():
            acc[slot] += back[i][...].astype(F32)


def owner_kernel(returned, mine, *refs):
    others, out = refs[:-1], refs[-1]
    total = mine[...] + returned[...]
    for part in others:
        total = total + part[...].astype(F32)
    out[...] = total.astype(BF16)


def spread_kernel(chips, piece, *refs):
    pieces, (grad_k, grad_v) = refs[: 2 * chips], refs[2 * chips :]
    place = lax.axis_index("head")
    core, chip = lax.rem(place, 2), lax.div(place, 2)

    def lay(out, which):
        for d in range(chips):
            source = lax.rem(chip + chips - d, chips)
            span = pl.ds(pl.multiple_of(source * piece, piece), piece)
            out[:, span, :] = pieces[2 * d + which][...]

    @pl.when(core == 0)
    def _():
        lay(grad_k, 0)
        lay(grad_v, 1)

    @pl.when(core != 0)
    def _():
        lay(grad_k, 1)
        lay(grad_v, 0)


def params(size):
    return pltpu.CompilerParams(vmem_limit_bytes=min(size + 12 * 1024 * 1024, VMEM_LIMIT))


def body(queries, keys, values, dout, selected):
    tok_rows, head_count, feature = queries.shape
    blocks_here = selected.shape[0]
    block_len = tok_rows // blocks_here
    ctx_count = lax.axis_size("ctx")
    heads = lax.axis_size("head")
    chips = heads // 2
    piece = block_len // chips
    scaling = 1.0 / math.sqrt(feature)
    factor = scaling * math.log2(math.e)
    shifts = ctx_count - 1
    far = [s for s in range(shifts) if 2 * (s + 1) >= ctx_count]
    near = [s for s in range(shifts) if 2 * (s + 1) < ctx_count]
    far_in = [s for s in range(shifts) if 2 * (s + 2) >= ctx_count]
    near_in = [s for s in range(shifts) if 2 * (s + 2) < ctx_count]

    q2 = queries.reshape(tok_rows, feature)
    do2 = dout.reshape(tok_rows, feature)
    key_blocks = keys.reshape(blocks_here, block_len, feature)
    value_blocks = values.reshape(blocks_here, block_len, feature)
    remote_shape = (shifts, block_len, feature)
    local_shape = (blocks_here, block_len, feature)

    smem = pl.BlockSpec(memory_space=pltpu.SMEM)
    whole = pl.BlockSpec(memory_space=pltpu.VMEM)
    hbm = pl.BlockSpec(memory_space=pltpu.HBM)
    stat_type = jax.ShapeDtypeStruct((blocks_here, 8, block_len), F32)
    far_type = jax.ShapeDtypeStruct(remote_shape, BF16)
    own_type = jax.ShapeDtypeStruct(local_shape, BF16)
    block_type = jax.ShapeDtypeStruct((block_len, feature), BF16)
    piece_type = jax.ShapeDtypeStruct((piece, feature), BF16)
    qt_type = jax.ShapeDtypeStruct((blocks_here, feature, block_len), F32)
    pair_flops = 2 * block_len * block_len * feature
    block_bytes = block_len * feature * 2
    pair_bytes = block_len * block_len * 4

    def pieces_type(count, dtype):
        return jax.ShapeDtypeStruct((count, piece, feature), dtype)

    def cost(matmuls, size):
        return pl.CostEstimate(
            flops=matmuls * pair_flops, bytes_accessed=size, transcendentals=matmuls * block_len**2
        )

    def swap(array):
        return lax.ppermute(array, "head", [(h, h ^ 1) for h in range(heads)])

    def to_chip(array, d):
        return lax.ppermute(array, "head", [(h, (h + 2 * d) % heads) for h in range(heads)])

    def to_owner(array, s):
        return lax.ppermute(array, "ctx", [(c, c - s - 1) for c in range(s + 1, ctx_count)])

    def to_reader(array, s):
        return lax.ppermute(array, "ctx", [(c - s - 1, c) for c in range(s + 1, ctx_count)])

    everyone = lax.all_to_all(
        jnp.broadcast_to(selected.reshape(1, 3 * blocks_here), (ctx_count, 3 * blocks_here)),
        "ctx", split_axis=0, concat_axis=0, tiled=True,
    )
    asked, *sent = pl.pallas_call(
        functools.partial(pick_kernel, blocks_here, ctx_count, chips, far_in, piece),
        in_specs=[smem, hbm, hbm],
        out_specs=[smem] + [whole] * shifts,
        out_shape=[jax.ShapeDtypeStruct((shifts,), jnp.int32)]
        + [piece_type if s in far_in else block_type for s in range(shifts)],
        scratch_shapes=[pltpu.SemaphoreType.DMA((shifts,))],
        name="pick_rows",
    )(everyone, key_blocks, value_blocks)

    far_mine = jnp.stack([to_reader(sent[s], s) for s in far_in])
    near_parts = [to_reader(sent[s], s) for s in near_in]
    far_mine, chosen = lax.optimization_barrier((far_mine, selected))
    far_more = [to_chip(far_mine, d) for d in range(1, chips)]
    stats = pl.pallas_call(
        functools.partial(local_stats_kernel, factor, blocks_here),
        in_specs=[smem] + [whole] * 4,
        out_specs=whole,
        out_shape=stat_type,
        scratch_shapes=[pltpu.VMEM((block_len, block_len), F32)] * 2,
        compiler_params=params(4 * blocks_here * block_bytes + 2 * pair_bytes),
        cost_estimate=cost(30, 4 * tok_rows * feature * 2),
        name="local_stats",
    )(chosen, q2, do2, key_blocks, value_blocks)
    near_parts, far_held, stats = lax.optimization_barrier((near_parts, far_mine, stats))
    near_mine = jnp.stack(near_parts)
    row_sets = [near_mine, swap(near_mine), far_held, swap(far_held)]
    for part in far_more:
        row_sets += [part, swap(part)]

    keep_far, send_far, final, grad_qt = pl.pallas_call(
        functools.partial(
            remote_kernel, factor, scaling, blocks_here, chips, far_in, near_in, piece
        ),
        in_specs=[smem] + [whole] * (3 + len(row_sets)),
        out_specs=[whole] * 4,
        out_shape=[far_type, far_type, stat_type, qt_type],
        scratch_shapes=[
            pltpu.VMEM((2,) + remote_shape, BF16),
            pltpu.VMEM((2,) + remote_shape, F32),
            pltpu.VMEM((3, block_len, block_len), F32),
            pltpu.VMEM((3, block_len, block_len), F32),
            pltpu.VMEM((4, 8, block_len), F32),
        ],
        compiler_params=params((10 * shifts + 4 * blocks_here) * block_bytes + 6 * pair_bytes),
        cost_estimate=cost(60, 8 * tok_rows * feature * 2),
        name="remote_pairs",
    )(chosen, q2, do2, stats, *row_sets)

    def head_sums(mine, parts, count):
        return pl.pallas_call(
            functools.partial(head_sum_kernel, count),
            in_specs=[whole] * (1 + len(parts)),
            out_specs=[whole] * count,
            out_shape=[piece_type] * count,
            compiler_params=params(4 * count * block_bytes),
            name="head_sum",
        )(mine, *parts)

    chip_far = pl.pallas_call(
        functools.partial(chip_sum_kernel, chips, piece, far, near),
        in_specs=[whole, whole],
        out_specs=[whole] * (chips + len(near)),
        out_shape=[pieces_type(len(far), F32)]
        + [pieces_type(len(far), BF16)] * (chips - 1)
        + [block_type] * len(near),
        compiler_params=params(4 * shifts * block_bytes),
        name="chip_sum",
    )(keep_far, swap(send_far))
    chip_far, final = lax.optimization_barrier((chip_far, final))
    far_sums, near_sums = chip_far[:chips], chip_far[chips:]
    far_parts = [to_chip(far_sums[d], d) for d in range(1, chips)]
    near_back = [to_owner(near_sums[i], s) for i, s in enumerate(near)]
    keep_own, send_own, grad_q = pl.pallas_call(
        functools.partial(local_kernel, factor, scaling, blocks_here),
        in_specs=[smem] + [whole] * 6,
        out_specs=[whole] * 3,
        out_shape=[own_type, own_type, jax.ShapeDtypeStruct((tok_rows, feature), BF16)],
        scratch_shapes=[
            pltpu.VMEM((2,) + local_shape, F32),
            pltpu.VMEM((feature, block_len), F32),
        ],
        compiler_params=params(14 * blocks_here * block_bytes),
        cost_estimate=cost(60, 8 * tok_rows * feature * 2),
        name="local_pairs",
    )(chosen, q2, do2, key_blocks, value_blocks, final, grad_qt)
    far_parts, near_back, keep_own, send_own = lax.optimization_barrier(
        (far_parts, near_back, keep_own, send_own)
    )
    own_sums = pl.pallas_call(
        functools.partial(own_sum_kernel, chips, piece, near),
        in_specs=[smem] + [whole] * (2 + len(near)),
        out_specs=[whole] * chips,
        out_shape=[pieces_type(blocks_here, F32)]
        + [pieces_type(blocks_here, BF16)] * (chips - 1),
        scratch_shapes=[pltpu.VMEM(local_shape, F32)],
        compiler_params=params((8 * blocks_here + len(near)) * block_bytes),
        name="own_sum",
    )(asked, keep_own, swap(send_own), *near_back)
    own_parts = [to_chip(own_sums[d], d) for d in range(1, chips)]
    far_out = head_sums(far_sums[0], far_parts, len(far))
    far_back = [to_owner(far_out[i], s) for i, s in enumerate(far)]
    returned = pl.pallas_call(
        functools.partial(far_return_kernel, far),
        in_specs=[smem] + [whole] * len(far),
        out_specs=whole,
        out_shape=pieces_type(blocks_here, F32),
        compiler_params=params((2 * blocks_here + len(far)) * block_bytes),
        cost_estimate=cost(600, 8 * tok_rows * feature * 2),
        name="far_returns",
    )(asked, *far_back)
    mine = pl.pallas_call(
        owner_kernel,
        in_specs=[whole] * (1 + chips),
        out_specs=whole,
        out_shape=pieces_type(blocks_here, BF16),
        compiler_params=params(6 * blocks_here * block_bytes),
        name="owner_sum",
    )(returned, own_sums[0], *own_parts)
    spread = [mine, swap(mine)]
    for d in range(1, chips):
        part = to_chip(mine, d)
        spread += [part, swap(part)]
    grad_keys, grad_values = pl.pallas_call(
        functools.partial(spread_kernel, chips, piece),
        in_specs=[whole] * len(spread),
        out_specs=[whole] * 2,
        out_shape=[own_type] * 2,
        compiler_params=params(4 * blocks_here * block_bytes),
        name="spread",
    )(*spread)
    return (
        grad_q.reshape(tok_rows, head_count, feature),
        grad_keys.reshape(tok_rows, feature),
        grad_values.reshape(tok_rows, feature),
    )


def solution(mesh):
    return jax.shard_map(
        body,
        mesh=mesh,
        in_specs=(
            P("ctx", "head", None),
            P("ctx", None),
            P("ctx", None),
            P("ctx", "head", None),
            P("ctx", None),
        ),
        out_specs=(P("ctx", "head", None), P("ctx", None), P("ctx", None)),
        check_vma=False,
    )
```

```python
import functools
import math

import jax
import jax.numpy as jnp
from jax import lax
from jax.experimental import pallas as pl
from jax.experimental.pallas import tpu as pltpu
from jax.sharding import PartitionSpec as P

F32 = jnp.float32
BF16 = jnp.bfloat16
VMEM_LIMIT = 56 * 1024 * 1024


def dot_nt(a, b):
    return lax.dot_general(a, b, (((1,), (1,)), ((), ())), preferred_element_type=F32)


def dot_nn(a, b):
    return lax.dot_general(a, b, (((1,), (0,)), ((), ())), preferred_element_type=F32)


def slot_of(chosen, blocks_here, row, t):
    ctx_self = lax.axis_index("ctx")
    entry = chosen[row, t]
    owner = lax.div(entry, jnp.int32(blocks_here))
    apart = ctx_self - owner
    slot = jnp.where(apart == 0, entry - owner * blocks_here, blocks_here + apart - 1)
    return jnp.where(entry != ctx_self * blocks_here + row, slot, -1)


def pick_kernel(blocks_here, count, chips, far, piece, chosen, keys, values, asked, *refs):
    outs, sems = refs[:-1], refs[-1]
    ctx_self = lax.axis_index("ctx")
    place = lax.axis_index("head")
    core, chip = lax.rem(place, 2), lax.div(place, 2)
    first = ctx_self * blocks_here
    span = pl.ds(pl.multiple_of(chip * piece, piece), piece)

    def copy(source, s, slot):
        rows = source.at[slot, span, :] if s in far else source.at[slot]
        return pltpu.make_async_copy(rows, outs[s], sems.at[s])

    for s in range(count - 1):
        peer = ctx_self + s + 1
        near = jnp.minimum(peer, count - 1)
        found = jnp.int32(0)
        for row in range(blocks_here):
            for t in range(3):
                entry = chosen[near, row * 3 + t]
                hit = (entry >= first) & (entry < first + blocks_here)
                found = jnp.where(hit, entry - first + 1, found)
        found = jnp.where(peer < count, found, 0)
        asked[s] = found
        slot = jnp.maximum(found - 1, 0)

        @pl.when(core == 0)
        def _():
            copy(keys, s, slot).start()

        @pl.when(core != 0)
        def _():
            copy(values, s, slot).start()

    for s in range(count - 1):
        copy(keys, s, 0).wait()


def chip_sum_kernel(chips, piece, far, near, mine, theirs, *outs):
    chip = lax.div(lax.axis_index("head"), 2)
    for d in range(chips):
        target = lax.rem(chip + d, chips)
        span = pl.ds(pl.multiple_of(target * piece, piece), piece)
        for i, s in enumerate(far):
            total = mine[s, span, :].astype(F32) + theirs[s, span, :].astype(F32)
            outs[d][i] = total.astype(outs[d].dtype)
    for i, s in enumerate(near):
        outs[chips + i][...] = (mine[s].astype(F32) + theirs[s].astype(F32)).astype(BF16)


def own_sum_kernel(chips, piece, near, asked, mine, theirs, *refs):
    back, outs, acc = refs[: len(near)], refs[len(near) : -1], refs[-1]
    chip = lax.div(lax.axis_index("head"), 2)
    acc[...] = mine[...].astype(F32) + theirs[...].astype(F32)
    for i, s in enumerate(near):
        slot = asked[s] - 1

        @pl.when(slot >= 0)
        def _():
            acc[slot] += back[i][...].astype(F32)

    for d in range(chips):
        target = lax.rem(chip + d, chips)
        span = pl.ds(pl.multiple_of(target * piece, piece), piece)
        outs[d][...] = acc[:, span, :].astype(outs[d].dtype)


def head_sum_kernel(count, mine, *refs):
    parts, outs = refs[: len(refs) - count], refs[len(refs) - count :]
    for i in range(count):
        total = mine[i]
        for part in parts:
            total = total + part[i].astype(F32)
        outs[i][...] = total.astype(BF16)


def fold(array, reduce):
    rows, lanes = array.shape
    return reduce(array.reshape(rows // 8, 8, lanes), axis=0)


def causal(array, first_col, first_pos, other):
    col = lax.broadcasted_iota(jnp.int32, array.shape, 0) + first_col
    pos = lax.broadcasted_iota(jnp.int32, array.shape, 1) + first_pos
    return jnp.where(col <= pos, array, other)


def row_sums(s_ref, dp_ref, factor):
    block_len = s_ref.shape[0]
    step = min(64, block_len)
    spans = [pl.ds(c, step) for c in range(0, block_len, step)]
    top = fold(s_ref[spans[0], :], jnp.max)
    for span in spans[1:]:
        top = jnp.maximum(top, fold(s_ref[span, :], jnp.max))
    top = jnp.max(top, axis=0, keepdims=True) * factor
    total = weighted = jnp.zeros((8, block_len), F32)
    for span in spans:
        terms = jnp.exp2(s_ref[span, :] * factor - top)
        total = total + fold(terms, jnp.sum)
        weighted = weighted + fold(terms * dp_ref[span, :], jnp.sum)
    total = jnp.sum(total, axis=0, keepdims=True)
    return top, total, jnp.sum(weighted, axis=0, keepdims=True)


def local_stats_kernel(factor, blocks_here, chosen, q, do, keys, values, stats, s_buf, dp_buf):
    block_len = keys.shape[1]
    half = block_len // 2

    def per_row(row, _):
        start = row * block_len
        span = pl.ds(start, block_len)
        late = pl.ds(start + half, half)

        s_buf[:half, :] = causal(dot_nt(keys[row, :half], q[span, :]), 0, 0, -jnp.inf)
        s_buf[half:, :half] = jnp.full((half, half), -jnp.inf, F32)
        s_buf[half:, half:] = causal(dot_nt(keys[row, half:], q[late, :]), 0, 0, -jnp.inf)
        dp_buf[:half, :] = dot_nt(values[row, :half], do[span, :])
        dp_buf[half:, :half] = jnp.zeros((half, half), F32)
        dp_buf[half:, half:] = dot_nt(values[row, half:], do[late, :])
        top, total, weighted = row_sums(s_buf, dp_buf, factor)
        stats[row, 0:1, :] = top
        stats[row, 1:2, :] = total
        stats[row, 2:3, :] = weighted
        for t in range(3):
            slot = slot_of(chosen, blocks_here, row, t)

            @pl.when((slot >= 0) & (slot < blocks_here))
            def _():
                s_buf[...] = dot_nt(keys[slot], q[span, :])
                dp_buf[...] = dot_nt(values[slot], do[span, :])
                more_top, more, more_weighted = row_sums(s_buf, dp_buf, factor)
                old = stats[row, 0:1, :]
                top = jnp.maximum(old, more_top)
                scale_old = jnp.exp2(old - top)
                scale_new = jnp.exp2(more_top - top)
                stats[row, 0:1, :] = top
                stats[row, 1:2, :] = stats[row, 1:2, :] * scale_old + more * scale_new
                stats[row, 2:3, :] = stats[row, 2:3, :] * scale_old + more_weighted * scale_new

        return 0

    lax.fori_loop(0, blocks_here, per_row, 0)


def remote_kernel(
    factor, scaling, blocks_here, chips, far, near, piece, chosen, q, do, stats, *refs
):
    near_refs, far_refs, refs = refs[:2], refs[2 : 2 + 2 * chips], refs[2 + 2 * chips :]
    keep, send, final, grad_qt, rows, acc, s_buf, dp_buf, parts = refs
    place = lax.axis_index("head")
    core, chip = lax.rem(place, 2), lax.div(place, 2)
    block_len = rows.shape[2]

    def lay(kind, which):
        for i, s in enumerate(near):
            rows[kind, s] = near_refs[which][i]
        for d in range(chips):
            source = lax.rem(chip + chips - d, chips)
            span = pl.ds(pl.multiple_of(source * piece, piece), piece)
            for i, s in enumerate(far):
                rows[kind, s, span, :] = far_refs[2 * d + which][i]

    @pl.when(core == 0)
    def _():
        lay(0, 0)
        lay(1, 1)

    @pl.when(core != 0)
    def _():
        lay(0, 1)
        lay(1, 0)

    acc[...] = jnp.zeros_like(acc)

    def per_row(row, _):
        span = pl.ds(row * block_len, block_len)
        parts[0, 0:3, :] = stats[row, 0:3, :]
        for t in range(3):
            slot = slot_of(chosen, blocks_here, row, t) - blocks_here

            @pl.when(slot >= 0)
            def _():
                s_buf[t] = dot_nt(rows[0, slot], q[span, :])
                dp_buf[t] = dot_nt(rows[1, slot], do[span, :])
                top, total, weighted = row_sums(s_buf.at[t], dp_buf.at[t], factor)
                parts[t + 1, 0:1, :] = top
                parts[t + 1, 1:2, :] = total
                parts[t + 1, 2:3, :] = weighted

            @pl.when(slot < 0)
            def _():
                parts[t + 1, 0:1, :] = jnp.full((1, block_len), -jnp.inf, F32)
                parts[t + 1, 1:3, :] = jnp.zeros((2, block_len), F32)

        top = parts[0, 0:1, :]
        for t in range(3):
            top = jnp.maximum(top, parts[t + 1, 0:1, :])
        total = jnp.zeros_like(top)
        weighted = jnp.zeros_like(top)
        for t in range(4):
            scale = jnp.exp2(parts[t, 0:1, :] - top)
            total = total + scale * parts[t, 1:2, :]
            weighted = weighted + scale * parts[t, 2:3, :]
        final[row, 0:1, :] = top + jnp.log2(total)
        final[row, 1:2, :] = weighted / total
        grad_qt[row] = jnp.zeros_like(grad_qt[row])
        for t in range(3):
            slot = slot_of(chosen, blocks_here, row, t) - blocks_here

            @pl.when(slot >= 0)
            def _():
                level = final[row, 0:1, :]
                delta = final[row, 1:2, :]
                weights = jnp.exp2(s_buf[t] * factor - level)
                dscores = (weights * (dp_buf[t] - delta)).astype(BF16)
                acc[1, slot] += dot_nn(weights.astype(BF16), do[span, :])
                acc[0, slot] += dot_nn(dscores, q[span, :])
                grad_qt[row] += dot_nn(rows[0, slot].T, dscores)

        return 0

    lax.fori_loop(0, blocks_here, per_row, 0)
    keep_scale = jnp.where(core == 0, scaling, 1.0)
    send_scale = jnp.where(core == 0, 1.0, scaling)
    keep[...] = (acc[core] * keep_scale).astype(BF16)
    send[...] = (acc[1 - core] * send_scale).astype(BF16)


def local_kernel(
    factor, scaling, blocks_here, chosen, q, do, keys, values, final, grad_qt,
    keep, send, grad_q,
    acc, total_qt,
):
    core = lax.rem(lax.axis_index("head"), 2)
    block_len = keys.shape[1]
    half = block_len // 2
    acc[...] = jnp.zeros_like(acc)

    def per_row(row, _):
        start = row * block_len
        span = pl.ds(start, block_len)

        def rows_from(ref, first):
            return ref[pl.ds(start + first, block_len - first), :]

        def products(slot, c, first):
            cut = pl.ds(c, half)
            scores = dot_nt(keys[slot, cut, :], rows_from(q, first))
            return scores, dot_nt(values[slot, cut, :], rows_from(do, first))

        def pair(slot, seconds, masked):
            parts = ((0, 0), (half, seconds))
            ready = [products(slot, c, first) for c, first in parts]
            sides = []
            for (c, first), (scores, dprobs) in zip(parts, ready):
                weights = jnp.exp2(scores * factor - final[row, 0:1, first:])
                if masked:
                    weights = causal(weights, c, first, 0.0)
                dscores = (weights * (dprobs - final[row, 1:2, first:])).astype(BF16)
                sides.append((weights.astype(BF16), dscores))
            for (c, first), (weights, dscores) in zip(parts, sides):
                cut = pl.ds(c, half)
                acc[1, slot, cut, :] += dot_nn(weights, rows_from(do, first))
                acc[0, slot, cut, :] += dot_nn(dscores, rows_from(q, first))
                total_qt[:, first:] += dot_nn(keys[slot, cut, :].T, dscores)

        total_qt[...] = grad_qt[row]
        pair(row, half, True)
        for t in range(3):
            slot = slot_of(chosen, blocks_here, row, t)

            @pl.when((slot >= 0) & (slot < blocks_here))
            def _():
                pair(slot, 0, False)

        grad_q[span, :] = (total_qt[...].T * scaling).astype(BF16)
        return 0

    lax.fori_loop(0, blocks_here, per_row, 0)
    keep_scale = jnp.where(core == 0, scaling, 1.0)
    send_scale = jnp.where(core == 0, 1.0, scaling)
    keep[...] = (acc[core] * keep_scale).astype(BF16)
    send[...] = (acc[1 - core] * send_scale).astype(BF16)


def far_return_kernel(far, asked, *refs):
    back, acc = refs[:-1], refs[-1]
    acc[...] = jnp.zeros_like(acc)
    for i, s in enumerate(far):
        slot = asked[s] - 1

        @pl.when(slot >= 0)
        def _():
            acc[slot] += back[i][...].astype(F32)


def owner_kernel(returned, mine, *refs):
    others, out = refs[:-1], refs[-1]
    total = mine[...] + returned[...]
    for part in others:
        total = total + part[...].astype(F32)
    out[...] = total.astype(BF16)


def spread_kernel(chips, piece, *refs):
    pieces, (grad_k, grad_v) = refs[: 2 * chips], refs[2 * chips :]
    place = lax.axis_index("head")
    core, chip = lax.rem(place, 2), lax.div(place, 2)

    def lay(out, which):
        for d in range(chips):
            source = lax.rem(chip + chips - d, chips)
            span = pl.ds(pl.multiple_of(source * piece, piece), piece)
            out[:, span, :] = pieces[2 * d + which][...]

    @pl.when(core == 0)
    def _():
        lay(grad_k, 0)
        lay(grad_v, 1)

    @pl.when(core != 0)
    def _():
        lay(grad_k, 1)
        lay(grad_v, 0)


def params(size):
    return pltpu.CompilerParams(vmem_limit_bytes=min(size + 12 * 1024 * 1024, VMEM_LIMIT))


def body(queries, keys, values, dout, selected):
    tok_rows, head_count, feature = queries.shape
    blocks_here = selected.shape[0]
    block_len = tok_rows // blocks_here
    ctx_count = lax.axis_size("ctx")
    heads = lax.axis_size("head")
    chips = heads // 2
    piece = block_len // chips
    scaling = 1.0 / math.sqrt(feature)
    factor = scaling * math.log2(math.e)
    shifts = ctx_count - 1
    far = [s for s in range(shifts) if 2 * (s + 1) >= ctx_count]
    near = [s for s in range(shifts) if 2 * (s + 1) < ctx_count]

    q2 = queries.reshape(tok_rows, feature)
    do2 = dout.reshape(tok_rows, feature)
    key_blocks = keys.reshape(blocks_here, block_len, feature)
    value_blocks = values.reshape(blocks_here, block_len, feature)
    remote_shape = (shifts, block_len, feature)
    local_shape = (blocks_here, block_len, feature)

    smem = pl.BlockSpec(memory_space=pltpu.SMEM)
    whole = pl.BlockSpec(memory_space=pltpu.VMEM)
    hbm = pl.BlockSpec(memory_space=pltpu.HBM)
    stat_type = jax.ShapeDtypeStruct((blocks_here, 8, block_len), F32)
    far_type = jax.ShapeDtypeStruct(remote_shape, BF16)
    own_type = jax.ShapeDtypeStruct(local_shape, BF16)
    block_type = jax.ShapeDtypeStruct((block_len, feature), BF16)
    piece_type = jax.ShapeDtypeStruct((piece, feature), BF16)
    qt_type = jax.ShapeDtypeStruct((blocks_here, feature, block_len), F32)
    pair_flops = 2 * block_len * block_len * feature
    block_bytes = block_len * feature * 2
    pair_bytes = block_len * block_len * 4

    def pieces_type(count, dtype):
        return jax.ShapeDtypeStruct((count, piece, feature), dtype)

    def cost(matmuls, size):
        return pl.CostEstimate(
            flops=matmuls * pair_flops, bytes_accessed=size, transcendentals=matmuls * block_len**2
        )

    def swap(array):
        return lax.ppermute(array, "head", [(h, h ^ 1) for h in range(heads)])

    def to_chip(array, d):
        return lax.ppermute(array, "head", [(h, (h + 2 * d) % heads) for h in range(heads)])

    def to_owner(array, s):
        return lax.ppermute(array, "ctx", [(c, c - s - 1) for c in range(s + 1, ctx_count)])

    def to_reader(array, s):
        return lax.ppermute(array, "ctx", [(c - s - 1, c) for c in range(s + 1, ctx_count)])

    everyone = lax.all_gather(selected.reshape(3 * blocks_here), "ctx")
    asked, *sent = pl.pallas_call(
        functools.partial(pick_kernel, blocks_here, ctx_count, chips, far, piece),
        in_specs=[smem, hbm, hbm],
        out_specs=[smem] + [whole] * shifts,
        out_shape=[jax.ShapeDtypeStruct((shifts,), jnp.int32)]
        + [piece_type if s in far else block_type for s in range(shifts)],
        scratch_shapes=[pltpu.SemaphoreType.DMA((shifts,))],
        name="pick_rows",
    )(everyone, key_blocks, value_blocks)

    far_mine = jnp.stack([to_reader(sent[s], s) for s in far])
    near_parts = [to_reader(sent[s], s) for s in near]
    far_mine, chosen = lax.optimization_barrier((far_mine, selected))
    far_more = [to_chip(far_mine, d) for d in range(1, chips)]
    stats = pl.pallas_call(
        functools.partial(local_stats_kernel, factor, blocks_here),
        in_specs=[smem] + [whole] * 4,
        out_specs=whole,
        out_shape=stat_type,
        scratch_shapes=[pltpu.VMEM((block_len, block_len), F32)] * 2,
        compiler_params=params(4 * blocks_here * block_bytes + 2 * pair_bytes),
        cost_estimate=cost(30, 4 * tok_rows * feature * 2),
        name="local_stats",
    )(chosen, q2, do2, key_blocks, value_blocks)
    near_parts, far_held, stats = lax.optimization_barrier((near_parts, far_mine, stats))
    near_mine = jnp.stack(near_parts)
    row_sets = [near_mine, swap(near_mine), far_held, swap(far_held)]
    for part in far_more:
        row_sets += [part, swap(part)]

    keep_far, send_far, final, grad_qt = pl.pallas_call(
        functools.partial(remote_kernel, factor, scaling, blocks_here, chips, far, near, piece),
        in_specs=[smem] + [whole] * (3 + len(row_sets)),
        out_specs=[whole] * 4,
        out_shape=[far_type, far_type, stat_type, qt_type],
        scratch_shapes=[
            pltpu.VMEM((2,) + remote_shape, BF16),
            pltpu.VMEM((2,) + remote_shape, F32),
            pltpu.VMEM((3, block_len, block_len), F32),
            pltpu.VMEM((3, block_len, block_len), F32),
            pltpu.VMEM((4, 8, block_len), F32),
        ],
        compiler_params=params((10 * shifts + 4 * blocks_here) * block_bytes + 6 * pair_bytes),
        cost_estimate=cost(60, 8 * tok_rows * feature * 2),
        name="remote_pairs",
    )(chosen, q2, do2, stats, *row_sets)

    def head_sums(mine, parts, count):
        return pl.pallas_call(
            functools.partial(head_sum_kernel, count),
            in_specs=[whole] * (1 + len(parts)),
            out_specs=[whole] * count,
            out_shape=[piece_type] * count,
            compiler_params=params(4 * count * block_bytes),
            name="head_sum",
        )(mine, *parts)

    chip_far = pl.pallas_call(
        functools.partial(chip_sum_kernel, chips, piece, far, near),
        in_specs=[whole, whole],
        out_specs=[whole] * (chips + len(near)),
        out_shape=[pieces_type(len(far), F32)]
        + [pieces_type(len(far), BF16)] * (chips - 1)
        + [block_type] * len(near),
        compiler_params=params(4 * shifts * block_bytes),
        name="chip_sum",
    )(keep_far, swap(send_far))
    chip_far, final = lax.optimization_barrier((chip_far, final))
    far_sums, near_sums = chip_far[:chips], chip_far[chips:]
    far_parts = [to_chip(far_sums[d], d) for d in range(1, chips)]
    near_back = [to_owner(near_sums[i], s) for i, s in enumerate(near)]
    keep_own, send_own, grad_q = pl.pallas_call(
        functools.partial(local_kernel, factor, scaling, blocks_here),
        in_specs=[smem] + [whole] * 6,
        out_specs=[whole] * 3,
        out_shape=[own_type, own_type, jax.ShapeDtypeStruct((tok_rows, feature), BF16)],
        scratch_shapes=[
            pltpu.VMEM((2,) + local_shape, F32),
            pltpu.VMEM((feature, block_len), F32),
        ],
        compiler_params=params(14 * blocks_here * block_bytes),
        cost_estimate=cost(60, 8 * tok_rows * feature * 2),
        name="local_pairs",
    )(chosen, q2, do2, key_blocks, value_blocks, final, grad_qt)
    far_parts, near_back, keep_own, send_own = lax.optimization_barrier(
        (far_parts, near_back, keep_own, send_own)
    )
    own_sums = pl.pallas_call(
        functools.partial(own_sum_kernel, chips, piece, near),
        in_specs=[smem] + [whole] * (2 + len(near)),
        out_specs=[whole] * chips,
        out_shape=[pieces_type(blocks_here, F32)]
        + [pieces_type(blocks_here, BF16)] * (chips - 1),
        scratch_shapes=[pltpu.VMEM(local_shape, F32)],
        compiler_params=params((8 * blocks_here + len(near)) * block_bytes),
        name="own_sum",
    )(asked, keep_own, swap(send_own), *near_back)
    own_parts = [to_chip(own_sums[d], d) for d in range(1, chips)]
    far_out = head_sums(far_sums[0], far_parts, len(far))
    far_back = [to_owner(far_out[i], s) for i, s in enumerate(far)]
    returned = pl.pallas_call(
        functools.partial(far_return_kernel, far),
        in_specs=[smem] + [whole] * len(far),
        out_specs=whole,
        out_shape=pieces_type(blocks_here, F32),
        compiler_params=params((2 * blocks_here + len(far)) * block_bytes),
        cost_estimate=cost(600, 8 * tok_rows * feature * 2),
        name="far_returns",
    )(asked, *far_back)
    mine = pl.pallas_call(
        owner_kernel,
        in_specs=[whole] * (1 + chips),
        out_specs=whole,
        out_shape=pieces_type(blocks_here, BF16),
        compiler_params=params(6 * blocks_here * block_bytes),
        name="owner_sum",
    )(returned, own_sums[0], *own_parts)
    spread = [mine, swap(mine)]
    for d in range(1, chips):
        part = to_chip(mine, d)
        spread += [part, swap(part)]
    grad_keys, grad_values = pl.pallas_call(
        functools.partial(spread_kernel, chips, piece),
        in_specs=[whole] * len(spread),
        out_specs=[whole] * 2,
        out_shape=[own_type] * 2,
        compiler_params=params(4 * blocks_here * block_bytes),
        name="spread",
    )(*spread)
    return (
        grad_q.reshape(tok_rows, head_count, feature),
        grad_keys.reshape(tok_rows, feature),
        grad_values.reshape(tok_rows, feature),
    )


def solution(mesh):
    return jax.shard_map(
        body,
        mesh=mesh,
        in_specs=(
            P("ctx", "head", None),
            P("ctx", None),
            P("ctx", None),
            P("ctx", "head", None),
            P("ctx", None),
        ),
        out_specs=(P("ctx", "head", None), P("ctx", None), P("ctx", None)),
        check_vma=False,
    )
```

```python
import functools
import math

import jax
import jax.numpy as jnp
from jax import lax
from jax.experimental import pallas as pl
from jax.experimental.pallas import tpu as pltpu
from jax.sharding import PartitionSpec as P

F32 = jnp.float32
BF16 = jnp.bfloat16
VMEM_LIMIT = 56 * 1024 * 1024


def dot_nt(a, b):
    return lax.dot_general(a, b, (((1,), (1,)), ((), ())), preferred_element_type=F32)


def dot_nn(a, b):
    return lax.dot_general(a, b, (((1,), (0,)), ((), ())), preferred_element_type=F32)


def slot_of(chosen, blocks_here, row, t):
    ctx_self = lax.axis_index("ctx")
    entry = chosen[row, t]
    owner = lax.div(entry, jnp.int32(blocks_here))
    apart = ctx_self - owner
    slot = jnp.where(apart == 0, entry - owner * blocks_here, blocks_here + apart - 1)
    return jnp.where(entry != ctx_self * blocks_here + row, slot, -1)


def pick_kernel(blocks_here, count, chips, far, piece, chosen, keys, values, asked, *refs):
    outs, sems = refs[:-1], refs[-1]
    ctx_self = lax.axis_index("ctx")
    place = lax.axis_index("head")
    core, chip = lax.rem(place, 2), lax.div(place, 2)
    first = ctx_self * blocks_here
    span = pl.ds(pl.multiple_of(chip * piece, piece), piece)

    def copy(source, s, slot):
        rows = source.at[slot, span, :] if s in far else source.at[slot]
        return pltpu.make_async_copy(rows, outs[s], sems.at[s])

    for s in range(count - 1):
        peer = ctx_self + s + 1
        near = jnp.minimum(peer, count - 1)
        found = jnp.int32(0)
        for row in range(blocks_here):
            for t in range(3):
                entry = chosen[near, row * 3 + t]
                hit = (entry >= first) & (entry < first + blocks_here)
                found = jnp.where(hit, entry - first + 1, found)
        found = jnp.where(peer < count, found, 0)
        asked[s] = found
        slot = jnp.maximum(found - 1, 0)

        @pl.when(core == 0)
        def _():
            copy(keys, s, slot).start()

        @pl.when(core != 0)
        def _():
            copy(values, s, slot).start()

    for s in range(count - 1):
        copy(keys, s, 0).wait()


def chip_sum_kernel(chips, piece, far, near, mine, theirs, *outs):
    chip = lax.div(lax.axis_index("head"), 2)
    for d in range(chips):
        target = lax.rem(chip + d, chips)
        span = pl.ds(pl.multiple_of(target * piece, piece), piece)
        for i, s in enumerate(far):
            total = mine[s, span, :].astype(F32) + theirs[s, span, :].astype(F32)
            outs[d][i] = total.astype(outs[d].dtype)
    for i, s in enumerate(near):
        outs[chips + i][...] = (mine[s].astype(F32) + theirs[s].astype(F32)).astype(BF16)


def own_sum_kernel(chips, piece, near, asked, mine, theirs, *refs):
    back, outs, acc = refs[: len(near)], refs[len(near) : -1], refs[-1]
    chip = lax.div(lax.axis_index("head"), 2)
    acc[...] = mine[...].astype(F32) + theirs[...].astype(F32)
    for i, s in enumerate(near):
        slot = asked[s] - 1

        @pl.when(slot >= 0)
        def _():
            acc[slot] += back[i][...].astype(F32)

    for d in range(chips):
        target = lax.rem(chip + d, chips)
        span = pl.ds(pl.multiple_of(target * piece, piece), piece)
        outs[d][...] = acc[:, span, :].astype(outs[d].dtype)


def head_sum_kernel(count, mine, *refs):
    parts, outs = refs[: len(refs) - count], refs[len(refs) - count :]
    for i in range(count):
        total = mine[i]
        for part in parts:
            total = total + part[i].astype(F32)
        outs[i][...] = total.astype(BF16)


def fold(array, reduce):
    rows, lanes = array.shape
    return reduce(array.reshape(rows // 8, 8, lanes), axis=0)


def causal(array, first_col, first_pos, other):
    col = lax.broadcasted_iota(jnp.int32, array.shape, 0) + first_col
    pos = lax.broadcasted_iota(jnp.int32, array.shape, 1) + first_pos
    return jnp.where(col <= pos, array, other)


def row_sums(s_ref, dp_ref, factor):
    block_len = s_ref.shape[0]
    step = min(64, block_len)
    spans = [pl.ds(c, step) for c in range(0, block_len, step)]
    top = fold(s_ref[spans[0], :], jnp.max)
    for span in spans[1:]:
        top = jnp.maximum(top, fold(s_ref[span, :], jnp.max))
    top = jnp.max(top, axis=0, keepdims=True) * factor
    total = weighted = jnp.zeros((8, block_len), F32)
    for span in spans:
        terms = jnp.exp2(s_ref[span, :] * factor - top)
        total = total + fold(terms, jnp.sum)
        weighted = weighted + fold(terms * dp_ref[span, :], jnp.sum)
    total = jnp.sum(total, axis=0, keepdims=True)
    return top, total, jnp.sum(weighted, axis=0, keepdims=True)


def local_stats_kernel(factor, blocks_here, chosen, q, do, keys, values, stats, s_buf, dp_buf):
    block_len = keys.shape[1]
    half = block_len // 2

    def per_row(row, _):
        start = row * block_len
        span = pl.ds(start, block_len)
        late = pl.ds(start + half, half)

        s_buf[:half, :] = causal(dot_nt(keys[row, :half], q[span, :]), 0, 0, -jnp.inf)
        s_buf[half:, :half] = jnp.full((half, half), -jnp.inf, F32)
        s_buf[half:, half:] = causal(dot_nt(keys[row, half:], q[late, :]), 0, 0, -jnp.inf)
        dp_buf[:half, :] = dot_nt(values[row, :half], do[span, :])
        dp_buf[half:, :half] = jnp.zeros((half, half), F32)
        dp_buf[half:, half:] = dot_nt(values[row, half:], do[late, :])
        top, total, weighted = row_sums(s_buf, dp_buf, factor)
        stats[row, 0:1, :] = top
        stats[row, 1:2, :] = total
        stats[row, 2:3, :] = weighted
        for t in range(3):
            slot = slot_of(chosen, blocks_here, row, t)

            @pl.when((slot >= 0) & (slot < blocks_here))
            def _():
                s_buf[...] = dot_nt(keys[slot], q[span, :])
                dp_buf[...] = dot_nt(values[slot], do[span, :])
                more_top, more, more_weighted = row_sums(s_buf, dp_buf, factor)
                old = stats[row, 0:1, :]
                top = jnp.maximum(old, more_top)
                scale_old = jnp.exp2(old - top)
                scale_new = jnp.exp2(more_top - top)
                stats[row, 0:1, :] = top
                stats[row, 1:2, :] = stats[row, 1:2, :] * scale_old + more * scale_new
                stats[row, 2:3, :] = stats[row, 2:3, :] * scale_old + more_weighted * scale_new

        return 0

    lax.fori_loop(0, blocks_here, per_row, 0)


def remote_kernel(
    factor, scaling, blocks_here, chips, far, near, piece, chosen, q, do, stats, *refs
):
    near_refs, far_refs, refs = refs[:2], refs[2 : 2 + 2 * chips], refs[2 + 2 * chips :]
    keep, send, final, grad_qt, rows, acc, s_buf, dp_buf, parts = refs
    place = lax.axis_index("head")
    core, chip = lax.rem(place, 2), lax.div(place, 2)
    block_len = rows.shape[2]

    def lay(kind, which):
        for i, s in enumerate(near):
            rows[kind, s] = near_refs[which][i]
        for d in range(chips):
            source = lax.rem(chip + chips - d, chips)
            span = pl.ds(pl.multiple_of(source * piece, piece), piece)
            for i, s in enumerate(far):
                rows[kind, s, span, :] = far_refs[2 * d + which][i]

    @pl.when(core == 0)
    def _():
        lay(0, 0)
        lay(1, 1)

    @pl.when(core != 0)
    def _():
        lay(0, 1)
        lay(1, 0)

    acc[...] = jnp.zeros_like(acc)

    def per_row(row, _):
        span = pl.ds(row * block_len, block_len)
        parts[0, 0:3, :] = stats[row, 0:3, :]
        for t in range(3):
            slot = slot_of(chosen, blocks_here, row, t) - blocks_here

            @pl.when(slot >= 0)
            def _():
                s_buf[t] = dot_nt(rows[0, slot], q[span, :])
                dp_buf[t] = dot_nt(rows[1, slot], do[span, :])
                top, total, weighted = row_sums(s_buf.at[t], dp_buf.at[t], factor)
                parts[t + 1, 0:1, :] = top
                parts[t + 1, 1:2, :] = total
                parts[t + 1, 2:3, :] = weighted

            @pl.when(slot < 0)
            def _():
                parts[t + 1, 0:1, :] = jnp.full((1, block_len), -jnp.inf, F32)
                parts[t + 1, 1:3, :] = jnp.zeros((2, block_len), F32)

        top = parts[0, 0:1, :]
        for t in range(3):
            top = jnp.maximum(top, parts[t + 1, 0:1, :])
        total = jnp.zeros_like(top)
        weighted = jnp.zeros_like(top)
        for t in range(4):
            scale = jnp.exp2(parts[t, 0:1, :] - top)
            total = total + scale * parts[t, 1:2, :]
            weighted = weighted + scale * parts[t, 2:3, :]
        final[row, 0:1, :] = top + jnp.log2(total)
        final[row, 1:2, :] = weighted / total
        grad_qt[row] = jnp.zeros_like(grad_qt[row])
        for t in range(3):
            slot = slot_of(chosen, blocks_here, row, t) - blocks_here

            @pl.when(slot >= 0)
            def _():
                level = final[row, 0:1, :]
                delta = final[row, 1:2, :]
                weights = jnp.exp2(s_buf[t] * factor - level)
                dscores = (weights * (dp_buf[t] - delta)).astype(BF16)
                acc[1, slot] += dot_nn(weights.astype(BF16), do[span, :])
                acc[0, slot] += dot_nn(dscores, q[span, :])
                grad_qt[row] += dot_nn(rows[0, slot].T, dscores)

        return 0

    lax.fori_loop(0, blocks_here, per_row, 0)
    keep_scale = jnp.where(core == 0, scaling, 1.0)
    send_scale = jnp.where(core == 0, 1.0, scaling)
    keep[...] = (acc[core] * keep_scale).astype(BF16)
    send[...] = (acc[1 - core] * send_scale).astype(BF16)


def local_rows(factor, scaling, blocks_here, rows, args, grad_q, acc, total_qt):
    chosen, q, do, keys, values, final, grad_qt = args
    block_len = keys.shape[1]
    half = block_len // 2

    def per_row(row, _):
        start = row * block_len
        span = pl.ds(start, block_len)

        def rows_from(ref, first):
            return ref[pl.ds(start + first, block_len - first), :]

        def products(slot, c, first):
            cut = pl.ds(c, half)
            scores = dot_nt(keys[slot, cut, :], rows_from(q, first))
            return scores, dot_nt(values[slot, cut, :], rows_from(do, first))

        def pair(slot, seconds, masked):
            parts = ((0, 0), (half, seconds))
            ready = [products(slot, c, first) for c, first in parts]
            sides = []
            for (c, first), (scores, dprobs) in zip(parts, ready):
                weights = jnp.exp2(scores * factor - final[row, 0:1, first:])
                if masked:
                    weights = causal(weights, c, first, 0.0)
                dscores = (weights * (dprobs - final[row, 1:2, first:])).astype(BF16)
                sides.append((weights.astype(BF16), dscores))
            for (c, first), (weights, dscores) in zip(parts, sides):
                cut = pl.ds(c, half)
                acc[1, slot, cut, :] += dot_nn(weights, rows_from(do, first))
                acc[0, slot, cut, :] += dot_nn(dscores, rows_from(q, first))
                total_qt[:, first:] += dot_nn(keys[slot, cut, :].T, dscores)

        total_qt[...] = grad_qt[row]
        pair(row, half, True)
        for t in range(3):
            slot = slot_of(chosen, blocks_here, row, t)

            @pl.when((slot >= 0) & (slot < blocks_here))
            def _():
                pair(slot, 0, False)

        grad_q[span, :] = (total_qt[...].T * scaling).astype(BF16)
        return 0

    lax.fori_loop(rows[0], rows[1], per_row, 0)


def early_kernel(factor, scaling, blocks_here, *refs):
    args, (acc, grad_q, total_qt) = refs[:7], refs[7:]
    acc[...] = jnp.zeros_like(acc)
    rows = (0, blocks_here // 2)
    local_rows(factor, scaling, blocks_here, rows, args, grad_q, acc, total_qt)


def late_kernel(factor, scaling, blocks_here, *refs):
    args, (acc_in, grad_in, keep, send, grad_q, acc, total_qt) = refs[:7], refs[7:]
    core = lax.rem(lax.axis_index("head"), 2)
    acc[...] = acc_in[...]
    grad_q[: grad_in.shape[0], :] = grad_in[...]
    rows = (blocks_here // 2, blocks_here)
    local_rows(factor, scaling, blocks_here, rows, args, grad_q, acc, total_qt)
    keep_scale = jnp.where(core == 0, scaling, 1.0)
    send_scale = jnp.where(core == 0, 1.0, scaling)
    keep[...] = (acc[core] * keep_scale).astype(BF16)
    send[...] = (acc[1 - core] * send_scale).astype(BF16)


def far_return_kernel(far, asked, *refs):
    back, acc = refs[:-1], refs[-1]
    acc[...] = jnp.zeros_like(acc)
    for i, s in enumerate(far):
        slot = asked[s] - 1

        @pl.when(slot >= 0)
        def _():
            acc[slot] += back[i][...].astype(F32)


def owner_kernel(returned, mine, *refs):
    others, out = refs[:-1], refs[-1]
    total = mine[...] + returned[...]
    for part in others:
        total = total + part[...].astype(F32)
    out[...] = total.astype(BF16)


def spread_kernel(chips, piece, *refs):
    pieces, (grad_k, grad_v) = refs[: 2 * chips], refs[2 * chips :]
    place = lax.axis_index("head")
    core, chip = lax.rem(place, 2), lax.div(place, 2)

    def lay(out, which):
        for d in range(chips):
            source = lax.rem(chip + chips - d, chips)
            span = pl.ds(pl.multiple_of(source * piece, piece), piece)
            out[:, span, :] = pieces[2 * d + which][...]

    @pl.when(core == 0)
    def _():
        lay(grad_k, 0)
        lay(grad_v, 1)

    @pl.when(core != 0)
    def _():
        lay(grad_k, 1)
        lay(grad_v, 0)


def params(size):
    return pltpu.CompilerParams(vmem_limit_bytes=min(size + 12 * 1024 * 1024, VMEM_LIMIT))


def body(queries, keys, values, dout, selected):
    tok_rows, head_count, feature = queries.shape
    blocks_here = selected.shape[0]
    block_len = tok_rows // blocks_here
    ctx_count = lax.axis_size("ctx")
    heads = lax.axis_size("head")
    chips = heads // 2
    piece = block_len // chips
    scaling = 1.0 / math.sqrt(feature)
    factor = scaling * math.log2(math.e)
    shifts = ctx_count - 1
    far = [s for s in range(shifts) if 2 * (s + 1) >= ctx_count]
    near = [s for s in range(shifts) if 2 * (s + 1) < ctx_count]

    q2 = queries.reshape(tok_rows, feature)
    do2 = dout.reshape(tok_rows, feature)
    key_blocks = keys.reshape(blocks_here, block_len, feature)
    value_blocks = values.reshape(blocks_here, block_len, feature)
    remote_shape = (shifts, block_len, feature)
    local_shape = (blocks_here, block_len, feature)

    smem = pl.BlockSpec(memory_space=pltpu.SMEM)
    whole = pl.BlockSpec(memory_space=pltpu.VMEM)
    hbm = pl.BlockSpec(memory_space=pltpu.HBM)
    stat_type = jax.ShapeDtypeStruct((blocks_here, 8, block_len), F32)
    far_type = jax.ShapeDtypeStruct(remote_shape, BF16)
    own_type = jax.ShapeDtypeStruct(local_shape, BF16)
    block_type = jax.ShapeDtypeStruct((block_len, feature), BF16)
    piece_type = jax.ShapeDtypeStruct((piece, feature), BF16)
    qt_type = jax.ShapeDtypeStruct((blocks_here, feature, block_len), F32)
    pair_flops = 2 * block_len * block_len * feature
    block_bytes = block_len * feature * 2
    pair_bytes = block_len * block_len * 4

    def pieces_type(count, dtype):
        return jax.ShapeDtypeStruct((count, piece, feature), dtype)

    def cost(matmuls, size):
        return pl.CostEstimate(
            flops=matmuls * pair_flops, bytes_accessed=size, transcendentals=matmuls * block_len**2
        )

    def swap(array):
        return lax.ppermute(array, "head", [(h, h ^ 1) for h in range(heads)])

    def to_chip(array, d):
        return lax.ppermute(array, "head", [(h, (h + 2 * d) % heads) for h in range(heads)])

    def to_owner(array, s):
        return lax.ppermute(array, "ctx", [(c, c - s - 1) for c in range(s + 1, ctx_count)])

    def to_reader(array, s):
        return lax.ppermute(array, "ctx", [(c - s - 1, c) for c in range(s + 1, ctx_count)])

    everyone = lax.all_to_all(
        jnp.broadcast_to(selected.reshape(1, 3 * blocks_here), (ctx_count, 3 * blocks_here)),
        "ctx", split_axis=0, concat_axis=0, tiled=True,
    )
    asked, *sent = pl.pallas_call(
        functools.partial(pick_kernel, blocks_here, ctx_count, chips, far, piece),
        in_specs=[smem, hbm, hbm],
        out_specs=[smem] + [whole] * shifts,
        out_shape=[jax.ShapeDtypeStruct((shifts,), jnp.int32)]
        + [piece_type if s in far else block_type for s in range(shifts)],
        scratch_shapes=[pltpu.SemaphoreType.DMA((shifts,))],
        name="pick_rows",
    )(everyone, key_blocks, value_blocks)

    far_mine = jnp.stack([to_reader(sent[s], s) for s in far])
    near_parts = [to_reader(sent[s], s) for s in near]
    far_mine, chosen = lax.optimization_barrier((far_mine, selected))
    far_more = [to_chip(far_mine, d) for d in range(1, chips)]
    stats = pl.pallas_call(
        functools.partial(local_stats_kernel, factor, blocks_here),
        in_specs=[smem] + [whole] * 4,
        out_specs=whole,
        out_shape=stat_type,
        scratch_shapes=[pltpu.VMEM((block_len, block_len), F32)] * 2,
        compiler_params=params(4 * blocks_here * block_bytes + 2 * pair_bytes),
        cost_estimate=cost(30, 4 * tok_rows * feature * 2),
        name="local_stats",
    )(chosen, q2, do2, key_blocks, value_blocks)
    near_parts, far_held, stats = lax.optimization_barrier((near_parts, far_mine, stats))
    near_mine = jnp.stack(near_parts)
    row_sets = [near_mine, swap(near_mine), far_held, swap(far_held)]
    for part in far_more:
        row_sets += [part, swap(part)]

    keep_far, send_far, final, grad_qt = pl.pallas_call(
        functools.partial(remote_kernel, factor, scaling, blocks_here, chips, far, near, piece),
        in_specs=[smem] + [whole] * (3 + len(row_sets)),
        out_specs=[whole] * 4,
        out_shape=[far_type, far_type, stat_type, qt_type],
        scratch_shapes=[
            pltpu.VMEM((2,) + remote_shape, BF16),
            pltpu.VMEM((2,) + remote_shape, F32),
            pltpu.VMEM((3, block_len, block_len), F32),
            pltpu.VMEM((3, block_len, block_len), F32),
            pltpu.VMEM((4, 8, block_len), F32),
        ],
        compiler_params=params((10 * shifts + 4 * blocks_here) * block_bytes + 6 * pair_bytes),
        cost_estimate=cost(60, 8 * tok_rows * feature * 2),
        name="remote_pairs",
    )(chosen, q2, do2, stats, *row_sets)

    def head_sums(mine, parts, count):
        return pl.pallas_call(
            functools.partial(head_sum_kernel, count),
            in_specs=[whole] * (1 + len(parts)),
            out_specs=[whole] * count,
            out_shape=[piece_type] * count,
            compiler_params=params(4 * count * block_bytes),
            name="head_sum",
        )(mine, *parts)

    chip_far = pl.pallas_call(
        functools.partial(chip_sum_kernel, chips, piece, far, near),
        in_specs=[whole, whole],
        out_specs=[whole] * (chips + len(near)),
        out_shape=[pieces_type(len(far), F32)]
        + [pieces_type(len(far), BF16)] * (chips - 1)
        + [block_type] * len(near),
        compiler_params=params(4 * shifts * block_bytes),
        name="chip_sum",
    )(keep_far, swap(send_far))
    chip_far, final = lax.optimization_barrier((chip_far, final))
    far_sums, near_sums = chip_far[:chips], chip_far[chips:]
    own_args = (chosen, q2, do2, key_blocks, value_blocks, final, grad_qt)
    acc_type = jax.ShapeDtypeStruct((2,) + local_shape, F32)
    early_type = jax.ShapeDtypeStruct((blocks_here // 2 * block_len, feature), BF16)
    early, early_q = pl.pallas_call(
        functools.partial(early_kernel, factor, scaling, blocks_here),
        in_specs=[smem] + [whole] * 6,
        out_specs=[whole] * 2,
        out_shape=[acc_type, early_type],
        scratch_shapes=[pltpu.VMEM((feature, block_len), F32)],
        compiler_params=params(14 * blocks_here * block_bytes),
        cost_estimate=cost(30, 8 * tok_rows * feature * 2),
        name="early_local_pairs",
    )(*own_args)
    near_sums, early = lax.optimization_barrier((near_sums, early))
    near_back = [to_owner(near_sums[i], s) for i, s in enumerate(near)]
    far_parts = [to_chip(far_sums[d], d) for d in range(1, chips)]
    keep_own, send_own, grad_q = pl.pallas_call(
        functools.partial(late_kernel, factor, scaling, blocks_here),
        in_specs=[smem] + [whole] * 8,
        out_specs=[whole] * 3,
        out_shape=[own_type, own_type, jax.ShapeDtypeStruct((tok_rows, feature), BF16)],
        scratch_shapes=[pltpu.VMEM(acc_type.shape, F32), pltpu.VMEM((feature, block_len), F32)],
        compiler_params=params(18 * blocks_here * block_bytes),
        cost_estimate=cost(30, 8 * tok_rows * feature * 2),
        name="late_local_pairs",
    )(*own_args, early, early_q)
    near_back, far_parts, keep_own, send_own = lax.optimization_barrier(
        (near_back, far_parts, keep_own, send_own)
    )
    own_sums = pl.pallas_call(
        functools.partial(own_sum_kernel, chips, piece, near),
        in_specs=[smem] + [whole] * (2 + len(near)),
        out_specs=[whole] * chips,
        out_shape=[pieces_type(blocks_here, F32)]
        + [pieces_type(blocks_here, BF16)] * (chips - 1),
        scratch_shapes=[pltpu.VMEM(local_shape, F32)],
        compiler_params=params((8 * blocks_here + len(near)) * block_bytes),
        name="own_sum",
    )(asked, keep_own, swap(send_own), *near_back)
    own_parts = [to_chip(own_sums[d], d) for d in range(1, chips)]
    far_out = head_sums(far_sums[0], far_parts, len(far))
    far_back = [to_owner(far_out[i], s) for i, s in enumerate(far)]
    returned = pl.pallas_call(
        functools.partial(far_return_kernel, far),
        in_specs=[smem] + [whole] * len(far),
        out_specs=whole,
        out_shape=pieces_type(blocks_here, F32),
        compiler_params=params((2 * blocks_here + len(far)) * block_bytes),
        cost_estimate=cost(600, 8 * tok_rows * feature * 2),
        name="far_returns",
    )(asked, *far_back)
    mine = pl.pallas_call(
        owner_kernel,
        in_specs=[whole] * (1 + chips),
        out_specs=whole,
        out_shape=pieces_type(blocks_here, BF16),
        compiler_params=params(6 * blocks_here * block_bytes),
        name="owner_sum",
    )(returned, own_sums[0], *own_parts)
    spread = [mine, swap(mine)]
    for d in range(1, chips):
        part = to_chip(mine, d)
        spread += [part, swap(part)]
    grad_keys, grad_values = pl.pallas_call(
        functools.partial(spread_kernel, chips, piece),
        in_specs=[whole] * len(spread),
        out_specs=[whole] * 2,
        out_shape=[own_type] * 2,
        compiler_params=params(4 * blocks_here * block_bytes),
        name="spread",
    )(*spread)
    return (
        grad_q.reshape(tok_rows, head_count, feature),
        grad_keys.reshape(tok_rows, feature),
        grad_values.reshape(tok_rows, feature),
    )


def solution(mesh):
    return jax.shard_map(
        body,
        mesh=mesh,
        in_specs=(
            P("ctx", "head", None),
            P("ctx", None),
            P("ctx", None),
            P("ctx", "head", None),
            P("ctx", None),
        ),
        out_specs=(P("ctx", "head", None), P("ctx", None), P("ctx", None)),
        check_vma=False,
    )
```

```python
import functools
import math

import jax
import jax.numpy as jnp
from jax import lax
from jax.experimental import pallas as pl
from jax.experimental.pallas import tpu as pltpu
from jax.sharding import PartitionSpec as P

F32 = jnp.float32
BF16 = jnp.bfloat16
VMEM_LIMIT = 56 * 1024 * 1024


def dot_nt(a, b):
    return lax.dot_general(a, b, (((1,), (1,)), ((), ())), preferred_element_type=F32)


def dot_nn(a, b):
    return lax.dot_general(a, b, (((1,), (0,)), ((), ())), preferred_element_type=F32)


def slot_of(chosen, blocks_here, row, t):
    ctx_self = lax.axis_index("ctx")
    entry = chosen[row, t]
    owner = lax.div(entry, jnp.int32(blocks_here))
    apart = ctx_self - owner
    slot = jnp.where(apart == 0, entry - owner * blocks_here, blocks_here + apart - 1)
    return jnp.where(entry != ctx_self * blocks_here + row, slot, -1)


def pick_kernel(blocks_here, count, chips, far, piece, chosen, keys, values, asked, *refs):
    outs, sems = refs[:-1], refs[-1]
    ctx_self = lax.axis_index("ctx")
    place = lax.axis_index("head")
    core, chip = lax.rem(place, 2), lax.div(place, 2)
    first = ctx_self * blocks_here
    span = pl.ds(pl.multiple_of(chip * piece, piece), piece)

    def copy(source, s, slot):
        rows = source.at[slot, span, :] if s in far else source.at[slot]
        return pltpu.make_async_copy(rows, outs[s], sems.at[s])

    for s in range(count - 1):
        peer = ctx_self + s + 1
        near = jnp.minimum(peer, count - 1)
        found = jnp.int32(0)
        for row in range(blocks_here):
            for t in range(3):
                entry = chosen[near, row * 3 + t]
                hit = (entry >= first) & (entry < first + blocks_here)
                found = jnp.where(hit, entry - first + 1, found)
        found = jnp.where(peer < count, found, 0)
        asked[s] = found
        slot = jnp.maximum(found - 1, 0)

        @pl.when(core == 0)
        def _():
            copy(keys, s, slot).start()

        @pl.when(core != 0)
        def _():
            copy(values, s, slot).start()

    for s in range(count - 1):
        copy(keys, s, 0).wait()


def chip_sum_kernel(chips, piece, far, near, mine, theirs, *outs):
    chip = lax.div(lax.axis_index("head"), 2)
    for d in range(chips):
        target = lax.rem(chip + d, chips)
        span = pl.ds(pl.multiple_of(target * piece, piece), piece)
        for i, s in enumerate(far):
            total = mine[s, span, :].astype(F32) + theirs[s, span, :].astype(F32)
            outs[d][i] = total.astype(outs[d].dtype)
    for i, s in enumerate(near):
        outs[chips + i][...] = (mine[s].astype(F32) + theirs[s].astype(F32)).astype(BF16)


def own_sum_kernel(chips, piece, near, asked, mine, theirs, *refs):
    back, outs, acc = refs[: len(near)], refs[len(near) : -1], refs[-1]
    chip = lax.div(lax.axis_index("head"), 2)
    acc[...] = mine[...].astype(F32) + theirs[...].astype(F32)
    for i, s in enumerate(near):
        slot = asked[s] - 1

        @pl.when(slot >= 0)
        def _():
            acc[slot] += back[i][...].astype(F32)

    for d in range(chips):
        target = lax.rem(chip + d, chips)
        span = pl.ds(pl.multiple_of(target * piece, piece), piece)
        outs[d][...] = acc[:, span, :].astype(outs[d].dtype)


def head_sum_kernel(count, mine, *refs):
    parts, outs = refs[: len(refs) - count], refs[len(refs) - count :]
    for i in range(count):
        total = mine[i]
        for part in parts:
            total = total + part[i].astype(F32)
        outs[i][...] = total.astype(BF16)


def fold(array, reduce):
    rows, lanes = array.shape
    return reduce(array.reshape(rows // 8, 8, lanes), axis=0)


def causal(array, first_col, first_pos, other):
    col = lax.broadcasted_iota(jnp.int32, array.shape, 0) + first_col
    pos = lax.broadcasted_iota(jnp.int32, array.shape, 1) + first_pos
    return jnp.where(col <= pos, array, other)


def row_sums(s_ref, dp_ref, factor):
    block_len = s_ref.shape[0]
    step = min(64, block_len)
    spans = [pl.ds(c, step) for c in range(0, block_len, step)]
    top = fold(s_ref[spans[0], :], jnp.max)
    for span in spans[1:]:
        top = jnp.maximum(top, fold(s_ref[span, :], jnp.max))
    top = jnp.max(top, axis=0, keepdims=True) * factor
    total = weighted = jnp.zeros((8, block_len), F32)
    for span in spans:
        terms = jnp.exp2(s_ref[span, :] * factor - top)
        total = total + fold(terms, jnp.sum)
        weighted = weighted + fold(terms * dp_ref[span, :], jnp.sum)
    total = jnp.sum(total, axis=0, keepdims=True)
    return top, total, jnp.sum(weighted, axis=0, keepdims=True)


def local_stats_kernel(factor, blocks_here, chosen, q, do, keys, values, stats, s_buf, dp_buf):
    block_len = keys.shape[1]
    half = block_len // 2

    def per_row(row, _):
        start = row * block_len
        span = pl.ds(start, block_len)
        late = pl.ds(start + half, half)

        s_buf[:half, :] = causal(dot_nt(keys[row, :half], q[span, :]), 0, 0, -jnp.inf)
        s_buf[half:, :half] = jnp.full((half, half), -jnp.inf, F32)
        s_buf[half:, half:] = causal(dot_nt(keys[row, half:], q[late, :]), 0, 0, -jnp.inf)
        dp_buf[:half, :] = dot_nt(values[row, :half], do[span, :])
        dp_buf[half:, :half] = jnp.zeros((half, half), F32)
        dp_buf[half:, half:] = dot_nt(values[row, half:], do[late, :])
        top, total, weighted = row_sums(s_buf, dp_buf, factor)
        stats[row, 0:1, :] = top
        stats[row, 1:2, :] = total
        stats[row, 2:3, :] = weighted
        for t in range(3):
            slot = slot_of(chosen, blocks_here, row, t)

            @pl.when((slot >= 0) & (slot < blocks_here))
            def _():
                s_buf[...] = dot_nt(keys[slot], q[span, :])
                dp_buf[...] = dot_nt(values[slot], do[span, :])
                more_top, more, more_weighted = row_sums(s_buf, dp_buf, factor)
                old = stats[row, 0:1, :]
                top = jnp.maximum(old, more_top)
                scale_old = jnp.exp2(old - top)
                scale_new = jnp.exp2(more_top - top)
                stats[row, 0:1, :] = top
                stats[row, 1:2, :] = stats[row, 1:2, :] * scale_old + more * scale_new
                stats[row, 2:3, :] = stats[row, 2:3, :] * scale_old + more_weighted * scale_new

        return 0

    lax.fori_loop(0, blocks_here, per_row, 0)


def remote_kernel(
    factor, scaling, blocks_here, chips, far, near, piece, chosen, q, do, stats, *refs
):
    near_refs, far_refs, refs = refs[:2], refs[2 : 2 + 2 * chips], refs[2 + 2 * chips :]
    keep, send, final, grad_qt, rows, acc, s_buf, dp_buf, parts = refs
    place = lax.axis_index("head")
    core, chip = lax.rem(place, 2), lax.div(place, 2)
    block_len = rows.shape[2]

    def lay(kind, which):
        for i, s in enumerate(near):
            rows[kind, s] = near_refs[which][i]
        for d in range(chips):
            source = lax.rem(chip + chips - d, chips)
            span = pl.ds(pl.multiple_of(source * piece, piece), piece)
            for i, s in enumerate(far):
                rows[kind, s, span, :] = far_refs[2 * d + which][i]

    @pl.when(core == 0)
    def _():
        lay(0, 0)
        lay(1, 1)

    @pl.when(core != 0)
    def _():
        lay(0, 1)
        lay(1, 0)

    acc[...] = jnp.zeros_like(acc)

    def per_row(row, _):
        span = pl.ds(row * block_len, block_len)
        parts[0, 0:3, :] = stats[row, 0:3, :]
        for t in range(3):
            slot = slot_of(chosen, blocks_here, row, t) - blocks_here

            @pl.when(slot >= 0)
            def _():
                s_buf[t] = dot_nt(rows[0, slot], q[span, :])
                dp_buf[t] = dot_nt(rows[1, slot], do[span, :])
                top, total, weighted = row_sums(s_buf.at[t], dp_buf.at[t], factor)
                parts[t + 1, 0:1, :] = top
                parts[t + 1, 1:2, :] = total
                parts[t + 1, 2:3, :] = weighted

            @pl.when(slot < 0)
            def _():
                parts[t + 1, 0:1, :] = jnp.full((1, block_len), -jnp.inf, F32)
                parts[t + 1, 1:3, :] = jnp.zeros((2, block_len), F32)

        top = parts[0, 0:1, :]
        for t in range(3):
            top = jnp.maximum(top, parts[t + 1, 0:1, :])
        total = jnp.zeros_like(top)
        weighted = jnp.zeros_like(top)
        for t in range(4):
            scale = jnp.exp2(parts[t, 0:1, :] - top)
            total = total + scale * parts[t, 1:2, :]
            weighted = weighted + scale * parts[t, 2:3, :]
        final[row, 0:1, :] = top + jnp.log2(total)
        final[row, 1:2, :] = weighted / total
        grad_qt[row] = jnp.zeros_like(grad_qt[row])
        for t in range(3):
            slot = slot_of(chosen, blocks_here, row, t) - blocks_here

            @pl.when(slot >= 0)
            def _():
                level = final[row, 0:1, :]
                delta = final[row, 1:2, :]
                weights = jnp.exp2(s_buf[t] * factor - level)
                dscores = (weights * (dp_buf[t] - delta)).astype(BF16)
                acc[1, slot] += dot_nn(weights.astype(BF16), do[span, :])
                acc[0, slot] += dot_nn(dscores, q[span, :])
                grad_qt[row] += dot_nn(rows[0, slot].T, dscores)

        return 0

    lax.fori_loop(0, blocks_here, per_row, 0)
    keep_scale = jnp.where(core == 0, scaling, 1.0)
    send_scale = jnp.where(core == 0, 1.0, scaling)
    keep[...] = (acc[core] * keep_scale).astype(BF16)
    send[...] = (acc[1 - core] * send_scale).astype(BF16)


def local_kernel(
    factor, scaling, blocks_here, chosen, q, do, keys, values, final, grad_qt,
    keep, send, grad_q,
    acc, total_qt,
):
    core = lax.rem(lax.axis_index("head"), 2)
    block_len = keys.shape[1]
    half = block_len // 2
    acc[...] = jnp.zeros_like(acc)

    def per_row(row, _):
        start = row * block_len
        span = pl.ds(start, block_len)

        def rows_from(ref, first):
            return ref[pl.ds(start + first, block_len - first), :]

        def products(slot, c, first):
            cut = pl.ds(c, half)
            scores = dot_nt(keys[slot, cut, :], rows_from(q, first))
            return scores, dot_nt(values[slot, cut, :], rows_from(do, first))

        def pair(slot, seconds, masked):
            parts = ((0, 0), (half, seconds))
            ready = [products(slot, c, first) for c, first in parts]
            sides = []
            for (c, first), (scores, dprobs) in zip(parts, ready):
                weights = jnp.exp2(scores * factor - final[row, 0:1, first:])
                if masked:
                    weights = causal(weights, c, first, 0.0)
                dscores = (weights * (dprobs - final[row, 1:2, first:])).astype(BF16)
                sides.append((weights.astype(BF16), dscores))
            for (c, first), (weights, dscores) in zip(parts, sides):
                cut = pl.ds(c, half)
                acc[1, slot, cut, :] += dot_nn(weights, rows_from(do, first))
                acc[0, slot, cut, :] += dot_nn(dscores, rows_from(q, first))
                total_qt[:, first:] += dot_nn(keys[slot, cut, :].T, dscores)

        total_qt[...] = grad_qt[row]
        pair(row, half, True)
        for t in range(3):
            slot = slot_of(chosen, blocks_here, row, t)

            @pl.when((slot >= 0) & (slot < blocks_here))
            def _():
                pair(slot, 0, False)

        grad_q[span, :] = (total_qt[...].T * scaling).astype(BF16)
        return 0

    lax.fori_loop(0, blocks_here, per_row, 0)
    keep_scale = jnp.where(core == 0, scaling, 1.0)
    send_scale = jnp.where(core == 0, 1.0, scaling)
    keep[...] = (acc[core] * keep_scale).astype(BF16)
    send[...] = (acc[1 - core] * send_scale).astype(BF16)


def far_return_kernel(far, asked, *refs):
    back, acc = refs[:-1], refs[-1]
    acc[...] = jnp.zeros_like(acc)
    for i, s in enumerate(far):
        slot = asked[s] - 1

        @pl.when(slot >= 0)
        def _():
            acc[slot] += back[i][...].astype(F32)


def owner_kernel(returned, mine, *refs):
    others, out = refs[:-1], refs[-1]
    total = mine[...] + returned[...]
    for part in others:
        total = total + part[...].astype(F32)
    out[...] = total.astype(BF16)


def spread_kernel(chips, piece, *refs):
    pieces, (grad_k, grad_v) = refs[: 2 * chips], refs[2 * chips :]
    place = lax.axis_index("head")
    core, chip = lax.rem(place, 2), lax.div(place, 2)

    def lay(out, which):
        for d in range(chips):
            source = lax.rem(chip + chips - d, chips)
            span = pl.ds(pl.multiple_of(source * piece, piece), piece)
            out[:, span, :] = pieces[2 * d + which][...]

    @pl.when(core == 0)
    def _():
        lay(grad_k, 0)
        lay(grad_v, 1)

    @pl.when(core != 0)
    def _():
        lay(grad_k, 1)
        lay(grad_v, 0)


def params(size):
    return pltpu.CompilerParams(vmem_limit_bytes=min(size + 12 * 1024 * 1024, VMEM_LIMIT))


def body(queries, keys, values, dout, selected):
    tok_rows, head_count, feature = queries.shape
    blocks_here = selected.shape[0]
    block_len = tok_rows // blocks_here
    ctx_count = lax.axis_size("ctx")
    heads = lax.axis_size("head")
    chips = heads // 2
    piece = block_len // chips
    scaling = 1.0 / math.sqrt(feature)
    factor = scaling * math.log2(math.e)
    shifts = ctx_count - 1
    far_in = [s for s in range(shifts) if 2 * (s + 1) >= ctx_count]
    near_in = [s for s in range(shifts) if 2 * (s + 1) < ctx_count]
    far = [s for s in range(shifts) if 2 * (s + 2) >= ctx_count]
    near = [s for s in range(shifts) if 2 * (s + 2) < ctx_count]

    q2 = queries.reshape(tok_rows, feature)
    do2 = dout.reshape(tok_rows, feature)
    key_blocks = keys.reshape(blocks_here, block_len, feature)
    value_blocks = values.reshape(blocks_here, block_len, feature)
    remote_shape = (shifts, block_len, feature)
    local_shape = (blocks_here, block_len, feature)

    smem = pl.BlockSpec(memory_space=pltpu.SMEM)
    whole = pl.BlockSpec(memory_space=pltpu.VMEM)
    hbm = pl.BlockSpec(memory_space=pltpu.HBM)
    stat_type = jax.ShapeDtypeStruct((blocks_here, 8, block_len), F32)
    far_type = jax.ShapeDtypeStruct(remote_shape, BF16)
    own_type = jax.ShapeDtypeStruct(local_shape, BF16)
    block_type = jax.ShapeDtypeStruct((block_len, feature), BF16)
    piece_type = jax.ShapeDtypeStruct((piece, feature), BF16)
    qt_type = jax.ShapeDtypeStruct((blocks_here, feature, block_len), F32)
    pair_flops = 2 * block_len * block_len * feature
    block_bytes = block_len * feature * 2
    pair_bytes = block_len * block_len * 4

    def pieces_type(count, dtype):
        return jax.ShapeDtypeStruct((count, piece, feature), dtype)

    def cost(matmuls, size):
        return pl.CostEstimate(
            flops=matmuls * pair_flops, bytes_accessed=size, transcendentals=matmuls * block_len**2
        )

    def swap(array):
        return lax.ppermute(array, "head", [(h, h ^ 1) for h in range(heads)])

    def to_chip(array, d):
        return lax.ppermute(array, "head", [(h, (h + 2 * d) % heads) for h in range(heads)])

    def to_owner(array, s):
        return lax.ppermute(array, "ctx", [(c, c - s - 1) for c in range(s + 1, ctx_count)])

    def to_reader(array, s):
        return lax.ppermute(array, "ctx", [(c - s - 1, c) for c in range(s + 1, ctx_count)])

    everyone = lax.all_to_all(
        jnp.broadcast_to(selected.reshape(1, 3 * blocks_here), (ctx_count, 3 * blocks_here)),
        "ctx", split_axis=0, concat_axis=0, tiled=True,
    )
    asked, *sent = pl.pallas_call(
        functools.partial(pick_kernel, blocks_here, ctx_count, chips, far_in, piece),
        in_specs=[smem, hbm, hbm],
        out_specs=[smem] + [whole] * shifts,
        out_shape=[jax.ShapeDtypeStruct((shifts,), jnp.int32)]
        + [piece_type if s in far_in else block_type for s in range(shifts)],
        scratch_shapes=[pltpu.SemaphoreType.DMA((shifts,))],
        name="pick_rows",
    )(everyone, key_blocks, value_blocks)

    far_mine = jnp.stack([to_reader(sent[s], s) for s in far_in])
    near_parts = [to_reader(sent[s], s) for s in near_in]
    far_mine, chosen = lax.optimization_barrier((far_mine, selected))
    far_more = [to_chip(far_mine, d) for d in range(1, chips)]
    stats = pl.pallas_call(
        functools.partial(local_stats_kernel, factor, blocks_here),
        in_specs=[smem] + [whole] * 4,
        out_specs=whole,
        out_shape=stat_type,
        scratch_shapes=[pltpu.VMEM((block_len, block_len), F32)] * 2,
        compiler_params=params(4 * blocks_here * block_bytes + 2 * pair_bytes),
        cost_estimate=cost(30, 4 * tok_rows * feature * 2),
        name="local_stats",
    )(chosen, q2, do2, key_blocks, value_blocks)
    near_parts, far_held, stats = lax.optimization_barrier((near_parts, far_mine, stats))
    near_mine = jnp.stack(near_parts)
    row_sets = [near_mine, swap(near_mine), far_held, swap(far_held)]
    for part in far_more:
        row_sets += [part, swap(part)]

    keep_far, send_far, final, grad_qt = pl.pallas_call(
        functools.partial(
            remote_kernel, factor, scaling, blocks_here, chips, far_in, near_in, piece
        ),
        in_specs=[smem] + [whole] * (3 + len(row_sets)),
        out_specs=[whole] * 4,
        out_shape=[far_type, far_type, stat_type, qt_type],
        scratch_shapes=[
            pltpu.VMEM((2,) + remote_shape, BF16),
            pltpu.VMEM((2,) + remote_shape, F32),
            pltpu.VMEM((3, block_len, block_len), F32),
            pltpu.VMEM((3, block_len, block_len), F32),
            pltpu.VMEM((4, 8, block_len), F32),
        ],
        compiler_params=params((10 * shifts + 4 * blocks_here) * block_bytes + 6 * pair_bytes),
        cost_estimate=cost(60, 8 * tok_rows * feature * 2),
        name="remote_pairs",
    )(chosen, q2, do2, stats, *row_sets)

    def head_sums(mine, parts, count):
        return pl.pallas_call(
            functools.partial(head_sum_kernel, count),
            in_specs=[whole] * (1 + len(parts)),
            out_specs=[whole] * count,
            out_shape=[piece_type] * count,
            compiler_params=params(4 * count * block_bytes),
            name="head_sum",
        )(mine, *parts)

    chip_far = pl.pallas_call(
        functools.partial(chip_sum_kernel, chips, piece, far, near),
        in_specs=[whole, whole],
        out_specs=[whole] * (chips + len(near)),
        out_shape=[pieces_type(len(far), F32)]
        + [pieces_type(len(far), BF16)] * (chips - 1)
        + [block_type] * len(near),
        compiler_params=params(4 * shifts * block_bytes),
        name="chip_sum",
    )(keep_far, swap(send_far))
    chip_far, final = lax.optimization_barrier((chip_far, final))
    far_sums, near_sums = chip_far[:chips], chip_far[chips:]
    far_parts = [to_chip(far_sums[d], d) for d in range(1, chips)]
    near_back = [to_owner(near_sums[i], s) for i, s in enumerate(near)]
    keep_own, send_own, grad_q = pl.pallas_call(
        functools.partial(local_kernel, factor, scaling, blocks_here),
        in_specs=[smem] + [whole] * 6,
        out_specs=[whole] * 3,
        out_shape=[own_type, own_type, jax.ShapeDtypeStruct((tok_rows, feature), BF16)],
        scratch_shapes=[
            pltpu.VMEM((2,) + local_shape, F32),
            pltpu.VMEM((feature, block_len), F32),
        ],
        compiler_params=params(14 * blocks_here * block_bytes),
        cost_estimate=cost(60, 8 * tok_rows * feature * 2),
        name="local_pairs",
    )(chosen, q2, do2, key_blocks, value_blocks, final, grad_qt)
    far_parts, near_back, keep_own, send_own = lax.optimization_barrier(
        (far_parts, near_back, keep_own, send_own)
    )
    own_sums = pl.pallas_call(
        functools.partial(own_sum_kernel, chips, piece, near),
        in_specs=[smem] + [whole] * (2 + len(near)),
        out_specs=[whole] * chips,
        out_shape=[pieces_type(blocks_here, F32)]
        + [pieces_type(blocks_here, BF16)] * (chips - 1),
        scratch_shapes=[pltpu.VMEM(local_shape, F32)],
        compiler_params=params((8 * blocks_here + len(near)) * block_bytes),
        name="own_sum",
    )(asked, keep_own, swap(send_own), *near_back)
    own_parts = [to_chip(own_sums[d], d) for d in range(1, chips)]
    far_out = head_sums(far_sums[0], far_parts, len(far))
    far_back = [to_owner(far_out[i], s) for i, s in enumerate(far)]
    returned = pl.pallas_call(
        functools.partial(far_return_kernel, far),
        in_specs=[smem] + [whole] * len(far),
        out_specs=whole,
        out_shape=pieces_type(blocks_here, F32),
        compiler_params=params((2 * blocks_here + len(far)) * block_bytes),
        cost_estimate=cost(600, 8 * tok_rows * feature * 2),
        name="far_returns",
    )(asked, *far_back)
    mine = pl.pallas_call(
        owner_kernel,
        in_specs=[whole] * (1 + chips),
        out_specs=whole,
        out_shape=pieces_type(blocks_here, BF16),
        compiler_params=params(6 * blocks_here * block_bytes),
        name="owner_sum",
    )(returned, own_sums[0], *own_parts)
    spread = [mine, swap(mine)]
    for d in range(1, chips):
        part = to_chip(mine, d)
        spread += [part, swap(part)]
    grad_keys, grad_values = pl.pallas_call(
        functools.partial(spread_kernel, chips, piece),
        in_specs=[whole] * len(spread),
        out_specs=[whole] * 2,
        out_shape=[own_type] * 2,
        compiler_params=params(4 * blocks_here * block_bytes),
        name="spread",
    )(*spread)
    return (
        grad_q.reshape(tok_rows, head_count, feature),
        grad_keys.reshape(tok_rows, feature),
        grad_values.reshape(tok_rows, feature),
    )


def solution(mesh):
    return jax.shard_map(
        body,
        mesh=mesh,
        in_specs=(
            P("ctx", "head", None),
            P("ctx", None),
            P("ctx", None),
            P("ctx", "head", None),
            P("ctx", None),
        ),
        out_specs=(P("ctx", "head", None), P("ctx", None), P("ctx", None)),
        check_vma=False,
    )
```

```python
import functools
import math

import jax
import jax.numpy as jnp
from jax import lax
from jax.experimental import pallas as pl
from jax.experimental.pallas import tpu as pltpu
from jax.sharding import PartitionSpec as P

F32 = jnp.float32
BF16 = jnp.bfloat16
VMEM_LIMIT = 56 * 1024 * 1024


def dot_nt(a, b):
    return lax.dot_general(a, b, (((1,), (1,)), ((), ())), preferred_element_type=F32)


def dot_nn(a, b):
    return lax.dot_general(a, b, (((1,), (0,)), ((), ())), preferred_element_type=F32)


def slot_of(chosen, blocks_here, row, t):
    ctx_self = lax.axis_index("ctx")
    entry = chosen[row, t]
    owner = lax.div(entry, jnp.int32(blocks_here))
    apart = ctx_self - owner
    slot = jnp.where(apart == 0, entry - owner * blocks_here, blocks_here + apart - 1)
    return jnp.where(entry != ctx_self * blocks_here + row, slot, -1)


def pick_kernel(blocks_here, count, chips, far, piece, chosen, keys, values, asked, *refs):
    outs, sems = refs[:-1], refs[-1]
    ctx_self = lax.axis_index("ctx")
    place = lax.axis_index("head")
    core, chip = lax.rem(place, 2), lax.div(place, 2)
    first = ctx_self * blocks_here
    span = pl.ds(pl.multiple_of(chip * piece, piece), piece)

    def copy(source, s, slot):
        rows = source.at[slot, span, :] if s in far else source.at[slot]
        return pltpu.make_async_copy(rows, outs[s], sems.at[s])

    for s in range(count - 1):
        peer = ctx_self + s + 1
        near = jnp.minimum(peer, count - 1)
        found = jnp.int32(0)
        for row in range(blocks_here):
            for t in range(3):
                entry = chosen[near, row * 3 + t]
                hit = (entry >= first) & (entry < first + blocks_here)
                found = jnp.where(hit, entry - first + 1, found)
        found = jnp.where(peer < count, found, 0)
        asked[s] = found
        slot = jnp.maximum(found - 1, 0)

        @pl.when(core == 0)
        def _():
            copy(keys, s, slot).start()

        @pl.when(core != 0)
        def _():
            copy(values, s, slot).start()

    for s in range(count - 1):
        copy(keys, s, 0).wait()


def chip_sum_kernel(chips, piece, far, near, mine, theirs, *outs):
    chip = lax.div(lax.axis_index("head"), 2)
    for d in range(chips):
        target = lax.rem(chip + d, chips)
        span = pl.ds(pl.multiple_of(target * piece, piece), piece)
        for i, s in enumerate(far):
            total = mine[s, span, :].astype(F32) + theirs[s, span, :].astype(F32)
            outs[d][i] = total.astype(outs[d].dtype)
    for i, s in enumerate(near):
        outs[chips + i][...] = (mine[s].astype(F32) + theirs[s].astype(F32)).astype(BF16)


def own_sum_kernel(chips, piece, near, asked, mine, theirs, *refs):
    back, outs, acc = refs[: len(near)], refs[len(near) : -1], refs[-1]
    chip = lax.div(lax.axis_index("head"), 2)
    acc[...] = mine[...].astype(F32) + theirs[...].astype(F32)
    for i, s in enumerate(near):
        slot = asked[s] - 1

        @pl.when(slot >= 0)
        def _():
            acc[slot] += back[i][...].astype(F32)

    for d in range(chips):
        target = lax.rem(chip + d, chips)
        span = pl.ds(pl.multiple_of(target * piece, piece), piece)
        outs[d][...] = acc[:, span, :].astype(outs[d].dtype)


def head_sum_kernel(count, mine, *refs):
    parts, outs = refs[: len(refs) - count], refs[len(refs) - count :]
    for i in range(count):
        total = mine[i]
        for part in parts:
            total = total + part[i].astype(F32)
        outs[i][...] = total.astype(BF16)


def fold(array, reduce):
    rows, lanes = array.shape
    return reduce(array.reshape(rows // 8, 8, lanes), axis=0)


def causal(array, first_col, first_pos, other):
    col = lax.broadcasted_iota(jnp.int32, array.shape, 0) + first_col
    pos = lax.broadcasted_iota(jnp.int32, array.shape, 1) + first_pos
    return jnp.where(col <= pos, array, other)


def row_sums(s_ref, dp_ref, factor):
    block_len = s_ref.shape[0]
    step = min(64, block_len)
    spans = [pl.ds(c, step) for c in range(0, block_len, step)]
    top = fold(s_ref[spans[0], :], jnp.max)
    for span in spans[1:]:
        top = jnp.maximum(top, fold(s_ref[span, :], jnp.max))
    top = jnp.max(top, axis=0, keepdims=True) * factor
    total = weighted = jnp.zeros((8, block_len), F32)
    for span in spans:
        terms = jnp.exp2(s_ref[span, :] * factor - top)
        total = total + fold(terms, jnp.sum)
        weighted = weighted + fold(terms * dp_ref[span, :], jnp.sum)
    total = jnp.sum(total, axis=0, keepdims=True)
    return top, total, jnp.sum(weighted, axis=0, keepdims=True)


def local_stats_kernel(factor, blocks_here, chosen, q, do, keys, values, stats, s_buf, dp_buf):
    block_len = keys.shape[1]
    half = block_len // 2

    def per_row(row, _):
        start = row * block_len
        span = pl.ds(start, block_len)
        late = pl.ds(start + half, half)

        s_buf[:half, :] = causal(dot_nt(keys[row, :half], q[span, :]), 0, 0, -jnp.inf)
        s_buf[half:, :half] = jnp.full((half, half), -jnp.inf, F32)
        s_buf[half:, half:] = causal(dot_nt(keys[row, half:], q[late, :]), 0, 0, -jnp.inf)
        dp_buf[:half, :] = dot_nt(values[row, :half], do[span, :])
        dp_buf[half:, :half] = jnp.zeros((half, half), F32)
        dp_buf[half:, half:] = dot_nt(values[row, half:], do[late, :])
        top, total, weighted = row_sums(s_buf, dp_buf, factor)
        stats[row, 0:1, :] = top
        stats[row, 1:2, :] = total
        stats[row, 2:3, :] = weighted
        for t in range(3):
            slot = slot_of(chosen, blocks_here, row, t)

            @pl.when((slot >= 0) & (slot < blocks_here))
            def _():
                s_buf[...] = dot_nt(keys[slot], q[span, :])
                dp_buf[...] = dot_nt(values[slot], do[span, :])
                more_top, more, more_weighted = row_sums(s_buf, dp_buf, factor)
                old = stats[row, 0:1, :]
                top = jnp.maximum(old, more_top)
                scale_old = jnp.exp2(old - top)
                scale_new = jnp.exp2(more_top - top)
                stats[row, 0:1, :] = top
                stats[row, 1:2, :] = stats[row, 1:2, :] * scale_old + more * scale_new
                stats[row, 2:3, :] = stats[row, 2:3, :] * scale_old + more_weighted * scale_new

        return 0

    lax.fori_loop(0, blocks_here, per_row, 0)


def remote_kernel(
    factor, scaling, blocks_here, chips, far, near, piece, chosen, q, do, stats, *refs
):
    near_refs, far_refs, refs = refs[:2], refs[2 : 2 + 2 * chips], refs[2 + 2 * chips :]
    keep, send, final, grad_qt, rows, acc, s_buf, dp_buf, parts = refs
    place = lax.axis_index("head")
    core, chip = lax.rem(place, 2), lax.div(place, 2)
    block_len = rows.shape[2]

    def lay(kind, which):
        for i, s in enumerate(near):
            rows[kind, s] = near_refs[which][i]
        for d in range(chips):
            source = lax.rem(chip + chips - d, chips)
            span = pl.ds(pl.multiple_of(source * piece, piece), piece)
            for i, s in enumerate(far):
                rows[kind, s, span, :] = far_refs[2 * d + which][i]

    @pl.when(core == 0)
    def _():
        lay(0, 0)
        lay(1, 1)

    @pl.when(core != 0)
    def _():
        lay(0, 1)
        lay(1, 0)

    acc[...] = jnp.zeros_like(acc)

    def per_row(row, _):
        span = pl.ds(row * block_len, block_len)
        parts[0, 0:3, :] = stats[row, 0:3, :]
        for t in range(3):
            slot = slot_of(chosen, blocks_here, row, t) - blocks_here

            @pl.when(slot >= 0)
            def _():
                s_buf[t] = dot_nt(rows[0, slot], q[span, :])
                dp_buf[t] = dot_nt(rows[1, slot], do[span, :])
                top, total, weighted = row_sums(s_buf.at[t], dp_buf.at[t], factor)
                parts[t + 1, 0:1, :] = top
                parts[t + 1, 1:2, :] = total
                parts[t + 1, 2:3, :] = weighted

            @pl.when(slot < 0)
            def _():
                parts[t + 1, 0:1, :] = jnp.full((1, block_len), -jnp.inf, F32)
                parts[t + 1, 1:3, :] = jnp.zeros((2, block_len), F32)

        top = parts[0, 0:1, :]
        for t in range(3):
            top = jnp.maximum(top, parts[t + 1, 0:1, :])
        total = jnp.zeros_like(top)
        weighted = jnp.zeros_like(top)
        for t in range(4):
            scale = jnp.exp2(parts[t, 0:1, :] - top)
            total = total + scale * parts[t, 1:2, :]
            weighted = weighted + scale * parts[t, 2:3, :]
        final[row, 0:1, :] = top + jnp.log2(total)
        final[row, 1:2, :] = weighted / total
        grad_qt[row] = jnp.zeros_like(grad_qt[row])
        for t in range(3):
            slot = slot_of(chosen, blocks_here, row, t) - blocks_here

            @pl.when(slot >= 0)
            def _():
                level = final[row, 0:1, :]
                delta = final[row, 1:2, :]
                weights = jnp.exp2(s_buf[t] * factor - level)
                dscores = (weights * (dp_buf[t] - delta)).astype(BF16)
                acc[1, slot] += dot_nn(weights.astype(BF16), do[span, :])
                acc[0, slot] += dot_nn(dscores, q[span, :])
                grad_qt[row] += dot_nn(rows[0, slot].T, dscores)

        return 0

    lax.fori_loop(0, blocks_here, per_row, 0)
    keep_scale = jnp.where(core == 0, scaling, 1.0)
    send_scale = jnp.where(core == 0, 1.0, scaling)
    keep[...] = (acc[core] * keep_scale).astype(BF16)
    send[...] = (acc[1 - core] * send_scale).astype(BF16)


def local_kernel(
    factor, scaling, blocks_here, chosen, q, do, keys, values, final, grad_qt,
    keep, send, grad_q,
    acc, total_qt,
):
    core = lax.rem(lax.axis_index("head"), 2)
    block_len = keys.shape[1]
    half = block_len // 2
    acc[...] = jnp.zeros_like(acc)

    def per_row(row, _):
        start = row * block_len
        span = pl.ds(start, block_len)

        def rows_from(ref, first):
            return ref[pl.ds(start + first, block_len - first), :]

        def products(slot, c, first):
            cut = pl.ds(c, half)
            scores = dot_nt(keys[slot, cut, :], rows_from(q, first))
            return scores, dot_nt(values[slot, cut, :], rows_from(do, first))

        def pair(slot, seconds, masked):
            parts = ((0, 0), (half, seconds))
            ready = [products(slot, c, first) for c, first in parts]
            sides = []
            for (c, first), (scores, dprobs) in zip(parts, ready):
                weights = jnp.exp2(scores * factor - final[row, 0:1, first:])
                if masked:
                    weights = causal(weights, c, first, 0.0)
                dscores = (weights * (dprobs - final[row, 1:2, first:])).astype(BF16)
                sides.append((weights.astype(BF16), dscores))
            for (c, first), (weights, dscores) in zip(parts, sides):
                cut = pl.ds(c, half)
                acc[1, slot, cut, :] += dot_nn(weights, rows_from(do, first))
                acc[0, slot, cut, :] += dot_nn(dscores, rows_from(q, first))
                total_qt[:, first:] += dot_nn(keys[slot, cut, :].T, dscores)

        total_qt[...] = grad_qt[row]
        pair(row, half, True)
        for t in range(3):
            slot = slot_of(chosen, blocks_here, row, t)

            @pl.when((slot >= 0) & (slot < blocks_here))
            def _():
                pair(slot, 0, False)

        grad_q[span, :] = (total_qt[...].T * scaling).astype(BF16)
        return 0

    lax.fori_loop(0, blocks_here, per_row, 0)
    keep_scale = jnp.where(core == 0, scaling, 1.0)
    send_scale = jnp.where(core == 0, 1.0, scaling)
    keep[...] = (acc[core] * keep_scale).astype(BF16)
    send[...] = (acc[1 - core] * send_scale).astype(BF16)


def far_return_kernel(far, asked, *refs):
    back, acc = refs[:-1], refs[-1]
    acc[...] = jnp.zeros_like(acc)
    for i, s in enumerate(far):
        slot = asked[s] - 1

        @pl.when(slot >= 0)
        def _():
            acc[slot] += back[i][...].astype(F32)


def owner_kernel(returned, mine, *refs):
    others, out = refs[:-1], refs[-1]
    total = mine[...] + returned[...]
    for part in others:
        total = total + part[...].astype(F32)
    out[...] = total.astype(BF16)


def spread_kernel(chips, piece, *refs):
    pieces, (grad_k, grad_v) = refs[: 2 * chips], refs[2 * chips :]
    place = lax.axis_index("head")
    core, chip = lax.rem(place, 2), lax.div(place, 2)

    def lay(out, which):
        for d in range(chips):
            source = lax.rem(chip + chips - d, chips)
            span = pl.ds(pl.multiple_of(source * piece, piece), piece)
            out[:, span, :] = pieces[2 * d + which][...]

    @pl.when(core == 0)
    def _():
        lay(grad_k, 0)
        lay(grad_v, 1)

    @pl.when(core != 0)
    def _():
        lay(grad_k, 1)
        lay(grad_v, 0)


def params(size):
    return pltpu.CompilerParams(vmem_limit_bytes=min(size + 12 * 1024 * 1024, VMEM_LIMIT))


def body(queries, keys, values, dout, selected):
    tok_rows, head_count, feature = queries.shape
    blocks_here = selected.shape[0]
    block_len = tok_rows // blocks_here
    ctx_count = lax.axis_size("ctx")
    heads = lax.axis_size("head")
    chips = heads // 2
    piece = block_len // chips
    scaling = 1.0 / math.sqrt(feature)
    factor = scaling * math.log2(math.e)
    shifts = ctx_count - 1
    far_in = [s for s in range(shifts) if 2 * (s + 1) >= ctx_count]
    near_in = [s for s in range(shifts) if 2 * (s + 1) < ctx_count]
    far = [s for s in range(shifts - 1) if 2 * (s + 2) >= ctx_count]
    near = [s for s in range(shifts) if s not in far]

    q2 = queries.reshape(tok_rows, feature)
    do2 = dout.reshape(tok_rows, feature)
    key_blocks = keys.reshape(blocks_here, block_len, feature)
    value_blocks = values.reshape(blocks_here, block_len, feature)
    remote_shape = (shifts, block_len, feature)
    local_shape = (blocks_here, block_len, feature)

    smem = pl.BlockSpec(memory_space=pltpu.SMEM)
    whole = pl.BlockSpec(memory_space=pltpu.VMEM)
    hbm = pl.BlockSpec(memory_space=pltpu.HBM)
    stat_type = jax.ShapeDtypeStruct((blocks_here, 8, block_len), F32)
    far_type = jax.ShapeDtypeStruct(remote_shape, BF16)
    own_type = jax.ShapeDtypeStruct(local_shape, BF16)
    block_type = jax.ShapeDtypeStruct((block_len, feature), BF16)
    piece_type = jax.ShapeDtypeStruct((piece, feature), BF16)
    qt_type = jax.ShapeDtypeStruct((blocks_here, feature, block_len), F32)
    pair_flops = 2 * block_len * block_len * feature
    block_bytes = block_len * feature * 2
    pair_bytes = block_len * block_len * 4

    def pieces_type(count, dtype):
        return jax.ShapeDtypeStruct((count, piece, feature), dtype)

    def cost(matmuls, size):
        return pl.CostEstimate(
            flops=matmuls * pair_flops, bytes_accessed=size, transcendentals=matmuls * block_len**2
        )

    def swap(array):
        return lax.ppermute(array, "head", [(h, h ^ 1) for h in range(heads)])

    def to_chip(array, d):
        return lax.ppermute(array, "head", [(h, (h + 2 * d) % heads) for h in range(heads)])

    def to_owner(array, s):
        return lax.ppermute(array, "ctx", [(c, c - s - 1) for c in range(s + 1, ctx_count)])

    def to_reader(array, s):
        return lax.ppermute(array, "ctx", [(c - s - 1, c) for c in range(s + 1, ctx_count)])

    everyone = lax.all_to_all(
        jnp.broadcast_to(selected.reshape(1, 3 * blocks_here), (ctx_count, 3 * blocks_here)),
        "ctx", split_axis=0, concat_axis=0, tiled=True,
    )
    asked, *sent = pl.pallas_call(
        functools.partial(pick_kernel, blocks_here, ctx_count, chips, far_in, piece),
        in_specs=[smem, hbm, hbm],
        out_specs=[smem] + [whole] * shifts,
        out_shape=[jax.ShapeDtypeStruct((shifts,), jnp.int32)]
        + [piece_type if s in far_in else block_type for s in range(shifts)],
        scratch_shapes=[pltpu.SemaphoreType.DMA((shifts,))],
        name="pick_rows",
    )(everyone, key_blocks, value_blocks)

    far_mine = jnp.stack([to_reader(sent[s], s) for s in far_in])
    near_parts = [to_reader(sent[s], s) for s in near_in]
    far_mine, chosen = lax.optimization_barrier((far_mine, selected))
    far_more = [to_chip(far_mine, d) for d in range(1, chips)]
    stats = pl.pallas_call(
        functools.partial(local_stats_kernel, factor, blocks_here),
        in_specs=[smem] + [whole] * 4,
        out_specs=whole,
        out_shape=stat_type,
        scratch_shapes=[pltpu.VMEM((block_len, block_len), F32)] * 2,
        compiler_params=params(4 * blocks_here * block_bytes + 2 * pair_bytes),
        cost_estimate=cost(30, 4 * tok_rows * feature * 2),
        name="local_stats",
    )(chosen, q2, do2, key_blocks, value_blocks)
    near_parts, far_held, stats = lax.optimization_barrier((near_parts, far_mine, stats))
    near_mine = jnp.stack(near_parts)
    row_sets = [near_mine, swap(near_mine), far_held, swap(far_held)]
    for part in far_more:
        row_sets += [part, swap(part)]

    keep_far, send_far, final, grad_qt = pl.pallas_call(
        functools.partial(
            remote_kernel, factor, scaling, blocks_here, chips, far_in, near_in, piece
        ),
        in_specs=[smem] + [whole] * (3 + len(row_sets)),
        out_specs=[whole] * 4,
        out_shape=[far_type, far_type, stat_type, qt_type],
        scratch_shapes=[
            pltpu.VMEM((2,) + remote_shape, BF16),
            pltpu.VMEM((2,) + remote_shape, F32),
            pltpu.VMEM((3, block_len, block_len), F32),
            pltpu.VMEM((3, block_len, block_len), F32),
            pltpu.VMEM((4, 8, block_len), F32),
        ],
        compiler_params=params((10 * shifts + 4 * blocks_here) * block_bytes + 6 * pair_bytes),
        cost_estimate=cost(60, 8 * tok_rows * feature * 2),
        name="remote_pairs",
    )(chosen, q2, do2, stats, *row_sets)

    def head_sums(mine, parts, count):
        return pl.pallas_call(
            functools.partial(head_sum_kernel, count),
            in_specs=[whole] * (1 + len(parts)),
            out_specs=[whole] * count,
            out_shape=[piece_type] * count,
            compiler_params=params(4 * count * block_bytes),
            name="head_sum",
        )(mine, *parts)

    chip_far = pl.pallas_call(
        functools.partial(chip_sum_kernel, chips, piece, far, near),
        in_specs=[whole, whole],
        out_specs=[whole] * (chips + len(near)),
        out_shape=[pieces_type(len(far), F32)]
        + [pieces_type(len(far), BF16)] * (chips - 1)
        + [block_type] * len(near),
        compiler_params=params(4 * shifts * block_bytes),
        name="chip_sum",
    )(keep_far, swap(send_far))
    chip_far, final = lax.optimization_barrier((chip_far, final))
    far_sums, near_sums = chip_far[:chips], chip_far[chips:]
    far_parts = [to_chip(far_sums[d], d) for d in range(1, chips)]
    near_back = [to_owner(near_sums[i], s) for i, s in enumerate(near)]
    keep_own, send_own, grad_q = pl.pallas_call(
        functools.partial(local_kernel, factor, scaling, blocks_here),
        in_specs=[smem] + [whole] * 6,
        out_specs=[whole] * 3,
        out_shape=[own_type, own_type, jax.ShapeDtypeStruct((tok_rows, feature), BF16)],
        scratch_shapes=[
            pltpu.VMEM((2,) + local_shape, F32),
            pltpu.VMEM((feature, block_len), F32),
        ],
        compiler_params=params(14 * blocks_here * block_bytes),
        cost_estimate=cost(60, 8 * tok_rows * feature * 2),
        name="local_pairs",
    )(chosen, q2, do2, key_blocks, value_blocks, final, grad_qt)
    far_parts, near_back, keep_own, send_own = lax.optimization_barrier(
        (far_parts, near_back, keep_own, send_own)
    )
    own_sums = pl.pallas_call(
        functools.partial(own_sum_kernel, chips, piece, near),
        in_specs=[smem] + [whole] * (2 + len(near)),
        out_specs=[whole] * chips,
        out_shape=[pieces_type(blocks_here, F32)]
        + [pieces_type(blocks_here, BF16)] * (chips - 1),
        scratch_shapes=[pltpu.VMEM(local_shape, F32)],
        compiler_params=params((8 * blocks_here + len(near)) * block_bytes),
        name="own_sum",
    )(asked, keep_own, swap(send_own), *near_back)
    own_parts = [to_chip(own_sums[d], d) for d in range(1, chips)]
    far_out = head_sums(far_sums[0], far_parts, len(far))
    far_back = [to_owner(far_out[i], s) for i, s in enumerate(far)]
    returned = pl.pallas_call(
        functools.partial(far_return_kernel, far),
        in_specs=[smem] + [whole] * len(far),
        out_specs=whole,
        out_shape=pieces_type(blocks_here, F32),
        compiler_params=params((2 * blocks_here + len(far)) * block_bytes),
        cost_estimate=cost(600, 8 * tok_rows * feature * 2),
        name="far_returns",
    )(asked, *far_back)
    mine = pl.pallas_call(
        owner_kernel,
        in_specs=[whole] * (1 + chips),
        out_specs=whole,
        out_shape=pieces_type(blocks_here, BF16),
        compiler_params=params(6 * blocks_here * block_bytes),
        name="owner_sum",
    )(returned, own_sums[0], *own_parts)
    spread = [mine, swap(mine)]
    for d in range(1, chips):
        part = to_chip(mine, d)
        spread += [part, swap(part)]
    grad_keys, grad_values = pl.pallas_call(
        functools.partial(spread_kernel, chips, piece),
        in_specs=[whole] * len(spread),
        out_specs=[whole] * 2,
        out_shape=[own_type] * 2,
        compiler_params=params(4 * blocks_here * block_bytes),
        name="spread",
    )(*spread)
    return (
        grad_q.reshape(tok_rows, head_count, feature),
        grad_keys.reshape(tok_rows, feature),
        grad_values.reshape(tok_rows, feature),
    )


def solution(mesh):
    return jax.shard_map(
        body,
        mesh=mesh,
        in_specs=(
            P("ctx", "head", None),
            P("ctx", None),
            P("ctx", None),
            P("ctx", "head", None),
            P("ctx", None),
        ),
        out_specs=(P("ctx", "head", None), P("ctx", None), P("ctx", None)),
        check_vma=False,
    )
```

```python
import functools
import math

import jax
import jax.numpy as jnp
from jax import lax
from jax.experimental import pallas as pl
from jax.experimental.pallas import tpu as pltpu
from jax.sharding import PartitionSpec as P

F32 = jnp.float32
BF16 = jnp.bfloat16
VMEM_LIMIT = 56 * 1024 * 1024


def dot_nt(a, b):
    return lax.dot_general(a, b, (((1,), (1,)), ((), ())), preferred_element_type=F32)


def dot_nn(a, b):
    return lax.dot_general(a, b, (((1,), (0,)), ((), ())), preferred_element_type=F32)


def slot_of(chosen, blocks_here, row, t):
    ctx_self = lax.axis_index("ctx")
    entry = chosen[row, t]
    owner = lax.div(entry, jnp.int32(blocks_here))
    apart = ctx_self - owner
    slot = jnp.where(apart == 0, entry - owner * blocks_here, blocks_here + apart - 1)
    return jnp.where(entry != ctx_self * blocks_here + row, slot, -1)


def pick_kernel(blocks_here, count, chips, far, piece, chosen, keys, values, asked, *refs):
    outs, sems = refs[:-1], refs[-1]
    ctx_self = lax.axis_index("ctx")
    place = lax.axis_index("head")
    core, chip = lax.rem(place, 2), lax.div(place, 2)
    first = ctx_self * blocks_here
    span = pl.ds(pl.multiple_of(chip * piece, piece), piece)

    def copy(source, s, slot):
        rows = source.at[slot, span, :] if s in far else source.at[slot]
        return pltpu.make_async_copy(rows, outs[s], sems.at[s])

    for s in range(count - 1):
        peer = ctx_self + s + 1
        near = jnp.minimum(peer, count - 1)
        found = jnp.int32(0)
        for row in range(blocks_here):
            for t in range(3):
                entry = chosen[near, row * 3 + t]
                hit = (entry >= first) & (entry < first + blocks_here)
                found = jnp.where(hit, entry - first + 1, found)
        found = jnp.where(peer < count, found, 0)
        asked[s] = found
        slot = jnp.maximum(found - 1, 0)

        @pl.when(core == 0)
        def _():
            copy(keys, s, slot).start()

        @pl.when(core != 0)
        def _():
            copy(values, s, slot).start()

    for s in range(count - 1):
        copy(keys, s, 0).wait()


def chip_sum_kernel(chips, piece, far, near, mine, theirs, *outs):
    chip = lax.div(lax.axis_index("head"), 2)
    for d in range(chips):
        target = lax.rem(chip + d, chips)
        span = pl.ds(pl.multiple_of(target * piece, piece), piece)
        for i, s in enumerate(far):
            total = mine[s, span, :].astype(F32) + theirs[s, span, :].astype(F32)
            outs[d][i] = total.astype(outs[d].dtype)
    for i, s in enumerate(near):
        outs[chips + i][...] = (mine[s].astype(F32) + theirs[s].astype(F32)).astype(BF16)


def own_sum_kernel(chips, piece, near, asked, mine, theirs, *refs):
    back, outs, acc = refs[: len(near)], refs[len(near) : -1], refs[-1]
    chip = lax.div(lax.axis_index("head"), 2)
    acc[...] = mine[...].astype(F32) + theirs[...].astype(F32)
    for i, s in enumerate(near):
        slot = asked[s] - 1

        @pl.when(slot >= 0)
        def _():
            acc[slot] += back[i][...].astype(F32)

    for d in range(chips):
        target = lax.rem(chip + d, chips)
        span = pl.ds(pl.multiple_of(target * piece, piece), piece)
        outs[d][...] = acc[:, span, :].astype(outs[d].dtype)


def head_sum_kernel(count, mine, *refs):
    parts, outs = refs[: len(refs) - count], refs[len(refs) - count :]
    for i in range(count):
        total = mine[i]
        for part in parts:
            total = total + part[i].astype(F32)
        outs[i][...] = total.astype(BF16)


def fold(array, reduce):
    rows, lanes = array.shape
    return reduce(array.reshape(rows // 8, 8, lanes), axis=0)


def causal(array, first_col, first_pos, other):
    col = lax.broadcasted_iota(jnp.int32, array.shape, 0) + first_col
    pos = lax.broadcasted_iota(jnp.int32, array.shape, 1) + first_pos
    return jnp.where(col <= pos, array, other)


def row_sums(s_ref, dp_ref, factor):
    block_len = s_ref.shape[0]
    step = min(64, block_len)
    spans = [pl.ds(c, step) for c in range(0, block_len, step)]
    top = fold(s_ref[spans[0], :], jnp.max)
    for span in spans[1:]:
        top = jnp.maximum(top, fold(s_ref[span, :], jnp.max))
    top = jnp.max(top, axis=0, keepdims=True) * factor
    total = weighted = jnp.zeros((8, block_len), F32)
    for span in spans:
        terms = jnp.exp2(s_ref[span, :] * factor - top)
        total = total + fold(terms, jnp.sum)
        weighted = weighted + fold(terms * dp_ref[span, :], jnp.sum)
    total = jnp.sum(total, axis=0, keepdims=True)
    return top, total, jnp.sum(weighted, axis=0, keepdims=True)


def local_stats_kernel(factor, blocks_here, chosen, q, do, keys, values, stats, s_buf, dp_buf):
    block_len = keys.shape[1]
    half = block_len // 2

    def per_row(row, _):
        start = row * block_len
        span = pl.ds(start, block_len)
        late = pl.ds(start + half, half)

        s_buf[:half, :] = causal(dot_nt(keys[row, :half], q[span, :]), 0, 0, -jnp.inf)
        s_buf[half:, :half] = jnp.full((half, half), -jnp.inf, F32)
        s_buf[half:, half:] = causal(dot_nt(keys[row, half:], q[late, :]), 0, 0, -jnp.inf)
        dp_buf[:half, :] = dot_nt(values[row, :half], do[span, :])
        dp_buf[half:, :half] = jnp.zeros((half, half), F32)
        dp_buf[half:, half:] = dot_nt(values[row, half:], do[late, :])
        top, total, weighted = row_sums(s_buf, dp_buf, factor)
        stats[row, 0:1, :] = top
        stats[row, 1:2, :] = total
        stats[row, 2:3, :] = weighted
        for t in range(3):
            slot = slot_of(chosen, blocks_here, row, t)

            @pl.when((slot >= 0) & (slot < blocks_here))
            def _():
                s_buf[...] = dot_nt(keys[slot], q[span, :])
                dp_buf[...] = dot_nt(values[slot], do[span, :])
                more_top, more, more_weighted = row_sums(s_buf, dp_buf, factor)
                old = stats[row, 0:1, :]
                top = jnp.maximum(old, more_top)
                scale_old = jnp.exp2(old - top)
                scale_new = jnp.exp2(more_top - top)
                stats[row, 0:1, :] = top
                stats[row, 1:2, :] = stats[row, 1:2, :] * scale_old + more * scale_new
                stats[row, 2:3, :] = stats[row, 2:3, :] * scale_old + more_weighted * scale_new

        return 0

    lax.fori_loop(0, blocks_here, per_row, 0)


def remote_kernel(
    factor, scaling, blocks_here, chips, far, near, piece, chosen, q, do, stats, *refs
):
    near_refs, far_refs, refs = refs[:2], refs[2 : 2 + 2 * chips], refs[2 + 2 * chips :]
    keep, send, final, grad_qt, rows, acc, s_buf, dp_buf, parts = refs
    place = lax.axis_index("head")
    core, chip = lax.rem(place, 2), lax.div(place, 2)
    block_len = rows.shape[2]

    def lay(kind, which):
        for i, s in enumerate(near):
            rows[kind, s] = near_refs[which][i]
        for d in range(chips):
            source = lax.rem(chip + chips - d, chips)
            span = pl.ds(pl.multiple_of(source * piece, piece), piece)
            for i, s in enumerate(far):
                rows[kind, s, span, :] = far_refs[2 * d + which][i]

    @pl.when(core == 0)
    def _():
        lay(0, 0)
        lay(1, 1)

    @pl.when(core != 0)
    def _():
        lay(0, 1)
        lay(1, 0)

    acc[...] = jnp.zeros_like(acc)

    def per_row(row, _):
        span = pl.ds(row * block_len, block_len)
        parts[0, 0:3, :] = stats[row, 0:3, :]
        for t in range(3):
            slot = slot_of(chosen, blocks_here, row, t) - blocks_here

            @pl.when(slot >= 0)
            def _():
                s_buf[t] = dot_nt(rows[0, slot], q[span, :])
                dp_buf[t] = dot_nt(rows[1, slot], do[span, :])
                top, total, weighted = row_sums(s_buf.at[t], dp_buf.at[t], factor)
                parts[t + 1, 0:1, :] = top
                parts[t + 1, 1:2, :] = total
                parts[t + 1, 2:3, :] = weighted

            @pl.when(slot < 0)
            def _():
                parts[t + 1, 0:1, :] = jnp.full((1, block_len), -jnp.inf, F32)
                parts[t + 1, 1:3, :] = jnp.zeros((2, block_len), F32)

        top = parts[0, 0:1, :]
        for t in range(3):
            top = jnp.maximum(top, parts[t + 1, 0:1, :])
        total = jnp.zeros_like(top)
        weighted = jnp.zeros_like(top)
        for t in range(4):
            scale = jnp.exp2(parts[t, 0:1, :] - top)
            total = total + scale * parts[t, 1:2, :]
            weighted = weighted + scale * parts[t, 2:3, :]
        final[row, 0:1, :] = top + jnp.log2(total)
        final[row, 1:2, :] = weighted / total
        grad_qt[row] = jnp.zeros_like(grad_qt[row])
        for t in range(3):
            slot = slot_of(chosen, blocks_here, row, t) - blocks_here

            @pl.when(slot >= 0)
            def _():
                level = final[row, 0:1, :]
                delta = final[row, 1:2, :]
                weights = jnp.exp2(s_buf[t] * factor - level)
                dscores = (weights * (dp_buf[t] - delta)).astype(BF16)
                acc[1, slot] += dot_nn(weights.astype(BF16), do[span, :])
                acc[0, slot] += dot_nn(dscores, q[span, :])
                grad_qt[row] += dot_nn(rows[0, slot].T, dscores)

        return 0

    lax.fori_loop(0, blocks_here, per_row, 0)
    keep_scale = jnp.where(core == 0, scaling, 1.0)
    send_scale = jnp.where(core == 0, 1.0, scaling)
    keep[...] = (acc[core] * keep_scale).astype(BF16)
    send[...] = (acc[1 - core] * send_scale).astype(BF16)


def local_kernel(
    factor, scaling, blocks_here, chosen, q, do, keys, values, final, grad_qt,
    keep, send, grad_q,
    acc, total_qt,
):
    core = lax.rem(lax.axis_index("head"), 2)
    block_len = keys.shape[1]
    half = block_len // 2
    acc[...] = jnp.zeros_like(acc)

    def per_row(row, _):
        start = row * block_len
        span = pl.ds(start, block_len)

        def rows_from(ref, first):
            return ref[pl.ds(start + first, block_len - first), :]

        def products(slot, c, first):
            cut = pl.ds(c, half)
            scores = dot_nt(keys[slot, cut, :], rows_from(q, first))
            return scores, dot_nt(values[slot, cut, :], rows_from(do, first))

        def pair(slot, seconds, masked):
            parts = ((0, 0), (half, seconds))
            ready = [products(slot, c, first) for c, first in parts]
            sides = []
            for (c, first), (scores, dprobs) in zip(parts, ready):
                weights = jnp.exp2(scores * factor - final[row, 0:1, first:])
                if masked:
                    weights = causal(weights, c, first, 0.0)
                dscores = (weights * (dprobs - final[row, 1:2, first:])).astype(BF16)
                sides.append((weights.astype(BF16), dscores))
            for (c, first), (weights, dscores) in zip(parts, sides):
                cut = pl.ds(c, half)
                acc[1, slot, cut, :] += dot_nn(weights, rows_from(do, first))
                acc[0, slot, cut, :] += dot_nn(dscores, rows_from(q, first))
                total_qt[:, first:] += dot_nn(keys[slot, cut, :].T, dscores)

        total_qt[...] = grad_qt[row]
        pair(row, half, True)
        for t in range(3):
            slot = slot_of(chosen, blocks_here, row, t)

            @pl.when((slot >= 0) & (slot < blocks_here))
            def _():
                pair(slot, 0, False)

        grad_q[span, :] = (total_qt[...].T * scaling).astype(BF16)
        return 0

    lax.fori_loop(0, blocks_here, per_row, 0)
    keep_scale = jnp.where(core == 0, scaling, 1.0)
    send_scale = jnp.where(core == 0, 1.0, scaling)
    keep[...] = (acc[core] * keep_scale).astype(BF16)
    send[...] = (acc[1 - core] * send_scale).astype(BF16)


def far_return_kernel(far, asked, *refs):
    back, acc = refs[:-1], refs[-1]
    acc[...] = jnp.zeros_like(acc)
    for i, s in enumerate(far):
        slot = asked[s] - 1

        @pl.when(slot >= 0)
        def _():
            acc[slot] += back[i][...].astype(F32)


def owner_kernel(returned, mine, *refs):
    others, out = refs[:-1], refs[-1]
    total = mine[...] + returned[...]
    for part in others:
        total = total + part[...].astype(F32)
    out[...] = total.astype(BF16)


def spread_kernel(chips, piece, *refs):
    pieces, (grad_k, grad_v) = refs[: 2 * chips], refs[2 * chips :]
    place = lax.axis_index("head")
    core, chip = lax.rem(place, 2), lax.div(place, 2)

    def lay(out, which):
        for d in range(chips):
            source = lax.rem(chip + chips - d, chips)
            span = pl.ds(pl.multiple_of(source * piece, piece), piece)
            out[:, span, :] = pieces[2 * d + which][...]

    @pl.when(core == 0)
    def _():
        lay(grad_k, 0)
        lay(grad_v, 1)

    @pl.when(core != 0)
    def _():
        lay(grad_k, 1)
        lay(grad_v, 0)


def params(size):
    return pltpu.CompilerParams(vmem_limit_bytes=min(size + 12 * 1024 * 1024, VMEM_LIMIT))


def body(queries, keys, values, dout, selected):
    tok_rows, head_count, feature = queries.shape
    blocks_here = selected.shape[0]
    block_len = tok_rows // blocks_here
    ctx_count = lax.axis_size("ctx")
    heads = lax.axis_size("head")
    chips = heads // 2
    piece = block_len // chips
    scaling = 1.0 / math.sqrt(feature)
    factor = scaling * math.log2(math.e)
    shifts = ctx_count - 1
    far = [s for s in range(shifts - 1) if 2 * (s + 2) >= ctx_count]
    near = [s for s in range(shifts) if s not in far]

    q2 = queries.reshape(tok_rows, feature)
    do2 = dout.reshape(tok_rows, feature)
    key_blocks = keys.reshape(blocks_here, block_len, feature)
    value_blocks = values.reshape(blocks_here, block_len, feature)
    remote_shape = (shifts, block_len, feature)
    local_shape = (blocks_here, block_len, feature)

    smem = pl.BlockSpec(memory_space=pltpu.SMEM)
    whole = pl.BlockSpec(memory_space=pltpu.VMEM)
    hbm = pl.BlockSpec(memory_space=pltpu.HBM)
    stat_type = jax.ShapeDtypeStruct((blocks_here, 8, block_len), F32)
    far_type = jax.ShapeDtypeStruct(remote_shape, BF16)
    own_type = jax.ShapeDtypeStruct(local_shape, BF16)
    block_type = jax.ShapeDtypeStruct((block_len, feature), BF16)
    piece_type = jax.ShapeDtypeStruct((piece, feature), BF16)
    qt_type = jax.ShapeDtypeStruct((blocks_here, feature, block_len), F32)
    pair_flops = 2 * block_len * block_len * feature
    block_bytes = block_len * feature * 2
    pair_bytes = block_len * block_len * 4

    def pieces_type(count, dtype):
        return jax.ShapeDtypeStruct((count, piece, feature), dtype)

    def cost(matmuls, size):
        return pl.CostEstimate(
            flops=matmuls * pair_flops, bytes_accessed=size, transcendentals=matmuls * block_len**2
        )

    def swap(array):
        return lax.ppermute(array, "head", [(h, h ^ 1) for h in range(heads)])

    def to_chip(array, d):
        return lax.ppermute(array, "head", [(h, (h + 2 * d) % heads) for h in range(heads)])

    def to_owner(array, s):
        return lax.ppermute(array, "ctx", [(c, c - s - 1) for c in range(s + 1, ctx_count)])

    def to_reader(array, s):
        return lax.ppermute(array, "ctx", [(c - s - 1, c) for c in range(s + 1, ctx_count)])

    everyone = lax.all_to_all(
        jnp.broadcast_to(selected.reshape(1, 3 * blocks_here), (ctx_count, 3 * blocks_here)),
        "ctx", split_axis=0, concat_axis=0, tiled=True,
    )
    asked, *sent = pl.pallas_call(
        functools.partial(pick_kernel, blocks_here, ctx_count, chips, far, piece),
        in_specs=[smem, hbm, hbm],
        out_specs=[smem] + [whole] * shifts,
        out_shape=[jax.ShapeDtypeStruct((shifts,), jnp.int32)]
        + [piece_type if s in far else block_type for s in range(shifts)],
        scratch_shapes=[pltpu.SemaphoreType.DMA((shifts,))],
        name="pick_rows",
    )(everyone, key_blocks, value_blocks)

    far_mine = jnp.stack([to_reader(sent[s], s) for s in far])
    near_parts = [to_reader(sent[s], s) for s in near]
    far_mine, chosen = lax.optimization_barrier((far_mine, selected))
    far_more = [to_chip(far_mine, d) for d in range(1, chips)]
    stats = pl.pallas_call(
        functools.partial(local_stats_kernel, factor, blocks_here),
        in_specs=[smem] + [whole] * 4,
        out_specs=whole,
        out_shape=stat_type,
        scratch_shapes=[pltpu.VMEM((block_len, block_len), F32)] * 2,
        compiler_params=params(4 * blocks_here * block_bytes + 2 * pair_bytes),
        cost_estimate=cost(30, 4 * tok_rows * feature * 2),
        name="local_stats",
    )(chosen, q2, do2, key_blocks, value_blocks)
    near_parts, far_held, stats = lax.optimization_barrier((near_parts, far_mine, stats))
    near_mine = jnp.stack(near_parts)
    row_sets = [near_mine, swap(near_mine), far_held, swap(far_held)]
    for part in far_more:
        row_sets += [part, swap(part)]

    keep_far, send_far, final, grad_qt = pl.pallas_call(
        functools.partial(
            remote_kernel, factor, scaling, blocks_here, chips, far, near, piece
        ),
        in_specs=[smem] + [whole] * (3 + len(row_sets)),
        out_specs=[whole] * 4,
        out_shape=[far_type, far_type, stat_type, qt_type],
        scratch_shapes=[
            pltpu.VMEM((2,) + remote_shape, BF16),
            pltpu.VMEM((2,) + remote_shape, F32),
            pltpu.VMEM((3, block_len, block_len), F32),
            pltpu.VMEM((3, block_len, block_len), F32),
            pltpu.VMEM((4, 8, block_len), F32),
        ],
        compiler_params=params((10 * shifts + 4 * blocks_here) * block_bytes + 6 * pair_bytes),
        cost_estimate=cost(60, 8 * tok_rows * feature * 2),
        name="remote_pairs",
    )(chosen, q2, do2, stats, *row_sets)

    def head_sums(mine, parts, count):
        return pl.pallas_call(
            functools.partial(head_sum_kernel, count),
            in_specs=[whole] * (1 + len(parts)),
            out_specs=[whole] * count,
            out_shape=[piece_type] * count,
            compiler_params=params(4 * count * block_bytes),
            name="head_sum",
        )(mine, *parts)

    chip_far = pl.pallas_call(
        functools.partial(chip_sum_kernel, chips, piece, far, near),
        in_specs=[whole, whole],
        out_specs=[whole] * (chips + len(near)),
        out_shape=[pieces_type(len(far), F32)]
        + [pieces_type(len(far), BF16)] * (chips - 1)
        + [block_type] * len(near),
        compiler_params=params(4 * shifts * block_bytes),
        name="chip_sum",
    )(keep_far, swap(send_far))
    chip_far, final = lax.optimization_barrier((chip_far, final))
    far_sums, near_sums = chip_far[:chips], chip_far[chips:]
    far_parts = [to_chip(far_sums[d], d) for d in range(1, chips)]
    near_back = [to_owner(near_sums[i], s) for i, s in enumerate(near)]
    keep_own, send_own, grad_q = pl.pallas_call(
        functools.partial(local_kernel, factor, scaling, blocks_here),
        in_specs=[smem] + [whole] * 6,
        out_specs=[whole] * 3,
        out_shape=[own_type, own_type, jax.ShapeDtypeStruct((tok_rows, feature), BF16)],
        scratch_shapes=[
            pltpu.VMEM((2,) + local_shape, F32),
            pltpu.VMEM((feature, block_len), F32),
        ],
        compiler_params=params(14 * blocks_here * block_bytes),
        cost_estimate=cost(60, 8 * tok_rows * feature * 2),
        name="local_pairs",
    )(chosen, q2, do2, key_blocks, value_blocks, final, grad_qt)
    far_parts, near_back, keep_own, send_own = lax.optimization_barrier(
        (far_parts, near_back, keep_own, send_own)
    )
    own_sums = pl.pallas_call(
        functools.partial(own_sum_kernel, chips, piece, near),
        in_specs=[smem] + [whole] * (2 + len(near)),
        out_specs=[whole] * chips,
        out_shape=[pieces_type(blocks_here, F32)]
        + [pieces_type(blocks_here, BF16)] * (chips - 1),
        scratch_shapes=[pltpu.VMEM(local_shape, F32)],
        compiler_params=params((8 * blocks_here + len(near)) * block_bytes),
        name="own_sum",
    )(asked, keep_own, swap(send_own), *near_back)
    own_parts = [to_chip(own_sums[d], d) for d in range(1, chips)]
    far_out = head_sums(far_sums[0], far_parts, len(far))
    far_back = [to_owner(far_out[i], s) for i, s in enumerate(far)]
    returned = pl.pallas_call(
        functools.partial(far_return_kernel, far),
        in_specs=[smem] + [whole] * len(far),
        out_specs=whole,
        out_shape=pieces_type(blocks_here, F32),
        compiler_params=params((2 * blocks_here + len(far)) * block_bytes),
        cost_estimate=cost(600, 8 * tok_rows * feature * 2),
        name="far_returns",
    )(asked, *far_back)
    mine = pl.pallas_call(
        owner_kernel,
        in_specs=[whole] * (1 + chips),
        out_specs=whole,
        out_shape=pieces_type(blocks_here, BF16),
        compiler_params=params(6 * blocks_here * block_bytes),
        name="owner_sum",
    )(returned, own_sums[0], *own_parts)
    spread = [mine, swap(mine)]
    for d in range(1, chips):
        part = to_chip(mine, d)
        spread += [part, swap(part)]
    grad_keys, grad_values = pl.pallas_call(
        functools.partial(spread_kernel, chips, piece),
        in_specs=[whole] * len(spread),
        out_specs=[whole] * 2,
        out_shape=[own_type] * 2,
        compiler_params=params(4 * blocks_here * block_bytes),
        name="spread",
    )(*spread)
    return (
        grad_q.reshape(tok_rows, head_count, feature),
        grad_keys.reshape(tok_rows, feature),
        grad_values.reshape(tok_rows, feature),
    )


def solution(mesh):
    return jax.shard_map(
        body,
        mesh=mesh,
        in_specs=(
            P("ctx", "head", None),
            P("ctx", None),
            P("ctx", None),
            P("ctx", "head", None),
            P("ctx", None),
        ),
        out_specs=(P("ctx", "head", None), P("ctx", None), P("ctx", None)),
        check_vma=False,
    )
```

```python
import functools
import math

import jax
import jax.numpy as jnp
from jax import lax
from jax.experimental import pallas as pl
from jax.experimental.pallas import tpu as pltpu
from jax.sharding import PartitionSpec as P

F32 = jnp.float32
BF16 = jnp.bfloat16
VMEM_LIMIT = 56 * 1024 * 1024


def dot_nt(a, b):
    return lax.dot_general(a, b, (((1,), (1,)), ((), ())), preferred_element_type=F32)


def dot_nn(a, b):
    return lax.dot_general(a, b, (((1,), (0,)), ((), ())), preferred_element_type=F32)


def slot_of(chosen, blocks_here, row, t):
    ctx_self = lax.axis_index("ctx")
    entry = chosen[row, t]
    owner = lax.div(entry, jnp.int32(blocks_here))
    apart = ctx_self - owner
    slot = jnp.where(apart == 0, entry - owner * blocks_here, blocks_here + apart - 1)
    return jnp.where(entry != ctx_self * blocks_here + row, slot, -1)


def pick_kernel(blocks_here, count, chips, far, piece, chosen, keys, values, asked, *refs):
    outs, sems = refs[:-1], refs[-1]
    ctx_self = lax.axis_index("ctx")
    place = lax.axis_index("head")
    core, chip = lax.rem(place, 2), lax.div(place, 2)
    first = ctx_self * blocks_here
    span = pl.ds(pl.multiple_of(chip * piece, piece), piece)

    def copy(source, s, slot):
        rows = source.at[slot, span, :] if s in far else source.at[slot]
        return pltpu.make_async_copy(rows, outs[s], sems.at[s])

    for s in range(count - 1):
        peer = ctx_self + s + 1
        near = jnp.minimum(peer, count - 1)
        found = jnp.int32(0)
        for row in range(blocks_here):
            for t in range(3):
                entry = chosen[near, row * 3 + t]
                hit = (entry >= first) & (entry < first + blocks_here)
                found = jnp.where(hit, entry - first + 1, found)
        found = jnp.where(peer < count, found, 0)
        asked[s] = found
        slot = jnp.maximum(found - 1, 0)

        @pl.when(core == 0)
        def _():
            copy(keys, s, slot).start()

        @pl.when(core != 0)
        def _():
            copy(values, s, slot).start()

    for s in range(count - 1):
        copy(keys, s, 0).wait()


def chip_sum_kernel(chips, piece, far, near, mine, theirs, *outs):
    chip = lax.div(lax.axis_index("head"), 2)
    for d in range(chips):
        target = lax.rem(chip + d, chips)
        span = pl.ds(pl.multiple_of(target * piece, piece), piece)
        for i, s in enumerate(far):
            total = mine[s, span, :].astype(F32) + theirs[s, span, :].astype(F32)
            outs[d][i] = total.astype(outs[d].dtype)
    for i, s in enumerate(near):
        outs[chips + i][...] = (mine[s].astype(F32) + theirs[s].astype(F32)).astype(BF16)


def own_sum_kernel(chips, piece, near, asked, mine, theirs, *refs):
    back, outs, acc = refs[: len(near)], refs[len(near) : -1], refs[-1]
    chip = lax.div(lax.axis_index("head"), 2)
    acc[...] = mine[...].astype(F32) + theirs[...].astype(F32)
    for i, s in enumerate(near):
        slot = asked[s] - 1

        @pl.when(slot >= 0)
        def _():
            acc[slot] += back[i][...].astype(F32)

    for d in range(chips):
        target = lax.rem(chip + d, chips)
        span = pl.ds(pl.multiple_of(target * piece, piece), piece)
        outs[d][...] = acc[:, span, :].astype(outs[d].dtype)


def head_sum_kernel(count, mine, *refs):
    parts, outs = refs[: len(refs) - count], refs[len(refs) - count :]
    for i in range(count):
        total = mine[i]
        for part in parts:
            total = total + part[i].astype(F32)
        outs[i][...] = total.astype(BF16)


def fold(array, reduce):
    rows, lanes = array.shape
    return reduce(array.reshape(rows // 8, 8, lanes), axis=0)


def causal(array, first_col, first_pos, other):
    col = lax.broadcasted_iota(jnp.int32, array.shape, 0) + first_col
    pos = lax.broadcasted_iota(jnp.int32, array.shape, 1) + first_pos
    return jnp.where(col <= pos, array, other)


def row_sums(s_ref, dp_ref, factor):
    block_len = s_ref.shape[0]
    step = min(64, block_len)
    spans = [pl.ds(c, step) for c in range(0, block_len, step)]
    top = fold(s_ref[spans[0], :], jnp.max)
    for span in spans[1:]:
        top = jnp.maximum(top, fold(s_ref[span, :], jnp.max))
    top = jnp.max(top, axis=0, keepdims=True) * factor
    total = weighted = jnp.zeros((8, block_len), F32)
    for span in spans:
        terms = jnp.exp2(s_ref[span, :] * factor - top)
        total = total + fold(terms, jnp.sum)
        weighted = weighted + fold(terms * dp_ref[span, :], jnp.sum)
    total = jnp.sum(total, axis=0, keepdims=True)
    return top, total, jnp.sum(weighted, axis=0, keepdims=True)


def local_stats_kernel(factor, blocks_here, chosen, q, do, keys, values, stats, s_buf, dp_buf):
    block_len = keys.shape[1]
    half = block_len // 2

    def per_row(row, _):
        start = row * block_len
        span = pl.ds(start, block_len)
        late = pl.ds(start + half, half)

        s_buf[:half, :] = causal(dot_nt(keys[row, :half], q[span, :]), 0, 0, -jnp.inf)
        s_buf[half:, :half] = jnp.full((half, half), -jnp.inf, F32)
        s_buf[half:, half:] = causal(dot_nt(keys[row, half:], q[late, :]), 0, 0, -jnp.inf)
        dp_buf[:half, :] = dot_nt(values[row, :half], do[span, :])
        dp_buf[half:, :half] = jnp.zeros((half, half), F32)
        dp_buf[half:, half:] = dot_nt(values[row, half:], do[late, :])
        top, total, weighted = row_sums(s_buf, dp_buf, factor)
        stats[row, 0:1, :] = top
        stats[row, 1:2, :] = total
        stats[row, 2:3, :] = weighted
        for t in range(3):
            slot = slot_of(chosen, blocks_here, row, t)

            @pl.when((slot >= 0) & (slot < blocks_here))
            def _():
                s_buf[...] = dot_nt(keys[slot], q[span, :])
                dp_buf[...] = dot_nt(values[slot], do[span, :])
                more_top, more, more_weighted = row_sums(s_buf, dp_buf, factor)
                old = stats[row, 0:1, :]
                top = jnp.maximum(old, more_top)
                scale_old = jnp.exp2(old - top)
                scale_new = jnp.exp2(more_top - top)
                stats[row, 0:1, :] = top
                stats[row, 1:2, :] = stats[row, 1:2, :] * scale_old + more * scale_new
                stats[row, 2:3, :] = stats[row, 2:3, :] * scale_old + more_weighted * scale_new

        return 0

    lax.fori_loop(0, blocks_here, per_row, 0)


def remote_kernel(
    factor, scaling, blocks_here, chips, far, near, piece, chosen, q, do, stats, *refs
):
    near_refs, far_refs, refs = refs[:2], refs[2 : 2 + 2 * chips], refs[2 + 2 * chips :]
    keep, send, final, grad_qt, rows, acc, s_buf, dp_buf, parts = refs
    place = lax.axis_index("head")
    core, chip = lax.rem(place, 2), lax.div(place, 2)
    block_len = rows.shape[2]

    def lay(kind, which):
        for i, s in enumerate(near):
            rows[kind, s] = near_refs[which][i]
        for d in range(chips):
            source = lax.rem(chip + chips - d, chips)
            span = pl.ds(pl.multiple_of(source * piece, piece), piece)
            for i, s in enumerate(far):
                rows[kind, s, span, :] = far_refs[2 * d + which][i]

    @pl.when(core == 0)
    def _():
        lay(0, 0)
        lay(1, 1)

    @pl.when(core != 0)
    def _():
        lay(0, 1)
        lay(1, 0)

    acc[...] = jnp.zeros_like(acc)

    def per_row(row, _):
        span = pl.ds(row * block_len, block_len)
        parts[0, 0:3, :] = stats[row, 0:3, :]
        for t in range(3):
            slot = slot_of(chosen, blocks_here, row, t) - blocks_here

            @pl.when(slot >= 0)
            def _():
                s_buf[t] = dot_nt(rows[0, slot], q[span, :])
                dp_buf[t] = dot_nt(rows[1, slot], do[span, :])
                top, total, weighted = row_sums(s_buf.at[t], dp_buf.at[t], factor)
                parts[t + 1, 0:1, :] = top
                parts[t + 1, 1:2, :] = total
                parts[t + 1, 2:3, :] = weighted

            @pl.when(slot < 0)
            def _():
                parts[t + 1, 0:1, :] = jnp.full((1, block_len), -jnp.inf, F32)
                parts[t + 1, 1:3, :] = jnp.zeros((2, block_len), F32)

        top = parts[0, 0:1, :]
        for t in range(3):
            top = jnp.maximum(top, parts[t + 1, 0:1, :])
        total = jnp.zeros_like(top)
        weighted = jnp.zeros_like(top)
        for t in range(4):
            scale = jnp.exp2(parts[t, 0:1, :] - top)
            total = total + scale * parts[t, 1:2, :]
            weighted = weighted + scale * parts[t, 2:3, :]
        final[row, 0:1, :] = top + jnp.log2(total)
        final[row, 1:2, :] = weighted / total
        grad_qt[row] = jnp.zeros_like(grad_qt[row])
        for t in range(3):
            slot = slot_of(chosen, blocks_here, row, t) - blocks_here

            @pl.when(slot >= 0)
            def _():
                level = final[row, 0:1, :]
                delta = final[row, 1:2, :]
                weights = jnp.exp2(s_buf[t] * factor - level)
                dscores = (weights * (dp_buf[t] - delta)).astype(BF16)
                acc[1, slot] += dot_nn(weights.astype(BF16), do[span, :])
                acc[0, slot] += dot_nn(dscores, q[span, :])
                grad_qt[row] += dot_nn(rows[0, slot].T, dscores)

        return 0

    lax.fori_loop(0, blocks_here, per_row, 0)
    keep_scale = jnp.where(core == 0, scaling, 1.0)
    send_scale = jnp.where(core == 0, 1.0, scaling)
    keep[...] = (acc[core] * keep_scale).astype(BF16)
    send[...] = (acc[1 - core] * send_scale).astype(BF16)


def local_kernel(
    factor, scaling, blocks_here, chosen, q, do, keys, values, final, grad_qt,
    keep, send, grad_q,
    acc, total_qt,
):
    core = lax.rem(lax.axis_index("head"), 2)
    block_len = keys.shape[1]
    half = block_len // 2
    acc[...] = jnp.zeros_like(acc)

    def per_row(row, _):
        start = row * block_len
        span = pl.ds(start, block_len)

        def rows_from(ref, first):
            return ref[pl.ds(start + first, block_len - first), :]

        def products(slot, c, first):
            cut = pl.ds(c, half)
            scores = dot_nt(keys[slot, cut, :], rows_from(q, first))
            return scores, dot_nt(values[slot, cut, :], rows_from(do, first))

        def pair(slot, seconds, masked):
            parts = ((0, 0), (half, seconds))
            ready = [products(slot, c, first) for c, first in parts]
            sides = []
            for (c, first), (scores, dprobs) in zip(parts, ready):
                weights = jnp.exp2(scores * factor - final[row, 0:1, first:])
                if masked:
                    weights = causal(weights, c, first, 0.0)
                dscores = (weights * (dprobs - final[row, 1:2, first:])).astype(BF16)
                sides.append((weights.astype(BF16), dscores))
            for (c, first), (weights, dscores) in zip(parts, sides):
                cut = pl.ds(c, half)
                acc[1, slot, cut, :] += dot_nn(weights, rows_from(do, first))
                acc[0, slot, cut, :] += dot_nn(dscores, rows_from(q, first))
                total_qt[:, first:] += dot_nn(keys[slot, cut, :].T, dscores)

        total_qt[...] = grad_qt[row]
        pair(row, half, True)
        for t in range(3):
            slot = slot_of(chosen, blocks_here, row, t)

            @pl.when((slot >= 0) & (slot < blocks_here))
            def _():
                pair(slot, 0, False)

        grad_q[span, :] = (total_qt[...].T * scaling).astype(BF16)
        return 0

    lax.fori_loop(0, blocks_here, per_row, 0)
    keep_scale = jnp.where(core == 0, scaling, 1.0)
    send_scale = jnp.where(core == 0, 1.0, scaling)
    keep[...] = (acc[core] * keep_scale).astype(BF16)
    send[...] = (acc[1 - core] * send_scale).astype(BF16)


def far_return_kernel(far, asked, *refs):
    back, acc = refs[:-1], refs[-1]
    acc[...] = jnp.zeros_like(acc)
    for i, s in enumerate(far):
        slot = asked[s] - 1

        @pl.when(slot >= 0)
        def _():
            acc[slot] += back[i][...].astype(F32)


def owner_kernel(returned, mine, *refs):
    others, out = refs[:-1], refs[-1]
    total = mine[...] + returned[...]
    for part in others:
        total = total + part[...].astype(F32)
    out[...] = total.astype(BF16)


def spread_kernel(chips, piece, *refs):
    pieces, (grad_k, grad_v) = refs[: 2 * chips], refs[2 * chips :]
    place = lax.axis_index("head")
    core, chip = lax.rem(place, 2), lax.div(place, 2)

    def lay(out, which):
        for d in range(chips):
            source = lax.rem(chip + chips - d, chips)
            span = pl.ds(pl.multiple_of(source * piece, piece), piece)
            out[:, span, :] = pieces[2 * d + which][...]

    @pl.when(core == 0)
    def _():
        lay(grad_k, 0)
        lay(grad_v, 1)

    @pl.when(core != 0)
    def _():
        lay(grad_k, 1)
        lay(grad_v, 0)


def params(size):
    return pltpu.CompilerParams(vmem_limit_bytes=min(size + 12 * 1024 * 1024, VMEM_LIMIT))


def body(queries, keys, values, dout, selected):
    tok_rows, head_count, feature = queries.shape
    blocks_here = selected.shape[0]
    block_len = tok_rows // blocks_here
    ctx_count = lax.axis_size("ctx")
    heads = lax.axis_size("head")
    chips = heads // 2
    piece = block_len // chips
    scaling = 1.0 / math.sqrt(feature)
    factor = scaling * math.log2(math.e)
    shifts = ctx_count - 1
    far = [s for s in reversed(range(shifts - 1)) if 2 * (s + 2) >= ctx_count]
    near = [s for s in range(shifts) if s not in far]

    q2 = queries.reshape(tok_rows, feature)
    do2 = dout.reshape(tok_rows, feature)
    key_blocks = keys.reshape(blocks_here, block_len, feature)
    value_blocks = values.reshape(blocks_here, block_len, feature)
    remote_shape = (shifts, block_len, feature)
    local_shape = (blocks_here, block_len, feature)

    smem = pl.BlockSpec(memory_space=pltpu.SMEM)
    whole = pl.BlockSpec(memory_space=pltpu.VMEM)
    hbm = pl.BlockSpec(memory_space=pltpu.HBM)
    stat_type = jax.ShapeDtypeStruct((blocks_here, 8, block_len), F32)
    far_type = jax.ShapeDtypeStruct(remote_shape, BF16)
    own_type = jax.ShapeDtypeStruct(local_shape, BF16)
    block_type = jax.ShapeDtypeStruct((block_len, feature), BF16)
    piece_type = jax.ShapeDtypeStruct((piece, feature), BF16)
    qt_type = jax.ShapeDtypeStruct((blocks_here, feature, block_len), F32)
    pair_flops = 2 * block_len * block_len * feature
    block_bytes = block_len * feature * 2
    pair_bytes = block_len * block_len * 4

    def pieces_type(count, dtype):
        return jax.ShapeDtypeStruct((count, piece, feature), dtype)

    def cost(matmuls, size):
        return pl.CostEstimate(
            flops=matmuls * pair_flops, bytes_accessed=size, transcendentals=matmuls * block_len**2
        )

    def swap(array):
        return lax.ppermute(array, "head", [(h, h ^ 1) for h in range(heads)])

    def to_chip(array, d):
        return lax.ppermute(array, "head", [(h, (h + 2 * d) % heads) for h in range(heads)])

    def to_owner(array, s):
        return lax.ppermute(array, "ctx", [(c, c - s - 1) for c in range(s + 1, ctx_count)])

    def to_reader(array, s):
        return lax.ppermute(array, "ctx", [(c - s - 1, c) for c in range(s + 1, ctx_count)])

    everyone = lax.all_to_all(
        jnp.broadcast_to(selected.reshape(1, 3 * blocks_here), (ctx_count, 3 * blocks_here)),
        "ctx", split_axis=0, concat_axis=0, tiled=True,
    )
    asked, *sent = pl.pallas_call(
        functools.partial(pick_kernel, blocks_here, ctx_count, chips, far, piece),
        in_specs=[smem, hbm, hbm],
        out_specs=[smem] + [whole] * shifts,
        out_shape=[jax.ShapeDtypeStruct((shifts,), jnp.int32)]
        + [piece_type if s in far else block_type for s in range(shifts)],
        scratch_shapes=[pltpu.SemaphoreType.DMA((shifts,))],
        name="pick_rows",
    )(everyone, key_blocks, value_blocks)

    far_mine = jnp.stack([to_reader(sent[s], s) for s in far])
    near_parts = [to_reader(sent[s], s) for s in near]
    far_mine, chosen = lax.optimization_barrier((far_mine, selected))
    far_more = [to_chip(far_mine, d) for d in range(1, chips)]
    stats = pl.pallas_call(
        functools.partial(local_stats_kernel, factor, blocks_here),
        in_specs=[smem] + [whole] * 4,
        out_specs=whole,
        out_shape=stat_type,
        scratch_shapes=[pltpu.VMEM((block_len, block_len), F32)] * 2,
        compiler_params=params(4 * blocks_here * block_bytes + 2 * pair_bytes),
        cost_estimate=cost(30, 4 * tok_rows * feature * 2),
        name="local_stats",
    )(chosen, q2, do2, key_blocks, value_blocks)
    near_parts, far_held, stats = lax.optimization_barrier((near_parts, far_mine, stats))
    near_mine = jnp.stack(near_parts)
    row_sets = [near_mine, swap(near_mine), far_held, swap(far_held)]
    for part in far_more:
        row_sets += [part, swap(part)]

    keep_far, send_far, final, grad_qt = pl.pallas_call(
        functools.partial(
            remote_kernel, factor, scaling, blocks_here, chips, far, near, piece
        ),
        in_specs=[smem] + [whole] * (3 + len(row_sets)),
        out_specs=[whole] * 4,
        out_shape=[far_type, far_type, stat_type, qt_type],
        scratch_shapes=[
            pltpu.VMEM((2,) + remote_shape, BF16),
            pltpu.VMEM((2,) + remote_shape, F32),
            pltpu.VMEM((3, block_len, block_len), F32),
            pltpu.VMEM((3, block_len, block_len), F32),
            pltpu.VMEM((4, 8, block_len), F32),
        ],
        compiler_params=params((10 * shifts + 4 * blocks_here) * block_bytes + 6 * pair_bytes),
        cost_estimate=cost(60, 8 * tok_rows * feature * 2),
        name="remote_pairs",
    )(chosen, q2, do2, stats, *row_sets)

    def head_sums(mine, parts, count):
        return pl.pallas_call(
            functools.partial(head_sum_kernel, count),
            in_specs=[whole] * (1 + len(parts)),
            out_specs=[whole] * count,
            out_shape=[piece_type] * count,
            compiler_params=params(4 * count * block_bytes),
            name="head_sum",
        )(mine, *parts)

    chip_far = pl.pallas_call(
        functools.partial(chip_sum_kernel, chips, piece, far, near),
        in_specs=[whole, whole],
        out_specs=[whole] * (chips + len(near)),
        out_shape=[pieces_type(len(far), F32)]
        + [pieces_type(len(far), BF16)] * (chips - 1)
        + [block_type] * len(near),
        compiler_params=params(4 * shifts * block_bytes),
        name="chip_sum",
    )(keep_far, swap(send_far))
    chip_far, final = lax.optimization_barrier((chip_far, final))
    far_sums, near_sums = chip_far[:chips], chip_far[chips:]
    far_parts = [to_chip(far_sums[d], d) for d in range(1, chips)]
    near_back = [to_owner(near_sums[i], s) for i, s in enumerate(near)]
    keep_own, send_own, grad_q = pl.pallas_call(
        functools.partial(local_kernel, factor, scaling, blocks_here),
        in_specs=[smem] + [whole] * 6,
        out_specs=[whole] * 3,
        out_shape=[own_type, own_type, jax.ShapeDtypeStruct((tok_rows, feature), BF16)],
        scratch_shapes=[
            pltpu.VMEM((2,) + local_shape, F32),
            pltpu.VMEM((feature, block_len), F32),
        ],
        compiler_params=params(14 * blocks_here * block_bytes),
        cost_estimate=cost(60, 8 * tok_rows * feature * 2),
        name="local_pairs",
    )(chosen, q2, do2, key_blocks, value_blocks, final, grad_qt)
    far_parts, near_back, keep_own, send_own = lax.optimization_barrier(
        (far_parts, near_back, keep_own, send_own)
    )
    own_sums = pl.pallas_call(
        functools.partial(own_sum_kernel, chips, piece, near),
        in_specs=[smem] + [whole] * (2 + len(near)),
        out_specs=[whole] * chips,
        out_shape=[pieces_type(blocks_here, F32)]
        + [pieces_type(blocks_here, BF16)] * (chips - 1),
        scratch_shapes=[pltpu.VMEM(local_shape, F32)],
        compiler_params=params((8 * blocks_here + len(near)) * block_bytes),
        name="own_sum",
    )(asked, keep_own, swap(send_own), *near_back)
    own_parts = [to_chip(own_sums[d], d) for d in range(1, chips)]
    far_out = head_sums(far_sums[0], far_parts, len(far))
    far_back = [to_owner(far_out[i], s) for i, s in enumerate(far)]
    returned = pl.pallas_call(
        functools.partial(far_return_kernel, far),
        in_specs=[smem] + [whole] * len(far),
        out_specs=whole,
        out_shape=pieces_type(blocks_here, F32),
        compiler_params=params((2 * blocks_here + len(far)) * block_bytes),
        cost_estimate=cost(600, 8 * tok_rows * feature * 2),
        name="far_returns",
    )(asked, *far_back)
    mine = pl.pallas_call(
        owner_kernel,
        in_specs=[whole] * (1 + chips),
        out_specs=whole,
        out_shape=pieces_type(blocks_here, BF16),
        compiler_params=params(6 * blocks_here * block_bytes),
        name="owner_sum",
    )(returned, own_sums[0], *own_parts)
    spread = [mine, swap(mine)]
    for d in range(1, chips):
        part = to_chip(mine, d)
        spread += [part, swap(part)]
    grad_keys, grad_values = pl.pallas_call(
        functools.partial(spread_kernel, chips, piece),
        in_specs=[whole] * len(spread),
        out_specs=[whole] * 2,
        out_shape=[own_type] * 2,
        compiler_params=params(4 * blocks_here * block_bytes),
        name="spread",
    )(*spread)
    return (
        grad_q.reshape(tok_rows, head_count, feature),
        grad_keys.reshape(tok_rows, feature),
        grad_values.reshape(tok_rows, feature),
    )


def solution(mesh):
    return jax.shard_map(
        body,
        mesh=mesh,
        in_specs=(
            P("ctx", "head", None),
            P("ctx", None),
            P("ctx", None),
            P("ctx", "head", None),
            P("ctx", None),
        ),
        out_specs=(P("ctx", "head", None), P("ctx", None), P("ctx", None)),
        check_vma=False,
    )
```

```python
import functools
import math

import jax
import jax.numpy as jnp
from jax import lax
from jax.experimental import pallas as pl
from jax.experimental.pallas import tpu as pltpu
from jax.sharding import PartitionSpec as P

F32 = jnp.float32
BF16 = jnp.bfloat16
VMEM_LIMIT = 56 * 1024 * 1024


def dot_nt(a, b):
    return lax.dot_general(a, b, (((1,), (1,)), ((), ())), preferred_element_type=F32)


def dot_nn(a, b):
    return lax.dot_general(a, b, (((1,), (0,)), ((), ())), preferred_element_type=F32)


def slot_of(chosen, blocks_here, row, t):
    ctx_self = lax.axis_index("ctx")
    entry = chosen[row, t]
    owner = lax.div(entry, jnp.int32(blocks_here))
    apart = ctx_self - owner
    slot = jnp.where(apart == 0, entry - owner * blocks_here, blocks_here + apart - 1)
    return jnp.where(entry != ctx_self * blocks_here + row, slot, -1)


def pick_kernel(blocks_here, count, chips, far, piece, chosen, keys, values, asked, *refs):
    outs, sems = refs[:-1], refs[-1]
    ctx_self = lax.axis_index("ctx")
    place = lax.axis_index("head")
    core, chip = lax.rem(place, 2), lax.div(place, 2)
    first = ctx_self * blocks_here
    span = pl.ds(pl.multiple_of(chip * piece, piece), piece)

    def copy(source, s, slot):
        rows = source.at[slot, span, :] if s in far else source.at[slot]
        return pltpu.make_async_copy(rows, outs[s], sems.at[s])

    for s in range(count - 1):
        peer = ctx_self + s + 1
        near = jnp.minimum(peer, count - 1)
        found = jnp.int32(0)
        for row in range(blocks_here):
            for t in range(3):
                entry = chosen[near, row * 3 + t]
                hit = (entry >= first) & (entry < first + blocks_here)
                found = jnp.where(hit, entry - first + 1, found)
        found = jnp.where(peer < count, found, 0)
        asked[s] = found
        slot = jnp.maximum(found - 1, 0)

        @pl.when(core == 0)
        def _():
            copy(keys, s, slot).start()

        @pl.when(core != 0)
        def _():
            copy(values, s, slot).start()

    for s in range(count - 1):
        copy(keys, s, 0).wait()


def chip_sum_kernel(chips, piece, far, near, mine, theirs, *outs):
    chip = lax.div(lax.axis_index("head"), 2)
    for d in range(chips):
        target = lax.rem(chip + d, chips)
        span = pl.ds(pl.multiple_of(target * piece, piece), piece)
        for i, s in enumerate(far):
            total = mine[s, span, :].astype(F32) + theirs[s, span, :].astype(F32)
            outs[d][i] = total.astype(outs[d].dtype)
    for i, s in enumerate(near):
        outs[chips + i][...] = (mine[s].astype(F32) + theirs[s].astype(F32)).astype(BF16)


def own_sum_kernel(chips, piece, near, asked, mine, theirs, *refs):
    back, outs, acc = refs[: len(near)], refs[len(near) : -1], refs[-1]
    chip = lax.div(lax.axis_index("head"), 2)
    acc[...] = mine[...].astype(F32) + theirs[...].astype(F32)
    for i, s in enumerate(near):
        slot = asked[s] - 1

        @pl.when(slot >= 0)
        def _():
            acc[slot] += back[i][...].astype(F32)

    for d in range(chips):
        target = lax.rem(chip + d, chips)
        span = pl.ds(pl.multiple_of(target * piece, piece), piece)
        outs[d][...] = acc[:, span, :].astype(outs[d].dtype)


def head_sum_kernel(count, mine, *refs):
    parts, outs = refs[: len(refs) - count], refs[len(refs) - count :]
    for i in range(count):
        total = mine[i]
        for part in parts:
            total = total + part[i].astype(F32)
        outs[i][...] = total.astype(BF16)


def fold(array, reduce):
    rows, lanes = array.shape
    return reduce(array.reshape(rows // 8, 8, lanes), axis=0)


def causal(array, first_col, first_pos, other):
    col = lax.broadcasted_iota(jnp.int32, array.shape, 0) + first_col
    pos = lax.broadcasted_iota(jnp.int32, array.shape, 1) + first_pos
    return jnp.where(col <= pos, array, other)


def row_sums(s_ref, dp_ref, factor):
    block_len = s_ref.shape[0]
    step = min(64, block_len)
    spans = [pl.ds(c, step) for c in range(0, block_len, step)]
    top = fold(s_ref[spans[0], :], jnp.max)
    for span in spans[1:]:
        top = jnp.maximum(top, fold(s_ref[span, :], jnp.max))
    top = jnp.max(top, axis=0, keepdims=True) * factor
    total = weighted = jnp.zeros((8, block_len), F32)
    for span in spans:
        terms = jnp.exp2(s_ref[span, :] * factor - top)
        total = total + fold(terms, jnp.sum)
        weighted = weighted + fold(terms * dp_ref[span, :], jnp.sum)
    total = jnp.sum(total, axis=0, keepdims=True)
    return top, total, jnp.sum(weighted, axis=0, keepdims=True)


def local_stats_kernel(factor, blocks_here, chosen, q, do, keys, values, stats, s_buf, dp_buf):
    block_len = keys.shape[1]
    half = block_len // 2

    def per_row(row, _):
        start = row * block_len
        span = pl.ds(start, block_len)
        late = pl.ds(start + half, half)

        s_buf[:half, :] = causal(dot_nt(keys[row, :half], q[span, :]), 0, 0, -jnp.inf)
        s_buf[half:, :half] = jnp.full((half, half), -jnp.inf, F32)
        s_buf[half:, half:] = causal(dot_nt(keys[row, half:], q[late, :]), 0, 0, -jnp.inf)
        dp_buf[:half, :] = dot_nt(values[row, :half], do[span, :])
        dp_buf[half:, :half] = jnp.zeros((half, half), F32)
        dp_buf[half:, half:] = dot_nt(values[row, half:], do[late, :])
        top, total, weighted = row_sums(s_buf, dp_buf, factor)
        stats[row, 0:1, :] = top
        stats[row, 1:2, :] = total
        stats[row, 2:3, :] = weighted
        for t in range(3):
            slot = slot_of(chosen, blocks_here, row, t)

            @pl.when((slot >= 0) & (slot < blocks_here))
            def _():
                s_buf[...] = dot_nt(keys[slot], q[span, :])
                dp_buf[...] = dot_nt(values[slot], do[span, :])
                more_top, more, more_weighted = row_sums(s_buf, dp_buf, factor)
                old = stats[row, 0:1, :]
                top = jnp.maximum(old, more_top)
                scale_old = jnp.exp2(old - top)
                scale_new = jnp.exp2(more_top - top)
                stats[row, 0:1, :] = top
                stats[row, 1:2, :] = stats[row, 1:2, :] * scale_old + more * scale_new
                stats[row, 2:3, :] = stats[row, 2:3, :] * scale_old + more_weighted * scale_new

        return 0

    lax.fori_loop(0, blocks_here, per_row, 0)


def remote_kernel(
    factor, scaling, blocks_here, chips, far, near, piece, chosen, q, do, stats, *refs
):
    near_refs, far_refs, refs = refs[:2], refs[2 : 2 + 2 * chips], refs[2 + 2 * chips :]
    keep, send, final, ds_far, rows, acc, s_buf, dp_buf, parts = refs
    place = lax.axis_index("head")
    core, chip = lax.rem(place, 2), lax.div(place, 2)
    block_len = rows.shape[2]

    def lay(kind, which):
        for i, s in enumerate(near):
            rows[kind, s] = near_refs[which][i]
        for d in range(chips):
            source = lax.rem(chip + chips - d, chips)
            span = pl.ds(pl.multiple_of(source * piece, piece), piece)
            for i, s in enumerate(far):
                rows[kind, s, span, :] = far_refs[2 * d + which][i]

    @pl.when(core == 0)
    def _():
        lay(0, 0)
        lay(1, 1)

    @pl.when(core != 0)
    def _():
        lay(0, 1)
        lay(1, 0)

    acc[...] = jnp.zeros_like(acc)

    def per_row(row, _):
        span = pl.ds(row * block_len, block_len)
        parts[0, 0:3, :] = stats[row, 0:3, :]
        for t in range(3):
            slot = slot_of(chosen, blocks_here, row, t) - blocks_here

            @pl.when(slot >= 0)
            def _():
                s_buf[t] = dot_nt(rows[0, slot], q[span, :])
                dp_buf[t] = dot_nt(rows[1, slot], do[span, :])
                top, total, weighted = row_sums(s_buf.at[t], dp_buf.at[t], factor)
                parts[t + 1, 0:1, :] = top
                parts[t + 1, 1:2, :] = total
                parts[t + 1, 2:3, :] = weighted

            @pl.when(slot < 0)
            def _():
                parts[t + 1, 0:1, :] = jnp.full((1, block_len), -jnp.inf, F32)
                parts[t + 1, 1:3, :] = jnp.zeros((2, block_len), F32)

        top = parts[0, 0:1, :]
        for t in range(3):
            top = jnp.maximum(top, parts[t + 1, 0:1, :])
        total = jnp.zeros_like(top)
        weighted = jnp.zeros_like(top)
        for t in range(4):
            scale = jnp.exp2(parts[t, 0:1, :] - top)
            total = total + scale * parts[t, 1:2, :]
            weighted = weighted + scale * parts[t, 2:3, :]
        final[row, 0:1, :] = top + jnp.log2(total)
        final[row, 1:2, :] = weighted / total
        for t in range(3):
            slot = slot_of(chosen, blocks_here, row, t) - blocks_here

            @pl.when(slot >= 0)
            def _():
                level = final[row, 0:1, :]
                delta = final[row, 1:2, :]
                weights = jnp.exp2(s_buf[t] * factor - level)
                dscores = (weights * (dp_buf[t] - delta)).astype(BF16)
                acc[1, slot] += dot_nn(weights.astype(BF16), do[span, :])
                acc[0, slot] += dot_nn(dscores, q[span, :])
                ds_far[row * 3 + t] = dscores

        return 0

    lax.fori_loop(0, blocks_here, per_row, 0)
    keep_scale = jnp.where(core == 0, scaling, 1.0)
    send_scale = jnp.where(core == 0, 1.0, scaling)
    keep[...] = (acc[core] * keep_scale).astype(BF16)
    send[...] = (acc[1 - core] * send_scale).astype(BF16)


def local_kernel(
    factor, scaling, blocks_here, chosen, q, do, keys, values, final,
    keep, send, ds_own,
    acc,
):
    core = lax.rem(lax.axis_index("head"), 2)
    block_len = keys.shape[1]
    half = block_len // 2
    acc[...] = jnp.zeros_like(acc)

    def per_row(row, _):
        start = row * block_len
        span = pl.ds(start, block_len)

        def rows_from(ref, first):
            return ref[pl.ds(start + first, block_len - first), :]

        def products(slot, c, first):
            cut = pl.ds(c, half)
            scores = dot_nt(keys[slot, cut, :], rows_from(q, first))
            return scores, dot_nt(values[slot, cut, :], rows_from(do, first))

        def pair(slot, t, seconds, masked):
            parts = ((0, 0), (half, seconds))
            ready = [products(slot, c, first) for c, first in parts]
            sides = []
            for (c, first), (scores, dprobs) in zip(parts, ready):
                weights = jnp.exp2(scores * factor - final[row, 0:1, first:])
                if masked:
                    weights = causal(weights, c, first, 0.0)
                dscores = (weights * (dprobs - final[row, 1:2, first:])).astype(BF16)
                sides.append((weights.astype(BF16), dscores))
            for (c, first), (weights, dscores) in zip(parts, sides):
                cut = pl.ds(c, half)
                acc[1, slot, cut, :] += dot_nn(weights, rows_from(do, first))
                acc[0, slot, cut, :] += dot_nn(dscores, rows_from(q, first))
                ds_own[row * 4 + t, cut, first:] = dscores

        ds_own[row * 4 + 3, half:, :half] = jnp.zeros((half, half), BF16)
        pair(row, 3, half, True)
        for t in range(3):
            slot = slot_of(chosen, blocks_here, row, t)

            @pl.when((slot >= 0) & (slot < blocks_here))
            def _():
                pair(slot, t, 0, False)

        return 0

    lax.fori_loop(0, blocks_here, per_row, 0)
    keep_scale = jnp.where(core == 0, scaling, 1.0)
    send_scale = jnp.where(core == 0, 1.0, scaling)
    keep[...] = (acc[core] * keep_scale).astype(BF16)
    send[...] = (acc[1 - core] * send_scale).astype(BF16)


def query_kernel(scaling, blocks_here, chosen, keys, rows, ds_far, ds_own, grad_q, total_qt):
    block_len = keys.shape[1]

    def per_row(row, _):
        total_qt[...] = dot_nn(keys[row].T, ds_own[row * 4 + 3])
        for t in range(3):
            slot = slot_of(chosen, blocks_here, row, t)

            @pl.when((slot >= 0) & (slot < blocks_here))
            def _():
                total_qt[...] += dot_nn(keys[slot].T, ds_own[row * 4 + t])

            @pl.when(slot >= blocks_here)
            def _():
                total_qt[...] += dot_nn(rows[0, slot - blocks_here].T, ds_far[row * 3 + t])

        span = pl.ds(row * block_len, block_len)
        grad_q[span, :] = (total_qt[...].T * scaling).astype(BF16)
        return 0

    lax.fori_loop(0, blocks_here, per_row, 0)


def far_return_kernel(far, asked, *refs):
    back, acc = refs[:-1], refs[-1]
    acc[...] = jnp.zeros_like(acc)
    for i, s in enumerate(far):
        slot = asked[s] - 1

        @pl.when(slot >= 0)
        def _():
            acc[slot] += back[i][...].astype(F32)


def owner_kernel(returned, mine, *refs):
    others, out = refs[:-1], refs[-1]
    total = mine[...] + returned[...]
    for part in others:
        total = total + part[...].astype(F32)
    out[...] = total.astype(BF16)


def spread_kernel(chips, piece, *refs):
    pieces, (grad_k, grad_v) = refs[: 2 * chips], refs[2 * chips :]
    place = lax.axis_index("head")
    core, chip = lax.rem(place, 2), lax.div(place, 2)

    def lay(out, which):
        for d in range(chips):
            source = lax.rem(chip + chips - d, chips)
            span = pl.ds(pl.multiple_of(source * piece, piece), piece)
            out[:, span, :] = pieces[2 * d + which][...]

    @pl.when(core == 0)
    def _():
        lay(grad_k, 0)
        lay(grad_v, 1)

    @pl.when(core != 0)
    def _():
        lay(grad_k, 1)
        lay(grad_v, 0)


def params(size):
    return pltpu.CompilerParams(vmem_limit_bytes=min(size + 12 * 1024 * 1024, VMEM_LIMIT))


def body(queries, keys, values, dout, selected):
    tok_rows, head_count, feature = queries.shape
    blocks_here = selected.shape[0]
    block_len = tok_rows // blocks_here
    ctx_count = lax.axis_size("ctx")
    heads = lax.axis_size("head")
    chips = heads // 2
    piece = block_len // chips
    scaling = 1.0 / math.sqrt(feature)
    factor = scaling * math.log2(math.e)
    shifts = ctx_count - 1
    far = [s for s in reversed(range(shifts - 1)) if 2 * (s + 2) >= ctx_count]
    near = [s for s in range(shifts) if s not in far]

    q2 = queries.reshape(tok_rows, feature)
    do2 = dout.reshape(tok_rows, feature)
    key_blocks = keys.reshape(blocks_here, block_len, feature)
    value_blocks = values.reshape(blocks_here, block_len, feature)
    remote_shape = (shifts, block_len, feature)
    local_shape = (blocks_here, block_len, feature)

    smem = pl.BlockSpec(memory_space=pltpu.SMEM)
    whole = pl.BlockSpec(memory_space=pltpu.VMEM)
    hbm = pl.BlockSpec(memory_space=pltpu.HBM)
    stat_type = jax.ShapeDtypeStruct((blocks_here, 8, block_len), F32)
    far_type = jax.ShapeDtypeStruct(remote_shape, BF16)
    own_type = jax.ShapeDtypeStruct(local_shape, BF16)
    block_type = jax.ShapeDtypeStruct((block_len, feature), BF16)
    piece_type = jax.ShapeDtypeStruct((piece, feature), BF16)
    square = (block_len, block_len)
    ds_bytes = block_len * block_len * 2
    pair_flops = 2 * block_len * block_len * feature
    block_bytes = block_len * feature * 2
    pair_bytes = block_len * block_len * 4

    def pieces_type(count, dtype):
        return jax.ShapeDtypeStruct((count, piece, feature), dtype)

    def cost(matmuls, size):
        return pl.CostEstimate(
            flops=matmuls * pair_flops, bytes_accessed=size, transcendentals=matmuls * block_len**2
        )

    def swap(array):
        return lax.ppermute(array, "head", [(h, h ^ 1) for h in range(heads)])

    def to_chip(array, d):
        return lax.ppermute(array, "head", [(h, (h + 2 * d) % heads) for h in range(heads)])

    def to_owner(array, s):
        return lax.ppermute(array, "ctx", [(c, c - s - 1) for c in range(s + 1, ctx_count)])

    def to_reader(array, s):
        return lax.ppermute(array, "ctx", [(c - s - 1, c) for c in range(s + 1, ctx_count)])

    everyone = lax.all_to_all(
        jnp.broadcast_to(selected.reshape(1, 3 * blocks_here), (ctx_count, 3 * blocks_here)),
        "ctx", split_axis=0, concat_axis=0, tiled=True,
    )
    asked, *sent = pl.pallas_call(
        functools.partial(pick_kernel, blocks_here, ctx_count, chips, far, piece),
        in_specs=[smem, hbm, hbm],
        out_specs=[smem] + [whole] * shifts,
        out_shape=[jax.ShapeDtypeStruct((shifts,), jnp.int32)]
        + [piece_type if s in far else block_type for s in range(shifts)],
        scratch_shapes=[pltpu.SemaphoreType.DMA((shifts,))],
        name="pick_rows",
    )(everyone, key_blocks, value_blocks)

    far_mine = jnp.stack([to_reader(sent[s], s) for s in far])
    near_parts = [to_reader(sent[s], s) for s in near]
    far_mine, chosen = lax.optimization_barrier((far_mine, selected))
    far_more = [to_chip(far_mine, d) for d in range(1, chips)]
    stats = pl.pallas_call(
        functools.partial(local_stats_kernel, factor, blocks_here),
        in_specs=[smem] + [whole] * 4,
        out_specs=whole,
        out_shape=stat_type,
        scratch_shapes=[pltpu.VMEM((block_len, block_len), F32)] * 2,
        compiler_params=params(4 * blocks_here * block_bytes + 2 * pair_bytes),
        cost_estimate=cost(30, 4 * tok_rows * feature * 2),
        name="local_stats",
    )(chosen, q2, do2, key_blocks, value_blocks)
    near_parts, far_held, stats = lax.optimization_barrier((near_parts, far_mine, stats))
    near_mine = jnp.stack(near_parts)
    row_sets = [near_mine, swap(near_mine), far_held, swap(far_held)]
    for part in far_more:
        row_sets += [part, swap(part)]

    keep_far, send_far, final, ds_far, far_rows = pl.pallas_call(
        functools.partial(
            remote_kernel, factor, scaling, blocks_here, chips, far, near, piece
        ),
        in_specs=[smem] + [whole] * (3 + len(row_sets)),
        out_specs=[whole] * 5,
        out_shape=[
            far_type,
            far_type,
            stat_type,
            jax.ShapeDtypeStruct((3 * blocks_here,) + square, BF16),
            jax.ShapeDtypeStruct((2,) + remote_shape, BF16),
        ],
        scratch_shapes=[
            pltpu.VMEM((2,) + remote_shape, F32),
            pltpu.VMEM((3, block_len, block_len), F32),
            pltpu.VMEM((3, block_len, block_len), F32),
            pltpu.VMEM((4, 8, block_len), F32),
        ],
        compiler_params=params(
            (10 * shifts + 4 * blocks_here) * block_bytes
            + 6 * pair_bytes
            + 3 * blocks_here * ds_bytes
        ),
        cost_estimate=cost(60, 8 * tok_rows * feature * 2),
        name="remote_pairs",
    )(chosen, q2, do2, stats, *row_sets)

    def head_sums(mine, parts, count):
        return pl.pallas_call(
            functools.partial(head_sum_kernel, count),
            in_specs=[whole] * (1 + len(parts)),
            out_specs=[whole] * count,
            out_shape=[piece_type] * count,
            compiler_params=params(4 * count * block_bytes),
            name="head_sum",
        )(mine, *parts)

    chip_far = pl.pallas_call(
        functools.partial(chip_sum_kernel, chips, piece, far, near),
        in_specs=[whole, whole],
        out_specs=[whole] * (chips + len(near)),
        out_shape=[pieces_type(len(far), F32)]
        + [pieces_type(len(far), BF16)] * (chips - 1)
        + [block_type] * len(near),
        compiler_params=params(4 * shifts * block_bytes),
        name="chip_sum",
    )(keep_far, swap(send_far))
    chip_far, final = lax.optimization_barrier((chip_far, final))
    far_sums, near_sums = chip_far[:chips], chip_far[chips:]
    far_parts = [to_chip(far_sums[d], d) for d in range(1, chips)]
    near_back = [to_owner(near_sums[i], s) for i, s in enumerate(near)]
    keep_own, send_own, ds_own = pl.pallas_call(
        functools.partial(local_kernel, factor, scaling, blocks_here),
        in_specs=[smem] + [whole] * 5,
        out_specs=[whole] * 3,
        out_shape=[
            own_type,
            own_type,
            jax.ShapeDtypeStruct((4 * blocks_here,) + square, BF16),
        ],
        scratch_shapes=[pltpu.VMEM((2,) + local_shape, F32)],
        compiler_params=params(12 * blocks_here * block_bytes + 4 * blocks_here * ds_bytes),
        cost_estimate=cost(60, 8 * tok_rows * feature * 2),
        name="local_pairs",
    )(chosen, q2, do2, key_blocks, value_blocks, final)
    far_parts, near_back, keep_own, send_own = lax.optimization_barrier(
        (far_parts, near_back, keep_own, send_own)
    )
    own_sums = pl.pallas_call(
        functools.partial(own_sum_kernel, chips, piece, near),
        in_specs=[smem] + [whole] * (2 + len(near)),
        out_specs=[whole] * chips,
        out_shape=[pieces_type(blocks_here, F32)]
        + [pieces_type(blocks_here, BF16)] * (chips - 1),
        scratch_shapes=[pltpu.VMEM(local_shape, F32)],
        compiler_params=params((8 * blocks_here + len(near)) * block_bytes),
        name="own_sum",
    )(asked, keep_own, swap(send_own), *near_back)
    own_parts = [to_chip(own_sums[d], d) for d in range(1, chips)]
    far_out = head_sums(far_sums[0], far_parts, len(far))
    far_back = [to_owner(far_out[i], s) for i, s in enumerate(far)]
    returned = pl.pallas_call(
        functools.partial(far_return_kernel, far),
        in_specs=[smem] + [whole] * len(far),
        out_specs=whole,
        out_shape=pieces_type(blocks_here, F32),
        compiler_params=params((2 * blocks_here + len(far)) * block_bytes),
        cost_estimate=cost(600, 8 * tok_rows * feature * 2),
        name="far_returns",
    )(asked, *far_back)
    mine = pl.pallas_call(
        owner_kernel,
        in_specs=[whole] * (1 + chips),
        out_specs=whole,
        out_shape=pieces_type(blocks_here, BF16),
        compiler_params=params(6 * blocks_here * block_bytes),
        name="owner_sum",
    )(returned, own_sums[0], *own_parts)
    mine, ds_own = lax.optimization_barrier((mine, ds_own))
    gathered = [to_chip(mine, d) for d in range(1, chips)]
    grad_q = pl.pallas_call(
        functools.partial(query_kernel, scaling, blocks_here),
        in_specs=[smem] + [whole] * 4,
        out_specs=whole,
        out_shape=jax.ShapeDtypeStruct((tok_rows, feature), BF16),
        scratch_shapes=[pltpu.VMEM((feature, block_len), F32)],
        compiler_params=params(
            (3 * blocks_here + 2 * shifts) * block_bytes + 7 * blocks_here * ds_bytes
        ),
        cost_estimate=cost(30, 8 * tok_rows * feature * 2),
        name="query_grads",
    )(chosen, key_blocks, far_rows, ds_far, ds_own)
    gathered, grad_q = lax.optimization_barrier((gathered, grad_q))
    spread = [mine, swap(mine)]
    for part in gathered:
        spread += [part, swap(part)]
    grad_keys, grad_values = pl.pallas_call(
        functools.partial(spread_kernel, chips, piece),
        in_specs=[whole] * len(spread),
        out_specs=[whole] * 2,
        out_shape=[own_type] * 2,
        compiler_params=params(4 * blocks_here * block_bytes),
        name="spread",
    )(*spread)
    return (
        grad_q.reshape(tok_rows, head_count, feature),
        grad_keys.reshape(tok_rows, feature),
        grad_values.reshape(tok_rows, feature),
    )


def solution(mesh):
    return jax.shard_map(
        body,
        mesh=mesh,
        in_specs=(
            P("ctx", "head", None),
            P("ctx", None),
            P("ctx", None),
            P("ctx", "head", None),
            P("ctx", None),
        ),
        out_specs=(P("ctx", "head", None), P("ctx", None), P("ctx", None)),
        check_vma=False,
    )
```

```python
import functools
import math

import jax
import jax.numpy as jnp
from jax import lax
from jax.experimental import pallas as pl
from jax.experimental.pallas import tpu as pltpu
from jax.sharding import PartitionSpec as P

F32 = jnp.float32
BF16 = jnp.bfloat16
VMEM_LIMIT = 56 * 1024 * 1024


def dot_nt(a, b):
    return lax.dot_general(a, b, (((1,), (1,)), ((), ())), preferred_element_type=F32)


def dot_nn(a, b):
    return lax.dot_general(a, b, (((1,), (0,)), ((), ())), preferred_element_type=F32)


def slot_of(chosen, blocks_here, row, t):
    ctx_self = lax.axis_index("ctx")
    entry = chosen[row, t]
    owner = lax.div(entry, jnp.int32(blocks_here))
    apart = ctx_self - owner
    slot = jnp.where(apart == 0, entry - owner * blocks_here, blocks_here + apart - 1)
    return jnp.where(entry != ctx_self * blocks_here + row, slot, -1)


def pick_kernel(blocks_here, count, chips, far, piece, chosen, keys, values, asked, *refs):
    outs, sems = refs[:-1], refs[-1]
    ctx_self = lax.axis_index("ctx")
    place = lax.axis_index("head")
    core, chip = lax.rem(place, 2), lax.div(place, 2)
    first = ctx_self * blocks_here
    span = pl.ds(pl.multiple_of(chip * piece, piece), piece)

    def copy(source, s, slot):
        rows = source.at[slot, span, :] if s in far else source.at[slot]
        return pltpu.make_async_copy(rows, outs[s], sems.at[s])

    for s in range(count - 1):
        peer = ctx_self + s + 1
        near = jnp.minimum(peer, count - 1)
        found = jnp.int32(0)
        for row in range(blocks_here):
            for t in range(3):
                entry = chosen[near, row * 3 + t]
                hit = (entry >= first) & (entry < first + blocks_here)
                found = jnp.where(hit, entry - first + 1, found)
        found = jnp.where(peer < count, found, 0)
        asked[s] = found
        slot = jnp.maximum(found - 1, 0)

        @pl.when(core == 0)
        def _():
            copy(keys, s, slot).start()

        @pl.when(core != 0)
        def _():
            copy(values, s, slot).start()

    for s in range(count - 1):
        copy(keys, s, 0).wait()


def chip_sum_kernel(chips, piece, far, near, mine, theirs, *outs):
    chip = lax.div(lax.axis_index("head"), 2)
    for d in range(chips):
        target = lax.rem(chip + d, chips)
        span = pl.ds(pl.multiple_of(target * piece, piece), piece)
        for i, s in enumerate(far):
            total = mine[s, span, :].astype(F32) + theirs[s, span, :].astype(F32)
            outs[d][i] = total.astype(outs[d].dtype)
    for i, s in enumerate(near):
        outs[chips + i][...] = (mine[s].astype(F32) + theirs[s].astype(F32)).astype(BF16)


def own_sum_kernel(chips, piece, near, asked, mine, theirs, *refs):
    back, outs, acc = refs[: len(near)], refs[len(near) : -1], refs[-1]
    chip = lax.div(lax.axis_index("head"), 2)
    acc[...] = mine[...].astype(F32) + theirs[...].astype(F32)
    for i, s in enumerate(near):
        slot = asked[s] - 1

        @pl.when(slot >= 0)
        def _():
            acc[slot] += back[i][...].astype(F32)

    for d in range(chips):
        target = lax.rem(chip + d, chips)
        span = pl.ds(pl.multiple_of(target * piece, piece), piece)
        outs[d][...] = acc[:, span, :].astype(outs[d].dtype)


def head_sum_kernel(count, mine, *refs):
    parts, outs = refs[: len(refs) - count], refs[len(refs) - count :]
    for i in range(count):
        total = mine[i]
        for part in parts:
            total = total + part[i].astype(F32)
        outs[i][...] = total.astype(BF16)


def fold(array, reduce):
    rows, lanes = array.shape
    return reduce(array.reshape(rows // 8, 8, lanes), axis=0)


def causal(array, first_col, first_pos, other):
    col = lax.broadcasted_iota(jnp.int32, array.shape, 0) + first_col
    pos = lax.broadcasted_iota(jnp.int32, array.shape, 1) + first_pos
    return jnp.where(col <= pos, array, other)


def row_sums(s_ref, dp_ref, factor):
    block_len = s_ref.shape[0]
    step = min(64, block_len)
    spans = [pl.ds(c, step) for c in range(0, block_len, step)]
    top = fold(s_ref[spans[0], :], jnp.max)
    for span in spans[1:]:
        top = jnp.maximum(top, fold(s_ref[span, :], jnp.max))
    top = jnp.max(top, axis=0, keepdims=True) * factor
    total = weighted = jnp.zeros((8, block_len), F32)
    for span in spans:
        terms = jnp.exp2(s_ref[span, :] * factor - top)
        total = total + fold(terms, jnp.sum)
        weighted = weighted + fold(terms * dp_ref[span, :], jnp.sum)
    total = jnp.sum(total, axis=0, keepdims=True)
    return top, total, jnp.sum(weighted, axis=0, keepdims=True)


def local_stats_kernel(factor, blocks_here, chosen, q, do, keys, values, stats, s_buf, dp_buf):
    block_len = keys.shape[1]
    half = block_len // 2

    def per_row(row, _):
        start = row * block_len
        span = pl.ds(start, block_len)
        late = pl.ds(start + half, half)

        s_buf[:half, :] = causal(dot_nt(keys[row, :half], q[span, :]), 0, 0, -jnp.inf)
        s_buf[half:, :half] = jnp.full((half, half), -jnp.inf, F32)
        s_buf[half:, half:] = causal(dot_nt(keys[row, half:], q[late, :]), 0, 0, -jnp.inf)
        dp_buf[:half, :] = dot_nt(values[row, :half], do[span, :])
        dp_buf[half:, :half] = jnp.zeros((half, half), F32)
        dp_buf[half:, half:] = dot_nt(values[row, half:], do[late, :])
        top, total, weighted = row_sums(s_buf, dp_buf, factor)
        stats[row, 0:1, :] = top
        stats[row, 1:2, :] = total
        stats[row, 2:3, :] = weighted
        for t in range(3):
            slot = slot_of(chosen, blocks_here, row, t)

            @pl.when((slot >= 0) & (slot < blocks_here))
            def _():
                s_buf[...] = dot_nt(keys[slot], q[span, :])
                dp_buf[...] = dot_nt(values[slot], do[span, :])
                more_top, more, more_weighted = row_sums(s_buf, dp_buf, factor)
                old = stats[row, 0:1, :]
                top = jnp.maximum(old, more_top)
                scale_old = jnp.exp2(old - top)
                scale_new = jnp.exp2(more_top - top)
                stats[row, 0:1, :] = top
                stats[row, 1:2, :] = stats[row, 1:2, :] * scale_old + more * scale_new
                stats[row, 2:3, :] = stats[row, 2:3, :] * scale_old + more_weighted * scale_new

        return 0

    lax.fori_loop(0, blocks_here, per_row, 0)


def remote_kernel(
    factor, scaling, blocks_here, chips, far, near, piece, chosen, q, do, stats, *refs
):
    near_refs, far_refs, refs = refs[:2], refs[2 : 2 + 2 * chips], refs[2 + 2 * chips :]
    keep, send, final, grad_qt, rows, acc, s_buf, dp_buf, parts = refs
    place = lax.axis_index("head")
    core, chip = lax.rem(place, 2), lax.div(place, 2)
    block_len = rows.shape[2]

    def lay(kind, which):
        for i, s in enumerate(near):
            rows[kind, s] = near_refs[which][i]
        for d in range(chips):
            source = lax.rem(chip + chips - d, chips)
            span = pl.ds(pl.multiple_of(source * piece, piece), piece)
            for i, s in enumerate(far):
                rows[kind, s, span, :] = far_refs[2 * d + which][i]

    @pl.when(core == 0)
    def _():
        lay(0, 0)
        lay(1, 1)

    @pl.when(core != 0)
    def _():
        lay(0, 1)
        lay(1, 0)

    acc[...] = jnp.zeros_like(acc)

    def per_row(row, _):
        span = pl.ds(row * block_len, block_len)
        parts[0, 0:3, :] = stats[row, 0:3, :]
        for t in range(3):
            slot = slot_of(chosen, blocks_here, row, t) - blocks_here

            @pl.when(slot >= 0)
            def _():
                s_buf[t] = dot_nt(rows[0, slot], q[span, :])
                dp_buf[t] = dot_nt(rows[1, slot], do[span, :])
                top, total, weighted = row_sums(s_buf.at[t], dp_buf.at[t], factor)
                parts[t + 1, 0:1, :] = top
                parts[t + 1, 1:2, :] = total
                parts[t + 1, 2:3, :] = weighted

            @pl.when(slot < 0)
            def _():
                parts[t + 1, 0:1, :] = jnp.full((1, block_len), -jnp.inf, F32)
                parts[t + 1, 1:3, :] = jnp.zeros((2, block_len), F32)

        top = parts[0, 0:1, :]
        for t in range(3):
            top = jnp.maximum(top, parts[t + 1, 0:1, :])
        total = jnp.zeros_like(top)
        weighted = jnp.zeros_like(top)
        for t in range(4):
            scale = jnp.exp2(parts[t, 0:1, :] - top)
            total = total + scale * parts[t, 1:2, :]
            weighted = weighted + scale * parts[t, 2:3, :]
        final[row, 0:1, :] = top + jnp.log2(total)
        final[row, 1:2, :] = weighted / total
        grad_qt[row] = jnp.zeros_like(grad_qt[row])
        for t in range(3):
            slot = slot_of(chosen, blocks_here, row, t) - blocks_here

            @pl.when(slot >= 0)
            def _():
                level = final[row, 0:1, :]
                delta = final[row, 1:2, :]
                weights = jnp.exp2(s_buf[t] * factor - level)
                dscores = (weights * (dp_buf[t] - delta)).astype(BF16)
                acc[1, slot] += dot_nn(weights.astype(BF16), do[span, :])
                acc[0, slot] += dot_nn(dscores, q[span, :])
                grad_qt[row] += dot_nn(rows[0, slot].T, dscores)

        return 0

    lax.fori_loop(0, blocks_here, per_row, 0)
    keep_scale = jnp.where(core == 0, scaling, 1.0)
    send_scale = jnp.where(core == 0, 1.0, scaling)
    keep[...] = (acc[core] * keep_scale).astype(BF16)
    send[...] = (acc[1 - core] * send_scale).astype(BF16)


def local_kernel(
    factor, scaling, blocks_here, chosen, q, do, keys, values, final,
    keep, send, ds_own,
    acc,
):
    core = lax.rem(lax.axis_index("head"), 2)
    block_len = keys.shape[1]
    half = block_len // 2
    acc[...] = jnp.zeros_like(acc)

    def per_row(row, _):
        start = row * block_len
        span = pl.ds(start, block_len)

        def rows_from(ref, first):
            return ref[pl.ds(start + first, block_len - first), :]

        def products(slot, c, first):
            cut = pl.ds(c, half)
            scores = dot_nt(keys[slot, cut, :], rows_from(q, first))
            return scores, dot_nt(values[slot, cut, :], rows_from(do, first))

        def pair(slot, t, seconds, masked):
            parts = ((0, 0), (half, seconds))
            ready = [products(slot, c, first) for c, first in parts]
            sides = []
            for (c, first), (scores, dprobs) in zip(parts, ready):
                weights = jnp.exp2(scores * factor - final[row, 0:1, first:])
                if masked:
                    weights = causal(weights, c, first, 0.0)
                dscores = (weights * (dprobs - final[row, 1:2, first:])).astype(BF16)
                sides.append((weights.astype(BF16), dscores))
            for (c, first), (weights, dscores) in zip(parts, sides):
                cut = pl.ds(c, half)
                acc[1, slot, cut, :] += dot_nn(weights, rows_from(do, first))
                acc[0, slot, cut, :] += dot_nn(dscores, rows_from(q, first))
                ds_own[row * 4 + t, cut, first:] = dscores

        ds_own[row * 4 + 3, half:, :half] = jnp.zeros((half, half), BF16)
        pair(row, 3, half, True)
        for t in range(3):
            slot = slot_of(chosen, blocks_here, row, t)

            @pl.when((slot >= 0) & (slot < blocks_here))
            def _():
                pair(slot, t, 0, False)

        return 0

    lax.fori_loop(0, blocks_here, per_row, 0)
    keep_scale = jnp.where(core == 0, scaling, 1.0)
    send_scale = jnp.where(core == 0, 1.0, scaling)
    keep[...] = (acc[core] * keep_scale).astype(BF16)
    send[...] = (acc[1 - core] * send_scale).astype(BF16)


def query_kernel(scaling, blocks_here, chosen, keys, grad_qt, ds_own, grad_q, total_qt):
    block_len = keys.shape[1]

    def per_row(row, _):
        total_qt[...] = grad_qt[row] + dot_nn(keys[row].T, ds_own[row * 4 + 3])
        for t in range(3):
            slot = slot_of(chosen, blocks_here, row, t)

            @pl.when((slot >= 0) & (slot < blocks_here))
            def _():
                total_qt[...] += dot_nn(keys[slot].T, ds_own[row * 4 + t])

        span = pl.ds(row * block_len, block_len)
        grad_q[span, :] = (total_qt[...].T * scaling).astype(BF16)
        return 0

    lax.fori_loop(0, blocks_here, per_row, 0)


def far_return_kernel(far, asked, *refs):
    back, acc = refs[:-1], refs[-1]
    acc[...] = jnp.zeros_like(acc)
    for i, s in enumerate(far):
        slot = asked[s] - 1

        @pl.when(slot >= 0)
        def _():
            acc[slot] += back[i][...].astype(F32)


def owner_kernel(returned, mine, *refs):
    others, out = refs[:-1], refs[-1]
    total = mine[...] + returned[...]
    for part in others:
        total = total + part[...].astype(F32)
    out[...] = total.astype(BF16)


def spread_kernel(chips, piece, *refs):
    pieces, (grad_k, grad_v) = refs[: 2 * chips], refs[2 * chips :]
    place = lax.axis_index("head")
    core, chip = lax.rem(place, 2), lax.div(place, 2)

    def lay(out, which):
        for d in range(chips):
            source = lax.rem(chip + chips - d, chips)
            span = pl.ds(pl.multiple_of(source * piece, piece), piece)
            out[:, span, :] = pieces[2 * d + which][...]

    @pl.when(core == 0)
    def _():
        lay(grad_k, 0)
        lay(grad_v, 1)

    @pl.when(core != 0)
    def _():
        lay(grad_k, 1)
        lay(grad_v, 0)


def params(size):
    return pltpu.CompilerParams(vmem_limit_bytes=min(size + 12 * 1024 * 1024, VMEM_LIMIT))


def body(queries, keys, values, dout, selected):
    tok_rows, head_count, feature = queries.shape
    blocks_here = selected.shape[0]
    block_len = tok_rows // blocks_here
    ctx_count = lax.axis_size("ctx")
    heads = lax.axis_size("head")
    chips = heads // 2
    piece = block_len // chips
    scaling = 1.0 / math.sqrt(feature)
    factor = scaling * math.log2(math.e)
    shifts = ctx_count - 1
    far = [s for s in reversed(range(shifts - 1)) if 2 * (s + 2) >= ctx_count]
    near = [s for s in range(shifts) if s not in far]

    q2 = queries.reshape(tok_rows, feature)
    do2 = dout.reshape(tok_rows, feature)
    key_blocks = keys.reshape(blocks_here, block_len, feature)
    value_blocks = values.reshape(blocks_here, block_len, feature)
    remote_shape = (shifts, block_len, feature)
    local_shape = (blocks_here, block_len, feature)

    smem = pl.BlockSpec(memory_space=pltpu.SMEM)
    whole = pl.BlockSpec(memory_space=pltpu.VMEM)
    hbm = pl.BlockSpec(memory_space=pltpu.HBM)
    stat_type = jax.ShapeDtypeStruct((blocks_here, 8, block_len), F32)
    far_type = jax.ShapeDtypeStruct(remote_shape, BF16)
    own_type = jax.ShapeDtypeStruct(local_shape, BF16)
    block_type = jax.ShapeDtypeStruct((block_len, feature), BF16)
    piece_type = jax.ShapeDtypeStruct((piece, feature), BF16)
    qt_type = jax.ShapeDtypeStruct((blocks_here, feature, block_len), F32)
    pair_flops = 2 * block_len * block_len * feature
    block_bytes = block_len * feature * 2
    pair_bytes = block_len * block_len * 4

    def pieces_type(count, dtype):
        return jax.ShapeDtypeStruct((count, piece, feature), dtype)

    def cost(matmuls, size):
        return pl.CostEstimate(
            flops=matmuls * pair_flops, bytes_accessed=size, transcendentals=matmuls * block_len**2
        )

    def swap(array):
        return lax.ppermute(array, "head", [(h, h ^ 1) for h in range(heads)])

    def to_chip(array, d):
        return lax.ppermute(array, "head", [(h, (h + 2 * d) % heads) for h in range(heads)])

    def to_owner(array, s):
        return lax.ppermute(array, "ctx", [(c, c - s - 1) for c in range(s + 1, ctx_count)])

    def to_reader(array, s):
        return lax.ppermute(array, "ctx", [(c - s - 1, c) for c in range(s + 1, ctx_count)])

    everyone = lax.all_to_all(
        jnp.broadcast_to(selected.reshape(1, 3 * blocks_here), (ctx_count, 3 * blocks_here)),
        "ctx", split_axis=0, concat_axis=0, tiled=True,
    )
    asked, *sent = pl.pallas_call(
        functools.partial(pick_kernel, blocks_here, ctx_count, chips, far, piece),
        in_specs=[smem, hbm, hbm],
        out_specs=[smem] + [whole] * shifts,
        out_shape=[jax.ShapeDtypeStruct((shifts,), jnp.int32)]
        + [piece_type if s in far else block_type for s in range(shifts)],
        scratch_shapes=[pltpu.SemaphoreType.DMA((shifts,))],
        name="pick_rows",
    )(everyone, key_blocks, value_blocks)

    far_mine = jnp.stack([to_reader(sent[s], s) for s in far])
    near_parts = [to_reader(sent[s], s) for s in near]
    far_mine, chosen = lax.optimization_barrier((far_mine, selected))
    far_more = [to_chip(far_mine, d) for d in range(1, chips)]
    stats = pl.pallas_call(
        functools.partial(local_stats_kernel, factor, blocks_here),
        in_specs=[smem] + [whole] * 4,
        out_specs=whole,
        out_shape=stat_type,
        scratch_shapes=[pltpu.VMEM((block_len, block_len), F32)] * 2,
        compiler_params=params(4 * blocks_here * block_bytes + 2 * pair_bytes),
        cost_estimate=cost(30, 4 * tok_rows * feature * 2),
        name="local_stats",
    )(chosen, q2, do2, key_blocks, value_blocks)
    near_parts, far_held, stats = lax.optimization_barrier((near_parts, far_mine, stats))
    near_mine = jnp.stack(near_parts)
    row_sets = [near_mine, swap(near_mine), far_held, swap(far_held)]
    for part in far_more:
        row_sets += [part, swap(part)]

    keep_far, send_far, final, grad_qt = pl.pallas_call(
        functools.partial(
            remote_kernel, factor, scaling, blocks_here, chips, far, near, piece
        ),
        in_specs=[smem] + [whole] * (3 + len(row_sets)),
        out_specs=[whole] * 4,
        out_shape=[far_type, far_type, stat_type, qt_type],
        scratch_shapes=[
            pltpu.VMEM((2,) + remote_shape, BF16),
            pltpu.VMEM((2,) + remote_shape, F32),
            pltpu.VMEM((3, block_len, block_len), F32),
            pltpu.VMEM((3, block_len, block_len), F32),
            pltpu.VMEM((4, 8, block_len), F32),
        ],
        compiler_params=params((10 * shifts + 4 * blocks_here) * block_bytes + 6 * pair_bytes),
        cost_estimate=cost(60, 8 * tok_rows * feature * 2),
        name="remote_pairs",
    )(chosen, q2, do2, stats, *row_sets)

    def head_sums(mine, parts, count):
        return pl.pallas_call(
            functools.partial(head_sum_kernel, count),
            in_specs=[whole] * (1 + len(parts)),
            out_specs=[whole] * count,
            out_shape=[piece_type] * count,
            compiler_params=params(4 * count * block_bytes),
            name="head_sum",
        )(mine, *parts)

    chip_far = pl.pallas_call(
        functools.partial(chip_sum_kernel, chips, piece, far, near),
        in_specs=[whole, whole],
        out_specs=[whole] * (chips + len(near)),
        out_shape=[pieces_type(len(far), F32)]
        + [pieces_type(len(far), BF16)] * (chips - 1)
        + [block_type] * len(near),
        compiler_params=params(4 * shifts * block_bytes),
        name="chip_sum",
    )(keep_far, swap(send_far))
    chip_far, final = lax.optimization_barrier((chip_far, final))
    far_sums, near_sums = chip_far[:chips], chip_far[chips:]
    far_parts = [to_chip(far_sums[d], d) for d in range(1, chips)]
    near_back = [to_owner(near_sums[i], s) for i, s in enumerate(near)]
    square = (block_len, block_len)
    ds_bytes = block_len * block_len * 2
    keep_own, send_own, ds_own = pl.pallas_call(
        functools.partial(local_kernel, factor, scaling, blocks_here),
        in_specs=[smem] + [whole] * 5,
        out_specs=[whole] * 3,
        out_shape=[
            own_type,
            own_type,
            jax.ShapeDtypeStruct((4 * blocks_here,) + square, BF16),
        ],
        scratch_shapes=[pltpu.VMEM((2,) + local_shape, F32)],
        compiler_params=params(12 * blocks_here * block_bytes + 4 * blocks_here * ds_bytes),
        cost_estimate=cost(60, 8 * tok_rows * feature * 2),
        name="local_pairs",
    )(chosen, q2, do2, key_blocks, value_blocks, final)
    far_parts, near_back, keep_own, send_own = lax.optimization_barrier(
        (far_parts, near_back, keep_own, send_own)
    )
    own_sums = pl.pallas_call(
        functools.partial(own_sum_kernel, chips, piece, near),
        in_specs=[smem] + [whole] * (2 + len(near)),
        out_specs=[whole] * chips,
        out_shape=[pieces_type(blocks_here, F32)]
        + [pieces_type(blocks_here, BF16)] * (chips - 1),
        scratch_shapes=[pltpu.VMEM(local_shape, F32)],
        compiler_params=params((8 * blocks_here + len(near)) * block_bytes),
        name="own_sum",
    )(asked, keep_own, swap(send_own), *near_back)
    own_parts = [to_chip(own_sums[d], d) for d in range(1, chips)]
    far_out = head_sums(far_sums[0], far_parts, len(far))
    far_back = [to_owner(far_out[i], s) for i, s in enumerate(far)]
    returned = pl.pallas_call(
        functools.partial(far_return_kernel, far),
        in_specs=[smem] + [whole] * len(far),
        out_specs=whole,
        out_shape=pieces_type(blocks_here, F32),
        compiler_params=params((2 * blocks_here + len(far)) * block_bytes),
        cost_estimate=cost(600, 8 * tok_rows * feature * 2),
        name="far_returns",
    )(asked, *far_back)
    mine = pl.pallas_call(
        owner_kernel,
        in_specs=[whole] * (1 + chips),
        out_specs=whole,
        out_shape=pieces_type(blocks_here, BF16),
        compiler_params=params(6 * blocks_here * block_bytes),
        name="owner_sum",
    )(returned, own_sums[0], *own_parts)
    mine, ds_own = lax.optimization_barrier((mine, ds_own))
    gathered = [to_chip(mine, d) for d in range(1, chips)]
    grad_q = pl.pallas_call(
        functools.partial(query_kernel, scaling, blocks_here),
        in_specs=[smem] + [whole] * 3,
        out_specs=whole,
        out_shape=jax.ShapeDtypeStruct((tok_rows, feature), BF16),
        scratch_shapes=[pltpu.VMEM((feature, block_len), F32)],
        compiler_params=params(5 * blocks_here * block_bytes + 4 * blocks_here * ds_bytes),
        cost_estimate=cost(30, 8 * tok_rows * feature * 2),
        name="query_grads",
    )(chosen, key_blocks, grad_qt, ds_own)
    gathered, grad_q = lax.optimization_barrier((gathered, grad_q))
    spread = [mine, swap(mine)]
    for part in gathered:
        spread += [part, swap(part)]
    grad_keys, grad_values = pl.pallas_call(
        functools.partial(spread_kernel, chips, piece),
        in_specs=[whole] * len(spread),
        out_specs=[whole] * 2,
        out_shape=[own_type] * 2,
        compiler_params=params(4 * blocks_here * block_bytes),
        name="spread",
    )(*spread)
    return (
        grad_q.reshape(tok_rows, head_count, feature),
        grad_keys.reshape(tok_rows, feature),
        grad_values.reshape(tok_rows, feature),
    )


def solution(mesh):
    return jax.shard_map(
        body,
        mesh=mesh,
        in_specs=(
            P("ctx", "head", None),
            P("ctx", None),
            P("ctx", None),
            P("ctx", "head", None),
            P("ctx", None),
        ),
        out_specs=(P("ctx", "head", None), P("ctx", None), P("ctx", None)),
        check_vma=False,
    )
```

```python
import functools
import math

import jax
import jax.numpy as jnp
from jax import lax
from jax.experimental import pallas as pl
from jax.experimental.pallas import tpu as pltpu
from jax.sharding import PartitionSpec as P

F32 = jnp.float32
BF16 = jnp.bfloat16
VMEM_LIMIT = 56 * 1024 * 1024


def dot_nt(a, b):
    return lax.dot_general(a, b, (((1,), (1,)), ((), ())), preferred_element_type=F32)


def dot_nn(a, b):
    return lax.dot_general(a, b, (((1,), (0,)), ((), ())), preferred_element_type=F32)


def slot_of(chosen, blocks_here, row, t):
    ctx_self = lax.axis_index("ctx")
    entry = chosen[row, t]
    owner = lax.div(entry, jnp.int32(blocks_here))
    apart = ctx_self - owner
    slot = jnp.where(apart == 0, entry - owner * blocks_here, blocks_here + apart - 1)
    return jnp.where(entry != ctx_self * blocks_here + row, slot, -1)


def pick_kernel(blocks_here, count, chips, far, piece, chosen, keys, values, asked, *refs):
    outs, sems = refs[:-1], refs[-1]
    ctx_self = lax.axis_index("ctx")
    place = lax.axis_index("head")
    core, chip = lax.rem(place, 2), lax.div(place, 2)
    first = ctx_self * blocks_here
    span = pl.ds(pl.multiple_of(chip * piece, piece), piece)

    def copy(source, s, slot):
        rows = source.at[slot, span, :] if s in far else source.at[slot]
        return pltpu.make_async_copy(rows, outs[s], sems.at[s])

    for s in range(count - 1):
        peer = ctx_self + s + 1
        near = jnp.minimum(peer, count - 1)
        found = jnp.int32(0)
        for row in range(blocks_here):
            for t in range(3):
                entry = chosen[near, row * 3 + t]
                hit = (entry >= first) & (entry < first + blocks_here)
                found = jnp.where(hit, entry - first + 1, found)
        found = jnp.where(peer < count, found, 0)
        asked[s] = found
        slot = jnp.maximum(found - 1, 0)

        @pl.when(core == 0)
        def _():
            copy(keys, s, slot).start()

        @pl.when(core != 0)
        def _():
            copy(values, s, slot).start()

    for s in range(count - 1):
        copy(keys, s, 0).wait()


def chip_sum_kernel(chips, piece, far, near, mine, theirs, *outs):
    chip = lax.div(lax.axis_index("head"), 2)
    for d in range(chips):
        target = lax.rem(chip + d, chips)
        span = pl.ds(pl.multiple_of(target * piece, piece), piece)
        for i, s in enumerate(far):
            total = mine[s, span, :].astype(F32) + theirs[s, span, :].astype(F32)
            outs[d][i] = total.astype(outs[d].dtype)
    for i, s in enumerate(near):
        outs[chips + i][...] = (mine[s].astype(F32) + theirs[s].astype(F32)).astype(BF16)


def own_sum_kernel(chips, piece, near, asked, mine, theirs, *refs):
    back, outs, acc = refs[: len(near)], refs[len(near) : -1], refs[-1]
    chip = lax.div(lax.axis_index("head"), 2)
    acc[...] = mine[...].astype(F32) + theirs[...].astype(F32)
    for i, s in enumerate(near):
        slot = asked[s] - 1

        @pl.when(slot >= 0)
        def _():
            acc[slot] += back[i][...].astype(F32)

    for d in range(chips):
        target = lax.rem(chip + d, chips)
        span = pl.ds(pl.multiple_of(target * piece, piece), piece)
        outs[d][...] = acc[:, span, :].astype(outs[d].dtype)


def head_sum_kernel(count, mine, *refs):
    parts, outs = refs[: len(refs) - count], refs[len(refs) - count :]
    for i in range(count):
        total = mine[i]
        for part in parts:
            total = total + part[i].astype(F32)
        outs[i][...] = total.astype(BF16)


def fold(array, reduce):
    rows, lanes = array.shape
    return reduce(array.reshape(rows // 8, 8, lanes), axis=0)


def causal(array, first_col, first_pos, other):
    col = lax.broadcasted_iota(jnp.int32, array.shape, 0) + first_col
    pos = lax.broadcasted_iota(jnp.int32, array.shape, 1) + first_pos
    return jnp.where(col <= pos, array, other)


def row_sums(s_ref, dp_ref, factor):
    block_len = s_ref.shape[0]
    step = min(64, block_len)
    spans = [pl.ds(c, step) for c in range(0, block_len, step)]
    top = fold(s_ref[spans[0], :], jnp.max)
    for span in spans[1:]:
        top = jnp.maximum(top, fold(s_ref[span, :], jnp.max))
    top = jnp.max(top, axis=0, keepdims=True) * factor
    total = weighted = jnp.zeros((8, block_len), F32)
    for span in spans:
        terms = jnp.exp2(s_ref[span, :] * factor - top)
        total = total + fold(terms, jnp.sum)
        weighted = weighted + fold(terms * dp_ref[span, :], jnp.sum)
    total = jnp.sum(total, axis=0, keepdims=True)
    return top, total, jnp.sum(weighted, axis=0, keepdims=True)


def local_stats_kernel(factor, blocks_here, chosen, q, do, keys, values, stats, s_buf, dp_buf):
    block_len = keys.shape[1]
    half = block_len // 2

    def per_row(row, _):
        start = row * block_len
        span = pl.ds(start, block_len)
        late = pl.ds(start + half, half)

        s_buf[:half, :] = causal(dot_nt(keys[row, :half], q[span, :]), 0, 0, -jnp.inf)
        s_buf[half:, :half] = jnp.full((half, half), -jnp.inf, F32)
        s_buf[half:, half:] = causal(dot_nt(keys[row, half:], q[late, :]), 0, 0, -jnp.inf)
        dp_buf[:half, :] = dot_nt(values[row, :half], do[span, :])
        dp_buf[half:, :half] = jnp.zeros((half, half), F32)
        dp_buf[half:, half:] = dot_nt(values[row, half:], do[late, :])
        top, total, weighted = row_sums(s_buf, dp_buf, factor)
        stats[row, 0:1, :] = top
        stats[row, 1:2, :] = total
        stats[row, 2:3, :] = weighted
        for t in range(3):
            slot = slot_of(chosen, blocks_here, row, t)

            @pl.when((slot >= 0) & (slot < blocks_here))
            def _():
                s_buf[...] = dot_nt(keys[slot], q[span, :])
                dp_buf[...] = dot_nt(values[slot], do[span, :])
                more_top, more, more_weighted = row_sums(s_buf, dp_buf, factor)
                old = stats[row, 0:1, :]
                top = jnp.maximum(old, more_top)
                scale_old = jnp.exp2(old - top)
                scale_new = jnp.exp2(more_top - top)
                stats[row, 0:1, :] = top
                stats[row, 1:2, :] = stats[row, 1:2, :] * scale_old + more * scale_new
                stats[row, 2:3, :] = stats[row, 2:3, :] * scale_old + more_weighted * scale_new

        return 0

    lax.fori_loop(0, blocks_here, per_row, 0)


def remote_kernel(
    factor, scaling, blocks_here, chips, far, near, piece, chosen, q, do, stats, *refs
):
    near_refs, far_refs, refs = refs[:2], refs[2 : 2 + 2 * chips], refs[2 + 2 * chips :]
    keep, send, final, grad_qt, rows, acc, s_buf, dp_buf, parts = refs
    place = lax.axis_index("head")
    core, chip = lax.rem(place, 2), lax.div(place, 2)
    block_len = rows.shape[2]

    def lay(kind, which):
        for i, s in enumerate(near):
            rows[kind, s] = near_refs[which][i]
        for d in range(chips):
            source = lax.rem(chip + chips - d, chips)
            span = pl.ds(pl.multiple_of(source * piece, piece), piece)
            for i, s in enumerate(far):
                rows[kind, s, span, :] = far_refs[2 * d + which][i]

    @pl.when(core == 0)
    def _():
        lay(0, 0)
        lay(1, 1)

    @pl.when(core != 0)
    def _():
        lay(0, 1)
        lay(1, 0)

    acc[...] = jnp.zeros_like(acc)

    def per_row(row, _):
        span = pl.ds(row * block_len, block_len)
        parts[0, 0:3, :] = stats[row, 0:3, :]
        for t in range(3):
            slot = slot_of(chosen, blocks_here, row, t) - blocks_here

            @pl.when(slot >= 0)
            def _():
                s_buf[t] = dot_nt(rows[0, slot], q[span, :])
                dp_buf[t] = dot_nt(rows[1, slot], do[span, :])
                top, total, weighted = row_sums(s_buf.at[t], dp_buf.at[t], factor)
                parts[t + 1, 0:1, :] = top
                parts[t + 1, 1:2, :] = total
                parts[t + 1, 2:3, :] = weighted

            @pl.when(slot < 0)
            def _():
                parts[t + 1, 0:1, :] = jnp.full((1, block_len), -jnp.inf, F32)
                parts[t + 1, 1:3, :] = jnp.zeros((2, block_len), F32)

        top = parts[0, 0:1, :]
        for t in range(3):
            top = jnp.maximum(top, parts[t + 1, 0:1, :])
        total = jnp.zeros_like(top)
        weighted = jnp.zeros_like(top)
        for t in range(4):
            scale = jnp.exp2(parts[t, 0:1, :] - top)
            total = total + scale * parts[t, 1:2, :]
            weighted = weighted + scale * parts[t, 2:3, :]
        final[row, 0:1, :] = top + jnp.log2(total)
        final[row, 1:2, :] = weighted / total
        grad_qt[row] = jnp.zeros_like(grad_qt[row])
        for t in range(3):
            slot = slot_of(chosen, blocks_here, row, t) - blocks_here

            @pl.when(slot >= 0)
            def _():
                level = final[row, 0:1, :]
                delta = final[row, 1:2, :]
                weights = jnp.exp2(s_buf[t] * factor - level)
                dscores = (weights * (dp_buf[t] - delta)).astype(BF16)
                acc[1, slot] += dot_nn(weights.astype(BF16), do[span, :])
                acc[0, slot] += dot_nn(dscores, q[span, :])
                grad_qt[row] += dot_nn(rows[0, slot].T, dscores)

        return 0

    lax.fori_loop(0, blocks_here, per_row, 0)
    keep_scale = jnp.where(core == 0, scaling, 1.0)
    send_scale = jnp.where(core == 0, 1.0, scaling)
    keep[...] = (acc[core] * keep_scale).astype(BF16)
    send[...] = (acc[1 - core] * send_scale).astype(BF16)


def local_kernel(
    factor, scaling, blocks_here, chosen, q, do, keys, values, final, grad_qt,
    keep, send, grad_q,
    acc, total_qt,
):
    core = lax.rem(lax.axis_index("head"), 2)
    block_len = keys.shape[1]
    half = block_len // 2
    acc[...] = jnp.zeros_like(acc)

    def per_row(row, _):
        start = row * block_len
        span = pl.ds(start, block_len)

        def rows_from(ref, first):
            return ref[pl.ds(start + first, block_len - first), :]

        def products(slot, c, first):
            cut = pl.ds(c, half)
            scores = dot_nt(keys[slot, cut, :], rows_from(q, first))
            return scores, dot_nt(values[slot, cut, :], rows_from(do, first))

        def pair(slot, seconds, masked):
            parts = ((0, 0), (half, seconds))
            ready = [products(slot, c, first) for c, first in parts]
            sides = []
            for (c, first), (scores, dprobs) in zip(parts, ready):
                weights = jnp.exp2(scores * factor - final[row, 0:1, first:])
                if masked:
                    weights = causal(weights, c, first, 0.0)
                dscores = (weights * (dprobs - final[row, 1:2, first:])).astype(BF16)
                sides.append((weights.astype(BF16), dscores))
            for (c, first), (weights, dscores) in zip(parts, sides):
                cut = pl.ds(c, half)
                acc[1, slot, cut, :] += dot_nn(weights, rows_from(do, first))
                acc[0, slot, cut, :] += dot_nn(dscores, rows_from(q, first))
                total_qt[:, first:] += dot_nn(keys[slot, cut, :].T, dscores)

        total_qt[...] = grad_qt[row]
        pair(row, half, True)
        for t in range(3):
            slot = slot_of(chosen, blocks_here, row, t)

            @pl.when((slot >= 0) & (slot < blocks_here))
            def _():
                pair(slot, 0, False)

        grad_q[span, :] = (total_qt[...].T * scaling).astype(BF16)
        return 0

    lax.fori_loop(0, blocks_here, per_row, 0)
    keep_scale = jnp.where(core == 0, scaling, 1.0)
    send_scale = jnp.where(core == 0, 1.0, scaling)
    keep[...] = (acc[core] * keep_scale).astype(BF16)
    send[...] = (acc[1 - core] * send_scale).astype(BF16)


def far_return_kernel(far, asked, *refs):
    back, acc = refs[:-1], refs[-1]
    acc[...] = jnp.zeros_like(acc)
    for i, s in enumerate(far):
        slot = asked[s] - 1

        @pl.when(slot >= 0)
        def _():
            acc[slot] += back[i][...].astype(F32)


def owner_kernel(returned, mine, *refs):
    others, out = refs[:-1], refs[-1]
    total = mine[...] + returned[...]
    for part in others:
        total = total + part[...].astype(F32)
    out[...] = total.astype(BF16)


def spread_kernel(chips, piece, *refs):
    pieces, (grad_k, grad_v) = refs[: 2 * chips], refs[2 * chips :]
    place = lax.axis_index("head")
    core, chip = lax.rem(place, 2), lax.div(place, 2)

    def lay(out, which):
        for d in range(chips):
            source = lax.rem(chip + chips - d, chips)
            span = pl.ds(pl.multiple_of(source * piece, piece), piece)
            out[:, span, :] = pieces[2 * d + which][...]

    @pl.when(core == 0)
    def _():
        lay(grad_k, 0)
        lay(grad_v, 1)

    @pl.when(core != 0)
    def _():
        lay(grad_k, 1)
        lay(grad_v, 0)


def params(size):
    return pltpu.CompilerParams(vmem_limit_bytes=min(size + 12 * 1024 * 1024, VMEM_LIMIT))


def body(queries, keys, values, dout, selected):
    tok_rows, head_count, feature = queries.shape
    blocks_here = selected.shape[0]
    block_len = tok_rows // blocks_here
    ctx_count = lax.axis_size("ctx")
    heads = lax.axis_size("head")
    chips = heads // 2
    piece = block_len // chips
    scaling = 1.0 / math.sqrt(feature)
    factor = scaling * math.log2(math.e)
    shifts = ctx_count - 1
    far = [s for s in reversed(range(shifts - 1)) if 2 * (s + 2) >= ctx_count]
    near = [shifts - 1] + [s for s in range(shifts - 1) if s not in far]

    q2 = queries.reshape(tok_rows, feature)
    do2 = dout.reshape(tok_rows, feature)
    key_blocks = keys.reshape(blocks_here, block_len, feature)
    value_blocks = values.reshape(blocks_here, block_len, feature)
    remote_shape = (shifts, block_len, feature)
    local_shape = (blocks_here, block_len, feature)

    smem = pl.BlockSpec(memory_space=pltpu.SMEM)
    whole = pl.BlockSpec(memory_space=pltpu.VMEM)
    hbm = pl.BlockSpec(memory_space=pltpu.HBM)
    stat_type = jax.ShapeDtypeStruct((blocks_here, 8, block_len), F32)
    far_type = jax.ShapeDtypeStruct(remote_shape, BF16)
    own_type = jax.ShapeDtypeStruct(local_shape, BF16)
    block_type = jax.ShapeDtypeStruct((block_len, feature), BF16)
    piece_type = jax.ShapeDtypeStruct((piece, feature), BF16)
    qt_type = jax.ShapeDtypeStruct((blocks_here, feature, block_len), F32)
    pair_flops = 2 * block_len * block_len * feature
    block_bytes = block_len * feature * 2
    pair_bytes = block_len * block_len * 4

    def pieces_type(count, dtype):
        return jax.ShapeDtypeStruct((count, piece, feature), dtype)

    def cost(matmuls, size):
        return pl.CostEstimate(
            flops=matmuls * pair_flops, bytes_accessed=size, transcendentals=matmuls * block_len**2
        )

    def swap(array):
        return lax.ppermute(array, "head", [(h, h ^ 1) for h in range(heads)])

    def to_chip(array, d):
        return lax.ppermute(array, "head", [(h, (h + 2 * d) % heads) for h in range(heads)])

    def to_owner(array, s):
        return lax.ppermute(array, "ctx", [(c, c - s - 1) for c in range(s + 1, ctx_count)])

    def to_reader(array, s):
        return lax.ppermute(array, "ctx", [(c - s - 1, c) for c in range(s + 1, ctx_count)])

    everyone = lax.all_to_all(
        jnp.broadcast_to(selected.reshape(1, 3 * blocks_here), (ctx_count, 3 * blocks_here)),
        "ctx", split_axis=0, concat_axis=0, tiled=True,
    )
    asked, *sent = pl.pallas_call(
        functools.partial(pick_kernel, blocks_here, ctx_count, chips, far, piece),
        in_specs=[smem, hbm, hbm],
        out_specs=[smem] + [whole] * shifts,
        out_shape=[jax.ShapeDtypeStruct((shifts,), jnp.int32)]
        + [piece_type if s in far else block_type for s in range(shifts)],
        scratch_shapes=[pltpu.SemaphoreType.DMA((shifts,))],
        name="pick_rows",
    )(everyone, key_blocks, value_blocks)

    far_mine = jnp.stack([to_reader(sent[s], s) for s in far])
    near_parts = [to_reader(sent[s], s) for s in near]
    far_mine, chosen = lax.optimization_barrier((far_mine, selected))
    far_more = [to_chip(far_mine, d) for d in range(1, chips)]
    stats = pl.pallas_call(
        functools.partial(local_stats_kernel, factor, blocks_here),
        in_specs=[smem] + [whole] * 4,
        out_specs=whole,
        out_shape=stat_type,
        scratch_shapes=[pltpu.VMEM((block_len, block_len), F32)] * 2,
        compiler_params=params(4 * blocks_here * block_bytes + 2 * pair_bytes),
        cost_estimate=cost(30, 4 * tok_rows * feature * 2),
        name="local_stats",
    )(chosen, q2, do2, key_blocks, value_blocks)
    near_parts, far_held, stats = lax.optimization_barrier((near_parts, far_mine, stats))
    near_mine = jnp.stack(near_parts)
    row_sets = [near_mine, swap(near_mine), far_held, swap(far_held)]
    for part in far_more:
        row_sets += [part, swap(part)]

    keep_far, send_far, final, grad_qt = pl.pallas_call(
        functools.partial(
            remote_kernel, factor, scaling, blocks_here, chips, far, near, piece
        ),
        in_specs=[smem] + [whole] * (3 + len(row_sets)),
        out_specs=[whole] * 4,
        out_shape=[far_type, far_type, stat_type, qt_type],
        scratch_shapes=[
            pltpu.VMEM((2,) + remote_shape, BF16),
            pltpu.VMEM((2,) + remote_shape, F32),
            pltpu.VMEM((3, block_len, block_len), F32),
            pltpu.VMEM((3, block_len, block_len), F32),
            pltpu.VMEM((4, 8, block_len), F32),
        ],
        compiler_params=params((10 * shifts + 4 * blocks_here) * block_bytes + 6 * pair_bytes),
        cost_estimate=cost(60, 8 * tok_rows * feature * 2),
        name="remote_pairs",
    )(chosen, q2, do2, stats, *row_sets)

    def head_sums(mine, parts, count):
        return pl.pallas_call(
            functools.partial(head_sum_kernel, count),
            in_specs=[whole] * (1 + len(parts)),
            out_specs=[whole] * count,
            out_shape=[piece_type] * count,
            compiler_params=params(4 * count * block_bytes),
            name="head_sum",
        )(mine, *parts)

    chip_far = pl.pallas_call(
        functools.partial(chip_sum_kernel, chips, piece, far, near),
        in_specs=[whole, whole],
        out_specs=[whole] * (chips + len(near)),
        out_shape=[pieces_type(len(far), F32)]
        + [pieces_type(len(far), BF16)] * (chips - 1)
        + [block_type] * len(near),
        compiler_params=params(4 * shifts * block_bytes),
        name="chip_sum",
    )(keep_far, swap(send_far))
    chip_far, final = lax.optimization_barrier((chip_far, final))
    far_sums, near_sums = chip_far[:chips], chip_far[chips:]
    far_parts = [to_chip(far_sums[d], d) for d in range(1, chips)]
    near_back = [to_owner(near_sums[i], s) for i, s in enumerate(near)]
    keep_own, send_own, grad_q = pl.pallas_call(
        functools.partial(local_kernel, factor, scaling, blocks_here),
        in_specs=[smem] + [whole] * 6,
        out_specs=[whole] * 3,
        out_shape=[own_type, own_type, jax.ShapeDtypeStruct((tok_rows, feature), BF16)],
        scratch_shapes=[
            pltpu.VMEM((2,) + local_shape, F32),
            pltpu.VMEM((feature, block_len), F32),
        ],
        compiler_params=params(14 * blocks_here * block_bytes),
        cost_estimate=cost(60, 8 * tok_rows * feature * 2),
        name="local_pairs",
    )(chosen, q2, do2, key_blocks, value_blocks, final, grad_qt)
    far_parts, near_back, keep_own, send_own = lax.optimization_barrier(
        (far_parts, near_back, keep_own, send_own)
    )
    own_sums = pl.pallas_call(
        functools.partial(own_sum_kernel, chips, piece, near),
        in_specs=[smem] + [whole] * (2 + len(near)),
        out_specs=[whole] * chips,
        out_shape=[pieces_type(blocks_here, F32)]
        + [pieces_type(blocks_here, BF16)] * (chips - 1),
        scratch_shapes=[pltpu.VMEM(local_shape, F32)],
        compiler_params=params((8 * blocks_here + len(near)) * block_bytes),
        name="own_sum",
    )(asked, keep_own, swap(send_own), *near_back)
    own_parts = [to_chip(own_sums[d], d) for d in range(1, chips)]
    far_out = head_sums(far_sums[0], far_parts, len(far))
    far_back = [to_owner(far_out[i], s) for i, s in enumerate(far)]
    returned = pl.pallas_call(
        functools.partial(far_return_kernel, far),
        in_specs=[smem] + [whole] * len(far),
        out_specs=whole,
        out_shape=pieces_type(blocks_here, F32),
        compiler_params=params((2 * blocks_here + len(far)) * block_bytes),
        cost_estimate=cost(600, 8 * tok_rows * feature * 2),
        name="far_returns",
    )(asked, *far_back)
    mine = pl.pallas_call(
        owner_kernel,
        in_specs=[whole] * (1 + chips),
        out_specs=whole,
        out_shape=pieces_type(blocks_here, BF16),
        compiler_params=params(6 * blocks_here * block_bytes),
        name="owner_sum",
    )(returned, own_sums[0], *own_parts)
    spread = [mine, swap(mine)]
    for d in range(1, chips):
        part = to_chip(mine, d)
        spread += [part, swap(part)]
    grad_keys, grad_values = pl.pallas_call(
        functools.partial(spread_kernel, chips, piece),
        in_specs=[whole] * len(spread),
        out_specs=[whole] * 2,
        out_shape=[own_type] * 2,
        compiler_params=params(4 * blocks_here * block_bytes),
        name="spread",
    )(*spread)
    return (
        grad_q.reshape(tok_rows, head_count, feature),
        grad_keys.reshape(tok_rows, feature),
        grad_values.reshape(tok_rows, feature),
    )


def solution(mesh):
    return jax.shard_map(
        body,
        mesh=mesh,
        in_specs=(
            P("ctx", "head", None),
            P("ctx", None),
            P("ctx", None),
            P("ctx", "head", None),
            P("ctx", None),
        ),
        out_specs=(P("ctx", "head", None), P("ctx", None), P("ctx", None)),
        check_vma=False,
    )
```
